32 devices in a mesh: docs: 2 (over y), seq: 16 (over z, x, core).
Axes of the slice: x: 2, y: 2, z: 4, core: 2. Of those that a mesh axis runs over, the one named last changes fastest.
Arguments:
- tokens: bfloat16 [8, 1024, 768], P('docs', 'seq'), may hold values from -6 to 6
- qkv_weight: bfloat16 [2, 768, 2304], P(None, ('docs', 'seq')), may hold values from -0.3125 to 0.3125
- out_weight: bfloat16 [2, 768, 768], P(None, ('docs', 'seq')), may hold values from -1.75 to 1.75
- up_weight: bfloat16 [2, 768, 3072], P(None, ('docs', 'seq')), may hold values from -0.21875 to 0.21875
- down_weight: bfloat16 [2, 3072, 768], P(None, ('docs', 'seq')), may hold values from -0.109375 to 0.109375
- norm_gains: bfloat16 [2, 2, 768], P(None, None, ('docs', 'seq')), may hold values from 0.25 to 1.75
- doc_lengths: int32 [8], P('docs'), may hold values from 128 to 1024, as said below
- global_ids: int32 [8, 2], P('docs'), may hold values from 0 to 15, as said below
- random_ids: int32 [16, 8, 3], P(None, 'docs'), may hold values from 0 to 15, all different within a row; in each aligned block of 4 rows (0 to 3, 4 to 7, ..., all dimensions but the last counted through in order) at most 2 rows name the same one
- cotangent: bfloat16 [8, 1024, 768], P('docs', 'seq'), may hold values from -6 to 6
Outputs:
- result: bfloat16 [8, 1024, 768], P('docs', 'seq')
- grad_tokens: float32 [8, 1024, 768], P('docs', 'seq')
- grad_qkv: float32 [2, 768, 2304], P(None, 'docs', 'seq')
- grad_out: float32 [2, 768, 768], P(None, 'docs', 'seq')
- grad_up: float32 [2, 768, 3072], P(None, 'docs', 'seq')
- grad_down: float32 [2, 3072, 768], P(None, 'docs', 'seq')
- grad_gains: float32 [2, 2, 768], P(None, None, ('docs', 'seq'))
The draws below stay inside these ranges and needn't reach their ends.
Inputs may be any that keep to these rules, and one draw needn't show every extreme that they name: `doc_lengths`: every document's length covers its global blocks; in each group of 4 documents (one index of docs) one document has all 1024 tokens. `global_ids`: the 2 global blocks of a document are distinct neighbouring block positions (modulo 16); the global blocks of a group's 4 documents together fill 2 * 4 consecutive positions modulo 16, so no position is global in more than 1 documents of a group, and one is in 1. `random_ids`: A query block's list names 3 different blocks; over the 4 documents of one group, the lists of one query block name no block more than 2 times, and some name one exactly 2 times.
All inputs are finite; a program needn't handle non-finite values.
Results may differ from the reference program's by a relative error of at most 0.035.
The reference program's roundings to bfloat16 on the way count: a program that leaves them out, or rounds other values in their place, can miss the bound.
Values may be sent and summed in bfloat16 or wider, within the bound.
A program may use at most 320 MiB of HBM per device.

```python
import math
import jax
import jax.numpy as jnp
import numpy as np
from jax import lax

D = 768
HEADS = 12
HEAD = 64
FF = 3072
BLOCK = 64
RAND = 3
GLOB = 2
LAYERS = 2
DOCS_DEV = 4
NB = 16
SEQ_LEN = 1024
DOCS = 8
CAP = 2


def global_layout(key):
    groups = DOCS // DOCS_DEV
    start_key, order_key, turn_key, choose_key, length_key = jax.random.split(key, 5)
    start = jax.random.randint(start_key, (groups, 1, 1), 0, NB)
    orders = jax.vmap(lambda subkey: jax.random.permutation(subkey, DOCS_DEV))(jax.random.split(order_key, groups))
    turn = jax.random.randint(turn_key, (groups, DOCS_DEV, 1), 0, GLOB)
    member = jnp.arange(GLOB, dtype=jnp.int32)[None, None, :]
    blocks = (start + GLOB * orders[:, :, None] + (member + turn) % GLOB) % NB
    blocks = blocks.reshape(DOCS, GLOB).astype(jnp.int32)
    needed = (jnp.max(blocks, axis=1) + 1) * BLOCK
    raw = jax.random.randint(length_key, (DOCS,), 0, 1 << 20)
    lengths = needed + raw % (SEQ_LEN - needed + 1)
    chosen = jax.random.randint(choose_key, (groups, 1), 0, DOCS_DEV)
    full = (jnp.arange(DOCS_DEV, dtype=jnp.int32)[None, :] == chosen).reshape(DOCS)
    lengths = jnp.where(full, SEQ_LEN, lengths).astype(jnp.int32)
    return (blocks, lengths)


def draw_global_ids(key, part):
    layout = global_layout(key)
    return layout[0]


def draw_doc_lengths(key, part):
    layout = global_layout(key)
    return layout[1]


def levels(key, dims, pieces, least, high):
    loudness = 1.0
    for axis_at, parts in pieces:
        draws = jax.random.uniform(jax.random.fold_in(jax.random.fold_in(key, 6), axis_at), (parts,), jnp.float32, least / len(pieces), high / len(pieces))
        loudness = loudness * jnp.repeat(jnp.exp(draws), dims[axis_at] // parts).reshape((-1,) + (1,) * (len(dims) - 1 - axis_at))
    return loudness


def shared_out(key, own, number, rows, count, top, limit, lean):
    order = jax.random.permutation(key, count)
    heavy_load, ordinary = load_shares(count, rows * top, limit, lean, True), load_shares(count, rows * top, limit, lean, False)
    places = jnp.arange(count)

    def named(tallies, turn):
        used = int((tallies > 0).sum())
        fixed = max(1, used // 4)
        moved = fixed + (places - fixed + turn * (used - fixed)) % max(1, count - fixed)
        return jnp.zeros((count,), jnp.int32).at[order[jnp.where(places < fixed, places, moved)]].set(jnp.asarray(tallies, jnp.int32))

    tallies = jnp.where(number % 4 == 0, named(heavy_load, number // 4), named(ordinary, number - number // 4 - 1))
    mixed = jax.random.permutation(jax.random.fold_in(own, 3), count)
    giver, sink = mixed[0:count // 2 * 2:2], mixed[1:count // 2 * 2:2]
    room = jnp.minimum(tallies[giver] - 1, limit - tallies[sink]) // 2
    room = jnp.where((giver == order[0]) | (sink == order[0]) | (tallies[sink] == 0), 0, jnp.maximum(room, 0))
    moved = jax.random.randint(jax.random.fold_in(own, 4), (count // 2,), 0, 1 << 20) % (room + 1)
    tallies = tallies.at[giver].add(-moved).at[sink].add(moved)
    items = jnp.searchsorted(jnp.cumsum(tallies), jnp.arange(rows * top), side="right").astype(jnp.int32)
    table = items.reshape(top, rows).T
    table = table[jax.random.permutation(jax.random.fold_in(own, 1), rows)]
    turn = jax.random.randint(jax.random.fold_in(own, 2), (rows, 1), 0, top)
    return jnp.take_along_axis(table, (jnp.arange(top)[None, :] + turn) % top, axis=1)


def load_shares(number_of, total, most, skew, full):
    loads = [(1 << 20) // math.isqrt(rank ** skew) + 1 for rank in range(1, number_of + 1)]
    largest = most if full else min(most, max(-(-total // number_of), total * loads[0] // sum(loads)))
    least = 1 if total - largest >= number_of - 1 else 0
    given, surplus = [largest] + [least] * (number_of - 1), total - largest - least * (number_of - 1)
    while surplus > 0:
        movable = [i for i in range(1, number_of) if given[i] < largest] or [i for i in range(1, number_of) if given[i] < most]
        pool, remaining = sum([loads[i] for i in movable]), surplus
        for i in movable:
            more = min(most - given[i], max(1, remaining * loads[i] // pool), surplus)
            given[i] = given[i] + more
            surplus = surplus - more
    return np.array(given)


def noise(own_key, extent, deviation, reach, cuts=(), held_as=jnp.bfloat16):
    values = jax.random.normal(own_key, extent, jnp.float32) * deviation
    if len(cuts) > 0:
        values = levels(own_key, extent, cuts, -0.22, 0.18) * values
    return jnp.clip(values, min=-reach, max=reach).astype(held_as)


def setup_inputs(seed: int = 0) -> dict:
    splits = jax.random.split(jax.random.key(seed), 11)
    tokens = noise(splits[0], (DOCS, SEQ_LEN, D), 1.0, 6.0, ((0, 2), (1, 16)))
    qkv_weight = noise(splits[1], (LAYERS, D, 3 * D), (D // 2) ** -0.5, 0.3125, ((1, 32),))
    out_weight = noise(splits[2], (LAYERS, D, D), (D // 64) ** -0.5, 1.75, ((1, 32),))
    up_weight = noise(splits[3], (LAYERS, D, FF), D ** -0.5, 0.21875, ((1, 32),))
    down_weight = noise(splits[4], (LAYERS, FF, D), FF ** -0.5, 0.109375, ((1, 32),))
    norm_gains = jnp.clip(1.0 + 0.15 * jax.random.normal(splits[5], (LAYERS, 2, D), jnp.float32), 0.25, 1.75).astype(jnp.bfloat16)
    doc_lengths = draw_doc_lengths(jax.random.fold_in(splits[10], 71), 0)
    global_ids = draw_global_ids(jax.random.fold_in(splits[10], 71), 0)
    random_ids_keys = jax.random.split(jax.random.fold_in(splits[8], 1), NB * DOCS // DOCS_DEV)
    random_ids_turns = jax.random.permutation(jax.random.fold_in(splits[8], 3), NB * DOCS // DOCS_DEV)
    random_ids = jax.vmap(lambda own, number: shared_out(jax.random.fold_in(splits[8], 2), own, number, DOCS_DEV, NB, RAND, CAP, 1))(random_ids_keys, random_ids_turns).reshape((NB, DOCS, RAND))
    cotangent = noise(splits[9], (DOCS, SEQ_LEN, D), 1.0, 6.0, ((0, 2), (1, 16)))
    return dict(tokens=tokens, qkv_weight=qkv_weight, out_weight=out_weight, up_weight=up_weight, down_weight=down_weight, norm_gains=norm_gains, doc_lengths=doc_lengths, global_ids=global_ids, random_ids=random_ids, cotangent=cotangent)


NEGATIVE = -1e+30
EPSILON = 1e-05

@jax.custom_vjp
def low(v):
    return lax.optimization_barrier(v.astype(jnp.bfloat16)).astype(jnp.float32)

@jax.custom_vjp
def low_back(v):
    return v

def low_keep(v):
    return (low(v), None)

def low_pass(kept, grad):
    return (grad,)

def back_keep(v):
    return (v, None)

def back_low(kept, grad):
    return (low(grad),)
low.defvjp(low_keep, low_pass)
low_back.defvjp(back_keep, back_low)

def product(left, right):
    return jnp.dot(left, right, precision=lax.Precision.HIGHEST)

def norm_rows(values, gain):
    centre = values - lax.optimization_barrier(jnp.mean(values, axis=-1, keepdims=True))
    spread = lax.optimization_barrier(jnp.mean(centre * centre, axis=-1, keepdims=True))
    return centre * lax.rsqrt(spread + EPSILON) * gain

def attend_document(inputs):
    query, key, value, length, global_blocks, random_blocks = inputs
    scale = HEAD ** (-0.5)
    inside = jnp.arange(SEQ_LEN, dtype=jnp.int32) < length
    query_blocks = query.reshape(NB, BLOCK, HEADS, HEAD)
    key_blocks = key.reshape(NB, BLOCK, HEADS, HEAD)
    value_blocks = value.reshape(NB, BLOCK, HEADS, HEAD)
    order = jnp.arange(NB, dtype=jnp.int32)
    window = jnp.stack([(order - 1) % NB, order, (order + 1) % NB], axis=1)
    listed = jnp.concatenate([window, random_blocks, jnp.broadcast_to(global_blocks[None, :], (NB, GLOB))], axis=1).astype(jnp.int32)
    span = listed.shape[1] * BLOCK
    listed_keys = key_blocks[listed].reshape(NB, span, HEADS, HEAD)
    listed_values = value_blocks[listed].reshape(NB, span, HEADS, HEAD)
    listed_inside = inside.reshape(NB, BLOCK)[listed].reshape(NB, span)
    scores = low_back(jnp.einsum('ibhd,ijhd->ihbj', query_blocks, listed_keys, precision=lax.Precision.HIGHEST) * scale)
    scores = jnp.where(listed_inside[:, None, None, :], scores, NEGATIVE)
    mixed = jnp.einsum('ihbj,ijhd->ibhd', low(jax.nn.softmax(scores, axis=-1)), listed_values, precision=lax.Precision.HIGHEST)
    whole_keys = key.reshape(SEQ_LEN, HEADS, HEAD)
    whole_values = value.reshape(SEQ_LEN, HEADS, HEAD)
    for member in range(GLOB):
        target = global_blocks[member]
        chosen = query_blocks[target]
        wide_scores = low_back(jnp.einsum('bhd,jhd->hbj', chosen, whole_keys, precision=lax.Precision.HIGHEST) * scale)
        wide_scores = jnp.where(inside[None, None, :], wide_scores, NEGATIVE)
        wide_mixed = jnp.einsum('hbj,jhd->bhd', low(jax.nn.softmax(wide_scores, axis=-1)), whole_values, precision=lax.Precision.HIGHEST)
        mixed = mixed.at[target].set(wide_mixed)
    return mixed.reshape(SEQ_LEN, HEADS * HEAD)

def encoder_layer(hidden, weight_qkv, weight_out, weight_up, weight_down, gain, inside_rows, doc_lengths, global_ids, random_lists):
    projected = low(low_back(product(low(hidden), weight_qkv)))
    query = projected[:, :D].reshape(DOCS, SEQ_LEN, D)
    key = projected[:, D:2 * D].reshape(DOCS, SEQ_LEN, D)
    value = projected[:, 2 * D:].reshape(DOCS, SEQ_LEN, D)
    mixed = lax.map(jax.checkpoint(attend_document), (query, key, value, doc_lengths, global_ids, random_lists))
    mixed = low(low_back(mixed.reshape(DOCS * SEQ_LEN, D)))
    after_attn = hidden + low_back(product(mixed, weight_out))
    normed = norm_rows(after_attn, gain[0])
    up_values = low_back(product(low(normed), weight_up))
    activated = low(jax.nn.gelu(up_values, approximate=True))
    after_ffn = normed + low_back(product(activated, weight_down))
    return jnp.where(inside_rows[:, None], norm_rows(after_ffn, gain[1]), 0.0)

def reference(tokens, qkv_weight, out_weight, up_weight, down_weight, norm_gains, doc_lengths, global_ids, random_ids, cotangent):
    inside_rows = (jnp.arange(SEQ_LEN, dtype=jnp.int32)[None, :] < doc_lengths[:, None]).reshape(DOCS * SEQ_LEN)
    random_lists = jnp.transpose(random_ids, (1, 0, 2))

    def forward(hidden, weight_qkv, weight_out, weight_up, weight_down, gains):
        for layer in range(LAYERS):
            hidden = encoder_layer(hidden, weight_qkv[layer], weight_out[layer], weight_up[layer], weight_down[layer], gains[layer], inside_rows, doc_lengths, global_ids, random_lists)
        return hidden
    output, pullback = jax.vjp(forward, tokens.reshape(DOCS * SEQ_LEN, D).astype(jnp.float32), qkv_weight.astype(jnp.float32), out_weight.astype(jnp.float32), up_weight.astype(jnp.float32), down_weight.astype(jnp.float32), norm_gains.astype(jnp.float32))
    grad_rows, grad_qkv, grad_out, grad_up, grad_down, grad_gains = pullback(cotangent.reshape(DOCS * SEQ_LEN, D).astype(jnp.float32))
    return (output.astype(jnp.bfloat16).reshape(DOCS, SEQ_LEN, D), grad_rows.reshape(DOCS, SEQ_LEN, D), grad_qkv, grad_out, grad_up, grad_down, grad_gains)
```

```python
import functools

import jax
import jax.numpy as jnp
from jax import lax
from jax.experimental import pallas as pl
from jax.experimental.pallas import tpu as pltpu
from jax.sharding import PartitionSpec as P

HEAD = 64
RAND = 3
GLOB = 2
LAYERS = 2


NEGATIVE = -1e30
EPSILON = 1e-05


def with_halo(cells, sides, width):
    for axis, dim in sides:
        count = lax.axis_size(axis)
        head = lax.slice_in_dim(cells, 0, width, axis=dim)
        tail = lax.slice_in_dim(cells, cells.shape[dim] - width, cells.shape[dim], axis=dim)
        cells = jnp.concatenate(
            [
                lax.ppermute(tail, axis, [(i, (i + 1) % count) for i in range(count)]),
                cells,
                lax.ppermute(head, axis, [((i + 1) % count, i) for i in range(count)]),
            ],
            axis=dim,
        )
    return cells


def combined_all(value, axis, join):
    pieces = jax.tree.map(lambda part: lax.all_gather(part, axis), value)
    head = jax.tree.map(lambda part: part[0], pieces)
    tail = jax.tree.map(lambda part: part[1:], pieces)
    so_far, _ = lax.scan(lambda so_far, piece: (join(so_far, piece), None), head, tail)
    return so_far


def norm_rows(values, gain):
    centre = values - jnp.mean(values, axis=-1, keepdims=True)
    spread = jnp.mean(centre * centre, axis=-1, keepdims=True)
    return centre * lax.rsqrt(spread + EPSILON) * gain


def gelu_tanh(values):
    return jax.nn.gelu(values, approximate=True)


def earlier_equal(values):
    length = values.shape[-1]
    order = jnp.arange(length, dtype=jnp.int32)
    before = order[None, :] < order[:, None]
    same = values[..., :, None] == values[..., None, :]
    return jnp.sum(jnp.logical_and(same, before), axis=-1)


def merge_stats(first, second):
    highest = jnp.maximum(first[0], second[0])
    return (
        highest,
        first[1] * jnp.exp(first[0] - highest) + second[1] * jnp.exp(second[0] - highest),
    )


def sparse_probs(query, key_part, key_inside, scale):
    scores = (
        jnp.einsum("kbhd,kjhd->khbj", query, key_part, preferred_element_type=jnp.float32) * scale
    )
    scores = jnp.where(key_inside[:, None, None, :], scores, NEGATIVE)
    expo = jnp.exp(scores - jnp.max(scores, axis=-1, keepdims=True))
    return expo / jnp.sum(expo, axis=-1, keepdims=True)


def global_scores(global_query, local_keys, inside, scale):
    scores = (
        jnp.einsum(
            "ksbhd,kjhd->kshbj", global_query, local_keys, preferred_element_type=jnp.float32
        )
        * scale
    )
    return jnp.where(inside[:, None, None, None, :], scores, NEGATIVE)


def local_any_mesh(
    tokens,
    qkv_weight,
    out_weight,
    up_weight,
    down_weight,
    norm_gains,
    doc_lengths,
    global_ids,
    random_ids,
    cotangent,
):
    nseq = lax.axis_size("seq")
    device = lax.axis_index("seq")
    docs_dev, block, width = tokens.shape
    count = docs_dev * block
    heads = width // HEAD
    scale = HEAD ** (-0.5)
    capacity = max(2, (docs_dev * RAND + nseq - 1) // nseq)
    global_capacity = (docs_dev * GLOB + nseq - 1) // nseq
    entries = docs_dev * RAND
    global_entries = docs_dev * GLOB
    offsets = jnp.arange(block, dtype=jnp.int32)
    inside = (device * block + offsets)[None, :] < doc_lengths[:, None]
    live_rows = inside.reshape(count, 1)
    wanted = random_ids.reshape(nseq, entries)
    wanted_rank = earlier_equal(wanted)
    slot_ids = jnp.arange(capacity, dtype=jnp.int32)
    hits = jnp.logical_and((wanted == device)[:, :, None], wanted_rank[:, :, None] == slot_ids)
    hits = jnp.any(hits.reshape(nseq, docs_dev, RAND, capacity), axis=2)
    hits = jnp.transpose(hits, (0, 2, 1))
    doc_ids = jnp.arange(docs_dev, dtype=jnp.int32)
    send_doc = jnp.sum(jnp.where(hits, doc_ids, 0), axis=2)
    send_live = jnp.any(hits, axis=2)
    owner_pick = hits.astype(jnp.float32)
    listed_here = lax.dynamic_index_in_dim(wanted, device, 0, keepdims=False)
    listed_rank = lax.dynamic_index_in_dim(wanted_rank, device, 0, keepdims=False)
    fetch_slot = listed_here * capacity + listed_rank
    global_block = global_ids.reshape(global_entries)
    global_rank = earlier_equal(global_block)
    global_slot = global_block * global_capacity + global_rank
    own_entry = global_block == device
    owned = jnp.logical_and(
        own_entry[:, None], global_rank[:, None] == jnp.arange(global_capacity, dtype=jnp.int32)
    )
    entry_doc = jnp.arange(global_entries, dtype=jnp.int32) // GLOB
    global_send_doc = jnp.sum(jnp.where(owned, entry_doc[:, None], 0), axis=0)
    global_send_live = jnp.any(owned, axis=0)
    own_flag = jnp.any(own_entry.reshape(docs_dev, GLOB), axis=1)
    own_slot = jnp.sum(jnp.where(own_entry, global_rank, 0).reshape(docs_dev, GLOB), axis=1)
    neighbours = jnp.stack([(device - 1) % nseq, device, (device + 1) % nseq])
    key_blocks = jnp.concatenate(
        [
            jnp.broadcast_to(neighbours[None, :], (docs_dev, 3)),
            listed_here.reshape(docs_dev, RAND),
            global_ids,
        ],
        axis=1,
    )
    span = key_blocks.shape[1] * block
    key_inside = (key_blocks[:, :, None] * block + offsets < doc_lengths[:, None, None]).reshape(
        docs_dev, span
    )
    keep_local = inside[:, None, None, None, :]
    hidden = tokens.reshape(count, width).astype(jnp.float32)
    held = []
    for layer in range(LAYERS):
        weights = (
            lax.all_gather(qkv_weight[layer], ("docs", "seq"), axis=0, tiled=True),
            lax.all_gather(out_weight[layer], ("docs", "seq"), axis=0, tiled=True),
            lax.all_gather(up_weight[layer], ("docs", "seq"), axis=0, tiled=True),
            lax.all_gather(down_weight[layer], ("docs", "seq"), axis=0, tiled=True),
            lax.all_gather(norm_gains[layer], ("docs", "seq"), axis=1, tiled=True),
        )
        weight_qkv, weight_out, weight_up, weight_down, gain_pair = weights
        gain_pair = gain_pair.astype(jnp.float32)
        lowered = hidden.astype(jnp.bfloat16)
        projected = (
            jnp.dot(lowered, weight_qkv, preferred_element_type=jnp.float32)
            .astype(jnp.bfloat16)
            .reshape(docs_dev, block, 3 * width)
        )
        pairs = projected[:, :, width:]
        window = with_halo(pairs, (("seq", 1),), block)
        outgoing = jnp.where(
            send_live[:, :, None, None],
            jnp.take(pairs, send_doc, axis=0),
            jnp.zeros((), jnp.bfloat16),
        )
        incoming = lax.all_to_all(outgoing, "seq", split_axis=0, concat_axis=0, tiled=True)
        fetched = jnp.take(
            incoming.reshape(nseq * capacity, block, 2 * width), fetch_slot, axis=0
        ).reshape(docs_dev, RAND * block, 2 * width)
        global_send = jnp.where(
            global_send_live[:, None, None],
            jnp.take(projected, global_send_doc, axis=0),
            jnp.zeros((), jnp.bfloat16),
        )
        gathered = lax.all_gather(global_send, "seq", axis=0, tiled=True)
        global_picked = jnp.take(gathered, global_slot, axis=0).reshape(
            docs_dev, GLOB, block, 3 * width
        )
        global_query = global_picked[..., :width].reshape(docs_dev, GLOB, block, heads, HEAD)
        listed_pairs = jnp.concatenate(
            [
                window,
                fetched,
                global_picked[..., width:].reshape(docs_dev, GLOB * block, 2 * width),
            ],
            axis=1,
        )
        query = projected[:, :, :width].reshape(docs_dev, block, heads, HEAD)
        key_part = listed_pairs[:, :, :width].reshape(docs_dev, span, heads, HEAD)
        value_part = listed_pairs[:, :, width:].reshape(docs_dev, span, heads, HEAD)
        probs = sparse_probs(query, key_part, key_inside, scale)
        mixed = jnp.einsum(
            "khbj,kjhd->kbhd",
            probs.astype(jnp.bfloat16),
            value_part,
            preferred_element_type=jnp.float32,
        )
        local_keys = projected[:, :, width : 2 * width].reshape(docs_dev, block, heads, HEAD)
        local_values = projected[:, :, 2 * width :].reshape(docs_dev, block, heads, HEAD)
        wide_scores = global_scores(global_query, local_keys, inside, scale)
        global_top = jnp.max(wide_scores, axis=-1)
        global_total = jnp.sum(
            jnp.where(keep_local, jnp.exp(wide_scores - global_top[..., None]), 0.0), axis=-1
        )
        global_top, global_total = combined_all((global_top, global_total), "seq", merge_stats)
        wide_probs = (
            jnp.where(keep_local, jnp.exp(wide_scores - global_top[..., None]), 0.0)
            / global_total[..., None]
        )
        wide_part = jnp.einsum(
            "kshbj,kjhd->ksbhd",
            wide_probs.astype(jnp.bfloat16),
            local_values,
            preferred_element_type=jnp.float32,
        )
        wide_buffer = (
            jnp.zeros((nseq * global_capacity, block, width), jnp.float32)
            .at[global_slot]
            .set(wide_part.reshape(global_entries, block, width))
        )
        wide_sum = lax.psum_scatter(wide_buffer, "seq", scatter_dimension=0, tiled=True)
        attended = jnp.where(
            own_flag[:, None, None],
            jnp.take(wide_sum, own_slot, axis=0),
            mixed.reshape(docs_dev, block, width),
        )
        attended = attended.reshape(count, width).astype(jnp.bfloat16)
        after_attn = hidden + jnp.dot(attended, weight_out, preferred_element_type=jnp.float32)
        normed = norm_rows(after_attn, gain_pair[0])
        normed_low = normed.astype(jnp.bfloat16)
        up_values = jnp.dot(normed_low, weight_up, preferred_element_type=jnp.float32)
        activated = gelu_tanh(up_values).astype(jnp.bfloat16)
        after_ffn = normed + jnp.dot(activated, weight_down, preferred_element_type=jnp.float32)
        held.append(
            (
                weights,
                lowered,
                projected,
                listed_pairs,
                global_query,
                global_top,
                global_total,
                attended,
                after_attn,
                normed_low,
                up_values,
                activated,
                after_ffn,
            )
        )
        hidden = jnp.where(live_rows, norm_rows(after_ffn, gain_pair[1]), 0.0)
    gradient = cotangent.reshape(count, width).astype(jnp.float32)
    layer_grads = []
    for layer in reversed(range(LAYERS)):
        (
            weights,
            lowered,
            projected,
            listed_pairs,
            global_query,
            global_top,
            global_total,
            attended,
            after_attn,
            normed_low,
            up_values,
            activated,
            after_ffn,
        ) = held[layer]
        weights = (
            lax.all_gather(qkv_weight[layer], ("docs", "seq"), axis=0, tiled=True),
            lax.all_gather(out_weight[layer], ("docs", "seq"), axis=0, tiled=True),
            lax.all_gather(up_weight[layer], ("docs", "seq"), axis=0, tiled=True),
            lax.all_gather(down_weight[layer], ("docs", "seq"), axis=0, tiled=True),
            lax.all_gather(norm_gains[layer], ("docs", "seq"), axis=1, tiled=True),
        )
        weight_qkv, weight_out, weight_up, weight_down, gain_pair = weights
        gain_pair = gain_pair.astype(jnp.float32)
        gradient = jnp.where(live_rows, gradient, 0.0)
        grad_ffn, grad_gain_out = jax.vjp(norm_rows, after_ffn, gain_pair[1])[1](gradient)
        grad_down_low = grad_ffn.astype(jnp.bfloat16)
        grad_down_layer = jnp.einsum(
            "rf,rd->fd", activated, grad_down_low, preferred_element_type=jnp.float32
        )
        grad_activated = jnp.einsum(
            "rd,fd->rf", grad_down_low, weight_down, preferred_element_type=jnp.float32
        )
        grad_up_low = jax.vjp(gelu_tanh, up_values)[1](grad_activated)[0].astype(jnp.bfloat16)
        grad_up_layer = jnp.einsum(
            "rd,rf->df", normed_low, grad_up_low, preferred_element_type=jnp.float32
        )
        grad_normed = grad_ffn + jnp.einsum(
            "rf,df->rd", grad_up_low, weight_up, preferred_element_type=jnp.float32
        )
        grad_attn, grad_gain_mid = jax.vjp(norm_rows, after_attn, gain_pair[0])[1](grad_normed)
        grad_attn_low = grad_attn.astype(jnp.bfloat16)
        grad_out_layer = jnp.einsum(
            "rd,re->de", attended, grad_attn_low, preferred_element_type=jnp.float32
        )
        grad_mixed = (
            jnp.einsum("re,de->rd", grad_attn_low, weight_out, preferred_element_type=jnp.float32)
            .astype(jnp.bfloat16)
            .reshape(docs_dev, block, width)
        )
        query = projected[:, :, :width].reshape(docs_dev, block, heads, HEAD)
        key_part = listed_pairs[:, :, :width].reshape(docs_dev, span, heads, HEAD)
        value_part = listed_pairs[:, :, width:].reshape(docs_dev, span, heads, HEAD)
        probs = sparse_probs(query, key_part, key_inside, scale)
        grad_sparse = jnp.where(
            own_flag[:, None, None], jnp.zeros((), jnp.bfloat16), grad_mixed
        ).reshape(docs_dev, block, heads, HEAD)
        grad_probs = jnp.einsum(
            "kbhd,kjhd->khbj", grad_sparse, value_part, preferred_element_type=jnp.float32
        )
        delta = jnp.sum(probs * grad_probs, axis=-1, keepdims=True)
        grad_scores = (probs * (grad_probs - delta)).astype(jnp.bfloat16)
        grad_query = (
            jnp.einsum("khbj,kjhd->kbhd", grad_scores, key_part, preferred_element_type=jnp.float32)
            * scale
        )
        grad_key_part = (
            jnp.einsum("khbj,kbhd->kjhd", grad_scores, query, preferred_element_type=jnp.float32)
            * scale
        )
        grad_value_part = jnp.einsum(
            "khbj,kbhd->kjhd",
            probs.astype(jnp.bfloat16),
            grad_sparse,
            preferred_element_type=jnp.float32,
        )
        grad_listed = jnp.concatenate(
            [
                grad_key_part.reshape(docs_dev, span, width),
                grad_value_part.reshape(docs_dev, span, width),
            ],
            axis=2,
        )
        wide_out = jnp.where(
            global_send_live[:, None, None],
            jnp.take(grad_mixed, global_send_doc, axis=0),
            jnp.zeros((), jnp.bfloat16),
        )
        wide_all = lax.all_gather(wide_out, "seq", axis=0, tiled=True)
        wide_grad = jnp.take(wide_all, global_slot, axis=0).reshape(
            docs_dev, GLOB, block, heads, HEAD
        )
        local_keys = projected[:, :, width : 2 * width].reshape(docs_dev, block, heads, HEAD)
        local_values = projected[:, :, 2 * width :].reshape(docs_dev, block, heads, HEAD)
        wide_scores = global_scores(global_query, local_keys, inside, scale)
        wide_probs = (
            jnp.where(keep_local, jnp.exp(wide_scores - global_top[..., None]), 0.0)
            / global_total[..., None]
        )
        wide_grad_probs = jnp.einsum(
            "ksbhd,kjhd->kshbj", wide_grad, local_values, preferred_element_type=jnp.float32
        )
        wide_delta = lax.psum(jnp.sum(wide_probs * wide_grad_probs, axis=-1), "seq")
        wide_grad_scores = (wide_probs * (wide_grad_probs - wide_delta[..., None])).astype(
            jnp.bfloat16
        )
        wide_grad_query = (
            jnp.einsum(
                "kshbj,kjhd->ksbhd",
                wide_grad_scores,
                local_keys,
                preferred_element_type=jnp.float32,
            )
            * scale
        )
        wide_grad_keys = (
            jnp.einsum(
                "kshbj,ksbhd->kjhd",
                wide_grad_scores,
                global_query,
                preferred_element_type=jnp.float32,
            )
            * scale
        )
        wide_grad_values = jnp.einsum(
            "kshbj,ksbhd->kjhd",
            wide_probs.astype(jnp.bfloat16),
            wide_grad,
            preferred_element_type=jnp.float32,
        )
        global_grads = jnp.concatenate(
            [
                wide_grad_query.reshape(global_entries, block, width),
                grad_listed[:, (3 + RAND) * block :, :].reshape(global_entries, block, 2 * width),
            ],
            axis=2,
        )
        global_buffer = (
            jnp.zeros((nseq * global_capacity, block, 3 * width), jnp.float32)
            .at[global_slot]
            .set(global_grads)
        )
        global_share = lax.psum_scatter(global_buffer, "seq", scatter_dimension=0, tiled=True)
        global_mine = jnp.where(
            own_flag[:, None, None], jnp.take(global_share, own_slot, axis=0), 0.0
        )
        grad_fetched = grad_listed[:, 3 * block : (3 + RAND) * block, :].reshape(
            entries, block, 2 * width
        )
        back_out = (
            jnp.zeros((nseq * capacity, block, 2 * width), jnp.float32)
            .at[fetch_slot]
            .set(grad_fetched)
            .reshape(nseq, capacity, block, 2 * width)
        )
        back_in = lax.all_to_all(back_out, "seq", split_axis=0, concat_axis=0, tiled=True)
        grad_random = jnp.einsum(
            "dck,dcbf->kbf", owner_pick, back_in, precision=lax.Precision.HIGHEST
        )
        grad_window = grad_listed[:, : 3 * block, :]
        edges = jnp.concatenate([grad_window[:, :block], grad_window[:, 2 * block :]], axis=1)
        beside_all = with_halo(edges, (("seq", 1),), block)
        grad_pairs = (
            grad_window[:, block : 2 * block]
            + beside_all[:, :block]
            + beside_all[:, 3 * block :]
            + grad_random
            + global_mine[:, :, width:]
        )
        grad_pairs = grad_pairs + jnp.concatenate(
            [
                wide_grad_keys.reshape(docs_dev, block, width),
                wide_grad_values.reshape(docs_dev, block, width),
            ],
            axis=2,
        )
        grad_queries = grad_query.reshape(docs_dev, block, width) + global_mine[:, :, :width]
        grad_projected = (
            jnp.concatenate([grad_queries, grad_pairs], axis=2)
            .reshape(count, 3 * width)
            .astype(jnp.bfloat16)
        )
        grad_qkv_layer = jnp.einsum(
            "rd,re->de", lowered, grad_projected, preferred_element_type=jnp.float32
        )
        gradient = grad_attn + jnp.einsum(
            "re,de->rd", grad_projected, weight_qkv, preferred_element_type=jnp.float32
        )
        group_shares = (
            lax.psum_scatter(grad_qkv_layer, "docs", scatter_dimension=0, tiled=True),
            lax.psum_scatter(grad_out_layer, "docs", scatter_dimension=0, tiled=True),
            lax.psum_scatter(grad_up_layer, "docs", scatter_dimension=0, tiled=True),
            lax.psum_scatter(grad_down_layer, "docs", scatter_dimension=0, tiled=True),
            lax.psum_scatter(
                jnp.stack([grad_gain_mid, grad_gain_out]), "docs", scatter_dimension=1, tiled=True
            ),
        )
        shares = (
            lax.psum_scatter(group_shares[0], "seq", scatter_dimension=1, tiled=True),
            lax.psum_scatter(group_shares[1], "seq", scatter_dimension=1, tiled=True),
            lax.psum_scatter(group_shares[2], "seq", scatter_dimension=1, tiled=True),
            lax.psum_scatter(group_shares[3], "seq", scatter_dimension=1, tiled=True),
            lax.psum_scatter(group_shares[4], "seq", scatter_dimension=1, tiled=True),
        )
        layer_grads.insert(0, shares)
    stacked = [
        jnp.stack([layer_grads[number][member] for number in range(LAYERS)]) for member in range(5)
    ]
    return (
        hidden.astype(jnp.bfloat16).reshape(docs_dev, block, width),
        gradient.reshape(docs_dev, block, width),
        stacked[0],
        stacked[1],
        stacked[2],
        stacked[3],
        stacked[4],
    )


PLANES = 4
GROUPS = 4
CHIPS = 16
GROUP_HEADS = 3
F32 = jnp.float32
BF16 = jnp.bfloat16


def fits(mesh, docs_dev, heads):
    return (
        mesh.shape["docs"] == 2
        and mesh.shape["seq"] == 16
        and docs_dev == PLANES
        and heads == GROUPS * GROUP_HEADS
    )


def swap(value, bits):
    return lax.ppermute(value, "seq", [(i, i ^ bits) for i in range(16)])


def swap_docs(value):
    return lax.ppermute(value, "docs", [(0, 1), (1, 0)])


def dot(left, right):
    return lax.dot_general(left, right, (((1,), (0,)), ((), ())), preferred_element_type=F32)


def dot_nt(left, right):
    return lax.dot_general(left, right, (((1,), (1,)), ((), ())), preferred_element_type=F32)


def dot_tn(left, right):
    return lax.dot_general(left, right, (((0,), (0,)), ((), ())), preferred_element_type=F32)


def vmem():
    return pl.BlockSpec(memory_space=pltpu.VMEM)


def smem():
    return pl.BlockSpec(memory_space=pltpu.SMEM)


def hbm():
    return pl.BlockSpec(memory_space=pl.ANY)


def params():
    return pltpu.CompilerParams(vmem_limit_bytes=56 * 2**20)


def join_weight(info, w_ref, w_scr):
    chip = info[1]
    for j in range(CHIPS):
        w_scr[48 * j : 48 * j + 48, :] = w_ref[j ^ chip]


def block_of(info, place):
    rc, rz, rx = place // 8, (place // 2) % 4, place % 2
    return info[0] ^ (rz * 4 + rx * 2 + rc)


def listed(lists, block):
    window = [(block + 15) % 16, block, (block + 1) % 16]
    return window + [lists[block, n] for n in range(RAND)] + [lists[16, n] for n in range(GLOB)]


def key_mask(ids, length):
    lane = lax.broadcasted_iota(jnp.int32, (1, 64 * len(ids)), 1)
    spot = lane // 64
    number = jnp.zeros_like(lane)
    for n, block in enumerate(ids):
        number = jnp.where(spot == n, block, number)
    return number * 64 + lane % 64 < length


def softmax_rows(scores, mask):
    scores = jnp.where(mask, scores, NEGATIVE)
    expo = jnp.exp(scores - jnp.max(scores, axis=-1, keepdims=True))
    return expo / jnp.sum(expo, axis=-1, keepdims=True)


def attend_kernel(info, lists, xo_ref, xr_ref, w_ref, qkv_ref, o_ref, w_scr, kv_scr, q_scr):
    join_weight(info, w_ref, w_scr)
    for half, ref in enumerate((xo_ref, xr_ref)):
        rows = dot(ref[...].reshape(512, ref.shape[-1]), w_scr[...]).astype(BF16)
        for p in range(8):
            block = block_of(info, 8 * half + p)
            part = rows[64 * p : 64 * p + 64]
            qkv_ref[block] = part
    spread_heads(qkv_ref, kv_scr, q_scr)
    length = info[2]

    def one(block, _):
        special = jnp.logical_or(block == lists[16, 0], block == lists[16, 1])

        @pl.when(jnp.logical_not(special))
        def _():
            ids = listed(lists, block)
            mask = key_mask(ids, length)
            outs = []
            for h in range(GROUP_HEADS):
                kv = jnp.concatenate([kv_scr[h, n] for n in ids], axis=0)
                probs = softmax_rows(dot_nt(q_scr[h, block], kv), mask)
                outs.append(dot(probs.astype(BF16), kv)[:, 64:])
            o_ref[block] = jnp.concatenate(outs, axis=1).astype(BF16)

        @pl.when(special)
        def _():
            mask = lax.broadcasted_iota(jnp.int32, (1, 1024), 1) < length
            outs = []
            for h in range(GROUP_HEADS):
                kv = kv_scr[h].reshape(1024, 128)
                probs = softmax_rows(dot_nt(q_scr[h, block], kv), mask)
                outs.append(dot(probs.astype(BF16), kv)[:, 64:])
            o_ref[block] = jnp.concatenate(outs, axis=1).astype(BF16)

        return 0

    lax.fori_loop(0, 16, one, 0)


def spread_heads(qkv_ref, kv_scr, q_scr):
    def one(block, _):
        row = qkv_ref[block]
        zero = jnp.zeros((64, 64), BF16)
        for h in range(GROUP_HEADS):
            kv_scr[h, block] = row[:, 128 * h : 128 * h + 128]
            query = row[:, 384 + 64 * h : 448 + 64 * h] * jnp.asarray(HEAD**-0.5, BF16)
            q_scr[h, block] = jnp.concatenate([query, zero], axis=1)
        return 0

    lax.fori_loop(0, 16, one, 0)


def attend(info, lists, x_own, x_other, weight):
    width = x_own.shape[-1]
    return pl.pallas_call(
        attend_kernel,
        out_shape=(
            jax.ShapeDtypeStruct((16, 64, 576), BF16),
            jax.ShapeDtypeStruct((16, 64, 192), BF16),
        ),
        in_specs=[smem(), smem(), vmem(), vmem(), vmem()],
        out_specs=(vmem(), vmem()),
        scratch_shapes=[
            pltpu.VMEM((width, 576), BF16),
            pltpu.VMEM((3, 16, 64, 128), BF16),
            pltpu.VMEM((3, 16, 64, 128), BF16),
        ],
        compiler_params=params(),
        cost_estimate=pl.CostEstimate(
            flops=3 * 10**9, bytes_accessed=6 * 10**6, transcendentals=2 * 10**6
        ),
        name="attend",
    )(info, lists, x_own, x_other, weight)


def attend_back_kernel(
    info,
    lists,
    qkv_ref,
    do_ref,
    xo_ref,
    xr_ref,
    w_ref,
    keep_ref,
    send_ref,
    grad_ref,
    w_scr,
    kv_scr,
    q_scr,
    do_scr,
    dkv_scr,
    dq_scr,
    dqkv_scr,
):
    join_weight(info, w_ref, w_scr)
    spread_heads(qkv_ref, kv_scr, q_scr)
    dkv_scr[...] = jnp.zeros_like(dkv_scr)
    length = info[2]

    def lay(block, _):
        row = do_ref[block]
        zero = jnp.zeros((64, 64), BF16)
        for h in range(GROUP_HEADS):
            do_scr[h, block] = jnp.concatenate([zero, row[:, 64 * h : 64 * h + 64]], axis=1)
        return 0

    lax.fori_loop(0, 16, lay, 0)

    def rows_back(block, h, kv, mask):
        both = jnp.concatenate([q_scr[h, block], do_scr[h, block]], axis=0)
        pair = dot_nt(both, kv)
        probs = softmax_rows(pair[:64], mask)
        grad_probs = pair[64:]
        delta = jnp.sum(probs * grad_probs, axis=-1, keepdims=True)
        grad_scores = (probs * (grad_probs - delta)).astype(BF16)
        dq = dot(grad_scores, kv)[:, :64] * (HEAD**-0.5)
        dkv = dot_tn(jnp.concatenate([grad_scores, probs.astype(BF16)], axis=0), both)
        return dq, dkv

    def one(block, _):
        special = jnp.logical_or(block == lists[16, 0], block == lists[16, 1])

        @pl.when(jnp.logical_not(special))
        def _():
            ids = listed(lists, block)
            mask = key_mask(ids, length)
            dqs = []
            for h in range(GROUP_HEADS):
                kv = jnp.concatenate([kv_scr[h, n] for n in ids], axis=0)
                dq, dkv = rows_back(block, h, kv, mask)
                dqs.append(dq)
                for at, n in enumerate(ids):
                    dkv_scr[h, n] += dkv[64 * at : 64 * at + 64]
            dq_scr[block] = jnp.concatenate(dqs, axis=1).astype(BF16)

        @pl.when(special)
        def _():
            mask = lax.broadcasted_iota(jnp.int32, (1, 1024), 1) < length
            dqs = []
            for h in range(GROUP_HEADS):
                dq, dkv = rows_back(block, h, kv_scr[h].reshape(1024, 128), mask)
                dqs.append(dq)
                dkv_scr[h] += dkv.reshape(16, 64, 128)
            dq_scr[block] = jnp.concatenate(dqs, axis=1).astype(BF16)

        return 0

    lax.fori_loop(0, 16, one, 0)

    for place in range(16):
        block = block_of(info, place)
        parts = [dkv_scr[h, block].astype(BF16) for h in range(GROUP_HEADS)]
        dqkv_scr[place] = jnp.concatenate(parts + [dq_scr[block]], axis=1)
    for half, ref in enumerate((keep_ref, send_ref)):
        rows = dqkv_scr[8 * half : 8 * half + 8].reshape(512, 576)
        ref[...] = dot_nt(rows, w_scr[...]).astype(BF16).reshape(ref.shape)
    top = dqkv_scr[0:8].reshape(512, 576)
    low = dqkv_scr[8:16].reshape(512, 576)
    width = xo_ref.shape[-1]
    grad = dot_tn(top, xo_ref[...].reshape(512, width))
    grad += dot_tn(low, xr_ref[...].reshape(512, width))
    order = [6, 7, 8, 0, 2, 4, 1, 3, 5]
    grad = jnp.concatenate([grad[64 * n : 64 * n + 64] for n in order], axis=0).astype(BF16)
    for quarter in range(PLANES):
        for side in range(2):
            grad_ref[side ^ info[4], quarter ^ info[3]] = grad[
                144 * quarter : 144 * quarter + 144, 384 * side : 384 * side + 384
            ]


def attend_back(info, lists, qkv, grad_o, x_own, x_other, weight):
    width = x_own.shape[-1]
    return pl.pallas_call(
        attend_back_kernel,
        out_shape=(
            jax.ShapeDtypeStruct((8, 64, width), BF16),
            jax.ShapeDtypeStruct((8, 64, width), BF16),
            jax.ShapeDtypeStruct((2, PLANES, 144, width // 2), BF16),
        ),
        in_specs=[smem(), smem(), vmem(), vmem(), vmem(), vmem(), vmem()],
        out_specs=(vmem(), vmem(), vmem()),
        scratch_shapes=[
            pltpu.VMEM((width, 576), BF16),
            pltpu.VMEM((3, 16, 64, 128), BF16),
            pltpu.VMEM((3, 16, 64, 128), BF16),
            pltpu.VMEM((3, 16, 64, 128), BF16),
            pltpu.VMEM((3, 16, 64, 128), F32),
            pltpu.VMEM((16, 64, 192), BF16),
            pltpu.VMEM((16, 64, 576), BF16),
        ],
        compiler_params=params(),
        cost_estimate=pl.CostEstimate(
            flops=8 * 10**9, bytes_accessed=10 * 10**6, transcendentals=2 * 10**6
        ),
        name="attend_back",
    )(info, lists, qkv, grad_o, x_own, x_other, weight)


def slot_a(chip_bits):
    return (chip_bits & 8) | ((chip_bits & 1) << 2) | ((chip_bits >> 1) & 3)


def slot_b(chip_bits):
    return ((chip_bits & 1) << 3) | ((chip_bits & 8) >> 1) | ((chip_bits >> 1) & 3)


def load_weights(info, ao_ref, ar_ref, bo_ref, br_ref, wu, wd, wo, sems):
    chip, core = info[1], info[5]

    def one(j, _):
        at_a, at_b = slot_a(j ^ chip), slot_b(j ^ chip)
        for side, (a, b) in enumerate(((ao_ref, bo_ref), (ar_ref, br_ref))):
            plane = core ^ side
            pltpu.make_async_copy(
                b.at[at_b, :, pl.ds(1536, 384)], wo.at[plane, j], sems.at[0]
            ).start()
            pltpu.make_async_copy(a.at[at_a], wu.at[plane, j], sems.at[1]).start()
            for part in range(2):
                pltpu.make_async_copy(
                    b.at[at_b, :, pl.ds(768 * part, 768)], wd.at[j, plane, part], sems.at[2]
                ).start()
        return 0

    lax.fori_loop(0, CHIPS, one, 0)


def wait_weight(scr, sem):
    pltpu.make_async_copy(scr, scr, sem).wait()


def inside_rows(info):
    row = lax.broadcasted_iota(jnp.int32, (256, 1), 0)
    length = jnp.zeros_like(row)
    for k in range(PLANES):
        length = jnp.where(row // 64 == k, info[8 + k], length)
    return info[0] * 64 + row % 64 < length


def norm_parts(values):
    centre = values - jnp.mean(values, axis=-1, keepdims=True)
    spread = jnp.mean(centre * centre, axis=-1, keepdims=True)
    rate = lax.rsqrt(spread + EPSILON)
    return centre * rate, rate


def norm_back(unit, rate, gain, grad):
    scaled = grad * gain
    inner = jnp.mean(scaled * unit, axis=-1, keepdims=True)
    outer = jnp.mean(scaled, axis=-1, keepdims=True)
    return rate * (scaled - outer - unit * inner), jnp.sum(grad * unit, axis=0, keepdims=True)


CURVE = 0.7978845608028654


def gelu_parts(values):
    square = values * values
    bend = jnp.tanh(CURVE * (values + 0.044715 * (square * values)))
    return 0.5 * values * (1.0 + bend), bend, square


def gelu_slope(values, bend, square):
    return 0.5 * (1.0 + bend) + 0.5 * values * (1.0 - bend * bend) * (
        CURVE * (1.0 + 3 * 0.044715 * square)
    )


def feed_kernel(
    info,
    o_ref,
    h_ref,
    gain_ref,
    ao_ref,
    ar_ref,
    bo_ref,
    br_ref,
    mixed_ref,
    h1_ref,
    up_ref,
    h2_ref,
    next_ref,
    low_ref,
    wu,
    wd,
    wo,
    act_scr,
    sems,
):
    load_weights(info, ao_ref, ar_ref, bo_ref, br_ref, wu, wd, wo, sems)
    for k in range(PLANES):
        mixed_ref[64 * k : 64 * k + 64, :] = jnp.concatenate(
            [o_ref[4 * k + g] for g in range(GROUPS)], axis=1
        )
    mixed = mixed_ref[...]
    wait_weight(wo, sems.at[0])
    attended = jnp.concatenate([dot(mixed, wo[side].reshape(768, 384)) for side in range(2)], axis=1)
    h1 = h_ref[...].reshape(256, 768).astype(F32) + attended
    h1_ref[...] = h1
    x1 = norm_parts(h1)[0] * gain_ref[0:1, :]
    x1_low = x1.astype(BF16)
    wait_weight(wu, sems.at[1])
    for side in range(2):
        for part in range(3):
            at = 1536 * side + 512 * part
            up = dot(x1_low, wu[side, :, :, 512 * part : 512 * part + 512].reshape(768, 512))
            up_ref[:, at : at + 512] = up
            act_scr[:, at : at + 512] = gelu_parts(up)[0].astype(BF16)
    wait_weight(wd, sems.at[2])
    h2 = x1 + dot(act_scr[...], wd[...].reshape(3072, 768))
    h2_ref[...] = h2
    out = jnp.where(inside_rows(info), norm_parts(h2)[0] * gain_ref[1:2, :], 0.0)
    next_ref[...] = out
    low = out.astype(BF16)
    for k in range(PLANES):
        low_ref[k ^ info[3]] = low[64 * k : 64 * k + 64]


WEIGHT_SCRATCH = [
    pltpu.VMEM((2, 16, 48, 1536), BF16),
    pltpu.VMEM((16, 2, 2, 48, 768), BF16),
    pltpu.VMEM((2, 16, 48, 384), BF16),
]


def feed(info, o, hidden, gains, weights):
    return pl.pallas_call(
        feed_kernel,
        out_shape=(
            jax.ShapeDtypeStruct((256, 768), BF16),
            jax.ShapeDtypeStruct((256, 768), F32),
            jax.ShapeDtypeStruct((256, 3072), F32),
            jax.ShapeDtypeStruct((256, 768), F32),
            jax.ShapeDtypeStruct((256, 768), F32),
            jax.ShapeDtypeStruct((4, 64, 768), BF16),
        ),
        in_specs=[smem(), vmem(), vmem(), vmem(), hbm(), hbm(), hbm(), hbm()],
        out_specs=tuple(vmem() for _ in range(6)),
        scratch_shapes=WEIGHT_SCRATCH
        + [pltpu.VMEM((256, 3072), BF16), pltpu.SemaphoreType.DMA((3,))],
        compiler_params=params(),
        cost_estimate=pl.CostEstimate(
            flops=3 * 10**9, bytes_accessed=20 * 10**6, transcendentals=10**6
        ),
        name="feed",
    )(info, o, hidden, gains, *weights)


def feed_back_kernel(
    has_extra,
    info,
    base_ref,
    extra_ref,
    gain_ref,
    mixed_ref,
    h1_ref,
    up_ref,
    h2_ref,
    ao_ref,
    ar_ref,
    bo_ref,
    br_ref,
    dh1_ref,
    do_ref,
    dgain_ref,
    keep_ref,
    send_ref,
    wu,
    wd,
    wo,
    gu,
    gd,
    go,
    act_scr,
    dup_scr,
    sems,
    out_sems,
):
    load_weights(info, ao_ref, ar_ref, bo_ref, br_ref, wu, wd, wo, sems)
    me, docs = info[0], info[4]
    if has_extra:
        parts = [
            base_ref[64 * k : 64 * k + 64, :] + extra_ref[k ^ info[3]].astype(F32)
            for k in range(PLANES)
        ]
        grad = jnp.concatenate(parts, axis=0)
    else:
        grad = base_ref[...].reshape(256, 768).astype(F32)
    grad = jnp.where(inside_rows(info), grad, 0.0)
    unit2, rate2 = norm_parts(h2_ref[...])
    dh2, dgain1 = norm_back(unit2, rate2, gain_ref[1:2, :], grad)
    dgain_ref[1:2, :] = dgain1
    df = dh2.astype(BF16)
    unit1, rate1 = norm_parts(h1_ref[...])
    x1_low = (unit1 * gain_ref[0:1, :]).astype(BF16)
    wait_weight(wd, sems.at[2])
    wait_weight(wu, sems.at[1])
    dx1 = dh2
    for part in range(8):
        at = 384 * part
        d_act = dot_nt(df, wd[2 * part : 2 * part + 2].reshape(384, 768))
        up = up_ref[:, at : at + 384]
        act, bend, square = gelu_parts(up)
        act = act.astype(BF16)
        dup = (gelu_slope(up, bend, square) * d_act).astype(BF16)
        side, start = part // 4, 384 * (part % 4)
        dx1 += dot_nt(dup, wu[side, :, :, start : start + 384].reshape(768, 384))
        gt_up = dot_tn(dup, x1_low).astype(BF16)
        for n in range(2):
            for half in range(2):
                gu[half, 2 * part + n] = gt_up[
                    192 * n : 192 * n + 192, 384 * half : 384 * half + 384
                ]
        gt_down = dot_tn(df, act).astype(BF16)
        row = 48 * (part % 4)
        for s in range(16):
            gd[part // 4, s, row : row + 48, :] = gt_down[48 * s : 48 * s + 48]
    dh1, dgain0 = norm_back(unit1, rate1, gain_ref[0:1, :], dx1)
    dgain_ref[0:1, :] = dgain0
    dh1_ref[...] = dh1
    da = dh1.astype(BF16)
    gt_out = dot_tn(da, mixed_ref[...]).astype(BF16)
    for s in range(16):
        for half in range(2):
            go[half, s] = gt_out[48 * s : 48 * s + 48, 384 * half : 384 * half + 384]
    wait_weight(wo, sems.at[0])
    do = dot_nt(da[:, 0:384], wo[0].reshape(768, 384))
    do += dot_nt(da[:, 384:768], wo[1].reshape(768, 384))
    do = do.astype(BF16)
    for k in range(PLANES):
        for g in range(GROUPS):
            do_ref[4 * k + g] = do[64 * k : 64 * k + 64, 192 * g : 192 * g + 192]

    def copies(ry, place):
        rx, rz = place // 4, place % 4
        out = []
        for rc, ref in enumerate((keep_ref, send_ref)):
            to = me ^ (rz * 4 + rx * 2 + rc)
            for scr, first, count in ((gu, 0, 192), (go, 192, 48), (gd, 240, 192)):
                out.append(
                    pltpu.make_async_copy(
                        scr.at[ry ^ docs, to],
                        ref.at[ry, place, pl.ds(first, count)],
                        out_sems.at[rc],
                    )
                )
        return out

    def start(n, _):
        for copy in copies(n // 8, n % 8):
            copy.start()
        return 0

    lax.fori_loop(0, 16, start, 0)
    pltpu.make_async_copy(keep_ref, keep_ref, out_sems.at[0]).wait()
    pltpu.make_async_copy(send_ref, send_ref, out_sems.at[1]).wait()


def feed_back(info, base, extra, gains, saved, weights):
    mixed, h1, up, h2 = saved
    has_extra = extra is not None
    if not has_extra:
        extra = jnp.zeros((8, 128), BF16)
    return pl.pallas_call(
        functools.partial(feed_back_kernel, has_extra),
        out_shape=(
            jax.ShapeDtypeStruct((256, 768), F32),
            jax.ShapeDtypeStruct((16, 64, 192), BF16),
            jax.ShapeDtypeStruct((2, 768), F32),
            jax.ShapeDtypeStruct((2, 8, 432, 384), BF16),
            jax.ShapeDtypeStruct((2, 8, 432, 384), BF16),
        ),
        in_specs=[smem()] + [vmem()] * 7 + [hbm()] * 4,
        out_specs=(vmem(), vmem(), vmem(), hbm(), hbm()),
        scratch_shapes=WEIGHT_SCRATCH
        + [
            pltpu.VMEM((2, 16, 192, 384), BF16),
            pltpu.VMEM((2, 16, 192, 384), BF16),
            pltpu.VMEM((2, 16, 48, 384), BF16),
            pltpu.VMEM((8, 128), BF16),
            pltpu.VMEM((8, 128), BF16),
            pltpu.SemaphoreType.DMA((3,)),
            pltpu.SemaphoreType.DMA((2,)),
        ],
        compiler_params=params(),
        cost_estimate=pl.CostEstimate(
            flops=6 * 10**9, bytes_accessed=40 * 10**6, transcendentals=10**6
        ),
        name="feed_back",
    )(info, base, extra, gains, mixed, h1, up, h2, *weights)


def in_core_order(core, own, other):
    return jnp.where(
        core == 0,
        jnp.concatenate([own, other], axis=0),
        jnp.concatenate([other, own], axis=0),
    )


def pick(stack, index):
    return lax.dynamic_index_in_dim(stack, index, 0, keepdims=False)


def gather_qkv(shard, me, core):
    rows, width = shard.shape[0], shard.shape[1] // 3
    parts = shard.reshape(rows, 3, GROUPS, GROUP_HEADS, HEAD)
    pairs = jnp.transpose(parts[:, 1:], (2, 0, 3, 1, 4)).reshape(GROUPS, rows, 384)
    query = jnp.transpose(parts[:, 0], (1, 0, 2, 3)).reshape(GROUPS, rows, 192)
    packed = jnp.concatenate([pairs, query], axis=2)
    group = me & 3
    got = [pick(packed, group)] + [swap(pick(packed, group ^ r), r) for r in range(1, 4)]
    held = jnp.stack([in_core_order(core, got[0], got[1]), in_core_order(core, got[2], got[3])])
    for bits in (4, 8):
        held = jnp.concatenate([held, swap(held, bits)], axis=0)
    return jnp.concatenate([held, swap_docs(held)], axis=0)


def gather_rest(out_shard, up_shard, down_shard, core):
    def mine(shard, side):
        half = shard.shape[1] // 2
        return lax.dynamic_slice_in_dim(shard, side * half, half, axis=1)

    got_up, got_out = swap((mine(up_shard, 1 - core), mine(out_shard, 1 - core)), 1)
    up = in_core_order(core, mine(up_shard, core), got_up)
    out = in_core_order(core, mine(out_shard, core), got_out)
    down = jnp.concatenate([down_shard[:48], down_shard[48:]], axis=1)
    held = jnp.concatenate([up, down, out], axis=1)[None]
    for bits in (4, 8):
        held = jnp.concatenate([held, swap(held, bits)], axis=0)
    first, second = held[:, :, :1536], held[:, :, 1536:]
    got_first, got_second = swap(first, 2), swap_docs(second)
    first = jnp.concatenate([first, got_first], axis=0)
    second = jnp.concatenate([second, got_second], axis=0)
    got_first, got_second = swap_docs(first), swap(second, 2)
    first = jnp.concatenate([first, got_first], axis=0)
    second = jnp.concatenate([second, got_second], axis=0)
    return first, swap(first, 1), second, swap(second, 1)


def spread_tokens(rows_of):
    pieces = []
    for rz in range(PLANES):
        piece = rows_of(rz) if rz == 0 else swap(rows_of(rz), rz * 4)
        pieces += [piece, swap(piece, 2)]
    own = jnp.stack(pieces)
    return own, swap(own, 1)


def add_low(first, second):
    return (first.astype(F32) + second.astype(F32)).astype(BF16)


def collect_tokens(keep, send):
    total = add_low(keep, swap(send, 1))
    back = []
    for rz in range(PLANES):
        piece = add_low(total[2 * rz], swap(total[2 * rz + 1], 2))
        back.append(piece if rz == 0 else swap(piece, rz * 4))
    return jnp.stack(back)


def reduce_rest(keep, send):
    got = swap(send, 1)
    cut = 224

    def along(total, mover):
        return add_low(total[0], mover(total[1]))

    first = add_low(keep[:, :, :cut], got[:, :, :cut])
    second = add_low(keep[:, :, cut:], got[:, :, cut:])
    first = along(first, swap_docs).reshape(2, 4, cut, 384)
    first = along(first, lambda v: swap(v, 2))
    second = second.reshape(2, 2, 4, 432 - cut, 384)
    second = add_low(second[:, 0], swap(second[:, 1], 2))
    second = along(second, swap_docs)
    done = []
    for part in (first, second):
        part = along(part.reshape((2, 2) + part.shape[1:]), lambda v: swap(v, 8))
        done.append(part[0].astype(F32) + swap(part[1], 4).astype(F32))
    total = jnp.concatenate(done, axis=0)
    down = total[240:].reshape(4, 48, 384)
    return (
        total[192:240].T,
        total[:192].T,
        jnp.transpose(down, (0, 2, 1)).reshape(1536, 48),
    )


def route_table():
    edges = []
    for device in range(16):
        z, group = device >> 2, device & 3
        for t in range(3):
            local = 3 * z + t
            number = 16 * (local // 4) + 4 * group + local % 4
            edges.append((device, t, number // 3, number % 3))
    rounds = []
    left = list(edges)
    for _ in range(3):
        match = {}

        def place(device, seen):
            for edge in left:
                if edge[0] == device and edge[2] not in seen:
                    seen.add(edge[2])
                    if edge[2] not in match or place(match[edge[2]][0], seen):
                        match[edge[2]] = edge
                        return True
            return False

        for device in range(16):
            place(device, set())
        chosen = sorted(match.values())
        rounds.append(chosen)
        left = [edge for edge in left if edge not in chosen]
    return rounds


def reduce_qkv(grad, me):
    total = add_low(grad[0], swap_docs(grad[1]))
    total = add_low(total[:2], swap(total[2:], 8))
    total = total[0].astype(F32) + swap(total[1], 4).astype(F32)
    granules = total.reshape(3, 48, 384)
    got = []
    spots = []
    for chosen in route_table():
        take = jnp.asarray([edge[1] for edge in chosen], jnp.int32)
        moved = lax.ppermute(
            pick(granules, take[me]), "seq", [(edge[0], edge[2]) for edge in chosen]
        )
        got.append(moved)
        spots.append([edge[3] for edge in sorted(chosen, key=lambda edge: edge[2])])
    where = jnp.asarray(spots, jnp.int32)[:, me]
    got = jnp.stack(got)
    place = jnp.arange(3, dtype=jnp.int32)
    source = jnp.sum(jnp.where(where[None, :] == place[:, None], place[None, :], 0), axis=1)
    return jnp.take(got, source, axis=0).reshape(144, 384).T


def local_two_by_sixteen(
    tokens,
    qkv_weight,
    out_weight,
    up_weight,
    down_weight,
    norm_gains,
    doc_lengths,
    global_ids,
    random_ids,
    cotangent,
):
    docs_dev, block, width = tokens.shape
    me = lax.axis_index("seq").astype(jnp.int32)
    docs = lax.axis_index("docs").astype(jnp.int32)
    plane, core = me >> 2, me & 1
    chip = docs * 8 + (me >> 1)
    zero = jnp.zeros((), jnp.int32)
    info = jnp.concatenate(
        [
            jnp.stack([me, chip, pick(doc_lengths, plane), plane, docs, core, zero, zero]),
            doc_lengths,
        ]
    )
    lists = jnp.concatenate(
        [
            lax.dynamic_index_in_dim(random_ids, plane, 1, keepdims=False),
            jnp.pad(pick(global_ids, plane), (0, 1))[None],
        ],
        axis=0,
    )
    gains = lax.all_gather(norm_gains, ("docs", "seq"), axis=2, tiled=True).astype(F32)
    hidden = tokens
    qkv_weights = [gather_qkv(qkv_weight[layer], me, core) for layer in range(LAYERS)]
    rest = [
        gather_rest(out_weight[layer], up_weight[layer], down_weight[layer], core)
        for layer in range(LAYERS)
    ]
    held = []
    rows_of = lambda rz: pick(tokens, plane ^ rz)
    for layer in range(LAYERS):
        x_own, x_other = spread_tokens(rows_of)
        qkv, o = attend(info, lists, x_own, x_other, qkv_weights[layer])
        o = lax.all_to_all(o, "seq", split_axis=0, concat_axis=0, tiled=True)
        mixed, h1, up, h2, hidden, low = feed(info, o, hidden, gains[layer], rest[layer])
        held.append((x_own, x_other, qkv, (mixed, h1, up, h2)))
        rows_of = functools.partial(lambda low, rz: low[rz], low)
    base, extra = cotangent, None
    grads = [None] * LAYERS
    gain_grads = [None] * LAYERS
    for layer in reversed(range(LAYERS)):
        x_own, x_other, qkv, saved = held[layer]
        base, grad_o, gain_grads[layer], keep, send = feed_back(
            info, base, extra, gains[layer], saved, rest[layer]
        )
        grad_o = lax.all_to_all(grad_o, "seq", split_axis=0, concat_axis=0, tiled=True)
        keep_rows, send_rows, grad_qkv = attend_back(
            info, lists, qkv, grad_o, x_own, x_other, qkv_weights[layer]
        )
        extra = collect_tokens(keep_rows, send_rows)
        grads[layer] = (reduce_qkv(grad_qkv, me),) + reduce_rest(keep, send)
    order = jnp.arange(docs_dev, dtype=jnp.int32) ^ plane
    grad_tokens = base.reshape(docs_dev, block, width) + jnp.take(extra, order, axis=0).astype(F32)
    stacked = [jnp.stack([grads[n][member] for n in range(LAYERS)]) for member in range(4)]
    total = lax.psum(jnp.stack(gain_grads), ("docs", "seq"))
    share = width // (2 * 16)
    mine = lax.dynamic_slice_in_dim(total, (docs * 16 + me) * share, share, axis=2)
    return (
        hidden.astype(BF16).reshape(docs_dev, block, width),
        grad_tokens,
        stacked[0],
        stacked[1],
        stacked[2],
        stacked[3],
        mine,
    )


def solution(mesh):
    def local(*args):
        docs_dev, _, width = args[0].shape
        if fits(mesh, docs_dev, width // HEAD):
            return local_two_by_sixteen(*args)
        return local_any_mesh(*args)

    return jax.shard_map(
        local,
        mesh=mesh,
        in_specs=(
            P("docs", "seq", None),
            P(None, ("docs", "seq"), None),
            P(None, ("docs", "seq"), None),
            P(None, ("docs", "seq"), None),
            P(None, ("docs", "seq"), None),
            P(None, None, ("docs", "seq")),
            P("docs"),
            P("docs", None),
            P(None, "docs", None),
            P("docs", "seq", None),
        ),
        out_specs=(
            P("docs", "seq", None),
            P("docs", "seq", None),
            P(None, "docs", "seq"),
            P(None, "docs", "seq"),
            P(None, "docs", "seq"),
            P(None, "docs", "seq"),
            P(None, None, ("docs", "seq")),
        ),
        check_vma=False,
    )
```

```python
import functools

import jax
import jax.numpy as jnp
from jax import lax
from jax.experimental import pallas as pl
from jax.experimental.pallas import tpu as pltpu
from jax.sharding import PartitionSpec as P

HEAD = 64
RAND = 3
GLOB = 2
LAYERS = 2


NEGATIVE = -1e30
EPSILON = 1e-05


def with_halo(cells, sides, width):
    for axis, dim in sides:
        count = lax.axis_size(axis)
        head = lax.slice_in_dim(cells, 0, width, axis=dim)
        tail = lax.slice_in_dim(cells, cells.shape[dim] - width, cells.shape[dim], axis=dim)
        cells = jnp.concatenate(
            [
                lax.ppermute(tail, axis, [(i, (i + 1) % count) for i in range(count)]),
                cells,
                lax.ppermute(head, axis, [((i + 1) % count, i) for i in range(count)]),
            ],
            axis=dim,
        )
    return cells


def combined_all(value, axis, join):
    pieces = jax.tree.map(lambda part: lax.all_gather(part, axis), value)
    head = jax.tree.map(lambda part: part[0], pieces)
    tail = jax.tree.map(lambda part: part[1:], pieces)
    so_far, _ = lax.scan(lambda so_far, piece: (join(so_far, piece), None), head, tail)
    return so_far


def norm_rows(values, gain):
    centre = values - jnp.mean(values, axis=-1, keepdims=True)
    spread = jnp.mean(centre * centre, axis=-1, keepdims=True)
    return centre * lax.rsqrt(spread + EPSILON) * gain


def gelu_tanh(values):
    return jax.nn.gelu(values, approximate=True)


def earlier_equal(values):
    length = values.shape[-1]
    order = jnp.arange(length, dtype=jnp.int32)
    before = order[None, :] < order[:, None]
    same = values[..., :, None] == values[..., None, :]
    return jnp.sum(jnp.logical_and(same, before), axis=-1)


def merge_stats(first, second):
    highest = jnp.maximum(first[0], second[0])
    return (
        highest,
        first[1] * jnp.exp(first[0] - highest) + second[1] * jnp.exp(second[0] - highest),
    )


def sparse_probs(query, key_part, key_inside, scale):
    scores = (
        jnp.einsum("kbhd,kjhd->khbj", query, key_part, preferred_element_type=jnp.float32) * scale
    )
    scores = jnp.where(key_inside[:, None, None, :], scores, NEGATIVE)
    expo = jnp.exp(scores - jnp.max(scores, axis=-1, keepdims=True))
    return expo / jnp.sum(expo, axis=-1, keepdims=True)


def global_scores(global_query, local_keys, inside, scale):
    scores = (
        jnp.einsum(
            "ksbhd,kjhd->kshbj", global_query, local_keys, preferred_element_type=jnp.float32
        )
        * scale
    )
    return jnp.where(inside[:, None, None, None, :], scores, NEGATIVE)


def local_any_mesh(
    tokens,
    qkv_weight,
    out_weight,
    up_weight,
    down_weight,
    norm_gains,
    doc_lengths,
    global_ids,
    random_ids,
    cotangent,
):
    nseq = lax.axis_size("seq")
    device = lax.axis_index("seq")
    docs_dev, block, width = tokens.shape
    count = docs_dev * block
    heads = width // HEAD
    scale = HEAD ** (-0.5)
    capacity = max(2, (docs_dev * RAND + nseq - 1) // nseq)
    global_capacity = (docs_dev * GLOB + nseq - 1) // nseq
    entries = docs_dev * RAND
    global_entries = docs_dev * GLOB
    offsets = jnp.arange(block, dtype=jnp.int32)
    inside = (device * block + offsets)[None, :] < doc_lengths[:, None]
    live_rows = inside.reshape(count, 1)
    wanted = random_ids.reshape(nseq, entries)
    wanted_rank = earlier_equal(wanted)
    slot_ids = jnp.arange(capacity, dtype=jnp.int32)
    hits = jnp.logical_and((wanted == device)[:, :, None], wanted_rank[:, :, None] == slot_ids)
    hits = jnp.any(hits.reshape(nseq, docs_dev, RAND, capacity), axis=2)
    hits = jnp.transpose(hits, (0, 2, 1))
    doc_ids = jnp.arange(docs_dev, dtype=jnp.int32)
    send_doc = jnp.sum(jnp.where(hits, doc_ids, 0), axis=2)
    send_live = jnp.any(hits, axis=2)
    owner_pick = hits.astype(jnp.float32)
    listed_here = lax.dynamic_index_in_dim(wanted, device, 0, keepdims=False)
    listed_rank = lax.dynamic_index_in_dim(wanted_rank, device, 0, keepdims=False)
    fetch_slot = listed_here * capacity + listed_rank
    global_block = global_ids.reshape(global_entries)
    global_rank = earlier_equal(global_block)
    global_slot = global_block * global_capacity + global_rank
    own_entry = global_block == device
    owned = jnp.logical_and(
        own_entry[:, None], global_rank[:, None] == jnp.arange(global_capacity, dtype=jnp.int32)
    )
    entry_doc = jnp.arange(global_entries, dtype=jnp.int32) // GLOB
    global_send_doc = jnp.sum(jnp.where(owned, entry_doc[:, None], 0), axis=0)
    global_send_live = jnp.any(owned, axis=0)
    own_flag = jnp.any(own_entry.reshape(docs_dev, GLOB), axis=1)
    own_slot = jnp.sum(jnp.where(own_entry, global_rank, 0).reshape(docs_dev, GLOB), axis=1)
    neighbours = jnp.stack([(device - 1) % nseq, device, (device + 1) % nseq])
    key_blocks = jnp.concatenate(
        [
            jnp.broadcast_to(neighbours[None, :], (docs_dev, 3)),
            listed_here.reshape(docs_dev, RAND),
            global_ids,
        ],
        axis=1,
    )
    span = key_blocks.shape[1] * block
    key_inside = (key_blocks[:, :, None] * block + offsets < doc_lengths[:, None, None]).reshape(
        docs_dev, span
    )
    keep_local = inside[:, None, None, None, :]
    hidden = tokens.reshape(count, width).astype(jnp.float32)
    held = []
    for layer in range(LAYERS):
        weights = (
            lax.all_gather(qkv_weight[layer], ("docs", "seq"), axis=0, tiled=True),
            lax.all_gather(out_weight[layer], ("docs", "seq"), axis=0, tiled=True),
            lax.all_gather(up_weight[layer], ("docs", "seq"), axis=0, tiled=True),
            lax.all_gather(down_weight[layer], ("docs", "seq"), axis=0, tiled=True),
            lax.all_gather(norm_gains[layer], ("docs", "seq"), axis=1, tiled=True),
        )
        weight_qkv, weight_out, weight_up, weight_down, gain_pair = weights
        gain_pair = gain_pair.astype(jnp.float32)
        lowered = hidden.astype(jnp.bfloat16)
        projected = (
            jnp.dot(lowered, weight_qkv, preferred_element_type=jnp.float32)
            .astype(jnp.bfloat16)
            .reshape(docs_dev, block, 3 * width)
        )
        pairs = projected[:, :, width:]
        window = with_halo(pairs, (("seq", 1),), block)
        outgoing = jnp.where(
            send_live[:, :, None, None],
            jnp.take(pairs, send_doc, axis=0),
            jnp.zeros((), jnp.bfloat16),
        )
        incoming = lax.all_to_all(outgoing, "seq", split_axis=0, concat_axis=0, tiled=True)
        fetched = jnp.take(
            incoming.reshape(nseq * capacity, block, 2 * width), fetch_slot, axis=0
        ).reshape(docs_dev, RAND * block, 2 * width)
        global_send = jnp.where(
            global_send_live[:, None, None],
            jnp.take(projected, global_send_doc, axis=0),
            jnp.zeros((), jnp.bfloat16),
        )
        gathered = lax.all_gather(global_send, "seq", axis=0, tiled=True)
        global_picked = jnp.take(gathered, global_slot, axis=0).reshape(
            docs_dev, GLOB, block, 3 * width
        )
        global_query = global_picked[..., :width].reshape(docs_dev, GLOB, block, heads, HEAD)
        listed_pairs = jnp.concatenate(
            [
                window,
                fetched,
                global_picked[..., width:].reshape(docs_dev, GLOB * block, 2 * width),
            ],
            axis=1,
        )
        query = projected[:, :, :width].reshape(docs_dev, block, heads, HEAD)
        key_part = listed_pairs[:, :, :width].reshape(docs_dev, span, heads, HEAD)
        value_part = listed_pairs[:, :, width:].reshape(docs_dev, span, heads, HEAD)
        probs = sparse_probs(query, key_part, key_inside, scale)
        mixed = jnp.einsum(
            "khbj,kjhd->kbhd",
            probs.astype(jnp.bfloat16),
            value_part,
            preferred_element_type=jnp.float32,
        )
        local_keys = projected[:, :, width : 2 * width].reshape(docs_dev, block, heads, HEAD)
        local_values = projected[:, :, 2 * width :].reshape(docs_dev, block, heads, HEAD)
        wide_scores = global_scores(global_query, local_keys, inside, scale)
        global_top = jnp.max(wide_scores, axis=-1)
        global_total = jnp.sum(
            jnp.where(keep_local, jnp.exp(wide_scores - global_top[..., None]), 0.0), axis=-1
        )
        global_top, global_total = combined_all((global_top, global_total), "seq", merge_stats)
        wide_probs = (
            jnp.where(keep_local, jnp.exp(wide_scores - global_top[..., None]), 0.0)
            / global_total[..., None]
        )
        wide_part = jnp.einsum(
            "kshbj,kjhd->ksbhd",
            wide_probs.astype(jnp.bfloat16),
            local_values,
            preferred_element_type=jnp.float32,
        )
        wide_buffer = (
            jnp.zeros((nseq * global_capacity, block, width), jnp.float32)
            .at[global_slot]
            .set(wide_part.reshape(global_entries, block, width))
        )
        wide_sum = lax.psum_scatter(wide_buffer, "seq", scatter_dimension=0, tiled=True)
        attended = jnp.where(
            own_flag[:, None, None],
            jnp.take(wide_sum, own_slot, axis=0),
            mixed.reshape(docs_dev, block, width),
        )
        attended = attended.reshape(count, width).astype(jnp.bfloat16)
        after_attn = hidden + jnp.dot(attended, weight_out, preferred_element_type=jnp.float32)
        normed = norm_rows(after_attn, gain_pair[0])
        normed_low = normed.astype(jnp.bfloat16)
        up_values = jnp.dot(normed_low, weight_up, preferred_element_type=jnp.float32)
        activated = gelu_tanh(up_values).astype(jnp.bfloat16)
        after_ffn = normed + jnp.dot(activated, weight_down, preferred_element_type=jnp.float32)
        held.append(
            (
                weights,
                lowered,
                projected,
                listed_pairs,
                global_query,
                global_top,
                global_total,
                attended,
                after_attn,
                normed_low,
                up_values,
                activated,
                after_ffn,
            )
        )
        hidden = jnp.where(live_rows, norm_rows(after_ffn, gain_pair[1]), 0.0)
    gradient = cotangent.reshape(count, width).astype(jnp.float32)
    layer_grads = []
    for layer in reversed(range(LAYERS)):
        (
            weights,
            lowered,
            projected,
            listed_pairs,
            global_query,
            global_top,
            global_total,
            attended,
            after_attn,
            normed_low,
            up_values,
            activated,
            after_ffn,
        ) = held[layer]
        weights = (
            lax.all_gather(qkv_weight[layer], ("docs", "seq"), axis=0, tiled=True),
            lax.all_gather(out_weight[layer], ("docs", "seq"), axis=0, tiled=True),
            lax.all_gather(up_weight[layer], ("docs", "seq"), axis=0, tiled=True),
            lax.all_gather(down_weight[layer], ("docs", "seq"), axis=0, tiled=True),
            lax.all_gather(norm_gains[layer], ("docs", "seq"), axis=1, tiled=True),
        )
        weight_qkv, weight_out, weight_up, weight_down, gain_pair = weights
        gain_pair = gain_pair.astype(jnp.float32)
        gradient = jnp.where(live_rows, gradient, 0.0)
        grad_ffn, grad_gain_out = jax.vjp(norm_rows, after_ffn, gain_pair[1])[1](gradient)
        grad_down_low = grad_ffn.astype(jnp.bfloat16)
        grad_down_layer = jnp.einsum(
            "rf,rd->fd", activated, grad_down_low, preferred_element_type=jnp.float32
        )
        grad_activated = jnp.einsum(
            "rd,fd->rf", grad_down_low, weight_down, preferred_element_type=jnp.float32
        )
        grad_up_low = jax.vjp(gelu_tanh, up_values)[1](grad_activated)[0].astype(jnp.bfloat16)
        grad_up_layer = jnp.einsum(
            "rd,rf->df", normed_low, grad_up_low, preferred_element_type=jnp.float32
        )
        grad_normed = grad_ffn + jnp.einsum(
            "rf,df->rd", grad_up_low, weight_up, preferred_element_type=jnp.float32
        )
        grad_attn, grad_gain_mid = jax.vjp(norm_rows, after_attn, gain_pair[0])[1](grad_normed)
        grad_attn_low = grad_attn.astype(jnp.bfloat16)
        grad_out_layer = jnp.einsum(
            "rd,re->de", attended, grad_attn_low, preferred_element_type=jnp.float32
        )
        grad_mixed = (
            jnp.einsum("re,de->rd", grad_attn_low, weight_out, preferred_element_type=jnp.float32)
            .astype(jnp.bfloat16)
            .reshape(docs_dev, block, width)
        )
        query = projected[:, :, :width].reshape(docs_dev, block, heads, HEAD)
        key_part = listed_pairs[:, :, :width].reshape(docs_dev, span, heads, HEAD)
        value_part = listed_pairs[:, :, width:].reshape(docs_dev, span, heads, HEAD)
        probs = sparse_probs(query, key_part, key_inside, scale)
        grad_sparse = jnp.where(
            own_flag[:, None, None], jnp.zeros((), jnp.bfloat16), grad_mixed
        ).reshape(docs_dev, block, heads, HEAD)
        grad_probs = jnp.einsum(
            "kbhd,kjhd->khbj", grad_sparse, value_part, preferred_element_type=jnp.float32
        )
        delta = jnp.sum(probs * grad_probs, axis=-1, keepdims=True)
        grad_scores = (probs * (grad_probs - delta)).astype(jnp.bfloat16)
        grad_query = (
            jnp.einsum("khbj,kjhd->kbhd", grad_scores, key_part, preferred_element_type=jnp.float32)
            * scale
        )
        grad_key_part = (
            jnp.einsum("khbj,kbhd->kjhd", grad_scores, query, preferred_element_type=jnp.float32)
            * scale
        )
        grad_value_part = jnp.einsum(
            "khbj,kbhd->kjhd",
            probs.astype(jnp.bfloat16),
            grad_sparse,
            preferred_element_type=jnp.float32,
        )
        grad_listed = jnp.concatenate(
            [
                grad_key_part.reshape(docs_dev, span, width),
                grad_value_part.reshape(docs_dev, span, width),
            ],
            axis=2,
        )
        wide_out = jnp.where(
            global_send_live[:, None, None],
            jnp.take(grad_mixed, global_send_doc, axis=0),
            jnp.zeros((), jnp.bfloat16),
        )
        wide_all = lax.all_gather(wide_out, "seq", axis=0, tiled=True)
        wide_grad = jnp.take(wide_all, global_slot, axis=0).reshape(
            docs_dev, GLOB, block, heads, HEAD
        )
        local_keys = projected[:, :, width : 2 * width].reshape(docs_dev, block, heads, HEAD)
        local_values = projected[:, :, 2 * width :].reshape(docs_dev, block, heads, HEAD)
        wide_scores = global_scores(global_query, local_keys, inside, scale)
        wide_probs = (
            jnp.where(keep_local, jnp.exp(wide_scores - global_top[..., None]), 0.0)
            / global_total[..., None]
        )
        wide_grad_probs = jnp.einsum(
            "ksbhd,kjhd->kshbj", wide_grad, local_values, preferred_element_type=jnp.float32
        )
        wide_delta = lax.psum(jnp.sum(wide_probs * wide_grad_probs, axis=-1), "seq")
        wide_grad_scores = (wide_probs * (wide_grad_probs - wide_delta[..., None])).astype(
            jnp.bfloat16
        )
        wide_grad_query = (
            jnp.einsum(
                "kshbj,kjhd->ksbhd",
                wide_grad_scores,
                local_keys,
                preferred_element_type=jnp.float32,
            )
            * scale
        )
        wide_grad_keys = (
            jnp.einsum(
                "kshbj,ksbhd->kjhd",
                wide_grad_scores,
                global_query,
                preferred_element_type=jnp.float32,
            )
            * scale
        )
        wide_grad_values = jnp.einsum(
            "kshbj,ksbhd->kjhd",
            wide_probs.astype(jnp.bfloat16),
            wide_grad,
            preferred_element_type=jnp.float32,
        )
        global_grads = jnp.concatenate(
            [
                wide_grad_query.reshape(global_entries, block, width),
                grad_listed[:, (3 + RAND) * block :, :].reshape(global_entries, block, 2 * width),
            ],
            axis=2,
        )
        global_buffer = (
            jnp.zeros((nseq * global_capacity, block, 3 * width), jnp.float32)
            .at[global_slot]
            .set(global_grads)
        )
        global_share = lax.psum_scatter(global_buffer, "seq", scatter_dimension=0, tiled=True)
        global_mine = jnp.where(
            own_flag[:, None, None], jnp.take(global_share, own_slot, axis=0), 0.0
        )
        grad_fetched = grad_listed[:, 3 * block : (3 + RAND) * block, :].reshape(
            entries, block, 2 * width
        )
        back_out = (
            jnp.zeros((nseq * capacity, block, 2 * width), jnp.float32)
            .at[fetch_slot]
            .set(grad_fetched)
            .reshape(nseq, capacity, block, 2 * width)
        )
        back_in = lax.all_to_all(back_out, "seq", split_axis=0, concat_axis=0, tiled=True)
        grad_random = jnp.einsum(
            "dck,dcbf->kbf", owner_pick, back_in, precision=lax.Precision.HIGHEST
        )
        grad_window = grad_listed[:, : 3 * block, :]
        edges = jnp.concatenate([grad_window[:, :block], grad_window[:, 2 * block :]], axis=1)
        beside_all = with_halo(edges, (("seq", 1),), block)
        grad_pairs = (
            grad_window[:, block : 2 * block]
            + beside_all[:, :block]
            + beside_all[:, 3 * block :]
            + grad_random
            + global_mine[:, :, width:]
        )
        grad_pairs = grad_pairs + jnp.concatenate(
            [
                wide_grad_keys.reshape(docs_dev, block, width),
                wide_grad_values.reshape(docs_dev, block, width),
            ],
            axis=2,
        )
        grad_queries = grad_query.reshape(docs_dev, block, width) + global_mine[:, :, :width]
        grad_projected = (
            jnp.concatenate([grad_queries, grad_pairs], axis=2)
            .reshape(count, 3 * width)
            .astype(jnp.bfloat16)
        )
        grad_qkv_layer = jnp.einsum(
            "rd,re->de", lowered, grad_projected, preferred_element_type=jnp.float32
        )
        gradient = grad_attn + jnp.einsum(
            "re,de->rd", grad_projected, weight_qkv, preferred_element_type=jnp.float32
        )
        group_shares = (
            lax.psum_scatter(grad_qkv_layer, "docs", scatter_dimension=0, tiled=True),
            lax.psum_scatter(grad_out_layer, "docs", scatter_dimension=0, tiled=True),
            lax.psum_scatter(grad_up_layer, "docs", scatter_dimension=0, tiled=True),
            lax.psum_scatter(grad_down_layer, "docs", scatter_dimension=0, tiled=True),
            lax.psum_scatter(
                jnp.stack([grad_gain_mid, grad_gain_out]), "docs", scatter_dimension=1, tiled=True
            ),
        )
        shares = (
            lax.psum_scatter(group_shares[0], "seq", scatter_dimension=1, tiled=True),
            lax.psum_scatter(group_shares[1], "seq", scatter_dimension=1, tiled=True),
            lax.psum_scatter(group_shares[2], "seq", scatter_dimension=1, tiled=True),
            lax.psum_scatter(group_shares[3], "seq", scatter_dimension=1, tiled=True),
            lax.psum_scatter(group_shares[4], "seq", scatter_dimension=1, tiled=True),
        )
        layer_grads.insert(0, shares)
    stacked = [
        jnp.stack([layer_grads[number][member] for number in range(LAYERS)]) for member in range(5)
    ]
    return (
        hidden.astype(jnp.bfloat16).reshape(docs_dev, block, width),
        gradient.reshape(docs_dev, block, width),
        stacked[0],
        stacked[1],
        stacked[2],
        stacked[3],
        stacked[4],
    )


PLANES = 4
GROUPS = 4
CHIPS = 16
GROUP_HEADS = 3
MESH = pl.DeviceIdType.MESH
F32 = jnp.float32
BF16 = jnp.bfloat16


def fits(mesh, docs_dev, heads):
    return (
        mesh.shape["docs"] == 2
        and mesh.shape["seq"] == 16
        and docs_dev == PLANES
        and heads == GROUPS * GROUP_HEADS
    )


def swap(value, bits):
    return lax.ppermute(value, "seq", [(i, i ^ bits) for i in range(16)])


def swap_docs(value):
    return lax.ppermute(value, "docs", [(0, 1), (1, 0)])


def dot(left, right):
    return lax.dot_general(left, right, (((1,), (0,)), ((), ())), preferred_element_type=F32)


def dot_nt(left, right):
    return lax.dot_general(left, right, (((1,), (1,)), ((), ())), preferred_element_type=F32)


def dot_tn(left, right):
    return lax.dot_general(left, right, (((0,), (0,)), ((), ())), preferred_element_type=F32)


def vmem():
    return pl.BlockSpec(memory_space=pltpu.VMEM)


def smem():
    return pl.BlockSpec(memory_space=pltpu.SMEM)


def hbm():
    return pl.BlockSpec(memory_space=pl.ANY)


def params():
    return pltpu.CompilerParams(vmem_limit_bytes=56 * 2**20)


def join_weight(flip, w_ref, w_scr):
    for j in range(CHIPS):
        w_scr[48 * j : 48 * j + 48, :] = w_ref[j ^ flip]


def block_of(info, place):
    rc, rz, rx = place // 8, (place // 2) % 4, place % 2
    return info[0] ^ (rz * 4 + rx * 2 + rc)


def halves_beside(rows):
    return jnp.concatenate([rows[:32], rows[32:]], axis=1)


def halves_below(rows):
    return jnp.concatenate([rows[:, :192], rows[:, 192:]], axis=0)


def listed(lists, block):
    window = [(block + 15) % 16, block, (block + 1) % 16]
    return window + [lists[block, n] for n in range(RAND)] + [lists[16, n] for n in range(GLOB)]


def key_mask(ids, length):
    lane = lax.broadcasted_iota(jnp.int32, (1, 64 * len(ids)), 1)
    spot = lane // 64
    number = jnp.zeros_like(lane)
    for n, block in enumerate(ids):
        number = jnp.where(spot == n, block, number)
    return number * 64 + lane % 64 < length


def softmax_rows(scores, mask):
    scores = jnp.where(mask, scores, NEGATIVE)
    expo = jnp.exp(scores - jnp.max(scores, axis=-1, keepdims=True))
    return expo / jnp.sum(expo, axis=-1, keepdims=True)


def attend_kernel(layer, info, lists, x_ref, w_ref, qkv_ref, o_ref, w_scr, kv_scr, q_scr):
    join_weight(info[6 + layer], w_ref, w_scr)
    for half in range(2):
        rows = dot(x_ref[8 * half : 8 * half + 8].reshape(512, x_ref.shape[-1]), w_scr[...])
        qkv_ref[8 * half : 8 * half + 8] = rows.astype(BF16).reshape(8, 64, 576)
    spread_heads(qkv_ref, kv_scr, q_scr)
    length = info[2]

    def one(block, _):
        special = jnp.logical_or(block == lists[16, 0], block == lists[16, 1])

        @pl.when(jnp.logical_not(special))
        def _():
            ids = listed(lists, block)
            mask = key_mask(ids, length)
            outs = []
            for h in range(GROUP_HEADS):
                kv = jnp.concatenate([kv_scr[h, n] for n in ids], axis=0)
                probs = softmax_rows(dot_nt(q_scr[h, block], kv), mask)
                outs.append(dot(probs.astype(BF16), kv)[:, 64:])
            o_ref[block] = halves_beside(jnp.concatenate(outs, axis=1).astype(BF16))

        @pl.when(special)
        def _():
            mask = lax.broadcasted_iota(jnp.int32, (1, 1024), 1) < length
            outs = []
            for h in range(GROUP_HEADS):
                kv = kv_scr[h].reshape(1024, 128)
                probs = softmax_rows(dot_nt(q_scr[h, block], kv), mask)
                outs.append(dot(probs.astype(BF16), kv)[:, 64:])
            o_ref[block] = halves_beside(jnp.concatenate(outs, axis=1).astype(BF16))

        return 0

    lax.fori_loop(0, 16, one, 0)


def spread_heads(qkv_ref, kv_scr, q_scr):
    def one(block, _):
        row = qkv_ref[block]
        zero = jnp.zeros((64, 64), BF16)
        for h in range(GROUP_HEADS):
            kv_scr[h, block] = row[:, 128 * h : 128 * h + 128]
            query = row[:, 384 + 64 * h : 448 + 64 * h] * jnp.asarray(HEAD**-0.5, BF16)
            q_scr[h, block] = jnp.concatenate([query, zero], axis=1)
        return 0

    lax.fori_loop(0, 16, one, 0)


def attend(layer, info, lists, x, weight):
    width = x.shape[-1]
    return pl.pallas_call(
        functools.partial(attend_kernel, layer),
        out_shape=(
            jax.ShapeDtypeStruct((16, 64, 576), BF16),
            jax.ShapeDtypeStruct((16, 32, 384), BF16),
        ),
        in_specs=[smem(), smem(), vmem(), vmem()],
        out_specs=(vmem(), vmem()),
        scratch_shapes=[
            pltpu.VMEM((width, 576), BF16),
            pltpu.VMEM((3, 16, 64, 128), BF16),
            pltpu.VMEM((3, 16, 64, 128), BF16),
        ],
        compiler_params=params(),
        cost_estimate=pl.CostEstimate(
            flops=3 * 10**9, bytes_accessed=6 * 10**6, transcendentals=2 * 10**6
        ),
        name="attend",
    )(info, lists, x, weight)


def attend_back_kernel(
    layer,
    info,
    lists,
    qkv_ref,
    do_ref,
    x_ref,
    w_ref,
    keep_ref,
    send_ref,
    grad_ref,
    w_scr,
    kv_scr,
    q_scr,
    do_scr,
    dkv_scr,
    dq_scr,
    dqkv_scr,
):
    join_weight(info[6 + layer], w_ref, w_scr)
    spread_heads(qkv_ref, kv_scr, q_scr)
    dkv_scr[...] = jnp.zeros_like(dkv_scr)
    length = info[2]

    def lay(block, _):
        row = halves_below(do_ref[block])
        zero = jnp.zeros((64, 64), BF16)
        for h in range(GROUP_HEADS):
            do_scr[h, block] = jnp.concatenate([zero, row[:, 64 * h : 64 * h + 64]], axis=1)
        return 0

    lax.fori_loop(0, 16, lay, 0)

    def rows_back(block, h, kv, mask):
        both = jnp.concatenate([q_scr[h, block], do_scr[h, block]], axis=0)
        pair = dot_nt(both, kv)
        probs = softmax_rows(pair[:64], mask)
        grad_probs = pair[64:]
        delta = jnp.sum(probs * grad_probs, axis=-1, keepdims=True)
        grad_scores = (probs * (grad_probs - delta)).astype(BF16)
        dq = dot(grad_scores, kv)[:, :64] * (HEAD**-0.5)
        dkv = dot_tn(jnp.concatenate([grad_scores, probs.astype(BF16)], axis=0), both)
        return dq, dkv

    def one(block, _):
        special = jnp.logical_or(block == lists[16, 0], block == lists[16, 1])

        @pl.when(jnp.logical_not(special))
        def _():
            ids = listed(lists, block)
            mask = key_mask(ids, length)
            dqs = []
            for h in range(GROUP_HEADS):
                kv = jnp.concatenate([kv_scr[h, n] for n in ids], axis=0)
                dq, dkv = rows_back(block, h, kv, mask)
                dqs.append(dq)
                for at, n in enumerate(ids):
                    dkv_scr[h, n] += dkv[64 * at : 64 * at + 64]
            dq_scr[block] = jnp.concatenate(dqs, axis=1).astype(BF16)

        @pl.when(special)
        def _():
            mask = lax.broadcasted_iota(jnp.int32, (1, 1024), 1) < length
            dqs = []
            for h in range(GROUP_HEADS):
                dq, dkv = rows_back(block, h, kv_scr[h].reshape(1024, 128), mask)
                dqs.append(dq)
                dkv_scr[h] += dkv.reshape(16, 64, 128)
            dq_scr[block] = jnp.concatenate(dqs, axis=1).astype(BF16)

        return 0

    lax.fori_loop(0, 16, one, 0)

    for block in range(16):
        parts = [dkv_scr[h, block].astype(BF16) for h in range(GROUP_HEADS)]
        dqkv_scr[block] = jnp.concatenate(parts + [dq_scr[block]], axis=1)
    for half, ref in enumerate((keep_ref, send_ref)):
        rows = [dqkv_scr[block_of(info, 8 * half + n)] for n in range(8)]
        rows = jnp.concatenate(rows, axis=0)
        ref[...] = dot_nt(rows, w_scr[...]).astype(BF16).reshape(ref.shape)
    width = x_ref.shape[-1]
    grad = dot_tn(dqkv_scr[...].reshape(1024, 576), x_ref[...].reshape(1024, width))
    order = [6, 7, 8, 0, 2, 4, 1, 3, 5]
    grad = jnp.concatenate([grad[64 * n : 64 * n + 64] for n in order], axis=0).astype(BF16)
    for quarter in range(PLANES):
        for side in range(2):
            grad_ref[side ^ info[4], quarter ^ info[3]] = grad[
                144 * quarter : 144 * quarter + 144, 384 * side : 384 * side + 384
            ]


def attend_back(layer, info, lists, qkv, grad_o, x, weight):
    width = x.shape[-1]
    return pl.pallas_call(
        functools.partial(attend_back_kernel, layer),
        out_shape=(
            jax.ShapeDtypeStruct((8, 64, width), BF16),
            jax.ShapeDtypeStruct((8, 64, width), BF16),
            jax.ShapeDtypeStruct((2, PLANES, 144, width // 2), BF16),
        ),
        in_specs=[smem(), smem(), vmem(), vmem(), vmem(), vmem()],
        out_specs=(vmem(), vmem(), vmem()),
        scratch_shapes=[
            pltpu.VMEM((width, 576), BF16),
            pltpu.VMEM((3, 16, 64, 128), BF16),
            pltpu.VMEM((3, 16, 64, 128), BF16),
            pltpu.VMEM((3, 16, 64, 128), BF16),
            pltpu.VMEM((3, 16, 64, 128), F32),
            pltpu.VMEM((16, 64, 192), BF16),
            pltpu.VMEM((16, 64, 576), BF16),
        ],
        compiler_params=params(),
        cost_estimate=pl.CostEstimate(
            flops=8 * 10**9, bytes_accessed=10 * 10**6, transcendentals=2 * 10**6
        ),
        name="attend_back",
    )(info, lists, qkv, grad_o, x, weight)


def slot_a(chip_bits):
    return (chip_bits & 8) | ((chip_bits & 1) << 2) | ((chip_bits >> 1) & 3)


def slot_b(chip_bits):
    return ((chip_bits & 1) << 3) | ((chip_bits & 8) >> 1) | ((chip_bits >> 1) & 3)


def load_weights(info, ao_ref, ar_ref, bo_ref, br_ref, wu, wd, wo, sems):
    chip, core = info[1], info[5]

    def one(j, _):
        at_a, at_b = slot_a(j ^ chip), slot_b(j ^ chip)
        for side, (a, b) in enumerate(((ao_ref, bo_ref), (ar_ref, br_ref))):
            plane = core ^ side
            pltpu.make_async_copy(
                b.at[at_b, :, pl.ds(1536, 384)], wo.at[plane, j], sems.at[0]
            ).start()
            pltpu.make_async_copy(a.at[at_a], wu.at[plane, j], sems.at[1]).start()
            for part in range(2):
                pltpu.make_async_copy(
                    b.at[at_b, :, pl.ds(768 * part, 768)], wd.at[j, plane, part], sems.at[2]
                ).start()
        return 0

    lax.fori_loop(0, CHIPS, one, 0)


def wait_weight(scr, sem):
    pltpu.make_async_copy(scr, scr, sem).wait()


def inside_rows(info):
    row = lax.broadcasted_iota(jnp.int32, (256, 1), 0)
    length = jnp.zeros_like(row)
    for k in range(PLANES):
        length = jnp.where(row // 64 == k, info[8 + k], length)
    return info[0] * 64 + row % 64 < length


def norm_parts(values):
    centre = values - jnp.mean(values, axis=-1, keepdims=True)
    spread = jnp.mean(centre * centre, axis=-1, keepdims=True)
    rate = lax.rsqrt(spread + EPSILON)
    return centre * rate, rate


def norm_back(unit, rate, gain, grad):
    scaled = grad * gain
    inner = jnp.mean(scaled * unit, axis=-1, keepdims=True)
    outer = jnp.mean(scaled, axis=-1, keepdims=True)
    return rate * (scaled - outer - unit * inner), jnp.sum(grad * unit, axis=0, keepdims=True)


CURVE = 0.7978845608028654


def gelu_parts(values):
    square = values * values
    bend = jnp.tanh(CURVE * (values + 0.044715 * (square * values)))
    return 0.5 * values * (1.0 + bend), bend, square


def gelu_slope(values, bend, square):
    return 0.5 * (1.0 + bend) + 0.5 * values * (1.0 - bend * bend) * (
        CURVE * (1.0 + 3 * 0.044715 * square)
    )


def feed_kernel(
    info,
    o_ref,
    h_ref,
    gain_ref,
    ao_ref,
    ar_ref,
    bo_ref,
    br_ref,
    mixed_ref,
    h1_ref,
    up_ref,
    h2_ref,
    next_ref,
    low_ref,
    wu,
    wd,
    wo,
    act_scr,
    sems,
):
    load_weights(info, ao_ref, ar_ref, bo_ref, br_ref, wu, wd, wo, sems)
    for k in range(PLANES):
        mixed_ref[64 * k : 64 * k + 64, :] = jnp.concatenate(
            [halves_below(o_ref[4 * k + g]) for g in range(GROUPS)], axis=1
        )
    mixed = mixed_ref[...]
    wait_weight(wo, sems.at[0])
    attended = jnp.concatenate([dot(mixed, wo[side].reshape(768, 384)) for side in range(2)], axis=1)
    h1 = h_ref[...].reshape(256, 768).astype(F32) + attended
    h1_ref[...] = h1
    x1 = norm_parts(h1)[0] * gain_ref[0:1, :]
    x1_low = x1.astype(BF16)
    wait_weight(wu, sems.at[1])
    for side in range(2):
        for part in range(3):
            at = 1536 * side + 512 * part
            up = dot(x1_low, wu[side, :, :, 512 * part : 512 * part + 512].reshape(768, 512))
            up_ref[:, at : at + 512] = up
            act_scr[:, at : at + 512] = gelu_parts(up)[0].astype(BF16)
    wait_weight(wd, sems.at[2])
    h2 = x1 + dot(act_scr[...], wd[...].reshape(3072, 768))
    h2_ref[...] = h2
    out = jnp.where(inside_rows(info), norm_parts(h2)[0] * gain_ref[1:2, :], 0.0)
    next_ref[...] = out
    low = out.astype(BF16)
    for k in range(PLANES):
        low_ref[k] = low[64 * k : 64 * k + 64]


WEIGHT_SCRATCH = [
    pltpu.VMEM((2, 16, 48, 1536), BF16),
    pltpu.VMEM((16, 2, 2, 48, 768), BF16),
    pltpu.VMEM((2, 16, 48, 384), BF16),
]


def feed(info, o, hidden, gains, weights):
    return pl.pallas_call(
        feed_kernel,
        out_shape=(
            jax.ShapeDtypeStruct((256, 768), BF16),
            jax.ShapeDtypeStruct((256, 768), F32),
            jax.ShapeDtypeStruct((256, 3072), F32),
            jax.ShapeDtypeStruct((256, 768), F32),
            jax.ShapeDtypeStruct((256, 768), F32),
            jax.ShapeDtypeStruct((4, 64, 768), BF16),
        ),
        in_specs=[smem(), vmem(), vmem(), vmem(), hbm(), hbm(), hbm(), hbm()],
        out_specs=tuple(vmem() for _ in range(6)),
        scratch_shapes=WEIGHT_SCRATCH
        + [pltpu.VMEM((256, 3072), BF16), pltpu.SemaphoreType.DMA((3,))],
        compiler_params=params(),
        cost_estimate=pl.CostEstimate(
            flops=3 * 10**9, bytes_accessed=20 * 10**6, transcendentals=10**6
        ),
        name="feed",
    )(info, o, hidden, gains, *weights)


def feed_back_kernel(
    has_extra,
    info,
    base_ref,
    extra_ref,
    gain_ref,
    mixed_ref,
    h1_ref,
    up_ref,
    h2_ref,
    ao_ref,
    ar_ref,
    bo_ref,
    br_ref,
    dh1_ref,
    do_ref,
    dgain_ref,
    keep_ref,
    send_ref,
    wu,
    wd,
    wo,
    gu,
    gd,
    go,
    act_scr,
    dup_scr,
    sems,
    out_sems,
):
    load_weights(info, ao_ref, ar_ref, bo_ref, br_ref, wu, wd, wo, sems)
    me, docs = info[0], info[4]
    if has_extra:
        parts = [
            base_ref[64 * k : 64 * k + 64, :] + extra_ref[k].astype(F32)
            for k in range(PLANES)
        ]
        grad = jnp.concatenate(parts, axis=0)
    else:
        grad = base_ref[...].reshape(256, 768).astype(F32)
    grad = jnp.where(inside_rows(info), grad, 0.0)
    unit2, rate2 = norm_parts(h2_ref[...])
    dh2, dgain1 = norm_back(unit2, rate2, gain_ref[1:2, :], grad)
    dgain_ref[1:2, :] = dgain1
    df = dh2.astype(BF16)
    unit1, rate1 = norm_parts(h1_ref[...])
    x1_low = (unit1 * gain_ref[0:1, :]).astype(BF16)
    wait_weight(wd, sems.at[2])
    wait_weight(wu, sems.at[1])
    dx1 = dh2
    for part in range(8):
        at = 384 * part
        d_act = dot_nt(df, wd[2 * part : 2 * part + 2].reshape(384, 768))
        up = up_ref[:, at : at + 384]
        act, bend, square = gelu_parts(up)
        act = act.astype(BF16)
        dup = (gelu_slope(up, bend, square) * d_act).astype(BF16)
        side, start = part // 4, 384 * (part % 4)
        dx1 += dot_nt(dup, wu[side, :, :, start : start + 384].reshape(768, 384))
        gt_up = dot_tn(dup, x1_low).astype(BF16)
        for n in range(2):
            for half in range(2):
                gu[half, 2 * part + n] = gt_up[
                    192 * n : 192 * n + 192, 384 * half : 384 * half + 384
                ]
        gt_down = dot_tn(df, act).astype(BF16)
        row = 48 * (part % 4)
        for s in range(16):
            gd[part // 4, s, row : row + 48, :] = gt_down[48 * s : 48 * s + 48]
    dh1, dgain0 = norm_back(unit1, rate1, gain_ref[0:1, :], dx1)
    dgain_ref[0:1, :] = dgain0
    dh1_ref[...] = dh1
    da = dh1.astype(BF16)
    gt_out = dot_tn(da, mixed_ref[...]).astype(BF16)
    for s in range(16):
        for half in range(2):
            go[half, s] = gt_out[48 * s : 48 * s + 48, 384 * half : 384 * half + 384]
    wait_weight(wo, sems.at[0])
    do = dot_nt(da[:, 0:384], wo[0].reshape(768, 384))
    do += dot_nt(da[:, 384:768], wo[1].reshape(768, 384))
    do = do.astype(BF16)
    for k in range(PLANES):
        for g in range(GROUPS):
            do_ref[4 * k + g] = halves_beside(do[64 * k : 64 * k + 64, 192 * g : 192 * g + 192])

    def copies(ry, place):
        rx, rz = place // 4, place % 4
        out = []
        for rc, ref in enumerate((keep_ref, send_ref)):
            to = me ^ (rz * 4 + rx * 2 + rc)
            for scr, first, count in ((gu, 0, 192), (go, 192, 48), (gd, 240, 192)):
                out.append(
                    pltpu.make_async_copy(
                        scr.at[ry ^ docs, to],
                        ref.at[ry, place, pl.ds(first, count)],
                        out_sems.at[rc],
                    )
                )
        return out

    def start(n, _):
        for copy in copies(n // 8, n % 8):
            copy.start()
        return 0

    lax.fori_loop(0, 16, start, 0)
    pltpu.make_async_copy(keep_ref, keep_ref, out_sems.at[0]).wait()
    pltpu.make_async_copy(send_ref, send_ref, out_sems.at[1]).wait()


def feed_back(info, base, extra, gains, saved, weights):
    mixed, h1, up, h2 = saved
    has_extra = extra is not None
    if not has_extra:
        extra = jnp.zeros((8, 128), BF16)
    return pl.pallas_call(
        functools.partial(feed_back_kernel, has_extra),
        out_shape=(
            jax.ShapeDtypeStruct((256, 768), F32),
            jax.ShapeDtypeStruct((16, 32, 384), BF16),
            jax.ShapeDtypeStruct((2, 768), F32),
            jax.ShapeDtypeStruct((2, 8, 432, 384), BF16),
            jax.ShapeDtypeStruct((2, 8, 432, 384), BF16),
        ),
        in_specs=[smem()] + [vmem()] * 7 + [hbm()] * 4,
        out_specs=(vmem(), vmem(), vmem(), hbm(), hbm()),
        scratch_shapes=WEIGHT_SCRATCH
        + [
            pltpu.VMEM((2, 16, 192, 384), BF16),
            pltpu.VMEM((2, 16, 192, 384), BF16),
            pltpu.VMEM((2, 16, 48, 384), BF16),
            pltpu.VMEM((8, 128), BF16),
            pltpu.VMEM((8, 128), BF16),
            pltpu.SemaphoreType.DMA((3,)),
            pltpu.SemaphoreType.DMA((2,)),
        ],
        compiler_params=params(),
        cost_estimate=pl.CostEstimate(
            flops=6 * 10**9, bytes_accessed=40 * 10**6, transcendentals=10**6
        ),
        name="feed_back",
    )(info, base, extra, gains, mixed, h1, up, h2, *weights)


def flip(index, bits):
    for bit in (1, 2, 4, 8):
        if bits & bit:
            index = index + bit - 2 * bit * ((index // bit) % 2)
    return index


def greet(peers):
    barrier = pltpu.get_barrier_semaphore()
    for peer in peers:
        pl.semaphore_signal(barrier, inc=1, device_id=peer, device_id_type=MESH)
    pl.semaphore_wait(barrier, len(peers))


def remote(source, target, sems, n, peer):
    return pltpu.make_async_remote_copy(
        source, target, sems.at[0, n], sems.at[1, n], device_id=peer, device_id_type=MESH
    )


def comm_params(number):
    return pltpu.CompilerParams(
        collective_id=number, has_side_effects=True, vmem_limit_bytes=16 * 2**20
    )


def spread_rows(low_ref, x_ref, sems, own_sem, started):
    docs, me = lax.axis_index("docs"), lax.axis_index("seq")
    plane = me // 4
    beside, mate = (docs, flip(me, 2)), (docs, flip(me, 1))
    hops = [
        remote(low_ref.at[flip(plane * 4, 4 * rz) // 4], x_ref.at[me], sems, rz, (docs, flip(me, 4 * rz)))
        for rz in range(1, 4)
    ]
    for copy in hops:
        copy.start()
    own = pltpu.make_async_copy(low_ref.at[plane], x_ref.at[me], own_sem)
    own.start()

    def forward(rz, n, peer, across):
        slot = flip(flip(me, 4 * rz), 2 if across else 0)
        source = low_ref.at[plane] if rz == 0 and not across else x_ref.at[slot]
        copy = remote(source, x_ref.at[slot], sems, n, peer)
        copy.start()
        return copy

    across, mates = [], []
    for rz in range(4):
        if rz > 0:
            hops[rz - 1].wait_recv()
        across.append(forward(rz, 4 + rz, beside, False))
        mates.append(forward(rz, 8 + rz, mate, False))
        started()
    for rz in range(4):
        across[rz].wait_recv()
        mates.append(forward(rz, 12 + rz, mate, True))
    for copy in mates:
        copy.wait_recv()
    for copy in hops + across + mates:
        copy.wait_send()
    own.wait()


def spread_peers():
    docs, me = lax.axis_index("docs"), lax.axis_index("seq")
    return [(docs, flip(me, bits)) for bits in (4, 8, 12, 2, 1)]


def spread_kernel(low_ref, x_ref, sems, own_sem):
    greet(spread_peers())
    spread_rows(low_ref, x_ref, sems, own_sem, lambda: None)


def spread(low, number):
    return pl.pallas_call(
        spread_kernel,
        out_shape=jax.ShapeDtypeStruct((16, 64, low.shape[-1]), BF16),
        in_specs=[hbm()],
        out_specs=hbm(),
        scratch_shapes=[pltpu.SemaphoreType.DMA((2, 16)), pltpu.SemaphoreType.DMA],
        compiler_params=comm_params(number),
        name="spread",
    )(low)


def open_kernel(low_ref, wq_ref, x_ref, w_ref, sems, own_sem, w_sems, w_own):
    docs, me = lax.axis_index("docs"), lax.axis_index("seq")
    plane = me // 4
    over = (1 - docs, me)
    greet(spread_peers() + [over])
    hops = [
        remote(wq_ref, w_ref.at[docs, plane], w_sems, rz, (docs, flip(me, 4 * rz)))
        for rz in range(1, 4)
    ]
    for copy in hops:
        copy.start()
    own = pltpu.make_async_copy(wq_ref, w_ref.at[docs, plane], w_own)
    own.start()
    moved = [remote(wq_ref, w_ref.at[docs, plane], w_sems, 4, over)]
    moved[0].start()

    def started():
        rz = len(moved)
        if rz < 4:
            hops[rz - 1].wait_recv()
            slot = w_ref.at[docs, flip(me, 4 * rz) // 4]
            moved.append(remote(slot, slot, w_sems, 4 + rz, over))
            moved[-1].start()

    spread_rows(low_ref, x_ref, sems, own_sem, started)
    for copy in moved:
        copy.wait_recv()
    for copy in hops + moved:
        copy.wait_send()
    own.wait()


def open_layer(low, wq, number):
    return pl.pallas_call(
        open_kernel,
        out_shape=(
            jax.ShapeDtypeStruct((16, 64, low.shape[-1]), BF16),
            jax.ShapeDtypeStruct((2, 4) + wq.shape, BF16),
        ),
        in_specs=[hbm(), hbm()],
        out_specs=(hbm(), hbm()),
        scratch_shapes=[
            pltpu.SemaphoreType.DMA((2, 16)),
            pltpu.SemaphoreType.DMA,
            pltpu.SemaphoreType.DMA((2, 8)),
            pltpu.SemaphoreType.DMA,
        ],
        compiler_params=comm_params(number),
        name="open_layer",
    )(low, wq)


def exchange_kernel(x_ref, o_ref, sems, own_sem):
    docs, me = lax.axis_index("docs"), lax.axis_index("seq")
    order = list(range(15, 0, -1))
    greet([(docs, flip(me, bits)) for bits in order])
    copies = []
    for bits in order:
        peer = flip(me, bits)
        copies.append(remote(x_ref.at[peer], o_ref.at[me], sems, bits, (docs, peer)))
        copies[-1].start()
    own = pltpu.make_async_copy(x_ref.at[me], o_ref.at[me], own_sem)
    own.start()
    for copy in copies:
        copy.wait_recv()
    for copy in copies:
        copy.wait_send()
    own.wait()


def exchange(x, number):
    return pl.pallas_call(
        exchange_kernel,
        out_shape=jax.ShapeDtypeStruct(x.shape, x.dtype),
        in_specs=[hbm()],
        out_specs=hbm(),
        scratch_shapes=[pltpu.SemaphoreType.DMA((2, 16)), pltpu.SemaphoreType.DMA],
        compiler_params=comm_params(number),
        name="exchange",
    )(x)


def collect_kernel(keep_ref, send_ref, out_ref, got_core, got_x, sum_x, near, sums, land, sems):
    docs, me = lax.axis_index("docs"), lax.axis_index("seq")
    plane = me // 4
    beside, mate = (docs, flip(me, 2)), (docs, flip(me, 1))
    greet(spread_peers())
    order = (3, 2, 1, 0)
    first = {}
    for rz in order:
        for rx in (1, 0):
            n = 2 * rz + rx
            first[n] = remote(send_ref.at[n], got_core.at[n], sems, n, mate)
            first[n].start()
    across, hops = {}, []
    for rz in order:
        n = 2 * rz + 1
        first[n].wait_recv()
        sum_x[rz] = (keep_ref[n].astype(F32) + got_core[n].astype(F32)).astype(BF16)
        across[rz] = remote(sum_x.at[rz], got_x.at[rz], sems, 8 + rz, beside)
        across[rz].start()
        n = 2 * rz
        first[n].wait_recv()
        near[rz] = keep_ref[n].astype(F32) + got_core[n].astype(F32)
    for rz in order:
        across[rz].wait_recv()
        total = (near[rz] + got_x[rz].astype(F32)).astype(BF16)
        if rz == 0:
            land[plane] = total
        else:
            sums[rz] = total
            copy = remote(sums.at[rz], land.at[plane], sems, 12 + rz, (docs, flip(me, 4 * rz)))
            copy.start()
            hops.append(copy)
    for copy in hops:
        copy.wait_recv()
    out_ref[...] = land[...]
    for copy in list(first.values()) + list(across.values()) + hops:
        copy.wait_send()


def collect(keep, send, number):
    width = keep.shape[-1]
    return pl.pallas_call(
        collect_kernel,
        out_shape=jax.ShapeDtypeStruct((PLANES, 64, width), BF16),
        in_specs=[vmem(), vmem()],
        out_specs=vmem(),
        scratch_shapes=[
            pltpu.VMEM((8, 64, width), BF16),
            pltpu.VMEM((4, 64, width), BF16),
            pltpu.VMEM((4, 64, width), BF16),
            pltpu.VMEM((4, 64, width), F32),
            pltpu.VMEM((4, 64, width), BF16),
            pltpu.VMEM((4, 64, width), BF16),
            pltpu.SemaphoreType.DMA((2, 16)),
        ],
        compiler_params=comm_params(number),
        name="collect",
    )(keep, send)


class Transfer:
    def __init__(self, steps):
        self.steps = steps
        self.result = None
        self.pending = next(steps)

    def go_on(self, arrived):
        try:
            self.pending = self.steps.send(arrived)
        except StopIteration as end:
            self.pending = ()
            self.result = end.value


def beside(result, *transfers):
    live = [transfer for transfer in transfers if transfer.result is None]
    result, arrived = lax.optimization_barrier((result, [transfer.pending for transfer in live]))
    for transfer, values in zip(live, arrived):
        transfer.go_on(values)
    return result


def in_core_order(core, own, other):
    return jnp.where(
        core == 0,
        jnp.concatenate([own, other], axis=0),
        jnp.concatenate([other, own], axis=0),
    )


def pick(stack, index):
    return lax.dynamic_index_in_dim(stack, index, 0, keepdims=False)


def pack_qkv(shard, me, core):
    rows = shard.shape[0]
    parts = shard.reshape(rows, 3, GROUPS, GROUP_HEADS, HEAD)
    pairs = jnp.transpose(parts[:, 1:], (2, 0, 3, 1, 4)).reshape(GROUPS, rows, 384)
    query = jnp.transpose(parts[:, 0], (1, 0, 2, 3)).reshape(GROUPS, rows, 192)
    packed = jnp.concatenate([pairs, query], axis=2)
    group = me & 3
    return [pick(packed, group)] + [swap(pick(packed, group ^ r), r) for r in range(1, 4)]


def gather_qkv(shard, me, core):
    got = yield pack_qkv(shard, me, core)
    held = jnp.stack([in_core_order(core, got[0], got[1]), in_core_order(core, got[2], got[3])])
    for bits in (4, 8):
        held = jnp.concatenate((yield (held, swap(held, bits))), axis=0)
    return jnp.concatenate((yield (held, swap_docs(held))), axis=0)


def gather_gains(shard):
    held = shard.reshape(1, -1)
    for bits in (1, 2, 4, 8):
        held = jnp.concatenate((yield (held, swap(held, bits))), axis=0)
    held = jnp.concatenate((yield (held, swap_docs(held))), axis=0)
    number = lax.axis_index("docs") * 16 + lax.axis_index("seq")
    held = jnp.take(held, jnp.arange(32) ^ number, axis=0).reshape((32,) + shard.shape)
    return jnp.transpose(held, (1, 2, 0, 3)).reshape(shard.shape[:2] + (-1,)).astype(F32)


def gather_rest(out_shard, up_shard, down_shard, core):
    def mine(shard, side):
        half = shard.shape[1] // 2
        return lax.dynamic_slice_in_dim(shard, side * half, half, axis=1)

    got_up, got_out = yield swap((mine(up_shard, 1 - core), mine(out_shard, 1 - core)), 1)
    up = in_core_order(core, mine(up_shard, core), got_up)
    out = in_core_order(core, mine(out_shard, core), got_out)
    down = jnp.concatenate([down_shard[:48], down_shard[48:]], axis=1)
    held = jnp.concatenate([up, down, out], axis=1)[None]
    for bits in (4, 8):
        held = jnp.concatenate((yield (held, swap(held, bits))), axis=0)
    first, second = held[:, :, :1536], held[:, :, 1536:]
    first, second, got_first, got_second = yield (
        first,
        second,
        swap(first, 2),
        swap_docs(second),
    )
    first = jnp.concatenate([first, got_first], axis=0)
    second = jnp.concatenate([second, got_second], axis=0)
    first, second, got_first, got_second = yield (
        first,
        second,
        swap_docs(first),
        swap(second, 2),
    )
    first = jnp.concatenate([first, got_first], axis=0)
    second = jnp.concatenate([second, got_second], axis=0)
    return (yield (first, swap(first, 1), second, swap(second, 1)))


def add_low(first, second):
    return (first.astype(F32) + second.astype(F32)).astype(BF16)


def add_full(first, second):
    return first.astype(F32) + second.astype(F32)


def reduce_rest(keep, send):
    cut = 224
    keep, got = yield (keep, swap(send, 1))
    first = add_low(keep[:, :, :cut], got[:, :, :cut])
    second = add_low(keep[:, :, cut:], got[:, :, cut:]).reshape(2, 2, 4, 432 - cut, 384)
    first, second, got_first, got_second = yield (
        first[0],
        second[:, 0],
        swap_docs(first[1]),
        swap(second[:, 1], 2),
    )
    first = add_low(first, got_first).reshape(2, 4, cut, 384)
    second = add_low(second, got_second)
    first, second, got_first, got_second = yield (
        first[0],
        second[0],
        swap(first[1], 2),
        swap_docs(second[1]),
    )
    held = jnp.concatenate([add_low(first, got_first), add_low(second, got_second)], axis=1)
    held = add_low(*(yield (held[:2], swap(held[2:], 8))))
    total = add_full(*(yield (held[0], swap(held[1], 4))))
    down = total[240:].reshape(4, 48, 384)
    return (
        total[192:240].T,
        total[:192].T,
        jnp.transpose(down, (0, 2, 1)).reshape(1536, 48),
    )


def route_table():
    edges = []
    for device in range(16):
        z, group = device >> 2, device & 3
        for t in range(3):
            local = 3 * z + t
            number = 16 * (local // 4) + 4 * group + local % 4
            edges.append((device, t, number // 3, number % 3))
    rounds = []
    left = list(edges)
    for _ in range(3):
        match = {}

        def place(device, seen):
            for edge in left:
                if edge[0] == device and edge[2] not in seen:
                    seen.add(edge[2])
                    if edge[2] not in match or place(match[edge[2]][0], seen):
                        match[edge[2]] = edge
                        return True
            return False

        for device in range(16):
            place(device, set())
        chosen = sorted(match.values())
        rounds.append(chosen)
        left = [edge for edge in left if edge not in chosen]
    return rounds


def reduce_qkv(grad, me):
    held = add_low(*(yield (grad[0], swap_docs(grad[1]))))
    held = add_low(*(yield (held[:2], swap(held[2:], 8))))
    total = add_full(*(yield (held[0], swap(held[1], 4))))
    granules = total.reshape(3, 48, 384)
    moved, spots = [], []
    for chosen in route_table():
        take = jnp.asarray([edge[1] for edge in chosen], jnp.int32)
        moved.append(
            lax.ppermute(
                pick(granules, take[me]), "seq", [(edge[0], edge[2]) for edge in chosen]
            )
        )
        spots.append([edge[3] for edge in sorted(chosen, key=lambda edge: edge[2])])
    got = jnp.stack((yield moved))
    where = jnp.asarray(spots, jnp.int32)[:, me]
    place = jnp.arange(3, dtype=jnp.int32)
    source = jnp.sum(jnp.where(where[None, :] == place[:, None], place[None, :], 0), axis=1)
    return jnp.take(got, source, axis=0).reshape(144, 384).T


def reduce_gains(grads):
    number = lax.axis_index("docs") * 16 + lax.axis_index("seq")
    shape = grads.shape[:2]
    held = jnp.transpose(grads.reshape(shape + (32, -1)), (2, 0, 1, 3)).reshape(32, -1)
    held = jnp.take(held, jnp.arange(32) ^ number, axis=0)
    held = add_full(*(yield (held[:16], swap_docs(held[16:]))))
    for bits in (8, 4, 2, 1):
        held = add_full(*(yield (held[:bits], swap(held[bits:], bits))))
    return held.reshape(shape + (-1,))


def local_two_by_sixteen(
    tokens,
    qkv_weight,
    out_weight,
    up_weight,
    down_weight,
    norm_gains,
    doc_lengths,
    global_ids,
    random_ids,
    cotangent,
):
    docs_dev, block, width = tokens.shape
    me = lax.axis_index("seq").astype(jnp.int32)
    docs = lax.axis_index("docs").astype(jnp.int32)
    plane, core = me >> 2, me & 1
    chip = docs * 8 + (me >> 1)
    info = jnp.concatenate(
        [
            jnp.stack(
                [me, chip, pick(doc_lengths, plane), plane, docs, core, jnp.zeros_like(me), chip]
            ),
            doc_lengths,
        ]
    )
    lists = jnp.concatenate(
        [
            lax.dynamic_index_in_dim(random_ids, plane, 1, keepdims=False),
            jnp.pad(pick(global_ids, plane), (0, 1))[None],
        ],
        axis=0,
    )

    def rest(layer):
        return Transfer(
            gather_rest(out_weight[layer], up_weight[layer], down_weight[layer], core)
        )

    got = pack_qkv(qkv_weight[0], me, core)
    pairs = [in_core_order(core, got[0], got[1]), in_core_order(core, got[2], got[3])]
    side = (me >> 1) & 1
    wq = jnp.where(side == 0, jnp.stack(pairs), jnp.stack(pairs[::-1]))
    rest_0, gains = rest(0), Transfer(gather_gains(norm_gains))
    wq, low = beside((wq, tokens), rest_0, gains)
    x, wq = beside(open_layer(low, wq, 0), rest_0, gains)
    weights = [wq.reshape(CHIPS, 48, 576), None]
    qkv, o = beside(attend(0, info, lists, x, weights[0]), rest_0, gains)
    held = [(x, qkv)]
    o = beside(exchange(o, 1), rest_0, gains)
    rest_1, wq = rest(1), Transfer(gather_qkv(qkv_weight[1], me, core))
    o = beside(o, rest_1, wq, gains)
    o = beside(o, rest_1, wq)
    o = beside(o, rest_1, wq, rest_0)
    o = beside(o, rest_0)
    gain = gains.result
    fed = beside(feed(info, o, tokens, gain[0], rest_0.result), wq)
    held[0] += (fed[:4],)
    x = beside(spread(fed[5], 2), rest_1)
    weights[1] = wq.result
    qkv, o = beside(attend(1, info, lists, x, weights[1]), rest_1)
    o = beside(exchange(o, 3), rest_1)
    fed_1 = feed(info, o, fed[4], gain[1], rest_1.result)
    held.append((x, qkv, fed_1[:4]))
    base, grad_o, gain_1, keep, send = feed_back(
        info, cotangent, None, gain[1], held[1][2], rest_1.result
    )
    rest_1 = Transfer(reduce_rest(keep, send))
    grad_o = beside(exchange(grad_o, 4), rest_1)
    keep, send, grad_qkv = beside(
        attend_back(1, info, lists, held[1][1], grad_o, held[1][0], weights[1]), rest_1
    )
    qkv_1 = Transfer(reduce_qkv(grad_qkv, me))
    extra = beside(collect(keep, send, 5), rest_1, qkv_1)
    base, grad_o, gain_0, keep, send = beside(
        feed_back(info, base, extra, gain[0], held[0][2], rest_0.result), rest_1, qkv_1
    )
    rest_0, gains = Transfer(reduce_rest(keep, send)), Transfer(reduce_gains(jnp.stack([gain_0, gain_1])))
    grad_o = beside(exchange(grad_o, 6), rest_0, rest_1, qkv_1, gains)
    keep, send, grad_qkv = beside(
        attend_back(0, info, lists, held[0][1], grad_o, held[0][0], weights[0]),
        rest_0,
        qkv_1,
        gains,
    )
    qkv_0 = Transfer(reduce_qkv(grad_qkv, me))
    extra = beside(collect(keep, send, 7), rest_0, qkv_0, gains)
    grad_tokens = base.reshape(docs_dev, block, width) + extra.astype(F32)
    while any(transfer.result is None for transfer in (rest_0, qkv_0, gains)):
        grad_tokens = beside(grad_tokens, rest_0, qkv_0, gains)
    return (
        fed_1[4].astype(BF16).reshape(docs_dev, block, width),
        grad_tokens,
        jnp.stack([qkv_0.result, qkv_1.result]),
        *(jnp.stack(pair) for pair in zip(rest_0.result, rest_1.result)),
        gains.result,
    )


def solution(mesh):
    def local(*args):
        docs_dev, _, width = args[0].shape
        if fits(mesh, docs_dev, width // HEAD):
            return local_two_by_sixteen(*args)
        return local_any_mesh(*args)

    return jax.shard_map(
        local,
        mesh=mesh,
        in_specs=(
            P("docs", "seq", None),
            P(None, ("docs", "seq"), None),
            P(None, ("docs", "seq"), None),
            P(None, ("docs", "seq"), None),
            P(None, ("docs", "seq"), None),
            P(None, None, ("docs", "seq")),
            P("docs"),
            P("docs", None),
            P(None, "docs", None),
            P("docs", "seq", None),
        ),
        out_specs=(
            P("docs", "seq", None),
            P("docs", "seq", None),
            P(None, "docs", "seq"),
            P(None, "docs", "seq"),
            P(None, "docs", "seq"),
            P(None, "docs", "seq"),
            P(None, None, ("docs", "seq")),
        ),
        check_vma=False,
    )
```

```python
import functools

import jax
import jax.numpy as jnp
from jax import lax
from jax.experimental import pallas as pl
from jax.experimental.pallas import tpu as pltpu
from jax.sharding import PartitionSpec as P

HEAD = 64
RAND = 3
GLOB = 2
LAYERS = 2


NEGATIVE = -1e30
EPSILON = 1e-05


def with_halo(cells, sides, width):
    for axis, dim in sides:
        count = lax.axis_size(axis)
        head = lax.slice_in_dim(cells, 0, width, axis=dim)
        tail = lax.slice_in_dim(cells, cells.shape[dim] - width, cells.shape[dim], axis=dim)
        cells = jnp.concatenate(
            [
                lax.ppermute(tail, axis, [(i, (i + 1) % count) for i in range(count)]),
                cells,
                lax.ppermute(head, axis, [((i + 1) % count, i) for i in range(count)]),
            ],
            axis=dim,
        )
    return cells


def combined_all(value, axis, join):
    pieces = jax.tree.map(lambda part: lax.all_gather(part, axis), value)
    head = jax.tree.map(lambda part: part[0], pieces)
    tail = jax.tree.map(lambda part: part[1:], pieces)
    so_far, _ = lax.scan(lambda so_far, piece: (join(so_far, piece), None), head, tail)
    return so_far


def norm_rows(values, gain):
    centre = values - jnp.mean(values, axis=-1, keepdims=True)
    spread = jnp.mean(centre * centre, axis=-1, keepdims=True)
    return centre * lax.rsqrt(spread + EPSILON) * gain


def gelu_tanh(values):
    return jax.nn.gelu(values, approximate=True)


def earlier_equal(values):
    length = values.shape[-1]
    order = jnp.arange(length, dtype=jnp.int32)
    before = order[None, :] < order[:, None]
    same = values[..., :, None] == values[..., None, :]
    return jnp.sum(jnp.logical_and(same, before), axis=-1)


def merge_stats(first, second):
    highest = jnp.maximum(first[0], second[0])
    return (
        highest,
        first[1] * jnp.exp(first[0] - highest) + second[1] * jnp.exp(second[0] - highest),
    )


def sparse_probs(query, key_part, key_inside, scale):
    scores = (
        jnp.einsum("kbhd,kjhd->khbj", query, key_part, preferred_element_type=jnp.float32) * scale
    )
    scores = jnp.where(key_inside[:, None, None, :], scores, NEGATIVE)
    expo = jnp.exp(scores - jnp.max(scores, axis=-1, keepdims=True))
    return expo / jnp.sum(expo, axis=-1, keepdims=True)


def global_scores(global_query, local_keys, inside, scale):
    scores = (
        jnp.einsum(
            "ksbhd,kjhd->kshbj", global_query, local_keys, preferred_element_type=jnp.float32
        )
        * scale
    )
    return jnp.where(inside[:, None, None, None, :], scores, NEGATIVE)


def local_any_mesh(
    tokens,
    qkv_weight,
    out_weight,
    up_weight,
    down_weight,
    norm_gains,
    doc_lengths,
    global_ids,
    random_ids,
    cotangent,
):
    nseq = lax.axis_size("seq")
    device = lax.axis_index("seq")
    docs_dev, block, width = tokens.shape
    count = docs_dev * block
    heads = width // HEAD
    scale = HEAD ** (-0.5)
    capacity = max(2, (docs_dev * RAND + nseq - 1) // nseq)
    global_capacity = (docs_dev * GLOB + nseq - 1) // nseq
    entries = docs_dev * RAND
    global_entries = docs_dev * GLOB
    offsets = jnp.arange(block, dtype=jnp.int32)
    inside = (device * block + offsets)[None, :] < doc_lengths[:, None]
    live_rows = inside.reshape(count, 1)
    wanted = random_ids.reshape(nseq, entries)
    wanted_rank = earlier_equal(wanted)
    slot_ids = jnp.arange(capacity, dtype=jnp.int32)
    hits = jnp.logical_and((wanted == device)[:, :, None], wanted_rank[:, :, None] == slot_ids)
    hits = jnp.any(hits.reshape(nseq, docs_dev, RAND, capacity), axis=2)
    hits = jnp.transpose(hits, (0, 2, 1))
    doc_ids = jnp.arange(docs_dev, dtype=jnp.int32)
    send_doc = jnp.sum(jnp.where(hits, doc_ids, 0), axis=2)
    send_live = jnp.any(hits, axis=2)
    owner_pick = hits.astype(jnp.float32)
    listed_here = lax.dynamic_index_in_dim(wanted, device, 0, keepdims=False)
    listed_rank = lax.dynamic_index_in_dim(wanted_rank, device, 0, keepdims=False)
    fetch_slot = listed_here * capacity + listed_rank
    global_block = global_ids.reshape(global_entries)
    global_rank = earlier_equal(global_block)
    global_slot = global_block * global_capacity + global_rank
    own_entry = global_block == device
    owned = jnp.logical_and(
        own_entry[:, None], global_rank[:, None] == jnp.arange(global_capacity, dtype=jnp.int32)
    )
    entry_doc = jnp.arange(global_entries, dtype=jnp.int32) // GLOB
    global_send_doc = jnp.sum(jnp.where(owned, entry_doc[:, None], 0), axis=0)
    global_send_live = jnp.any(owned, axis=0)
    own_flag = jnp.any(own_entry.reshape(docs_dev, GLOB), axis=1)
    own_slot = jnp.sum(jnp.where(own_entry, global_rank, 0).reshape(docs_dev, GLOB), axis=1)
    neighbours = jnp.stack([(device - 1) % nseq, device, (device + 1) % nseq])
    key_blocks = jnp.concatenate(
        [
            jnp.broadcast_to(neighbours[None, :], (docs_dev, 3)),
            listed_here.reshape(docs_dev, RAND),
            global_ids,
        ],
        axis=1,
    )
    span = key_blocks.shape[1] * block
    key_inside = (key_blocks[:, :, None] * block + offsets < doc_lengths[:, None, None]).reshape(
        docs_dev, span
    )
    keep_local = inside[:, None, None, None, :]
    hidden = tokens.reshape(count, width).astype(jnp.float32)
    held = []
    for layer in range(LAYERS):
        weights = (
            lax.all_gather(qkv_weight[layer], ("docs", "seq"), axis=0, tiled=True),
            lax.all_gather(out_weight[layer], ("docs", "seq"), axis=0, tiled=True),
            lax.all_gather(up_weight[layer], ("docs", "seq"), axis=0, tiled=True),
            lax.all_gather(down_weight[layer], ("docs", "seq"), axis=0, tiled=True),
            lax.all_gather(norm_gains[layer], ("docs", "seq"), axis=1, tiled=True),
        )
        weight_qkv, weight_out, weight_up, weight_down, gain_pair = weights
        gain_pair = gain_pair.astype(jnp.float32)
        lowered = hidden.astype(jnp.bfloat16)
        projected = (
            jnp.dot(lowered, weight_qkv, preferred_element_type=jnp.float32)
            .astype(jnp.bfloat16)
            .reshape(docs_dev, block, 3 * width)
        )
        pairs = projected[:, :, width:]
        window = with_halo(pairs, (("seq", 1),), block)
        outgoing = jnp.where(
            send_live[:, :, None, None],
            jnp.take(pairs, send_doc, axis=0),
            jnp.zeros((), jnp.bfloat16),
        )
        incoming = lax.all_to_all(outgoing, "seq", split_axis=0, concat_axis=0, tiled=True)
        fetched = jnp.take(
            incoming.reshape(nseq * capacity, block, 2 * width), fetch_slot, axis=0
        ).reshape(docs_dev, RAND * block, 2 * width)
        global_send = jnp.where(
            global_send_live[:, None, None],
            jnp.take(projected, global_send_doc, axis=0),
            jnp.zeros((), jnp.bfloat16),
        )
        gathered = lax.all_gather(global_send, "seq", axis=0, tiled=True)
        global_picked = jnp.take(gathered, global_slot, axis=0).reshape(
            docs_dev, GLOB, block, 3 * width
        )
        global_query = global_picked[..., :width].reshape(docs_dev, GLOB, block, heads, HEAD)
        listed_pairs = jnp.concatenate(
            [
                window,
                fetched,
                global_picked[..., width:].reshape(docs_dev, GLOB * block, 2 * width),
            ],
            axis=1,
        )
        query = projected[:, :, :width].reshape(docs_dev, block, heads, HEAD)
        key_part = listed_pairs[:, :, :width].reshape(docs_dev, span, heads, HEAD)
        value_part = listed_pairs[:, :, width:].reshape(docs_dev, span, heads, HEAD)
        probs = sparse_probs(query, key_part, key_inside, scale)
        mixed = jnp.einsum(
            "khbj,kjhd->kbhd",
            probs.astype(jnp.bfloat16),
            value_part,
            preferred_element_type=jnp.float32,
        )
        local_keys = projected[:, :, width : 2 * width].reshape(docs_dev, block, heads, HEAD)
        local_values = projected[:, :, 2 * width :].reshape(docs_dev, block, heads, HEAD)
        wide_scores = global_scores(global_query, local_keys, inside, scale)
        global_top = jnp.max(wide_scores, axis=-1)
        global_total = jnp.sum(
            jnp.where(keep_local, jnp.exp(wide_scores - global_top[..., None]), 0.0), axis=-1
        )
        global_top, global_total = combined_all((global_top, global_total), "seq", merge_stats)
        wide_probs = (
            jnp.where(keep_local, jnp.exp(wide_scores - global_top[..., None]), 0.0)
            / global_total[..., None]
        )
        wide_part = jnp.einsum(
            "kshbj,kjhd->ksbhd",
            wide_probs.astype(jnp.bfloat16),
            local_values,
            preferred_element_type=jnp.float32,
        )
        wide_buffer = (
            jnp.zeros((nseq * global_capacity, block, width), jnp.float32)
            .at[global_slot]
            .set(wide_part.reshape(global_entries, block, width))
        )
        wide_sum = lax.psum_scatter(wide_buffer, "seq", scatter_dimension=0, tiled=True)
        attended = jnp.where(
            own_flag[:, None, None],
            jnp.take(wide_sum, own_slot, axis=0),
            mixed.reshape(docs_dev, block, width),
        )
        attended = attended.reshape(count, width).astype(jnp.bfloat16)
        after_attn = hidden + jnp.dot(attended, weight_out, preferred_element_type=jnp.float32)
        normed = norm_rows(after_attn, gain_pair[0])
        normed_low = normed.astype(jnp.bfloat16)
        up_values = jnp.dot(normed_low, weight_up, preferred_element_type=jnp.float32)
        activated = gelu_tanh(up_values).astype(jnp.bfloat16)
        after_ffn = normed + jnp.dot(activated, weight_down, preferred_element_type=jnp.float32)
        held.append(
            (
                weights,
                lowered,
                projected,
                listed_pairs,
                global_query,
                global_top,
                global_total,
                attended,
                after_attn,
                normed_low,
                up_values,
                activated,
                after_ffn,
            )
        )
        hidden = jnp.where(live_rows, norm_rows(after_ffn, gain_pair[1]), 0.0)
    gradient = cotangent.reshape(count, width).astype(jnp.float32)
    layer_grads = []
    for layer in reversed(range(LAYERS)):
        (
            weights,
            lowered,
            projected,
            listed_pairs,
            global_query,
            global_top,
            global_total,
            attended,
            after_attn,
            normed_low,
            up_values,
            activated,
            after_ffn,
        ) = held[layer]
        weights = (
            lax.all_gather(qkv_weight[layer], ("docs", "seq"), axis=0, tiled=True),
            lax.all_gather(out_weight[layer], ("docs", "seq"), axis=0, tiled=True),
            lax.all_gather(up_weight[layer], ("docs", "seq"), axis=0, tiled=True),
            lax.all_gather(down_weight[layer], ("docs", "seq"), axis=0, tiled=True),
            lax.all_gather(norm_gains[layer], ("docs", "seq"), axis=1, tiled=True),
        )
        weight_qkv, weight_out, weight_up, weight_down, gain_pair = weights
        gain_pair = gain_pair.astype(jnp.float32)
        gradient = jnp.where(live_rows, gradient, 0.0)
        grad_ffn, grad_gain_out = jax.vjp(norm_rows, after_ffn, gain_pair[1])[1](gradient)
        grad_down_low = grad_ffn.astype(jnp.bfloat16)
        grad_down_layer = jnp.einsum(
            "rf,rd->fd", activated, grad_down_low, preferred_element_type=jnp.float32
        )
        grad_activated = jnp.einsum(
            "rd,fd->rf", grad_down_low, weight_down, preferred_element_type=jnp.float32
        )
        grad_up_low = jax.vjp(gelu_tanh, up_values)[1](grad_activated)[0].astype(jnp.bfloat16)
        grad_up_layer = jnp.einsum(
            "rd,rf->df", normed_low, grad_up_low, preferred_element_type=jnp.float32
        )
        grad_normed = grad_ffn + jnp.einsum(
            "rf,df->rd", grad_up_low, weight_up, preferred_element_type=jnp.float32
        )
        grad_attn, grad_gain_mid = jax.vjp(norm_rows, after_attn, gain_pair[0])[1](grad_normed)
        grad_attn_low = grad_attn.astype(jnp.bfloat16)
        grad_out_layer = jnp.einsum(
            "rd,re->de", attended, grad_attn_low, preferred_element_type=jnp.float32
        )
        grad_mixed = (
            jnp.einsum("re,de->rd", grad_attn_low, weight_out, preferred_element_type=jnp.float32)
            .astype(jnp.bfloat16)
            .reshape(docs_dev, block, width)
        )
        query = projected[:, :, :width].reshape(docs_dev, block, heads, HEAD)
        key_part = listed_pairs[:, :, :width].reshape(docs_dev, span, heads, HEAD)
        value_part = listed_pairs[:, :, width:].reshape(docs_dev, span, heads, HEAD)
        probs = sparse_probs(query, key_part, key_inside, scale)
        grad_sparse = jnp.where(
            own_flag[:, None, None], jnp.zeros((), jnp.bfloat16), grad_mixed
        ).reshape(docs_dev, block, heads, HEAD)
        grad_probs = jnp.einsum(
            "kbhd,kjhd->khbj", grad_sparse, value_part, preferred_element_type=jnp.float32
        )
        delta = jnp.sum(probs * grad_probs, axis=-1, keepdims=True)
        grad_scores = (probs * (grad_probs - delta)).astype(jnp.bfloat16)
        grad_query = (
            jnp.einsum("khbj,kjhd->kbhd", grad_scores, key_part, preferred_element_type=jnp.float32)
            * scale
        )
        grad_key_part = (
            jnp.einsum("khbj,kbhd->kjhd", grad_scores, query, preferred_element_type=jnp.float32)
            * scale
        )
        grad_value_part = jnp.einsum(
            "khbj,kbhd->kjhd",
            probs.astype(jnp.bfloat16),
            grad_sparse,
            preferred_element_type=jnp.float32,
        )
        grad_listed = jnp.concatenate(
            [
                grad_key_part.reshape(docs_dev, span, width),
                grad_value_part.reshape(docs_dev, span, width),
            ],
            axis=2,
        )
        wide_out = jnp.where(
            global_send_live[:, None, None],
            jnp.take(grad_mixed, global_send_doc, axis=0),
            jnp.zeros((), jnp.bfloat16),
        )
        wide_all = lax.all_gather(wide_out, "seq", axis=0, tiled=True)
        wide_grad = jnp.take(wide_all, global_slot, axis=0).reshape(
            docs_dev, GLOB, block, heads, HEAD
        )
        local_keys = projected[:, :, width : 2 * width].reshape(docs_dev, block, heads, HEAD)
        local_values = projected[:, :, 2 * width :].reshape(docs_dev, block, heads, HEAD)
        wide_scores = global_scores(global_query, local_keys, inside, scale)
        wide_probs = (
            jnp.where(keep_local, jnp.exp(wide_scores - global_top[..., None]), 0.0)
            / global_total[..., None]
        )
        wide_grad_probs = jnp.einsum(
            "ksbhd,kjhd->kshbj", wide_grad, local_values, preferred_element_type=jnp.float32
        )
        wide_delta = lax.psum(jnp.sum(wide_probs * wide_grad_probs, axis=-1), "seq")
        wide_grad_scores = (wide_probs * (wide_grad_probs - wide_delta[..., None])).astype(
            jnp.bfloat16
        )
        wide_grad_query = (
            jnp.einsum(
                "kshbj,kjhd->ksbhd",
                wide_grad_scores,
                local_keys,
                preferred_element_type=jnp.float32,
            )
            * scale
        )
        wide_grad_keys = (
            jnp.einsum(
                "kshbj,ksbhd->kjhd",
                wide_grad_scores,
                global_query,
                preferred_element_type=jnp.float32,
            )
            * scale
        )
        wide_grad_values = jnp.einsum(
            "kshbj,ksbhd->kjhd",
            wide_probs.astype(jnp.bfloat16),
            wide_grad,
            preferred_element_type=jnp.float32,
        )
        global_grads = jnp.concatenate(
            [
                wide_grad_query.reshape(global_entries, block, width),
                grad_listed[:, (3 + RAND) * block :, :].reshape(global_entries, block, 2 * width),
            ],
            axis=2,
        )
        global_buffer = (
            jnp.zeros((nseq * global_capacity, block, 3 * width), jnp.float32)
            .at[global_slot]
            .set(global_grads)
        )
        global_share = lax.psum_scatter(global_buffer, "seq", scatter_dimension=0, tiled=True)
        global_mine = jnp.where(
            own_flag[:, None, None], jnp.take(global_share, own_slot, axis=0), 0.0
        )
        grad_fetched = grad_listed[:, 3 * block : (3 + RAND) * block, :].reshape(
            entries, block, 2 * width
        )
        back_out = (
            jnp.zeros((nseq * capacity, block, 2 * width), jnp.float32)
            .at[fetch_slot]
            .set(grad_fetched)
            .reshape(nseq, capacity, block, 2 * width)
        )
        back_in = lax.all_to_all(back_out, "seq", split_axis=0, concat_axis=0, tiled=True)
        grad_random = jnp.einsum(
            "dck,dcbf->kbf", owner_pick, back_in, precision=lax.Precision.HIGHEST
        )
        grad_window = grad_listed[:, : 3 * block, :]
        edges = jnp.concatenate([grad_window[:, :block], grad_window[:, 2 * block :]], axis=1)
        beside_all = with_halo(edges, (("seq", 1),), block)
        grad_pairs = (
            grad_window[:, block : 2 * block]
            + beside_all[:, :block]
            + beside_all[:, 3 * block :]
            + grad_random
            + global_mine[:, :, width:]
        )
        grad_pairs = grad_pairs + jnp.concatenate(
            [
                wide_grad_keys.reshape(docs_dev, block, width),
                wide_grad_values.reshape(docs_dev, block, width),
            ],
            axis=2,
        )
        grad_queries = grad_query.reshape(docs_dev, block, width) + global_mine[:, :, :width]
        grad_projected = (
            jnp.concatenate([grad_queries, grad_pairs], axis=2)
            .reshape(count, 3 * width)
            .astype(jnp.bfloat16)
        )
        grad_qkv_layer = jnp.einsum(
            "rd,re->de", lowered, grad_projected, preferred_element_type=jnp.float32
        )
        gradient = grad_attn + jnp.einsum(
            "re,de->rd", grad_projected, weight_qkv, preferred_element_type=jnp.float32
        )
        group_shares = (
            lax.psum_scatter(grad_qkv_layer, "docs", scatter_dimension=0, tiled=True),
            lax.psum_scatter(grad_out_layer, "docs", scatter_dimension=0, tiled=True),
            lax.psum_scatter(grad_up_layer, "docs", scatter_dimension=0, tiled=True),
            lax.psum_scatter(grad_down_layer, "docs", scatter_dimension=0, tiled=True),
            lax.psum_scatter(
                jnp.stack([grad_gain_mid, grad_gain_out]), "docs", scatter_dimension=1, tiled=True
            ),
        )
        shares = (
            lax.psum_scatter(group_shares[0], "seq", scatter_dimension=1, tiled=True),
            lax.psum_scatter(group_shares[1], "seq", scatter_dimension=1, tiled=True),
            lax.psum_scatter(group_shares[2], "seq", scatter_dimension=1, tiled=True),
            lax.psum_scatter(group_shares[3], "seq", scatter_dimension=1, tiled=True),
            lax.psum_scatter(group_shares[4], "seq", scatter_dimension=1, tiled=True),
        )
        layer_grads.insert(0, shares)
    stacked = [
        jnp.stack([layer_grads[number][member] for number in range(LAYERS)]) for member in range(5)
    ]
    return (
        hidden.astype(jnp.bfloat16).reshape(docs_dev, block, width),
        gradient.reshape(docs_dev, block, width),
        stacked[0],
        stacked[1],
        stacked[2],
        stacked[3],
        stacked[4],
    )


PLANES = 4
GROUPS = 4
CHIPS = 16
GROUP_HEADS = 3
MESH = pl.DeviceIdType.MESH
F32 = jnp.float32
BF16 = jnp.bfloat16


def fits(mesh, docs_dev, heads):
    return (
        mesh.shape["docs"] == 2
        and mesh.shape["seq"] == 16
        and docs_dev == PLANES
        and heads == GROUPS * GROUP_HEADS
    )


def swap(value, bits):
    return lax.ppermute(value, "seq", [(i, i ^ bits) for i in range(16)])


def swap_docs(value):
    return lax.ppermute(value, "docs", [(0, 1), (1, 0)])


def dot(left, right):
    return lax.dot_general(left, right, (((1,), (0,)), ((), ())), preferred_element_type=F32)


def dot_nt(left, right):
    return lax.dot_general(left, right, (((1,), (1,)), ((), ())), preferred_element_type=F32)


def dot_tn(left, right):
    return lax.dot_general(left, right, (((0,), (0,)), ((), ())), preferred_element_type=F32)


def vmem():
    return pl.BlockSpec(memory_space=pltpu.VMEM)


def smem():
    return pl.BlockSpec(memory_space=pltpu.SMEM)


def hbm():
    return pl.BlockSpec(memory_space=pltpu.HBM)


def params():
    return pltpu.CompilerParams(vmem_limit_bytes=56 * 2**20)


QUERIES = 1024
BACK_QUERIES = 512


def key_features(own_random, own_global, length):
    block = jnp.arange(16, dtype=jnp.int32)
    window = jnp.stack([(block + 15) % 16, block, (block + 1) % 16], axis=1)
    ids = jnp.concatenate([window, own_random, jnp.broadcast_to(own_global, (16, GLOB))], axis=1)
    count = jnp.sum((ids[:, :, None] == block).astype(F32), axis=1).T
    special = jnp.any(own_global[None, :] == block[:, None], axis=1)
    count = jnp.where(special[None, :], 1.0, count)
    extra = jnp.where(count > 0, jnp.log(jnp.maximum(count, 1.0)), NEGATIVE)
    inside = jnp.arange(1024, dtype=jnp.int32)[:, None] < length
    extra = jnp.where(inside, jnp.repeat(extra, 64, axis=0), NEGATIVE)
    high = extra.astype(BF16)
    low = jnp.where(extra > 0, extra - high.astype(F32), 0.0).astype(BF16)
    return jnp.concatenate([high, low, jnp.zeros((1024, 32), BF16)], axis=1)


def halves_beside(rows):
    return jnp.concatenate([rows[:32], rows[32:]], axis=1)


def halves_below(rows):
    return jnp.concatenate([rows[:, :192], rows[:, 192:]], axis=0)


def spread_heads(qkv, feature_ref, key_scr, query_scr):
    row = lax.broadcasted_iota(jnp.int32, (1024, 64), 0) // 64
    lane = lax.broadcasted_iota(jnp.int32, (1024, 64), 1)
    place = jnp.where(jnp.logical_and(lane < 32, lane % 16 == row), 1.0, 0.0).astype(BF16)
    for h in range(GROUP_HEADS):
        key_scr[h] = jnp.concatenate([qkv[:, 128 * h : 128 * h + 64], feature_ref[...]], axis=1)
        query = qkv[:, 384 + 64 * h : 448 + 64 * h] * jnp.asarray(HEAD**-0.5, BF16)
        query_scr[h] = jnp.concatenate([query, place], axis=1)


def expo_columns(scores):
    expo = jnp.exp(scores - jnp.max(scores, axis=0, keepdims=True))
    return expo, 1.0 / jnp.sum(expo, axis=0, keepdims=True)


def attend_kernel(feature_ref, x_ref, w_ref, qkv_ref, o_ref, key_scr, query_scr, value_scr, o_scr):
    weight = w_ref[...].reshape(-1, 576)
    qkv = dot(x_ref[...].reshape(1024, x_ref.shape[-1]), weight).astype(BF16)
    qkv_ref[...] = qkv
    spread_heads(qkv, feature_ref, key_scr, query_scr)
    for h in range(GROUP_HEADS):
        value_scr[h] = qkv[:, 128 * h + 64 : 128 * h + 128].T

    def chunk(n, _):
        at = pl.multiple_of(n * QUERIES, QUERIES)
        for h in range(GROUP_HEADS):
            scores = dot_nt(key_scr[h], query_scr[h, pl.ds(at, QUERIES), :])
            expo, rate = expo_columns(scores)
            o_scr[n, 64 * h : 64 * h + 64, :] = dot(value_scr[h], (expo * rate).astype(BF16))
        rows = o_scr[n].T.astype(BF16)
        for m in range(QUERIES // 64):
            o_ref[n * (QUERIES // 64) + m] = halves_beside(rows[64 * m : 64 * m + 64])
        return 0

    lax.fori_loop(0, 1024 // QUERIES, chunk, 0)


def attend(features, x, weight):
    return pl.pallas_call(
        attend_kernel,
        out_shape=(
            jax.ShapeDtypeStruct((1024, 576), BF16),
            jax.ShapeDtypeStruct((16, 32, 384), BF16),
        ),
        in_specs=[vmem(), vmem(), vmem()],
        out_specs=(vmem(), vmem()),
        scratch_shapes=[
            pltpu.VMEM((3, 1024, 128), BF16),
            pltpu.VMEM((3, 1024, 128), BF16),
            pltpu.VMEM((3, 64, 1024), BF16),
            pltpu.VMEM((1024 // QUERIES, 192, QUERIES), F32),
        ],
        compiler_params=params(),
        cost_estimate=pl.CostEstimate(
            flops=3 * 10**9, bytes_accessed=6 * 10**6, transcendentals=3 * 10**6
        ),
        name="attend",
    )(features, x, weight)


def attend_back_kernel(
    info,
    feature_ref,
    qkv_ref,
    do_ref,
    x_ref,
    w_ref,
    keep_ref,
    send_ref,
    grad_ref,
    key_scr,
    query_scr,
    value_scr,
    turned_scr,
    side_scr,
    dkv_scr,
    dq_scr,
    dqkv_scr,
):
    weight = w_ref[...].reshape(-1, 576)
    qkv = qkv_ref[...]
    spread_heads(qkv, feature_ref, key_scr, query_scr)
    grad_o = jnp.concatenate([halves_below(do_ref[n]) for n in range(16)], axis=0)
    zero = jnp.zeros((1024, 64), BF16)
    for h in range(GROUP_HEADS):
        value_scr[h] = qkv[:, 128 * h + 64 : 128 * h + 128]
        turned_scr[h] = qkv[:, 128 * h : 128 * h + 64].T
        side_scr[0, h] = jnp.concatenate([query_scr[h, :, :64], zero], axis=1)
        side_scr[1, h] = jnp.concatenate([zero, grad_o[:, 64 * h : 64 * h + 64]], axis=1)
    dkv_scr[...] = jnp.zeros_like(dkv_scr)

    def chunk(n, _):
        at = pl.ds(pl.multiple_of(n * BACK_QUERIES, BACK_QUERIES), BACK_QUERIES)
        for h in range(GROUP_HEADS):
            expo, rate = expo_columns(dot_nt(key_scr[h], query_scr[h, at, :]))
            probs = expo * rate
            grad_probs = dot_nt(value_scr[h], side_scr[1, h, at, :][:, 64:])
            delta = jnp.sum(probs * grad_probs, axis=0, keepdims=True)
            grad_scores = (probs * (grad_probs - delta)).astype(BF16)
            dq_scr[n, 64 * h : 64 * h + 64, :] = dot(turned_scr[h], grad_scores) * (HEAD**-0.5)
            dkv_scr[h] += dot(grad_scores, side_scr[0, h, at, :]) + dot(
                probs.astype(BF16), side_scr[1, h, at, :]
            )
        dqkv_scr[at, 384:576] = dq_scr[n].T.astype(BF16)
        return 0

    lax.fori_loop(0, 1024 // BACK_QUERIES, chunk, 0, unroll=True)
    for h in range(GROUP_HEADS):
        dqkv_scr[:, 128 * h : 128 * h + 128] = dkv_scr[h].astype(BF16)
    for half, ref in enumerate((keep_ref, send_ref)):
        rows = []
        for n in range(8):
            block = info[0] ^ ((n // 2) * 4 + (n % 2) * 2 + half)
            rows.append(dqkv_scr[pl.ds(pl.multiple_of(block * 64, 64), 64), :])
        ref[...] = dot_nt(jnp.concatenate(rows, axis=0), weight).astype(BF16).reshape(ref.shape)
    width = x_ref.shape[-1]
    grad = dot_tn(dqkv_scr[...], x_ref[...].reshape(1024, width))
    order = [6, 7, 8, 0, 2, 4, 1, 3, 5]
    grad = jnp.concatenate([grad[64 * n : 64 * n + 64] for n in order], axis=0).astype(BF16)
    for quarter in range(PLANES):
        for side in range(2):
            apart = quarter ^ info[3]
            grad_ref[side ^ info[4], ((apart & 1) << 1) | (apart >> 1)] = grad[
                144 * quarter : 144 * quarter + 144, 384 * side : 384 * side + 384
            ]


def attend_back(info, features, qkv, grad_o, x, weight):
    width = x.shape[-1]
    return pl.pallas_call(
        attend_back_kernel,
        out_shape=(
            jax.ShapeDtypeStruct((8, 64, width), BF16),
            jax.ShapeDtypeStruct((8, 64, width), BF16),
            jax.ShapeDtypeStruct((2, PLANES, 144, width // 2), BF16),
        ),
        in_specs=[smem(), vmem(), vmem(), vmem(), vmem(), vmem()],
        out_specs=(vmem(), vmem(), vmem()),
        scratch_shapes=[
            pltpu.VMEM((3, 1024, 128), BF16),
            pltpu.VMEM((3, 1024, 128), BF16),
            pltpu.VMEM((3, 1024, 64), BF16),
            pltpu.VMEM((3, 64, 1024), BF16),
            pltpu.VMEM((2, 3, 1024, 128), BF16),
            pltpu.VMEM((3, 1024, 128), F32),
            pltpu.VMEM((1024 // BACK_QUERIES, 192, BACK_QUERIES), F32),
            pltpu.VMEM((1024, 576), BF16),
        ],
        compiler_params=params(),
        cost_estimate=pl.CostEstimate(
            flops=8 * 10**9, bytes_accessed=10 * 10**6, transcendentals=3 * 10**6
        ),
        name="attend_back",
    )(info, features, qkv, grad_o, x, weight)


def load_ordered(w_refs, wu, wd, wo, sems):
    up_ref, down_ref = w_refs
    pltpu.make_async_copy(down_ref.at[:, :, :, pl.ds(1536, 384)], wo, sems.at[0]).start()
    pltpu.make_async_copy(up_ref, wu, sems.at[1]).start()
    for plane in range(2):
        for part in range(2):
            source = down_ref.at[plane, :, :, pl.ds(768 * part, 768)]
            pltpu.make_async_copy(source, wd.at[:, plane, part], sems.at[2]).start()


def load_slots(info, w_refs, wu, wd, wo, sems):
    ao_ref, ar_ref, bo_ref, br_ref = w_refs
    chip, core = info[1], info[5]

    def one(j, _):
        apart = j ^ chip
        z = (j >> 1) & 3
        at_a = (apart & 8) | ((apart & 1) << 2) | z
        at_b = ((apart & 1) << 3) | ((apart & 8) >> 1) | z
        for side, (a, b) in enumerate(((ao_ref, bo_ref), (ar_ref, br_ref))):
            plane = core ^ side
            a, b = a.at[at_a], b.at[at_b]
            pltpu.make_async_copy(a.at[:, pl.ds(2304, 384)], wo.at[plane, j], sems.at[0]).start()
            pltpu.make_async_copy(a.at[:, pl.ds(0, 1536)], wu.at[plane, j], sems.at[1]).start()
            for part, source in enumerate((a.at[:, pl.ds(1536, 768)], b)):
                pltpu.make_async_copy(source, wd.at[j, plane, part], sems.at[2]).start()
        return 0

    lax.fori_loop(0, CHIPS, one, 0)


def load_weights(info, w_refs, *scratch):
    if len(w_refs) == 2:
        load_ordered(w_refs, *scratch)
    else:
        load_slots(info, w_refs, *scratch)


def wait_weight(scr, sem):
    pltpu.make_async_copy(scr, scr, sem).wait()


def inside_rows(info):
    row = lax.broadcasted_iota(jnp.int32, (256, 1), 0)
    length = jnp.zeros_like(row)
    for k in range(PLANES):
        length = jnp.where(row // 64 == k, info[8 + k], length)
    return info[0] * 64 + row % 64 < length


def norm_parts(values):
    centre = values - jnp.mean(values, axis=-1, keepdims=True)
    spread = jnp.mean(centre * centre, axis=-1, keepdims=True)
    rate = lax.rsqrt(spread + EPSILON)
    return centre * rate, rate


def norm_back(unit, rate, gain, grad):
    scaled = grad * gain
    inner = jnp.mean(scaled * unit, axis=-1, keepdims=True)
    outer = jnp.mean(scaled, axis=-1, keepdims=True)
    return rate * (scaled - outer - unit * inner), jnp.sum(grad * unit, axis=0, keepdims=True)


CURVE = 0.7978845608028654


def gelu_parts(values):
    square = values * values
    bend = jnp.tanh(CURVE * (values + 0.044715 * (square * values)))
    return 0.5 * values * (1.0 + bend), bend, square


def gelu_slope(values, bend, square):
    return 0.5 * (1.0 + bend) + 0.5 * values * (1.0 - bend * bend) * (
        CURVE * (1.0 + 3 * 0.044715 * square)
    )


def feed_kernel(pieces, info, o_ref, h_ref, gain_ref, *refs):
    w_refs, refs = refs[:pieces], refs[pieces:]
    mixed_ref, h1_ref, up_ref, h2_ref, next_ref, low_ref, wu, wd, wo, act_scr, sems = refs
    load_weights(info, w_refs, wu, wd, wo, sems)
    for k in range(PLANES):
        mixed_ref[64 * k : 64 * k + 64, :] = jnp.concatenate(
            [halves_below(o_ref[4 * k + g]) for g in range(GROUPS)], axis=1
        )
    mixed = mixed_ref[...]
    wait_weight(wo, sems.at[0])
    attended = jnp.concatenate([dot(mixed, wo[side].reshape(768, 384)) for side in range(2)], axis=1)
    h1 = h_ref[...].reshape(256, 768).astype(F32) + attended
    h1_ref[...] = h1
    x1 = norm_parts(h1)[0] * gain_ref[0:1, :]
    x1_low = x1.astype(BF16)
    wait_weight(wu, sems.at[1])
    for side in range(2):
        for part in range(3):
            at = 1536 * side + 512 * part
            up = dot(x1_low, wu[side, :, :, 512 * part : 512 * part + 512].reshape(768, 512))
            up_ref[:, at : at + 512] = up
            act_scr[:, at : at + 512] = gelu_parts(up)[0].astype(BF16)
    wait_weight(wd, sems.at[2])
    h2 = x1 + dot(act_scr[...], wd[...].reshape(3072, 768))
    h2_ref[...] = h2
    out = jnp.where(inside_rows(info), norm_parts(h2)[0] * gain_ref[1:2, :], 0.0)
    next_ref[...] = out
    low = out.astype(BF16)
    for k in range(PLANES):
        low_ref[k] = low[64 * k : 64 * k + 64]


WEIGHT_SCRATCH = [
    pltpu.VMEM((2, 16, 48, 1536), BF16),
    pltpu.VMEM((16, 2, 2, 48, 768), BF16),
    pltpu.VMEM((2, 16, 48, 384), BF16),
]


def feed(info, o, hidden, gains, weights):
    return pl.pallas_call(
        functools.partial(feed_kernel, len(weights)),
        out_shape=(
            jax.ShapeDtypeStruct((256, 768), BF16),
            jax.ShapeDtypeStruct((256, 768), F32),
            jax.ShapeDtypeStruct((256, 3072), F32),
            jax.ShapeDtypeStruct((256, 768), F32),
            jax.ShapeDtypeStruct((256, 768), F32),
            jax.ShapeDtypeStruct((4, 64, 768), BF16),
        ),
        in_specs=[smem(), vmem(), vmem(), vmem()] + [hbm() for _ in weights],
        out_specs=tuple(vmem() for _ in range(6)),
        scratch_shapes=WEIGHT_SCRATCH
        + [pltpu.VMEM((256, 3072), BF16), pltpu.SemaphoreType.DMA((3,))],
        compiler_params=params(),
        cost_estimate=pl.CostEstimate(
            flops=3 * 10**9, bytes_accessed=20 * 10**6, transcendentals=10**6
        ),
        name="feed",
    )(info, o, hidden, gains, *weights)


def feed_back_kernel(
    pieces,
    has_extra,
    info,
    base_ref,
    extra_ref,
    gain_ref,
    mixed_ref,
    h1_ref,
    up_ref,
    h2_ref,
    *refs,
):
    w_refs, refs = refs[:pieces], refs[pieces:]
    dh1_ref, do_ref, dgain_ref, keep_ref, send_ref, wu, wd, wo, gu, gd, go, sems, out_sems = refs
    load_weights(info, w_refs, wu, wd, wo, sems)
    me, docs = info[0], info[4]
    if has_extra:
        parts = [
            base_ref[64 * k : 64 * k + 64, :] + extra_ref[k].astype(F32)
            for k in range(PLANES)
        ]
        grad = jnp.concatenate(parts, axis=0)
    else:
        grad = base_ref[...].reshape(256, 768).astype(F32)
    grad = jnp.where(inside_rows(info), grad, 0.0)
    unit2, rate2 = norm_parts(h2_ref[...])
    dh2, dgain1 = norm_back(unit2, rate2, gain_ref[1:2, :], grad)
    dgain_ref[1:2, :] = dgain1
    df = dh2.astype(BF16)
    unit1, rate1 = norm_parts(h1_ref[...])
    x1_low = (unit1 * gain_ref[0:1, :]).astype(BF16)
    wait_weight(wd, sems.at[2])
    wait_weight(wu, sems.at[1])
    dx1 = dh2
    for part in range(8):
        at = 384 * part
        d_act = dot_nt(df, wd[2 * part : 2 * part + 2].reshape(384, 768))
        up = up_ref[:, at : at + 384]
        act, bend, square = gelu_parts(up)
        act = act.astype(BF16)
        dup = (gelu_slope(up, bend, square) * d_act).astype(BF16)
        side, start = part // 4, 384 * (part % 4)
        dx1 += dot_nt(dup, wu[side, :, :, start : start + 384].reshape(768, 384))
        gt_up = dot_tn(dup, x1_low).astype(BF16)
        for n in range(2):
            for half in range(2):
                gu[half, 2 * part + n] = gt_up[
                    192 * n : 192 * n + 192, 384 * half : 384 * half + 384
                ]
        gt_down = dot_tn(df, act).astype(BF16)
        row = 48 * (part % 4)
        for s in range(16):
            gd[part // 4, s, row : row + 48, :] = gt_down[48 * s : 48 * s + 48]
    dh1, dgain0 = norm_back(unit1, rate1, gain_ref[0:1, :], dx1)
    dgain_ref[0:1, :] = dgain0
    dh1_ref[...] = dh1
    da = dh1.astype(BF16)
    gt_out = dot_tn(da, mixed_ref[...]).astype(BF16)
    for s in range(16):
        for half in range(2):
            go[half, s] = gt_out[48 * s : 48 * s + 48, 384 * half : 384 * half + 384]
    wait_weight(wo, sems.at[0])
    do = dot_nt(da[:, 0:384], wo[0].reshape(768, 384))
    do += dot_nt(da[:, 384:768], wo[1].reshape(768, 384))
    do = do.astype(BF16)
    for k in range(PLANES):
        for g in range(GROUPS):
            do_ref[4 * k + g] = halves_beside(do[64 * k : 64 * k + 64, 192 * g : 192 * g + 192])

    def copies(ry, place):
        rx, rz = place // 4, (place % 2) * 2 + (place // 2) % 2
        out = []
        for rc, ref in enumerate((keep_ref, send_ref)):
            to = me ^ (rz * 4 + rx * 2 + rc)
            for scr, first, count in ((gu, 0, 192), (go, 192, 48), (gd, 240, 192)):
                out.append(
                    pltpu.make_async_copy(
                        scr.at[ry ^ docs, to],
                        ref.at[ry, place, pl.ds(first, count)],
                        out_sems.at[rc],
                    )
                )
        return out

    def start(n, _):
        for copy in copies(n // 8, n % 8):
            copy.start()
        return 0

    lax.fori_loop(0, 16, start, 0)
    pltpu.make_async_copy(keep_ref, keep_ref, out_sems.at[0]).wait()
    pltpu.make_async_copy(send_ref, send_ref, out_sems.at[1]).wait()


def feed_back(info, base, extra, gains, saved, weights):
    mixed, h1, up, h2 = saved
    has_extra = extra is not None
    if not has_extra:
        extra = jnp.zeros((8, 128), BF16)
    return pl.pallas_call(
        functools.partial(feed_back_kernel, len(weights), has_extra),
        out_shape=(
            jax.ShapeDtypeStruct((256, 768), F32),
            jax.ShapeDtypeStruct((16, 32, 384), BF16),
            jax.ShapeDtypeStruct((2, 768), F32),
            jax.ShapeDtypeStruct((2, 8, 432, 384), BF16),
            jax.ShapeDtypeStruct((2, 8, 432, 384), BF16),
        ),
        in_specs=[smem()] + [vmem()] * 7 + [hbm() for _ in weights],
        out_specs=(vmem(), vmem(), vmem(), hbm(), hbm()),
        scratch_shapes=WEIGHT_SCRATCH
        + [
            pltpu.VMEM((2, 16, 192, 384), BF16),
            pltpu.VMEM((2, 16, 192, 384), BF16),
            pltpu.VMEM((2, 16, 48, 384), BF16),
            pltpu.SemaphoreType.DMA((3,)),
            pltpu.SemaphoreType.DMA((2,)),
        ],
        compiler_params=params(),
        cost_estimate=pl.CostEstimate(
            flops=6 * 10**9, bytes_accessed=40 * 10**6, transcendentals=10**6
        ),
        name="feed_back",
    )(info, base, extra, gains, mixed, h1, up, h2, *weights)


def flip(index, bits):
    for bit in (1, 2, 4, 8):
        if bits & bit:
            index = index + bit - 2 * bit * ((index // bit) % 2)
    return index


def greet(peers):
    barrier = pltpu.get_barrier_semaphore()
    for peer in peers:
        pl.semaphore_signal(barrier, inc=1, device_id=peer, device_id_type=MESH)
    pl.semaphore_wait(barrier, len(peers))


def remote(source, target, sems, n, peer):
    return pltpu.make_async_remote_copy(
        source, target, sems.at[0, n], sems.at[1, n], device_id=peer, device_id_type=MESH
    )


def comm_params(number):
    return pltpu.CompilerParams(
        collective_id=number, has_side_effects=True, vmem_limit_bytes=16 * 2**20
    )


class Spread:
    def __init__(self, low_ref, x_ref, sems, own_sem):
        self.low_ref, self.x_ref, self.sems = low_ref, x_ref, sems
        self.docs, self.me = lax.axis_index("docs"), lax.axis_index("seq")
        self.own = pltpu.make_async_copy(low_ref.at[self.me // 4], x_ref.at[self.me], own_sem)
        self.hops, self.across, self.mates = [], [], []

    def send(self, source, slot, n, bits):
        peer = (self.docs, flip(self.me, bits))
        copy = remote(source, self.x_ref.at[slot], self.sems, n, peer)
        copy.start()
        return copy

    def begin(self):
        for rz in range(1, 4):
            source = self.low_ref.at[flip(self.me, 4 * rz) // 4]
            self.hops.append(self.send(source, self.me, rz, 4 * rz))
        self.own.start()
        source = self.low_ref.at[self.me // 4]
        self.across.append(self.send(source, self.me, 4, 2))
        self.mates.append(self.send(source, self.me, 8, 1))

    def forward(self, rz):
        self.hops[rz - 1].wait_recv()
        slot = flip(self.me, 4 * rz)
        self.across.append(self.send(self.x_ref.at[slot], slot, 4 + rz, 2))
        self.mates.append(self.send(self.x_ref.at[slot], slot, 8 + rz, 1))

    def from_beside(self):
        for rz in range(4):
            self.across[rz].wait_recv()
            slot = flip(flip(self.me, 4 * rz), 2)
            self.mates.append(self.send(self.x_ref.at[slot], slot, 12 + rz, 1))

    def finish(self):
        for copy in self.mates:
            copy.wait_recv()
        for copy in self.hops + self.across + self.mates:
            copy.wait_send()
        self.own.wait()


def spread_peers():
    docs, me = lax.axis_index("docs"), lax.axis_index("seq")
    return [(docs, flip(me, bits)) for bits in (4, 8, 12, 2, 1)]


def spread_kernel(low_ref, x_ref, sems, own_sem):
    greet(spread_peers())
    rows = Spread(low_ref, x_ref, sems, own_sem)
    rows.begin()
    for rz in range(1, 4):
        rows.forward(rz)
    rows.from_beside()
    rows.finish()


def spread(low, number):
    return pl.pallas_call(
        spread_kernel,
        out_shape=jax.ShapeDtypeStruct((16, 64, low.shape[-1]), BF16),
        in_specs=[hbm()],
        out_specs=hbm(),
        scratch_shapes=[pltpu.SemaphoreType.DMA((2, 16)), pltpu.SemaphoreType.DMA],
        compiler_params=comm_params(number),
        name="spread",
    )(low)


class Slabs:
    def __init__(self, source, w_ref, sems, own_sem, docs_first=False, z_only=False):
        self.source, self.w_ref, self.sems, self.z_only = source, w_ref, sems, z_only
        self.docs, self.me = lax.axis_index("docs"), lax.axis_index("seq")
        self.plane, self.x, self.core = self.me // 4, (self.me // 2) % 2, self.me % 2
        beside, over = (self.docs, flip(self.me, 2)), (1 - self.docs, self.me)
        self.peers = (over, beside) if docs_first else (beside, over)
        if docs_first:
            self.near = ((self.docs, self.x), (1 - self.docs, self.x))
            self.far = ((self.docs, 1 - self.x), (1 - self.docs, 1 - self.x))
        else:
            self.near = ((self.docs, self.x), (self.docs, 1 - self.x))
            self.far = ((1 - self.docs, self.x), (1 - self.docs, 1 - self.x))
        self.mate = (self.docs, flip(self.me, 1))
        self.own = pltpu.make_async_copy(source, self.slot(self.near[0], self.plane), own_sem)

    def slot(self, at, z):
        return self.w_ref.at[z] if self.z_only else self.w_ref.at[self.core, at[0], z, at[1]]

    def copy(self, at, z, own, send, recv, peer):
        slot = self.slot(at, z)
        return pltpu.make_async_remote_copy(
            self.source if own else slot,
            slot,
            self.sems.at[0, send],
            self.sems.at[1, recv],
            device_id=peer,
            device_id_type=MESH,
        )

    def line(self, z, own, step):
        peer = (self.docs, self.me + 4 * step)
        return self.copy(self.near[0], z, own, z + (0 if step > 0 else 4), z, peer)

    def first(self, z, own=False):
        return self.copy(self.near[0], z, own, 8 + z, 8 + z, self.peers[0])

    def second(self, z, n, own=False):
        return self.copy(self.near[n], z, own, 12 + 4 * n + z, 12 + 4 * n + z, self.peers[1])

    def core_copy(self, at, n, z, own=False):
        return self.copy(at, z, own, 20 + 4 * n + z, 20 + 4 * n + z, self.mate)

    def begin(self):
        self.own.start()
        for step in (1, -1):
            pl.when(self.has(self.plane + step))(self.line(self.plane, True, step).start)
        if not self.z_only:
            self.first(self.plane, True).start()
            self.core_copy(self.near[0], 0, self.plane, True).start()

    def has(self, z):
        return jnp.logical_and(z >= 0, z < PLANES)

    def each(self, distance, act):
        if distance == 0:
            act(self.plane, 0)
            return
        for step in (1, -1):
            z = self.plane - step * distance
            pl.when(self.has(z))(functools.partial(act, z, step))

    def from_line(self, distance):
        def act(z, step):
            self.line(z, False, step).wait_recv()
            pl.when(self.has(self.plane + step))(self.line(z, False, step).start)
            if not self.z_only:
                self.first(z).start()
                self.core_copy(self.near[0], 0, z).start()

        self.each(distance, act)

    def from_first(self, distance):
        def act(z, step):
            self.first(z).wait_recv()
            self.second(z, 0, distance == 0).start()
            self.second(z, 1).start()
            self.core_copy(self.near[1], 1, z).start()

        self.each(distance, act)

    def from_second(self, distance):
        def act(z, step):
            for n in range(2):
                self.second(z, n).wait_recv()
                self.core_copy(self.far[n], 2 + n, z).start()

        self.each(distance, act)

    def finish(self):
        for z in range(PLANES):
            for step in (1, -1):
                sent = jnp.logical_and(
                    (self.plane - z) * step >= 0, self.has(self.plane + step)
                )
                pl.when(sent)(self.line(z, False, step).wait_send)
            if not self.z_only:
                self.first(z).wait_send()
                for n, at in enumerate(self.near + self.far):
                    if n < 2:
                        self.second(z, n).wait_send()
                    self.core_copy(at, n, z).wait()
        self.own.wait()


class Rows:
    def __init__(self, source, w_ref, sems, own_sem):
        self.source, self.w_ref, self.sems = source, w_ref, sems
        self.docs, self.me = lax.axis_index("docs"), lax.axis_index("seq")
        self.over = (1 - self.docs, self.me)
        self.own = pltpu.make_async_copy(source, w_ref.at[self.docs, self.me // 4], own_sem)
        self.hops, self.moved = [], []

    def begin(self):
        target = self.w_ref.at[self.docs, self.me // 4]
        for rz in range(1, 4):
            peer = (self.docs, flip(self.me, 4 * rz))
            self.hops.append(remote(self.source, target, self.sems, rz, peer))
            self.hops[-1].start()
        self.own.start()
        self.moved.append(remote(self.source, target, self.sems, 4, self.over))
        self.moved[0].start()

    def forward(self, rz):
        self.hops[rz - 1].wait_recv()
        slot = self.w_ref.at[self.docs, flip(self.me, 4 * rz) // 4]
        self.moved.append(remote(slot, slot, self.sems, 4 + rz, self.over))
        self.moved[-1].start()

    def finish(self):
        for copy in self.moved:
            copy.wait_recv()
        for copy in self.hops + self.moved:
            copy.wait_send()
        self.own.wait()


class Tiles:
    def __init__(self, source, w_ref, sems, own_sem):
        self.source, self.w_ref, self.sems = source, w_ref, sems
        self.docs, self.me = lax.axis_index("docs"), lax.axis_index("seq")
        self.place = (self.docs, self.me // 4, (self.me // 2) % 2, self.me % 2)
        self.own = pltpu.make_async_copy(source, w_ref.at[self.place], own_sem)
        self.sent, self.last = [], []

    def send(self, part, n, peer):
        self.last.append(remote(part, part, self.sems, n, peer))
        self.last[-1].start()
        self.sent.append(self.last[-1])

    def arrived(self):
        for copy in self.last:
            copy.wait_recv()
        self.last = []

    def begin(self):
        self.own.start()
        self.own.wait()
        self.send(self.w_ref.at[self.place], 0, (self.docs, flip(self.me, 1)))

    def along_x(self):
        self.arrived()
        self.send(self.w_ref.at[self.place[:3]], 1, (self.docs, flip(self.me, 2)))

    def along_z(self):
        self.arrived()
        for rz in range(1, 4):
            self.send(self.w_ref.at[self.place[:2]], 1 + rz, (self.docs, flip(self.me, 4 * rz)))

    def along_docs(self):
        self.arrived()
        self.send(self.w_ref.at[self.docs], 5, (1 - self.docs, self.me))

    def finish(self):
        self.arrived()
        for copy in self.sent:
            copy.wait_send()


def open_kernel(*refs):
    low_ref, gain_ref, wq_ref, wq_1_ref, up_ref, down_ref, up_1_ref, down_1_ref = refs[:8]
    x_ref, gains_ref, w_ref, w_1_ref, wu_ref, wd_ref, wu_1_ref, wd_1_ref = refs[8:16]
    sems, gain_sems, own_sems, w_sems, w_1_sems, up_sems, down_sems, up_1_sems, down_1_sems = refs[16:]
    docs, me = lax.axis_index("docs"), lax.axis_index("seq")
    greet(spread_peers() + [(1 - docs, me)])
    gains = Tiles(gain_ref, gains_ref, gain_sems, own_sems.at[7])
    qkv = Rows(wq_ref, w_ref, w_sems, own_sems.at[0])
    qkv_1 = Rows(wq_1_ref, w_1_ref, w_1_sems, own_sems.at[1])
    whole = [
        Slabs(up_ref, wu_ref, up_sems, own_sems.at[2]),
        Slabs(down_ref, wd_ref, down_sems, own_sems.at[3], docs_first=True),
    ]
    lines = [
        Slabs(up_1_ref, wu_1_ref, up_1_sems, own_sems.at[4], z_only=True),
        Slabs(down_1_ref, wd_1_ref, down_1_sems, own_sems.at[5], z_only=True),
    ]
    rows = Spread(low_ref, x_ref, sems, own_sems.at[6])

    def every(parts, step, *arguments):
        for part in parts:
            getattr(part, step)(*arguments)

    every(whole, "begin")
    gains.begin()
    every(whole, "from_line", 1)
    every(whole, "from_first", 0)
    gains.along_x()
    rows.begin()
    qkv.begin()
    every(whole, "from_line", 2)
    every(whole, "from_first", 1)
    gains.along_z()
    every(whole, "from_line", 3)
    every(whole, "from_first", 2)
    every([rows], "forward", 1)
    every([rows], "forward", 2)
    every([rows], "forward", 3)
    gains.along_docs()
    qkv_1.begin()
    every(lines, "begin")
    every(whole, "from_first", 3)
    every(whole, "from_second", 0)
    for rz in range(1, 4):
        qkv.forward(rz)
    rows.from_beside()
    for rz in range(1, 4):
        qkv_1.forward(rz)
    for distance in range(1, 4):
        every(lines, "from_line", distance)
        every(whole, "from_second", distance)
    every([rows, gains, qkv, qkv_1] + whole + lines, "finish")


def open_layer(low, gain, wq, first, second, number):
    def whole(part):
        return jax.ShapeDtypeStruct((2, 2, PLANES, 2) + part.shape, BF16)

    def line(part):
        return jax.ShapeDtypeStruct((PLANES,) + part.shape, BF16)

    sems = pltpu.SemaphoreType.DMA
    return pl.pallas_call(
        open_kernel,
        out_shape=(
            jax.ShapeDtypeStruct((16, 64, low.shape[-1]), BF16),
            jax.ShapeDtypeStruct((2, PLANES, 2, 2) + gain.shape, BF16),
            jax.ShapeDtypeStruct((2, PLANES) + wq[0].shape, BF16),
            jax.ShapeDtypeStruct((2, PLANES) + wq[1].shape, BF16),
            whole(first[0]),
            whole(first[1]),
            line(second[0]),
            line(second[1]),
        ),
        in_specs=[hbm() for _ in range(8)],
        out_specs=tuple(hbm() for _ in range(8)),
        scratch_shapes=[
            sems((2, 16)),
            sems((2, 6)),
            sems((8,)),
            sems((2, 8)),
            sems((2, 8)),
            sems((2, 36)),
            sems((2, 36)),
            sems((2, 8)),
            sems((2, 8)),
        ],
        compiler_params=comm_params(number),
        name="open_layer",
    )(low, gain, *wq, *first, *second)


def exchange_kernel(x_ref, o_ref, sems, own_sem):
    docs, me = lax.axis_index("docs"), lax.axis_index("seq")
    order = list(range(15, 0, -1))
    greet([(docs, flip(me, bits)) for bits in order])
    copies = []
    for bits in order:
        peer = flip(me, bits)
        copies.append(remote(x_ref.at[peer], o_ref.at[me], sems, bits, (docs, peer)))
        copies[-1].start()
    own = pltpu.make_async_copy(x_ref.at[me], o_ref.at[me], own_sem)
    own.start()
    for copy in copies:
        copy.wait_recv()
    for copy in copies:
        copy.wait_send()
    own.wait()


def exchange(x, number):
    return pl.pallas_call(
        exchange_kernel,
        out_shape=jax.ShapeDtypeStruct(x.shape, x.dtype),
        in_specs=[hbm()],
        out_specs=hbm(),
        scratch_shapes=[pltpu.SemaphoreType.DMA((2, 16)), pltpu.SemaphoreType.DMA],
        compiler_params=comm_params(number),
        name="exchange",
    )(x)


def collect_kernel(keep_ref, send_ref, out_ref, got_core, got_x, sum_x, near, sums, land, sems):
    docs, me = lax.axis_index("docs"), lax.axis_index("seq")
    plane = me // 4
    beside, mate = (docs, flip(me, 2)), (docs, flip(me, 1))
    greet(spread_peers())
    order = (3, 2, 1, 0)
    first = {}
    for rz in order:
        for rx in (1, 0):
            n = 2 * rz + rx
            first[n] = remote(send_ref.at[n], got_core.at[n], sems, n, mate)
            first[n].start()
    across, hops = {}, []
    for rz in order:
        n = 2 * rz + 1
        first[n].wait_recv()
        sum_x[rz] = (keep_ref[n].astype(F32) + got_core[n].astype(F32)).astype(BF16)
        across[rz] = remote(sum_x.at[rz], got_x.at[rz], sems, 8 + rz, beside)
        across[rz].start()
        n = 2 * rz
        first[n].wait_recv()
        near[rz] = keep_ref[n].astype(F32) + got_core[n].astype(F32)
    for rz in order:
        across[rz].wait_recv()
        total = (near[rz] + got_x[rz].astype(F32)).astype(BF16)
        if rz == 0:
            land[plane] = total
        else:
            sums[rz] = total
            copy = remote(sums.at[rz], land.at[plane], sems, 12 + rz, (docs, flip(me, 4 * rz)))
            copy.start()
            hops.append(copy)
    for copy in hops:
        copy.wait_recv()
    out_ref[...] = land[...]
    for copy in list(first.values()) + list(across.values()) + hops:
        copy.wait_send()


def collect(keep, send, number):
    width = keep.shape[-1]
    return pl.pallas_call(
        collect_kernel,
        out_shape=jax.ShapeDtypeStruct((PLANES, 64, width), BF16),
        in_specs=[vmem(), vmem()],
        out_specs=vmem(),
        scratch_shapes=[
            pltpu.VMEM((8, 64, width), BF16),
            pltpu.VMEM((4, 64, width), BF16),
            pltpu.VMEM((4, 64, width), BF16),
            pltpu.VMEM((4, 64, width), F32),
            pltpu.VMEM((4, 64, width), BF16),
            pltpu.VMEM((4, 64, width), BF16),
            pltpu.SemaphoreType.DMA((2, 16)),
        ],
        compiler_params=comm_params(number),
        name="collect",
    )(keep, send)


class Transfer:
    def __init__(self, steps):
        self.steps = steps
        self.result = None
        self.pending = next(steps)

    def go_on(self, arrived):
        try:
            self.pending = self.steps.send(arrived)
        except StopIteration as end:
            self.pending = ()
            self.result = end.value


def beside(result, *transfers):
    live = [transfer for transfer in transfers if transfer.result is None]
    result, arrived = lax.optimization_barrier((result, [transfer.pending for transfer in live]))
    for transfer, values in zip(live, arrived):
        transfer.go_on(values)
    return result


def in_core_order(core, own, other):
    return jnp.where(
        core == 0,
        jnp.concatenate([own, other], axis=0),
        jnp.concatenate([other, own], axis=0),
    )


def pick(stack, index):
    return lax.dynamic_index_in_dim(stack, index, 0, keepdims=False)


def pack_qkv(shards, me, core):
    rows = shards.shape[1]
    parts = shards.reshape(LAYERS, rows, 3, GROUPS, GROUP_HEADS, HEAD)
    pairs = jnp.transpose(parts[:, :, 1:], (3, 0, 1, 4, 2, 5)).reshape(GROUPS, LAYERS, rows, 384)
    query = jnp.transpose(parts[:, :, 0], (2, 0, 1, 3, 4)).reshape(GROUPS, LAYERS, rows, 192)
    packed = jnp.concatenate([pairs, query], axis=3)
    group = me & 3
    got = [pick(packed, group)] + [swap(pick(packed, group ^ r), r) for r in range(1, 4)]

    def in_order(own, other):
        return jnp.where(
            core == 0,
            jnp.concatenate([own, other], axis=1),
            jnp.concatenate([other, own], axis=1),
        )

    here, there = in_order(got[0], got[1]), in_order(got[2], got[3])
    both = jnp.where(
        (me >> 1) & 1 == 0,
        jnp.stack([here, there], axis=1),
        jnp.stack([there, here], axis=1),
    )
    return [both[layer] for layer in range(LAYERS)]


def pack_rest(out_weight, up_weight, down_weight, core):
    def mine(shard, side):
        half = shard.shape[2] // 2
        return lax.dynamic_slice_in_dim(shard, side * half, half, axis=2)

    def both(side):
        return jnp.concatenate([mine(up_weight, side), mine(out_weight, side)], axis=2)

    own, got = both(core), swap(both(1 - core), 1)
    rows = jnp.where(
        core == 0,
        jnp.concatenate([own, got], axis=1),
        jnp.concatenate([got, own], axis=1),
    )
    parts = []
    for layer in range(LAYERS):
        up, out = rows[layer, :, :1536], rows[layer, :, 1536:]
        down = [down_weight[layer, :48], down_weight[layer, 48:]]
        if layer == 0:
            parts.append((up, jnp.concatenate(down + [out], axis=1)))
        else:
            parts.append((jnp.concatenate([up, down[0], out], axis=1), down[1]))
    return parts


def gather_rest(first, second):
    first, second, got_first, got_second = yield (
        first,
        second,
        swap(first, 2),
        swap_docs(second),
    )
    first = jnp.concatenate([first, got_first], axis=0)
    second = jnp.concatenate([second, got_second], axis=0)
    first, second, got_first, got_second = yield (
        first,
        second,
        swap_docs(first),
        swap(second, 2),
    )
    first = jnp.concatenate([first, got_first], axis=0)
    second = jnp.concatenate([second, got_second], axis=0)
    return (yield (first, swap(first, 1), second, swap(second, 1)))


def add_low(first, second):
    return (first.astype(F32) + second.astype(F32)).astype(BF16)


def add_full(first, second):
    return first.astype(F32) + second.astype(F32)


def reduce_rest(keep, send):
    cut = 224
    keep, got = yield (keep, swap(send, 1))
    first = add_low(keep[:, :, :cut], got[:, :, :cut])
    second = add_low(keep[:, :, cut:], got[:, :, cut:]).reshape(2, 2, 4, 432 - cut, 384)
    first, second, got_first, got_second = yield (
        first[0],
        second[:, 0],
        swap_docs(first[1]),
        swap(second[:, 1], 2),
    )
    first = add_low(first, got_first).reshape(2, 4, cut, 384)
    second = add_low(second, got_second)
    first, second, got_first, got_second = yield (
        first[0],
        second[0],
        swap(first[1], 2),
        swap_docs(second[1]),
    )
    held = jnp.concatenate([add_low(first, got_first), add_low(second, got_second)], axis=1)
    held = add_low(*(yield (held[:2], swap(held[2:], 4))))
    total = add_full(*(yield (held[0], swap(held[1], 8))))
    down = total[240:].reshape(4, 48, 384)
    return (
        total[192:240].T,
        total[:192].T,
        jnp.transpose(down, (0, 2, 1)).reshape(1536, 48),
    )


def route_table():
    edges = []
    for device in range(16):
        z, group = device >> 2, device & 3
        for t in range(3):
            local = 3 * z + t
            number = 16 * (local // 4) + 4 * group + local % 4
            edges.append((device, t, number // 3, number % 3))
    rounds = []
    left = list(edges)
    for _ in range(3):
        match = {}

        def place(device, seen):
            for edge in left:
                if edge[0] == device and edge[2] not in seen:
                    seen.add(edge[2])
                    if edge[2] not in match or place(match[edge[2]][0], seen):
                        match[edge[2]] = edge
                        return True
            return False

        for device in range(16):
            place(device, set())
        chosen = sorted(match.values())
        rounds.append(chosen)
        left = [edge for edge in left if edge not in chosen]
    return rounds


def reduce_qkv(grad, me):
    held = add_low(*(yield (grad[0], swap_docs(grad[1]))))
    held = add_low(*(yield (held[:2], swap(held[2:], 4))))
    total = add_full(*(yield (held[0], swap(held[1], 8))))
    granules = total.reshape(3, 48, 384)
    moved, spots = [], []
    for chosen in route_table():
        take = jnp.asarray([edge[1] for edge in chosen], jnp.int32)
        moved.append(
            lax.ppermute(
                pick(granules, take[me]), "seq", [(edge[0], edge[2]) for edge in chosen]
            )
        )
        spots.append([edge[3] for edge in sorted(chosen, key=lambda edge: edge[2])])
    got = jnp.stack((yield moved))
    where = jnp.asarray(spots, jnp.int32)[:, me]
    place = jnp.arange(3, dtype=jnp.int32)
    source = jnp.sum(jnp.where(where[None, :] == place[:, None], place[None, :], 0), axis=1)
    return jnp.take(got, source, axis=0).reshape(144, 384).T


def reduce_gains(grads):
    number = lax.axis_index("docs") * 16 + lax.axis_index("seq")
    shape = grads.shape[:2]
    held = jnp.transpose(grads.reshape(shape + (32, -1)), (2, 0, 1, 3)).reshape(32, -1)
    held = jnp.take(held, jnp.arange(32) ^ number, axis=0)
    held = add_full(*(yield (held[:16], swap_docs(held[16:]))))
    for bits in (8, 4, 2, 1):
        held = add_full(*(yield (held[:bits], swap(held[bits:], bits))))
    return held.reshape(shape + (-1,))


def local_two_by_sixteen(
    tokens,
    qkv_weight,
    out_weight,
    up_weight,
    down_weight,
    norm_gains,
    doc_lengths,
    global_ids,
    random_ids,
    cotangent,
):
    docs_dev, block, width = tokens.shape
    me = lax.axis_index("seq").astype(jnp.int32)
    docs = lax.axis_index("docs").astype(jnp.int32)
    plane, core = me >> 2, me & 1
    chip = docs * 8 + (me >> 1)
    info = jnp.concatenate(
        [
            jnp.stack(
                [me, chip, pick(doc_lengths, plane), plane, docs, core, jnp.zeros_like(me), chip]
            ),
            doc_lengths,
        ]
    )
    features = key_features(
        lax.dynamic_index_in_dim(random_ids, plane, 1, keepdims=False),
        pick(global_ids, plane),
        pick(doc_lengths, plane),
    )

    wq = pack_qkv(qkv_weight, me, core)
    parts = pack_rest(out_weight, up_weight, down_weight, core)
    own_gains = jnp.pad(norm_gains.reshape(1, -1), ((0, 15), (0, 128 - norm_gains.size)))
    opened = open_layer(tokens, own_gains, wq, *parts, 0)
    x, up, down = opened[0], opened[4], opened[5]
    gain = opened[1].reshape(32, 16, 128)[:, 0, : norm_gains.size].reshape((32,) + norm_gains.shape)
    gain = jnp.transpose(gain, (1, 2, 0, 3)).reshape(LAYERS, 2, width).astype(F32)
    weights = [weight.reshape(CHIPS, 48, 576) for weight in opened[2:4]]
    rest_0 = (up.reshape(2, CHIPS, 48, -1), down.reshape(2, CHIPS, 48, -1))
    rest_1 = Transfer(gather_rest(*opened[6:]))
    qkv, o = beside(attend(features, x, weights[0]), rest_1)
    held = [(x, qkv)]
    o = exchange(o, 1)
    fed = feed(info, o, tokens, gain[0], rest_0)
    held[0] += (fed[:4],)
    x = spread(fed[5], 2)
    qkv, o = beside(attend(features, x, weights[1]), rest_1)
    o = beside(exchange(o, 3), rest_1)
    fed_1 = feed(info, o, fed[4], gain[1], rest_1.result)
    held.append((x, qkv, fed_1[:4]))
    base, grad_o, gain_1, keep, send = feed_back(
        info, cotangent, None, gain[1], held[1][2], rest_1.result
    )
    rest_1 = Transfer(reduce_rest(keep, send))
    grad_o = beside(exchange(grad_o, 4), rest_1)
    keep, send, grad_qkv = beside(
        attend_back(info, features, held[1][1], grad_o, held[1][0], weights[1]), rest_1
    )
    qkv_1 = Transfer(reduce_qkv(grad_qkv, me))
    extra = beside(collect(keep, send, 5), rest_1, qkv_1)
    base, grad_o, gain_0, keep, send = beside(
        feed_back(info, base, extra, gain[0], held[0][2], rest_0), rest_1, qkv_1
    )
    rest_0, gains = Transfer(reduce_rest(keep, send)), Transfer(reduce_gains(jnp.stack([gain_0, gain_1])))
    grad_o = beside(exchange(grad_o, 6), rest_0, gains)
    keep, send, grad_qkv = beside(
        attend_back(info, features, held[0][1], grad_o, held[0][0], weights[0]),
        rest_0,
        rest_1,
        qkv_1,
        gains,
    )
    qkv_0 = Transfer(reduce_qkv(grad_qkv, me))
    extra = beside(collect(keep, send, 7), rest_0, qkv_0, qkv_1, gains)
    grad_tokens = base.reshape(docs_dev, block, width) + extra.astype(F32)
    while any(transfer.result is None for transfer in (rest_0, qkv_0, gains)):
        grad_tokens = beside(grad_tokens, rest_0, qkv_0, gains)
    return (
        fed_1[4].astype(BF16).reshape(docs_dev, block, width),
        grad_tokens,
        jnp.stack([qkv_0.result, qkv_1.result]),
        *(jnp.stack(pair) for pair in zip(rest_0.result, rest_1.result)),
        gains.result,
    )


def solution(mesh):
    def local(*args):
        docs_dev, _, width = args[0].shape
        if fits(mesh, docs_dev, width // HEAD):
            return local_two_by_sixteen(*args)
        return local_any_mesh(*args)

    return jax.shard_map(
        local,
        mesh=mesh,
        in_specs=(
            P("docs", "seq", None),
            P(None, ("docs", "seq"), None),
            P(None, ("docs", "seq"), None),
            P(None, ("docs", "seq"), None),
            P(None, ("docs", "seq"), None),
            P(None, None, ("docs", "seq")),
            P("docs"),
            P("docs", None),
            P(None, "docs", None),
            P("docs", "seq", None),
        ),
        out_specs=(
            P("docs", "seq", None),
            P("docs", "seq", None),
            P(None, "docs", "seq"),
            P(None, "docs", "seq"),
            P(None, "docs", "seq"),
            P(None, "docs", "seq"),
            P(None, None, ("docs", "seq")),
        ),
        check_vma=False,
    )
```

```python
import functools

import jax
import jax.numpy as jnp
from jax import lax
from jax.experimental import pallas as pl
from jax.experimental.pallas import tpu as pltpu
from jax.sharding import PartitionSpec as P

HEAD = 64
RAND = 3
GLOB = 2
LAYERS = 2


NEGATIVE = -1e30
EPSILON = 1e-05


def with_halo(cells, sides, width):
    for axis, dim in sides:
        count = lax.axis_size(axis)
        head = lax.slice_in_dim(cells, 0, width, axis=dim)
        tail = lax.slice_in_dim(cells, cells.shape[dim] - width, cells.shape[dim], axis=dim)
        cells = jnp.concatenate(
            [
                lax.ppermute(tail, axis, [(i, (i + 1) % count) for i in range(count)]),
                cells,
                lax.ppermute(head, axis, [((i + 1) % count, i) for i in range(count)]),
            ],
            axis=dim,
        )
    return cells


def combined_all(value, axis, join):
    pieces = jax.tree.map(lambda part: lax.all_gather(part, axis), value)
    head = jax.tree.map(lambda part: part[0], pieces)
    tail = jax.tree.map(lambda part: part[1:], pieces)
    so_far, _ = lax.scan(lambda so_far, piece: (join(so_far, piece), None), head, tail)
    return so_far


def norm_rows(values, gain):
    centre = values - jnp.mean(values, axis=-1, keepdims=True)
    spread = jnp.mean(centre * centre, axis=-1, keepdims=True)
    return centre * lax.rsqrt(spread + EPSILON) * gain


def gelu_tanh(values):
    return jax.nn.gelu(values, approximate=True)


def earlier_equal(values):
    length = values.shape[-1]
    order = jnp.arange(length, dtype=jnp.int32)
    before = order[None, :] < order[:, None]
    same = values[..., :, None] == values[..., None, :]
    return jnp.sum(jnp.logical_and(same, before), axis=-1)


def merge_stats(first, second):
    highest = jnp.maximum(first[0], second[0])
    return (
        highest,
        first[1] * jnp.exp(first[0] - highest) + second[1] * jnp.exp(second[0] - highest),
    )


def sparse_probs(query, key_part, key_inside, scale):
    scores = (
        jnp.einsum("kbhd,kjhd->khbj", query, key_part, preferred_element_type=jnp.float32) * scale
    )
    scores = jnp.where(key_inside[:, None, None, :], scores, NEGATIVE)
    expo = jnp.exp(scores - jnp.max(scores, axis=-1, keepdims=True))
    return expo / jnp.sum(expo, axis=-1, keepdims=True)


def global_scores(global_query, local_keys, inside, scale):
    scores = (
        jnp.einsum(
            "ksbhd,kjhd->kshbj", global_query, local_keys, preferred_element_type=jnp.float32
        )
        * scale
    )
    return jnp.where(inside[:, None, None, None, :], scores, NEGATIVE)


def local_any_mesh(
    tokens,
    qkv_weight,
    out_weight,
    up_weight,
    down_weight,
    norm_gains,
    doc_lengths,
    global_ids,
    random_ids,
    cotangent,
):
    nseq = lax.axis_size("seq")
    device = lax.axis_index("seq")
    docs_dev, block, width = tokens.shape
    count = docs_dev * block
    heads = width // HEAD
    scale = HEAD ** (-0.5)
    capacity = max(2, (docs_dev * RAND + nseq - 1) // nseq)
    global_capacity = (docs_dev * GLOB + nseq - 1) // nseq
    entries = docs_dev * RAND
    global_entries = docs_dev * GLOB
    offsets = jnp.arange(block, dtype=jnp.int32)
    inside = (device * block + offsets)[None, :] < doc_lengths[:, None]
    live_rows = inside.reshape(count, 1)
    wanted = random_ids.reshape(nseq, entries)
    wanted_rank = earlier_equal(wanted)
    slot_ids = jnp.arange(capacity, dtype=jnp.int32)
    hits = jnp.logical_and((wanted == device)[:, :, None], wanted_rank[:, :, None] == slot_ids)
    hits = jnp.any(hits.reshape(nseq, docs_dev, RAND, capacity), axis=2)
    hits = jnp.transpose(hits, (0, 2, 1))
    doc_ids = jnp.arange(docs_dev, dtype=jnp.int32)
    send_doc = jnp.sum(jnp.where(hits, doc_ids, 0), axis=2)
    send_live = jnp.any(hits, axis=2)
    owner_pick = hits.astype(jnp.float32)
    listed_here = lax.dynamic_index_in_dim(wanted, device, 0, keepdims=False)
    listed_rank = lax.dynamic_index_in_dim(wanted_rank, device, 0, keepdims=False)
    fetch_slot = listed_here * capacity + listed_rank
    global_block = global_ids.reshape(global_entries)
    global_rank = earlier_equal(global_block)
    global_slot = global_block * global_capacity + global_rank
    own_entry = global_block == device
    owned = jnp.logical_and(
        own_entry[:, None], global_rank[:, None] == jnp.arange(global_capacity, dtype=jnp.int32)
    )
    entry_doc = jnp.arange(global_entries, dtype=jnp.int32) // GLOB
    global_send_doc = jnp.sum(jnp.where(owned, entry_doc[:, None], 0), axis=0)
    global_send_live = jnp.any(owned, axis=0)
    own_flag = jnp.any(own_entry.reshape(docs_dev, GLOB), axis=1)
    own_slot = jnp.sum(jnp.where(own_entry, global_rank, 0).reshape(docs_dev, GLOB), axis=1)
    neighbours = jnp.stack([(device - 1) % nseq, device, (device + 1) % nseq])
    key_blocks = jnp.concatenate(
        [
            jnp.broadcast_to(neighbours[None, :], (docs_dev, 3)),
            listed_here.reshape(docs_dev, RAND),
            global_ids,
        ],
        axis=1,
    )
    span = key_blocks.shape[1] * block
    key_inside = (key_blocks[:, :, None] * block + offsets < doc_lengths[:, None, None]).reshape(
        docs_dev, span
    )
    keep_local = inside[:, None, None, None, :]
    hidden = tokens.reshape(count, width).astype(jnp.float32)
    held = []
    for layer in range(LAYERS):
        weights = (
            lax.all_gather(qkv_weight[layer], ("docs", "seq"), axis=0, tiled=True),
            lax.all_gather(out_weight[layer], ("docs", "seq"), axis=0, tiled=True),
            lax.all_gather(up_weight[layer], ("docs", "seq"), axis=0, tiled=True),
            lax.all_gather(down_weight[layer], ("docs", "seq"), axis=0, tiled=True),
            lax.all_gather(norm_gains[layer], ("docs", "seq"), axis=1, tiled=True),
        )
        weight_qkv, weight_out, weight_up, weight_down, gain_pair = weights
        gain_pair = gain_pair.astype(jnp.float32)
        lowered = hidden.astype(jnp.bfloat16)
        projected = (
            jnp.dot(lowered, weight_qkv, preferred_element_type=jnp.float32)
            .astype(jnp.bfloat16)
            .reshape(docs_dev, block, 3 * width)
        )
        pairs = projected[:, :, width:]
        window = with_halo(pairs, (("seq", 1),), block)
        outgoing = jnp.where(
            send_live[:, :, None, None],
            jnp.take(pairs, send_doc, axis=0),
            jnp.zeros((), jnp.bfloat16),
        )
        incoming = lax.all_to_all(outgoing, "seq", split_axis=0, concat_axis=0, tiled=True)
        fetched = jnp.take(
            incoming.reshape(nseq * capacity, block, 2 * width), fetch_slot, axis=0
        ).reshape(docs_dev, RAND * block, 2 * width)
        global_send = jnp.where(
            global_send_live[:, None, None],
            jnp.take(projected, global_send_doc, axis=0),
            jnp.zeros((), jnp.bfloat16),
        )
        gathered = lax.all_gather(global_send, "seq", axis=0, tiled=True)
        global_picked = jnp.take(gathered, global_slot, axis=0).reshape(
            docs_dev, GLOB, block, 3 * width
        )
        global_query = global_picked[..., :width].reshape(docs_dev, GLOB, block, heads, HEAD)
        listed_pairs = jnp.concatenate(
            [
                window,
                fetched,
                global_picked[..., width:].reshape(docs_dev, GLOB * block, 2 * width),
            ],
            axis=1,
        )
        query = projected[:, :, :width].reshape(docs_dev, block, heads, HEAD)
        key_part = listed_pairs[:, :, :width].reshape(docs_dev, span, heads, HEAD)
        value_part = listed_pairs[:, :, width:].reshape(docs_dev, span, heads, HEAD)
        probs = sparse_probs(query, key_part, key_inside, scale)
        mixed = jnp.einsum(
            "khbj,kjhd->kbhd",
            probs.astype(jnp.bfloat16),
            value_part,
            preferred_element_type=jnp.float32,
        )
        local_keys = projected[:, :, width : 2 * width].reshape(docs_dev, block, heads, HEAD)
        local_values = projected[:, :, 2 * width :].reshape(docs_dev, block, heads, HEAD)
        wide_scores = global_scores(global_query, local_keys, inside, scale)
        global_top = jnp.max(wide_scores, axis=-1)
        global_total = jnp.sum(
            jnp.where(keep_local, jnp.exp(wide_scores - global_top[..., None]), 0.0), axis=-1
        )
        global_top, global_total = combined_all((global_top, global_total), "seq", merge_stats)
        wide_probs = (
            jnp.where(keep_local, jnp.exp(wide_scores - global_top[..., None]), 0.0)
            / global_total[..., None]
        )
        wide_part = jnp.einsum(
            "kshbj,kjhd->ksbhd",
            wide_probs.astype(jnp.bfloat16),
            local_values,
            preferred_element_type=jnp.float32,
        )
        wide_buffer = (
            jnp.zeros((nseq * global_capacity, block, width), jnp.float32)
            .at[global_slot]
            .set(wide_part.reshape(global_entries, block, width))
        )
        wide_sum = lax.psum_scatter(wide_buffer, "seq", scatter_dimension=0, tiled=True)
        attended = jnp.where(
            own_flag[:, None, None],
            jnp.take(wide_sum, own_slot, axis=0),
            mixed.reshape(docs_dev, block, width),
        )
        attended = attended.reshape(count, width).astype(jnp.bfloat16)
        after_attn = hidden + jnp.dot(attended, weight_out, preferred_element_type=jnp.float32)
        normed = norm_rows(after_attn, gain_pair[0])
        normed_low = normed.astype(jnp.bfloat16)
        up_values = jnp.dot(normed_low, weight_up, preferred_element_type=jnp.float32)
        activated = gelu_tanh(up_values).astype(jnp.bfloat16)
        after_ffn = normed + jnp.dot(activated, weight_down, preferred_element_type=jnp.float32)
        held.append(
            (
                weights,
                lowered,
                projected,
                listed_pairs,
                global_query,
                global_top,
                global_total,
                attended,
                after_attn,
                normed_low,
                up_values,
                activated,
                after_ffn,
            )
        )
        hidden = jnp.where(live_rows, norm_rows(after_ffn, gain_pair[1]), 0.0)
    gradient = cotangent.reshape(count, width).astype(jnp.float32)
    layer_grads = []
    for layer in reversed(range(LAYERS)):
        (
            weights,
            lowered,
            projected,
            listed_pairs,
            global_query,
            global_top,
            global_total,
            attended,
            after_attn,
            normed_low,
            up_values,
            activated,
            after_ffn,
        ) = held[layer]
        weights = (
            lax.all_gather(qkv_weight[layer], ("docs", "seq"), axis=0, tiled=True),
            lax.all_gather(out_weight[layer], ("docs", "seq"), axis=0, tiled=True),
            lax.all_gather(up_weight[layer], ("docs", "seq"), axis=0, tiled=True),
            lax.all_gather(down_weight[layer], ("docs", "seq"), axis=0, tiled=True),
            lax.all_gather(norm_gains[layer], ("docs", "seq"), axis=1, tiled=True),
        )
        weight_qkv, weight_out, weight_up, weight_down, gain_pair = weights
        gain_pair = gain_pair.astype(jnp.float32)
        gradient = jnp.where(live_rows, gradient, 0.0)
        grad_ffn, grad_gain_out = jax.vjp(norm_rows, after_ffn, gain_pair[1])[1](gradient)
        grad_down_low = grad_ffn.astype(jnp.bfloat16)
        grad_down_layer = jnp.einsum(
            "rf,rd->fd", activated, grad_down_low, preferred_element_type=jnp.float32
        )
        grad_activated = jnp.einsum(
            "rd,fd->rf", grad_down_low, weight_down, preferred_element_type=jnp.float32
        )
        grad_up_low = jax.vjp(gelu_tanh, up_values)[1](grad_activated)[0].astype(jnp.bfloat16)
        grad_up_layer = jnp.einsum(
            "rd,rf->df", normed_low, grad_up_low, preferred_element_type=jnp.float32
        )
        grad_normed = grad_ffn + jnp.einsum(
            "rf,df->rd", grad_up_low, weight_up, preferred_element_type=jnp.float32
        )
        grad_attn, grad_gain_mid = jax.vjp(norm_rows, after_attn, gain_pair[0])[1](grad_normed)
        grad_attn_low = grad_attn.astype(jnp.bfloat16)
        grad_out_layer = jnp.einsum(
            "rd,re->de", attended, grad_attn_low, preferred_element_type=jnp.float32
        )
        grad_mixed = (
            jnp.einsum("re,de->rd", grad_attn_low, weight_out, preferred_element_type=jnp.float32)
            .astype(jnp.bfloat16)
            .reshape(docs_dev, block, width)
        )
        query = projected[:, :, :width].reshape(docs_dev, block, heads, HEAD)
        key_part = listed_pairs[:, :, :width].reshape(docs_dev, span, heads, HEAD)
        value_part = listed_pairs[:, :, width:].reshape(docs_dev, span, heads, HEAD)
        probs = sparse_probs(query, key_part, key_inside, scale)
        grad_sparse = jnp.where(
            own_flag[:, None, None], jnp.zeros((), jnp.bfloat16), grad_mixed
        ).reshape(docs_dev, block, heads, HEAD)
        grad_probs = jnp.einsum(
            "kbhd,kjhd->khbj", grad_sparse, value_part, preferred_element_type=jnp.float32
        )
        delta = jnp.sum(probs * grad_probs, axis=-1, keepdims=True)
        grad_scores = (probs * (grad_probs - delta)).astype(jnp.bfloat16)
        grad_query = (
            jnp.einsum("khbj,kjhd->kbhd", grad_scores, key_part, preferred_element_type=jnp.float32)
            * scale
        )
        grad_key_part = (
            jnp.einsum("khbj,kbhd->kjhd", grad_scores, query, preferred_element_type=jnp.float32)
            * scale
        )
        grad_value_part = jnp.einsum(
            "khbj,kbhd->kjhd",
            probs.astype(jnp.bfloat16),
            grad_sparse,
            preferred_element_type=jnp.float32,
        )
        grad_listed = jnp.concatenate(
            [
                grad_key_part.reshape(docs_dev, span, width),
                grad_value_part.reshape(docs_dev, span, width),
            ],
            axis=2,
        )
        wide_out = jnp.where(
            global_send_live[:, None, None],
            jnp.take(grad_mixed, global_send_doc, axis=0),
            jnp.zeros((), jnp.bfloat16),
        )
        wide_all = lax.all_gather(wide_out, "seq", axis=0, tiled=True)
        wide_grad = jnp.take(wide_all, global_slot, axis=0).reshape(
            docs_dev, GLOB, block, heads, HEAD
        )
        local_keys = projected[:, :, width : 2 * width].reshape(docs_dev, block, heads, HEAD)
        local_values = projected[:, :, 2 * width :].reshape(docs_dev, block, heads, HEAD)
        wide_scores = global_scores(global_query, local_keys, inside, scale)
        wide_probs = (
            jnp.where(keep_local, jnp.exp(wide_scores - global_top[..., None]), 0.0)
            / global_total[..., None]
        )
        wide_grad_probs = jnp.einsum(
            "ksbhd,kjhd->kshbj", wide_grad, local_values, preferred_element_type=jnp.float32
        )
        wide_delta = lax.psum(jnp.sum(wide_probs * wide_grad_probs, axis=-1), "seq")
        wide_grad_scores = (wide_probs * (wide_grad_probs - wide_delta[..., None])).astype(
            jnp.bfloat16
        )
        wide_grad_query = (
            jnp.einsum(
                "kshbj,kjhd->ksbhd",
                wide_grad_scores,
                local_keys,
                preferred_element_type=jnp.float32,
            )
            * scale
        )
        wide_grad_keys = (
            jnp.einsum(
                "kshbj,ksbhd->kjhd",
                wide_grad_scores,
                global_query,
                preferred_element_type=jnp.float32,
            )
            * scale
        )
        wide_grad_values = jnp.einsum(
            "kshbj,ksbhd->kjhd",
            wide_probs.astype(jnp.bfloat16),
            wide_grad,
            preferred_element_type=jnp.float32,
        )
        global_grads = jnp.concatenate(
            [
                wide_grad_query.reshape(global_entries, block, width),
                grad_listed[:, (3 + RAND) * block :, :].reshape(global_entries, block, 2 * width),
            ],
            axis=2,
        )
        global_buffer = (
            jnp.zeros((nseq * global_capacity, block, 3 * width), jnp.float32)
            .at[global_slot]
            .set(global_grads)
        )
        global_share = lax.psum_scatter(global_buffer, "seq", scatter_dimension=0, tiled=True)
        global_mine = jnp.where(
            own_flag[:, None, None], jnp.take(global_share, own_slot, axis=0), 0.0
        )
        grad_fetched = grad_listed[:, 3 * block : (3 + RAND) * block, :].reshape(
            entries, block, 2 * width
        )
        back_out = (
            jnp.zeros((nseq * capacity, block, 2 * width), jnp.float32)
            .at[fetch_slot]
            .set(grad_fetched)
            .reshape(nseq, capacity, block, 2 * width)
        )
        back_in = lax.all_to_all(back_out, "seq", split_axis=0, concat_axis=0, tiled=True)
        grad_random = jnp.einsum(
            "dck,dcbf->kbf", owner_pick, back_in, precision=lax.Precision.HIGHEST
        )
        grad_window = grad_listed[:, : 3 * block, :]
        edges = jnp.concatenate([grad_window[:, :block], grad_window[:, 2 * block :]], axis=1)
        beside_all = with_halo(edges, (("seq", 1),), block)
        grad_pairs = (
            grad_window[:, block : 2 * block]
            + beside_all[:, :block]
            + beside_all[:, 3 * block :]
            + grad_random
            + global_mine[:, :, width:]
        )
        grad_pairs = grad_pairs + jnp.concatenate(
            [
                wide_grad_keys.reshape(docs_dev, block, width),
                wide_grad_values.reshape(docs_dev, block, width),
            ],
            axis=2,
        )
        grad_queries = grad_query.reshape(docs_dev, block, width) + global_mine[:, :, :width]
        grad_projected = (
            jnp.concatenate([grad_queries, grad_pairs], axis=2)
            .reshape(count, 3 * width)
            .astype(jnp.bfloat16)
        )
        grad_qkv_layer = jnp.einsum(
            "rd,re->de", lowered, grad_projected, preferred_element_type=jnp.float32
        )
        gradient = grad_attn + jnp.einsum(
            "re,de->rd", grad_projected, weight_qkv, preferred_element_type=jnp.float32
        )
        group_shares = (
            lax.psum_scatter(grad_qkv_layer, "docs", scatter_dimension=0, tiled=True),
            lax.psum_scatter(grad_out_layer, "docs", scatter_dimension=0, tiled=True),
            lax.psum_scatter(grad_up_layer, "docs", scatter_dimension=0, tiled=True),
            lax.psum_scatter(grad_down_layer, "docs", scatter_dimension=0, tiled=True),
            lax.psum_scatter(
                jnp.stack([grad_gain_mid, grad_gain_out]), "docs", scatter_dimension=1, tiled=True
            ),
        )
        shares = (
            lax.psum_scatter(group_shares[0], "seq", scatter_dimension=1, tiled=True),
            lax.psum_scatter(group_shares[1], "seq", scatter_dimension=1, tiled=True),
            lax.psum_scatter(group_shares[2], "seq", scatter_dimension=1, tiled=True),
            lax.psum_scatter(group_shares[3], "seq", scatter_dimension=1, tiled=True),
            lax.psum_scatter(group_shares[4], "seq", scatter_dimension=1, tiled=True),
        )
        layer_grads.insert(0, shares)
    stacked = [
        jnp.stack([layer_grads[number][member] for number in range(LAYERS)]) for member in range(5)
    ]
    return (
        hidden.astype(jnp.bfloat16).reshape(docs_dev, block, width),
        gradient.reshape(docs_dev, block, width),
        stacked[0],
        stacked[1],
        stacked[2],
        stacked[3],
        stacked[4],
    )


PLANES = 4
GROUPS = 4
CHIPS = 16
GROUP_HEADS = 3
CUT = 288
MESH = pl.DeviceIdType.MESH
F32 = jnp.float32
BF16 = jnp.bfloat16


def fits(mesh, docs_dev, heads):
    return (
        mesh.shape["docs"] == 2
        and mesh.shape["seq"] == 16
        and docs_dev == PLANES
        and heads == GROUPS * GROUP_HEADS
    )


def swap(value, bits):
    return lax.ppermute(value, "seq", [(i, i ^ bits) for i in range(16)])


def swap_docs(value):
    return lax.ppermute(value, "docs", [(0, 1), (1, 0)])


def dot(left, right):
    return lax.dot_general(left, right, (((1,), (0,)), ((), ())), preferred_element_type=F32)


def dot_nt(left, right):
    return lax.dot_general(left, right, (((1,), (1,)), ((), ())), preferred_element_type=F32)


def dot_tn(left, right):
    return lax.dot_general(left, right, (((0,), (0,)), ((), ())), preferred_element_type=F32)


def vmem():
    return pl.BlockSpec(memory_space=pltpu.VMEM)


def smem():
    return pl.BlockSpec(memory_space=pltpu.SMEM)


def hbm():
    return pl.BlockSpec(memory_space=pltpu.HBM)


def params():
    return pltpu.CompilerParams(vmem_limit_bytes=56 * 2**20)


QUERIES = 1024
BACK_QUERIES = 512


def key_features(own_random, own_global, length):
    block = jnp.arange(16, dtype=jnp.int32)
    window = jnp.stack([(block + 15) % 16, block, (block + 1) % 16], axis=1)
    ids = jnp.concatenate([window, own_random, jnp.broadcast_to(own_global, (16, GLOB))], axis=1)
    count = jnp.sum((ids[:, :, None] == block).astype(F32), axis=1).T
    special = jnp.any(own_global[None, :] == block[:, None], axis=1)
    count = jnp.where(special[None, :], 1.0, count)
    extra = jnp.where(count > 0, jnp.log(jnp.maximum(count, 1.0)), NEGATIVE)
    inside = jnp.arange(1024, dtype=jnp.int32)[:, None] < length
    extra = jnp.where(inside, jnp.repeat(extra, 64, axis=0), NEGATIVE)
    high = extra.astype(BF16)
    low = jnp.where(extra > 0, extra - high.astype(F32), 0.0).astype(BF16)
    return jnp.concatenate([high, low, jnp.zeros((1024, 32), BF16)], axis=1)


def halves_beside(rows):
    return jnp.concatenate([rows[:32], rows[32:]], axis=1)


def halves_below(rows):
    return jnp.concatenate([rows[:, :192], rows[:, 192:]], axis=0)


def spread_heads(qkv, feature_ref, key_scr, query_scr):
    row = lax.broadcasted_iota(jnp.int32, (1024, 64), 0) // 64
    lane = lax.broadcasted_iota(jnp.int32, (1024, 64), 1)
    place = jnp.where(jnp.logical_and(lane < 32, lane % 16 == row), 1.0, 0.0).astype(BF16)
    for h in range(GROUP_HEADS):
        key_scr[h] = jnp.concatenate([qkv[:, 128 * h : 128 * h + 64], feature_ref[...]], axis=1)
        query = qkv[:, 384 + 64 * h : 448 + 64 * h] * jnp.asarray(HEAD**-0.5, BF16)
        query_scr[h] = jnp.concatenate([query, place], axis=1)


def expo_columns(scores):
    expo = jnp.exp(scores - jnp.max(scores, axis=0, keepdims=True))
    return expo, 1.0 / jnp.sum(expo, axis=0, keepdims=True)


def attend_kernel(feature_ref, x_ref, w_ref, qkv_ref, o_ref, key_scr, query_scr, value_scr, o_scr):
    weight = w_ref[...].reshape(-1, 576)
    qkv = dot(x_ref[...].reshape(1024, x_ref.shape[-1]), weight).astype(BF16)
    qkv_ref[...] = qkv
    spread_heads(qkv, feature_ref, key_scr, query_scr)
    for h in range(GROUP_HEADS):
        value_scr[h] = qkv[:, 128 * h + 64 : 128 * h + 128].T

    def chunk(n, _):
        at = pl.multiple_of(n * QUERIES, QUERIES)
        for h in range(GROUP_HEADS):
            scores = dot_nt(key_scr[h], query_scr[h, pl.ds(at, QUERIES), :])
            expo, rate = expo_columns(scores)
            o_scr[n, 64 * h : 64 * h + 64, :] = dot(value_scr[h], (expo * rate).astype(BF16))
        rows = o_scr[n].T.astype(BF16)
        for m in range(QUERIES // 64):
            o_ref[n * (QUERIES // 64) + m] = halves_beside(rows[64 * m : 64 * m + 64])
        return 0

    lax.fori_loop(0, 1024 // QUERIES, chunk, 0)


def attend(features, x, weight):
    return pl.pallas_call(
        attend_kernel,
        out_shape=(
            jax.ShapeDtypeStruct((1024, 576), BF16),
            jax.ShapeDtypeStruct((16, 32, 384), BF16),
        ),
        in_specs=[vmem(), vmem(), vmem()],
        out_specs=(vmem(), vmem()),
        scratch_shapes=[
            pltpu.VMEM((3, 1024, 128), BF16),
            pltpu.VMEM((3, 1024, 128), BF16),
            pltpu.VMEM((3, 64, 1024), BF16),
            pltpu.VMEM((1024 // QUERIES, 192, QUERIES), F32),
        ],
        compiler_params=params(),
        cost_estimate=pl.CostEstimate(
            flops=3 * 10**9, bytes_accessed=6 * 10**6, transcendentals=3 * 10**6
        ),
        name="attend",
    )(features, x, weight)


def attend_back_kernel(
    info,
    feature_ref,
    qkv_ref,
    do_ref,
    x_ref,
    w_ref,
    keep_ref,
    send_ref,
    grad_ref,
    key_scr,
    query_scr,
    value_scr,
    turned_scr,
    side_scr,
    dkv_scr,
    dq_scr,
    dqkv_scr,
):
    weight = w_ref[...].reshape(-1, 576)
    qkv = qkv_ref[...]
    spread_heads(qkv, feature_ref, key_scr, query_scr)
    grad_o = jnp.concatenate([halves_below(do_ref[n]) for n in range(16)], axis=0)
    zero = jnp.zeros((1024, 64), BF16)
    for h in range(GROUP_HEADS):
        value_scr[h] = qkv[:, 128 * h + 64 : 128 * h + 128]
        turned_scr[h] = qkv[:, 128 * h : 128 * h + 64].T
        side_scr[0, h] = jnp.concatenate([query_scr[h, :, :64], zero], axis=1)
        side_scr[1, h] = jnp.concatenate([zero, grad_o[:, 64 * h : 64 * h + 64]], axis=1)
    dkv_scr[...] = jnp.zeros_like(dkv_scr)

    def chunk(n, _):
        at = pl.ds(pl.multiple_of(n * BACK_QUERIES, BACK_QUERIES), BACK_QUERIES)
        for h in range(GROUP_HEADS):
            expo, rate = expo_columns(dot_nt(key_scr[h], query_scr[h, at, :]))
            probs = expo * rate
            grad_probs = dot_nt(value_scr[h], side_scr[1, h, at, :][:, 64:])
            delta = jnp.sum(probs * grad_probs, axis=0, keepdims=True)
            grad_scores = (probs * (grad_probs - delta)).astype(BF16)
            dq_scr[n, 64 * h : 64 * h + 64, :] = dot(turned_scr[h], grad_scores) * (HEAD**-0.5)
            dkv_scr[h] += dot(grad_scores, side_scr[0, h, at, :]) + dot(
                probs.astype(BF16), side_scr[1, h, at, :]
            )
        dqkv_scr[at, 384:576] = dq_scr[n].T.astype(BF16)
        return 0

    lax.fori_loop(0, 1024 // BACK_QUERIES, chunk, 0, unroll=True)
    for h in range(GROUP_HEADS):
        dqkv_scr[:, 128 * h : 128 * h + 128] = dkv_scr[h].astype(BF16)
    for half, ref in enumerate((keep_ref, send_ref)):
        rows = []
        for n in range(8):
            block = info[0] ^ ((n // 2) * 4 + (n % 2) * 2 + half)
            rows.append(dqkv_scr[pl.ds(pl.multiple_of(block * 64, 64), 64), :])
        ref[...] = dot_nt(jnp.concatenate(rows, axis=0), weight).astype(BF16).reshape(ref.shape)
    width = x_ref.shape[-1]
    grad = dot_tn(dqkv_scr[...], x_ref[...].reshape(1024, width))
    order = [6, 7, 8, 0, 2, 4, 1, 3, 5]
    grad = jnp.concatenate([grad[64 * n : 64 * n + 64] for n in order], axis=0).astype(BF16)
    for quarter in range(PLANES):
        for side in range(2):
            apart = quarter ^ info[3]
            grad_ref[side ^ info[4], ((apart & 1) << 1) | (apart >> 1)] = grad[
                144 * quarter : 144 * quarter + 144, 384 * side : 384 * side + 384
            ]


def attend_back(info, features, qkv, grad_o, x, weight):
    width = x.shape[-1]
    return pl.pallas_call(
        attend_back_kernel,
        out_shape=(
            jax.ShapeDtypeStruct((8, 64, width), BF16),
            jax.ShapeDtypeStruct((8, 64, width), BF16),
            jax.ShapeDtypeStruct((2, PLANES, 144, width // 2), BF16),
        ),
        in_specs=[smem(), vmem(), vmem(), vmem(), vmem(), vmem()],
        out_specs=(vmem(), vmem(), vmem()),
        scratch_shapes=[
            pltpu.VMEM((3, 1024, 128), BF16),
            pltpu.VMEM((3, 1024, 128), BF16),
            pltpu.VMEM((3, 1024, 64), BF16),
            pltpu.VMEM((3, 64, 1024), BF16),
            pltpu.VMEM((2, 3, 1024, 128), BF16),
            pltpu.VMEM((3, 1024, 128), F32),
            pltpu.VMEM((1024 // BACK_QUERIES, 192, BACK_QUERIES), F32),
            pltpu.VMEM((1024, 576), BF16),
        ],
        compiler_params=params(),
        cost_estimate=pl.CostEstimate(
            flops=8 * 10**9, bytes_accessed=10 * 10**6, transcendentals=3 * 10**6
        ),
        name="attend_back",
    )(info, features, qkv, grad_o, x, weight)


def load_ordered(w_refs, wu, wd, wo, sems):
    up_ref, down_ref = w_refs
    pltpu.make_async_copy(down_ref.at[:, :, :, pl.ds(1536, 384)], wo, sems.at[0]).start()
    pltpu.make_async_copy(up_ref, wu, sems.at[1]).start()
    for plane in range(2):
        for part in range(2):
            source = down_ref.at[plane, :, :, pl.ds(768 * part, 768)]
            pltpu.make_async_copy(source, wd.at[:, plane, part], sems.at[2]).start()


def load_slots(w_refs, wu, wd, wo, sems):
    ao_ref, ar_ref, bo_ref, br_ref = w_refs
    docs, me = lax.axis_index("docs"), lax.axis_index("seq")
    x, core = (me // 2) % 2, me % 2

    def one(j, _):
        over, z, across = j // 8, (j // 2) % 4, j % 2
        over, across = over + docs - 2 * over * docs, across + x - 2 * across * x
        at_a, at_b = 8 * over + 4 * across + z, 8 * across + 4 * over + z
        for plane, a, b in ((core, ao_ref, bo_ref), (1 - core, ar_ref, br_ref)):
            a, b = a.at[at_a], b.at[at_b]
            pltpu.make_async_copy(a.at[:, pl.ds(2304, 384)], wo.at[plane, j], sems.at[0]).start()
            pltpu.make_async_copy(a.at[:, pl.ds(0, 1536)], wu.at[plane, j], sems.at[1]).start()
            for part, source in enumerate((a.at[:, pl.ds(1536, 768)], b)):
                pltpu.make_async_copy(source, wd.at[j, plane, part], sems.at[2]).start()
        return 0

    lax.fori_loop(0, CHIPS, one, 0)


def load_weights(w_refs, *scratch):
    if len(w_refs) == 2:
        load_ordered(w_refs, *scratch)
    else:
        load_slots(w_refs, *scratch)


def wait_weight(scr, sem):
    pltpu.make_async_copy(scr, scr, sem).wait()


def inside_rows(info):
    row = lax.broadcasted_iota(jnp.int32, (256, 1), 0)
    length = jnp.zeros_like(row)
    for k in range(PLANES):
        length = jnp.where(row // 64 == k, info[8 + k], length)
    return info[0] * 64 + row % 64 < length


def norm_parts(values):
    centre = values - jnp.mean(values, axis=-1, keepdims=True)
    spread = jnp.mean(centre * centre, axis=-1, keepdims=True)
    rate = lax.rsqrt(spread + EPSILON)
    return centre * rate, rate


def norm_back(unit, rate, gain, grad):
    scaled = grad * gain
    inner = jnp.mean(scaled * unit, axis=-1, keepdims=True)
    outer = jnp.mean(scaled, axis=-1, keepdims=True)
    return rate * (scaled - outer - unit * inner), jnp.sum(grad * unit, axis=0, keepdims=True)


CURVE = 0.7978845608028654


def gelu_parts(values):
    square = values * values
    bend = jnp.tanh(CURVE * (values + 0.044715 * (square * values)))
    return 0.5 * values * (1.0 + bend), bend, square


def gelu_slope(values, bend, square):
    return 0.5 * (1.0 + bend) + 0.5 * values * (1.0 - bend * bend) * (
        CURVE * (1.0 + 3 * 0.044715 * square)
    )


def feed_kernel(pieces, info, o_ref, h_ref, gain_ref, *refs):
    w_refs, refs = refs[:pieces], refs[pieces:]
    mixed_ref, h1_ref, up_ref, h2_ref, next_ref, low_ref, wu, wd, wo, act_scr, sems = refs
    load_weights(w_refs, wu, wd, wo, sems)
    for k in range(PLANES):
        mixed_ref[64 * k : 64 * k + 64, :] = jnp.concatenate(
            [halves_below(o_ref[4 * k + g]) for g in range(GROUPS)], axis=1
        )
    mixed = mixed_ref[...]
    wait_weight(wo, sems.at[0])
    attended = jnp.concatenate([dot(mixed, wo[side].reshape(768, 384)) for side in range(2)], axis=1)
    h1 = h_ref[...].reshape(256, 768).astype(F32) + attended
    h1_ref[...] = h1
    x1 = norm_parts(h1)[0] * gain_ref[0:1, :]
    x1_low = x1.astype(BF16)
    wait_weight(wu, sems.at[1])
    for side in range(2):
        for part in range(3):
            at = 1536 * side + 512 * part
            up = dot(x1_low, wu[side, :, :, 512 * part : 512 * part + 512].reshape(768, 512))
            up_ref[:, at : at + 512] = up
            act_scr[:, at : at + 512] = gelu_parts(up)[0].astype(BF16)
    wait_weight(wd, sems.at[2])
    h2 = x1 + dot(act_scr[...], wd[...].reshape(3072, 768))
    h2_ref[...] = h2
    out = jnp.where(inside_rows(info), norm_parts(h2)[0] * gain_ref[1:2, :], 0.0)
    next_ref[...] = out
    low = out.astype(BF16)
    for k in range(PLANES):
        low_ref[k] = low[64 * k : 64 * k + 64]


WEIGHT_SCRATCH = [
    pltpu.VMEM((2, 16, 48, 1536), BF16),
    pltpu.VMEM((16, 2, 2, 48, 768), BF16),
    pltpu.VMEM((2, 16, 48, 384), BF16),
]


def feed(info, o, hidden, gains, weights):
    return pl.pallas_call(
        functools.partial(feed_kernel, len(weights)),
        out_shape=(
            jax.ShapeDtypeStruct((256, 768), BF16),
            jax.ShapeDtypeStruct((256, 768), F32),
            jax.ShapeDtypeStruct((256, 3072), F32),
            jax.ShapeDtypeStruct((256, 768), F32),
            jax.ShapeDtypeStruct((256, 768), F32),
            jax.ShapeDtypeStruct((4, 64, 768), BF16),
        ),
        in_specs=[smem(), vmem(), vmem(), vmem()] + [hbm() for _ in weights],
        out_specs=tuple(vmem() for _ in range(6)),
        scratch_shapes=WEIGHT_SCRATCH
        + [pltpu.VMEM((256, 3072), BF16), pltpu.SemaphoreType.DMA((3,))],
        compiler_params=params(),
        cost_estimate=pl.CostEstimate(
            flops=3 * 10**9, bytes_accessed=20 * 10**6, transcendentals=10**6
        ),
        name="feed",
    )(info, o, hidden, gains, *weights)


def feed_back_kernel(
    pieces,
    has_extra,
    info,
    base_ref,
    extra_ref,
    gain_ref,
    mixed_ref,
    h1_ref,
    up_ref,
    h2_ref,
    *refs,
):
    w_refs, refs = refs[:pieces], refs[pieces:]
    dh1_ref, do_ref, dgain_ref, *sum_refs, wu, wd, wo, gu, gd, go, got, sems, pair_sems, out_sems = refs
    load_weights(w_refs, wu, wd, wo, sems)
    docs, me = lax.axis_index("docs"), lax.axis_index("seq")
    mate = (docs, flip(me, 1))
    greet([mate])
    units = [(ry, place) for ry in range(2) for place in range(8)]

    def other_docs(ry):
        return docs if ry == 0 else 1 - docs

    def owner(place, rc):
        return flip(me, (place % 2) * 8 + (place // 2 % 2) * 4 + (place // 4) * 2 + rc)

    def exchange_units(scr, first, count, n):
        copies = []
        for ry, place in units:
            copies.append(
                pltpu.make_async_remote_copy(
                    scr.at[other_docs(ry), owner(place, 1)],
                    got.at[ry, place, pl.ds(first, count)],
                    pair_sems.at[0, n],
                    pair_sems.at[1, n],
                    device_id=mate,
                    device_id_type=MESH,
                )
            )
            copies[-1].start()
        return copies
    if has_extra:
        parts = [
            base_ref[64 * k : 64 * k + 64, :] + extra_ref[k].astype(F32)
            for k in range(PLANES)
        ]
        grad = jnp.concatenate(parts, axis=0)
    else:
        grad = base_ref[...].reshape(256, 768).astype(F32)
    grad = jnp.where(inside_rows(info), grad, 0.0)
    unit2, rate2 = norm_parts(h2_ref[...])
    dh2, dgain1 = norm_back(unit2, rate2, gain_ref[1:2, :], grad)
    dgain_ref[1:2, :] = dgain1
    df = dh2.astype(BF16)
    unit1, rate1 = norm_parts(h1_ref[...])
    x1_low = (unit1 * gain_ref[0:1, :]).astype(BF16)
    wait_weight(wd, sems.at[2])
    wait_weight(wu, sems.at[1])
    dx1 = dh2
    for part in range(8):
        at = 384 * part
        d_act = dot_nt(df, wd[2 * part : 2 * part + 2].reshape(384, 768))
        up = up_ref[:, at : at + 384]
        act, bend, square = gelu_parts(up)
        act = act.astype(BF16)
        dup = (gelu_slope(up, bend, square) * d_act).astype(BF16)
        side, start = part // 4, 384 * (part % 4)
        dx1 += dot_nt(dup, wu[side, :, :, start : start + 384].reshape(768, 384))
        gt_up = dot_tn(dup, x1_low).astype(BF16)
        for n in range(2):
            for half in range(2):
                gu[half, 2 * part + n] = gt_up[
                    192 * n : 192 * n + 192, 384 * half : 384 * half + 384
                ]
        gt_down = dot_tn(df, act).astype(BF16)
        row = 48 * (part % 4)
        for s in range(16):
            gd[part // 4, s, row : row + 48, :] = gt_down[48 * s : 48 * s + 48]
    exchange_units(gu, 0, 192, 0)
    exchange_units(gd, 240, 192, 1)
    dh1, dgain0 = norm_back(unit1, rate1, gain_ref[0:1, :], dx1)
    dgain_ref[0:1, :] = dgain0
    dh1_ref[...] = dh1
    da = dh1.astype(BF16)
    gt_out = dot_tn(da, mixed_ref[...]).astype(BF16)
    for s in range(16):
        for half in range(2):
            go[half, s] = gt_out[48 * s : 48 * s + 48, 384 * half : 384 * half + 384]
    exchange_units(go, 192, 48, 2)
    wait_weight(wo, sems.at[0])
    do = dot_nt(da[:, 0:384], wo[0].reshape(768, 384))
    do += dot_nt(da[:, 384:768], wo[1].reshape(768, 384))
    do = do.astype(BF16)
    for k in range(PLANES):
        for g in range(GROUPS):
            do_ref[4 * k + g] = halves_beside(do[64 * k : 64 * k + 64, 192 * g : 192 * g + 192])
    for n, (first, count) in enumerate(((0, 192), (240, 192), (192, 48))):
        part = got.at[:, :, pl.ds(first, count)]
        pltpu.make_async_copy(part, part, pair_sems.at[1, n]).wait()
    copies = []
    for ry, place in units:
        for scr, first, count in ((gu, 0, 192), (go, 192, 48), (gd, 240, 192)):
            span = slice(first, first + count)
            own = scr[other_docs(ry), owner(place, 0)].astype(F32)
            got[ry, place, span] = (own + got[ry, place, span].astype(F32)).astype(BF16)
        for ref, source in (
            (sum_refs[ry].at[place], got.at[ry, place, pl.ds(0, CUT)]),
            (sum_refs[2 + place // 4].at[ry, place % 4], got.at[ry, place, pl.ds(CUT, 432 - CUT)]),
        ):
            copies.append(pltpu.make_async_copy(source, ref, out_sems.at[len(copies)]))
            copies[-1].start()
    for n, scr in enumerate((gu, gd, go)):
        half = scr.at[:, pl.ds(0, 8)]
        pltpu.make_async_copy(half, half, pair_sems.at[0, n]).wait()
    for copy in copies:
        copy.wait()


def feed_back(info, base, extra, gains, saved, weights, number):
    mixed, h1, up, h2 = saved
    has_extra = extra is not None
    if not has_extra:
        extra = jnp.zeros((8, 128), BF16)
    return pl.pallas_call(
        functools.partial(feed_back_kernel, len(weights), has_extra),
        out_shape=(
            jax.ShapeDtypeStruct((256, 768), F32),
            jax.ShapeDtypeStruct((16, 32, 384), BF16),
            jax.ShapeDtypeStruct((2, 768), F32),
            jax.ShapeDtypeStruct((8, CUT, 384), BF16),
            jax.ShapeDtypeStruct((8, CUT, 384), BF16),
            jax.ShapeDtypeStruct((2, 4, 432 - CUT, 384), BF16),
            jax.ShapeDtypeStruct((2, 4, 432 - CUT, 384), BF16),
        ),
        in_specs=[smem()] + [vmem()] * 7 + [hbm() for _ in weights],
        out_specs=(vmem(), vmem(), vmem(), hbm(), hbm(), hbm(), hbm()),
        scratch_shapes=WEIGHT_SCRATCH
        + [
            pltpu.VMEM((2, 16, 192, 384), BF16),
            pltpu.VMEM((2, 16, 192, 384), BF16),
            pltpu.VMEM((2, 16, 48, 384), BF16),
            pltpu.VMEM((2, 8, 432, 384), BF16),
            pltpu.SemaphoreType.DMA((3,)),
            pltpu.SemaphoreType.DMA((2, 3)),
            pltpu.SemaphoreType.DMA((32,)),
        ],
        compiler_params=pltpu.CompilerParams(
            collective_id=number, has_side_effects=True, vmem_limit_bytes=56 * 2**20
        ),
        cost_estimate=pl.CostEstimate(
            flops=6 * 10**9, bytes_accessed=40 * 10**6, transcendentals=10**6
        ),
        name="feed_back",
    )(info, base, extra, gains, mixed, h1, up, h2, *weights)


def flip(index, bits):
    for bit in (1, 2, 4, 8):
        if bits & bit:
            index = index + bit - 2 * bit * ((index // bit) % 2)
    return index


def greet(peers):
    barrier = pltpu.get_barrier_semaphore()
    for peer in peers:
        pl.semaphore_signal(barrier, inc=1, device_id=peer, device_id_type=MESH)
    pl.semaphore_wait(barrier, len(peers))


def remote(source, target, sems, n, peer):
    return pltpu.make_async_remote_copy(
        source, target, sems.at[0, n], sems.at[1, n], device_id=peer, device_id_type=MESH
    )


def comm_params(number):
    return pltpu.CompilerParams(
        collective_id=number, has_side_effects=True, vmem_limit_bytes=16 * 2**20
    )


class Spread:
    def __init__(self, low_ref, x_ref, sems, own_sem):
        self.low_ref, self.x_ref, self.sems = low_ref, x_ref, sems
        self.docs, self.me = lax.axis_index("docs"), lax.axis_index("seq")
        self.own = pltpu.make_async_copy(low_ref.at[self.me // 4], x_ref.at[self.me], own_sem)
        self.hops, self.across, self.mates = [], [], []

    def send(self, source, slot, n, bits):
        peer = (self.docs, flip(self.me, bits))
        copy = remote(source, self.x_ref.at[slot], self.sems, n, peer)
        copy.start()
        return copy

    def begin(self):
        for rz in range(1, 4):
            source = self.low_ref.at[flip(self.me, 4 * rz) // 4]
            self.hops.append(self.send(source, self.me, rz, 4 * rz))
        self.own.start()
        source = self.low_ref.at[self.me // 4]
        self.across.append(self.send(source, self.me, 4, 2))
        self.mates.append(self.send(source, self.me, 8, 1))

    def forward(self, rz):
        self.hops[rz - 1].wait_recv()
        slot = flip(self.me, 4 * rz)
        self.across.append(self.send(self.x_ref.at[slot], slot, 4 + rz, 2))
        self.mates.append(self.send(self.x_ref.at[slot], slot, 8 + rz, 1))

    def from_beside(self):
        for rz in range(4):
            self.across[rz].wait_recv()
            slot = flip(flip(self.me, 4 * rz), 2)
            self.mates.append(self.send(self.x_ref.at[slot], slot, 12 + rz, 1))

    def finish(self):
        for copy in self.mates:
            copy.wait_recv()
        for copy in self.hops + self.across + self.mates:
            copy.wait_send()
        self.own.wait()


def spread_peers():
    docs, me = lax.axis_index("docs"), lax.axis_index("seq")
    return [(docs, flip(me, bits)) for bits in (4, 8, 12, 2, 1)]


def spread_kernel(low_ref, x_ref, sems, own_sem):
    greet(spread_peers())
    rows = Spread(low_ref, x_ref, sems, own_sem)
    rows.begin()
    for rz in range(1, 4):
        rows.forward(rz)
    rows.from_beside()
    rows.finish()


def spread(low, number):
    return pl.pallas_call(
        spread_kernel,
        out_shape=jax.ShapeDtypeStruct((16, 64, low.shape[-1]), BF16),
        in_specs=[hbm()],
        out_specs=hbm(),
        scratch_shapes=[pltpu.SemaphoreType.DMA((2, 16)), pltpu.SemaphoreType.DMA],
        compiler_params=comm_params(number),
        name="spread",
    )(low)


class Slabs:
    def __init__(self, source, w_ref, sems, own_sem, docs_first=False, z_only=False):
        self.source, self.w_ref, self.sems, self.z_only = source, w_ref, sems, z_only
        self.docs, self.me = lax.axis_index("docs"), lax.axis_index("seq")
        self.plane, self.x, self.core = self.me // 4, (self.me // 2) % 2, self.me % 2
        beside, over = (self.docs, flip(self.me, 2)), (1 - self.docs, self.me)
        self.peers = (over, beside) if docs_first else (beside, over)
        if docs_first:
            self.near = ((self.docs, self.x), (1 - self.docs, self.x))
            self.far = ((self.docs, 1 - self.x), (1 - self.docs, 1 - self.x))
        else:
            self.near = ((self.docs, self.x), (self.docs, 1 - self.x))
            self.far = ((1 - self.docs, self.x), (1 - self.docs, 1 - self.x))
        self.mate = (self.docs, flip(self.me, 1))
        self.own = pltpu.make_async_copy(source, self.slot(self.near[0], self.plane), own_sem)

    def slot(self, at, z):
        return self.w_ref.at[z] if self.z_only else self.w_ref.at[self.core, at[0], z, at[1]]

    def copy(self, at, z, own, send, recv, peer):
        slot = self.slot(at, z)
        return pltpu.make_async_remote_copy(
            self.source if own else slot,
            slot,
            self.sems.at[0, send],
            self.sems.at[1, recv],
            device_id=peer,
            device_id_type=MESH,
        )

    def line(self, z, own, step):
        peer = (self.docs, self.me + 4 * step)
        return self.copy(self.near[0], z, own, z + (0 if step > 0 else 4), z, peer)

    def first(self, z, own=False):
        return self.copy(self.near[0], z, own, 8 + z, 8 + z, self.peers[0])

    def second(self, z, n, own=False):
        return self.copy(self.near[n], z, own, 12 + 4 * n + z, 12 + 4 * n + z, self.peers[1])

    def core_copy(self, at, n, z, own=False):
        return self.copy(at, z, own, 20 + 4 * n + z, 20 + 4 * n + z, self.mate)

    def begin(self):
        self.own.start()
        for step in (1, -1):
            pl.when(self.has(self.plane + step))(self.line(self.plane, True, step).start)
        if not self.z_only:
            self.first(self.plane, True).start()
            self.core_copy(self.near[0], 0, self.plane, True).start()

    def has(self, z):
        return jnp.logical_and(z >= 0, z < PLANES)

    def each(self, distance, act):
        if distance == 0:
            act(self.plane, 0)
            return
        for step in (1, -1):
            z = self.plane - step * distance
            pl.when(self.has(z))(functools.partial(act, z, step))

    def from_line(self, distance):
        def act(z, step):
            self.line(z, False, step).wait_recv()
            pl.when(self.has(self.plane + step))(self.line(z, False, step).start)
            if not self.z_only:
                self.first(z).start()
                self.core_copy(self.near[0], 0, z).start()

        self.each(distance, act)

    def from_first(self, distance):
        def act(z, step):
            self.first(z).wait_recv()
            self.second(z, 0, distance == 0).start()
            self.second(z, 1).start()
            self.core_copy(self.near[1], 1, z).start()

        self.each(distance, act)

    def from_second(self, distance):
        def act(z, step):
            for n in range(2):
                self.second(z, n).wait_recv()
                self.core_copy(self.far[n], 2 + n, z).start()

        self.each(distance, act)

    def finish(self):
        for z in range(PLANES):
            for step in (1, -1):
                sent = jnp.logical_and(
                    (self.plane - z) * step >= 0, self.has(self.plane + step)
                )
                pl.when(sent)(self.line(z, False, step).wait_send)
            if not self.z_only:
                self.first(z).wait_send()
                for n, at in enumerate(self.near + self.far):
                    if n < 2:
                        self.second(z, n).wait_send()
                    self.core_copy(at, n, z).wait()
        self.own.wait()


class Rows:
    def __init__(self, source, w_ref, sems, own_sem):
        self.source, self.w_ref, self.sems = source, w_ref, sems
        self.docs, self.me = lax.axis_index("docs"), lax.axis_index("seq")
        self.over = (1 - self.docs, self.me)
        self.own = pltpu.make_async_copy(source, w_ref.at[self.docs, self.me // 4], own_sem)
        self.hops, self.moved = [], []

    def begin(self):
        target = self.w_ref.at[self.docs, self.me // 4]
        for rz in range(1, 4):
            peer = (self.docs, flip(self.me, 4 * rz))
            self.hops.append(remote(self.source, target, self.sems, rz, peer))
            self.hops[-1].start()
        self.own.start()
        self.moved.append(remote(self.source, target, self.sems, 4, self.over))
        self.moved[0].start()

    def forward(self, rz):
        self.hops[rz - 1].wait_recv()
        slot = self.w_ref.at[self.docs, flip(self.me, 4 * rz) // 4]
        self.moved.append(remote(slot, slot, self.sems, 4 + rz, self.over))
        self.moved[-1].start()

    def finish(self):
        for copy in self.moved:
            copy.wait_recv()
        for copy in self.hops + self.moved:
            copy.wait_send()
        self.own.wait()


class Tiles:
    def __init__(self, source, w_ref, sems, own_sem):
        self.source, self.w_ref, self.sems = source, w_ref, sems
        self.docs, self.me = lax.axis_index("docs"), lax.axis_index("seq")
        self.place = (self.docs, self.me // 4, (self.me // 2) % 2, self.me % 2)
        self.own = pltpu.make_async_copy(source, w_ref.at[self.place], own_sem)
        self.sent, self.last = [], []

    def send(self, part, n, peer):
        self.last.append(remote(part, part, self.sems, n, peer))
        self.last[-1].start()
        self.sent.append(self.last[-1])

    def arrived(self):
        for copy in self.last:
            copy.wait_recv()
        self.last = []

    def begin(self):
        self.own.start()
        self.own.wait()
        self.send(self.w_ref.at[self.place], 0, (self.docs, flip(self.me, 1)))

    def along_x(self):
        self.arrived()
        self.send(self.w_ref.at[self.place[:3]], 1, (self.docs, flip(self.me, 2)))

    def along_z(self):
        self.arrived()
        for rz in range(1, 4):
            self.send(self.w_ref.at[self.place[:2]], 1 + rz, (self.docs, flip(self.me, 4 * rz)))

    def along_docs(self):
        self.arrived()
        self.send(self.w_ref.at[self.docs], 5, (1 - self.docs, self.me))

    def finish(self):
        self.arrived()
        for copy in self.sent:
            copy.wait_send()


def open_kernel(*refs):
    low_ref, gain_ref, wq_ref, wq_1_ref, up_ref, down_ref, up_1_ref, down_1_ref = refs[:8]
    x_ref, gains_ref, w_ref, w_1_ref, wu_ref, wd_ref, wu_1_ref, wd_1_ref = refs[8:16]
    sems, gain_sems, own_sems, w_sems, w_1_sems, up_sems, down_sems, up_1_sems, down_1_sems = refs[16:]
    docs, me = lax.axis_index("docs"), lax.axis_index("seq")
    greet(spread_peers() + [(1 - docs, me)])
    gains = Tiles(gain_ref, gains_ref, gain_sems, own_sems.at[7])
    qkv = Rows(wq_ref, w_ref, w_sems, own_sems.at[0])
    qkv_1 = Rows(wq_1_ref, w_1_ref, w_1_sems, own_sems.at[1])
    whole = [
        Slabs(up_ref, wu_ref, up_sems, own_sems.at[2]),
        Slabs(down_ref, wd_ref, down_sems, own_sems.at[3], docs_first=True),
    ]
    lines = [
        Slabs(up_1_ref, wu_1_ref, up_1_sems, own_sems.at[4], z_only=True),
        Slabs(down_1_ref, wd_1_ref, down_1_sems, own_sems.at[5], z_only=True),
    ]
    rows = Spread(low_ref, x_ref, sems, own_sems.at[6])

    def every(parts, step, *arguments):
        for part in parts:
            getattr(part, step)(*arguments)

    every(whole, "begin")
    gains.begin()
    every(whole, "from_line", 1)
    every(whole, "from_first", 0)
    gains.along_x()
    rows.begin()
    qkv.begin()
    every(whole, "from_line", 2)
    every(whole, "from_first", 1)
    gains.along_z()
    every(whole, "from_line", 3)
    every(whole, "from_first", 2)
    every([rows], "forward", 1)
    every([rows], "forward", 2)
    every([rows], "forward", 3)
    gains.along_docs()
    qkv_1.begin()
    every(lines, "begin")
    every(whole, "from_first", 3)
    every(whole, "from_second", 0)
    for rz in range(1, 4):
        qkv.forward(rz)
    rows.from_beside()
    for rz in range(1, 4):
        qkv_1.forward(rz)
    for distance in range(1, 4):
        every(lines, "from_line", distance)
        every(whole, "from_second", distance)
    every([rows, gains, qkv, qkv_1] + whole + lines, "finish")


def open_layer(low, gain, wq, first, second, number):
    def whole(part):
        return jax.ShapeDtypeStruct((2, 2, PLANES, 2) + part.shape, BF16)

    def line(part):
        return jax.ShapeDtypeStruct((PLANES,) + part.shape, BF16)

    sems = pltpu.SemaphoreType.DMA
    return pl.pallas_call(
        open_kernel,
        out_shape=(
            jax.ShapeDtypeStruct((16, 64, low.shape[-1]), BF16),
            jax.ShapeDtypeStruct((2, PLANES, 2, 2) + gain.shape, BF16),
            jax.ShapeDtypeStruct((2, PLANES) + wq[0].shape, BF16),
            jax.ShapeDtypeStruct((2, PLANES) + wq[1].shape, BF16),
            whole(first[0]),
            whole(first[1]),
            line(second[0]),
            line(second[1]),
        ),
        in_specs=[hbm() for _ in range(8)],
        out_specs=tuple(hbm() for _ in range(8)),
        scratch_shapes=[
            sems((2, 16)),
            sems((2, 6)),
            sems((8,)),
            sems((2, 8)),
            sems((2, 8)),
            sems((2, 36)),
            sems((2, 36)),
            sems((2, 8)),
            sems((2, 8)),
        ],
        compiler_params=comm_params(number),
        name="open_layer",
    )(low, gain, *wq, *first, *second)


def exchange_kernel(x_ref, o_ref, sems, own_sem):
    docs, me = lax.axis_index("docs"), lax.axis_index("seq")
    order = list(range(15, 0, -1))
    greet([(docs, flip(me, bits)) for bits in order])
    copies = []
    for bits in order:
        peer = flip(me, bits)
        copies.append(remote(x_ref.at[peer], o_ref.at[me], sems, bits, (docs, peer)))
        copies[-1].start()
    own = pltpu.make_async_copy(x_ref.at[me], o_ref.at[me], own_sem)
    own.start()
    for copy in copies:
        copy.wait_recv()
    for copy in copies:
        copy.wait_send()
    own.wait()


def exchange(x, number):
    return pl.pallas_call(
        exchange_kernel,
        out_shape=jax.ShapeDtypeStruct(x.shape, x.dtype),
        in_specs=[hbm()],
        out_specs=hbm(),
        scratch_shapes=[pltpu.SemaphoreType.DMA((2, 16)), pltpu.SemaphoreType.DMA],
        compiler_params=comm_params(number),
        name="exchange",
    )(x)


class Collect:
    def __init__(self, keep_ref, send_ref, land, got_core, got_x, sum_x, near, sums, sems):
        self.keep_ref, self.send_ref, self.land, self.got_core = keep_ref, send_ref, land, got_core
        self.got_x, self.sum_x, self.near, self.sums, self.sems = got_x, sum_x, near, sums, sems
        self.docs, self.me = lax.axis_index("docs"), lax.axis_index("seq")
        self.order = (3, 2, 1, 0)
        self.first, self.across, self.hops = {}, {}, []

    def begin(self):
        mate = (self.docs, flip(self.me, 1))
        for rz in self.order:
            for n in (2 * rz + 1, 2 * rz):
                self.first[n] = remote(
                    self.send_ref.at[n], self.got_core.at[n], self.sems, n, mate
                )
                self.first[n].start()

    def along_x(self):
        beside = (self.docs, flip(self.me, 2))
        for rz in self.order:
            n = 2 * rz + 1
            self.first[n].wait_recv()
            self.sum_x[rz] = add_low(self.keep_ref[n], self.got_core[n])
            self.across[rz] = remote(
                self.sum_x.at[rz], self.got_x.at[rz], self.sems, 8 + rz, beside
            )
            self.across[rz].start()
            n = 2 * rz
            self.first[n].wait_recv()
            self.near[rz] = add_full(self.keep_ref[n], self.got_core[n])

    def along_z(self):
        plane = self.me // 4
        for rz in self.order:
            self.across[rz].wait_recv()
            total = add_low(self.near[rz], self.got_x[rz])
            if rz == 0:
                self.land[plane] = total
            else:
                self.sums[rz] = total
                peer = (self.docs, flip(self.me, 4 * rz))
                copy = remote(self.sums.at[rz], self.land.at[plane], self.sems, 12 + rz, peer)
                copy.start()
                self.hops.append(copy)

    def finish(self):
        for copy in self.hops:
            copy.wait_recv()
        for copy in list(self.first.values()) + list(self.across.values()) + self.hops:
            copy.wait_send()


def collect_scratch(width):
    return [
        pltpu.VMEM((4, 64, width), BF16),
        pltpu.VMEM((8, 64, width), BF16),
        pltpu.VMEM((4, 64, width), BF16),
        pltpu.VMEM((4, 64, width), BF16),
        pltpu.VMEM((4, 64, width), F32),
        pltpu.VMEM((4, 64, width), BF16),
        pltpu.SemaphoreType.DMA((2, 16)),
    ]


def collect_kernel(keep_ref, send_ref, out_ref, *scratch):
    greet(spread_peers())
    rows = Collect(keep_ref, send_ref, *scratch)
    rows.begin()
    rows.along_x()
    rows.along_z()
    rows.finish()
    out_ref[...] = scratch[0][...]


def collect(keep, send, number):
    width = keep.shape[-1]
    return pl.pallas_call(
        collect_kernel,
        out_shape=jax.ShapeDtypeStruct((PLANES, 64, width), BF16),
        in_specs=[vmem(), vmem()],
        out_specs=vmem(),
        scratch_shapes=collect_scratch(width),
        compiler_params=comm_params(number),
        name="collect",
    )(keep, send)


class Line:
    PLACE = (0, 2, 1, 3)

    def __init__(self, own, from_left, from_right, sems):
        self.own, self.landing, self.sems = own, (from_left, from_right), sems
        self.docs, self.me = lax.axis_index("docs"), lax.axis_index("seq")
        self.plane = self.me // 4

    def copy(self, place, target, step):
        side = 0 if step > 0 else 1
        return pltpu.make_async_remote_copy(
            self.own.at[place],
            self.landing[side].at[target],
            self.sems.at[0, side, target],
            self.sems.at[1, side, target],
            device_id=(self.docs, self.me + 4 * step),
            device_id_type=MESH,
        )

    def at(self, plane, act):
        pl.when(self.plane == plane)(act)

    def begin(self, rz):
        for plane, step in ((0, 1), (3, -1)):
            self.at(plane, self.copy(self.PLACE[rz], plane ^ rz, step).start)

    def forward(self, target, step):
        for plane in range(1, 3):
            if (target - plane) * step > 0:
                place, side = self.PLACE[plane ^ target], 0 if step > 0 else 1

                def act(place=place, side=side):
                    copy = self.copy(place, target, step)
                    copy.wait_recv()
                    self.own[place] = add_low(self.own[place], self.landing[side][target])
                    copy.start()

                self.at(plane, act)

    def total(self, out_ref, rows):
        for plane in range(PLANES):

            def act(plane=plane):
                total = self.own[0, rows].astype(F32)
                for side, step in ((0, 1), (1, -1)):
                    if 0 <= plane - step < PLANES:
                        total = total + self.landing[side][plane, rows].astype(F32)
                out_ref[...] = total

            self.at(plane, act)

    def arrived(self):
        for plane in range(PLANES):

            def act(plane=plane):
                for step in (1, -1):
                    if 0 <= plane - step < PLANES:
                        self.copy(0, plane, step).wait_recv()

            self.at(plane, act)

    def finish(self):
        for plane in range(PLANES):

            def act(plane=plane):
                for target in range(PLANES):
                    step = 1 if target > plane else -1
                    if target != plane:
                        self.copy(self.PLACE[plane ^ target], target, step).wait_send()

            self.at(plane, act)


class Everywhere:
    def __init__(self, total, got, sems):
        self.total, self.got, self.sems = total, got, sems
        docs, me = lax.axis_index("docs"), lax.axis_index("seq")
        self.peers = [(docs, flip(me, bits)) for bits in (1, 2, 4, 8)] + [(1 - docs, me)]
        self.copies = []

    def step(self):
        n = len(self.copies)
        if n > 0:
            self.copies[-1].wait_recv()
            self.total[n] = self.total[n - 1] + self.got[n - 1]
        if n < len(self.peers):
            copy = remote(self.total.at[n], self.got.at[n], self.sems, n, self.peers[n])
            copy.start()
            self.copies.append(copy)

    def finish(self):
        for copy in self.copies:
            copy.wait_send()


def close_kernel(
    keep_ref,
    send_ref,
    a_ref,
    a_got_ref,
    b_ref,
    b_got_ref,
    q0_ref,
    q1_ref,
    gain_ref,
    rows_ref,
    rest_ref,
    qkv_ref,
    gain_out_ref,
    *scratch,
):
    collect_scr, scratch = scratch[:7], scratch[7:]
    far_a, got_a, far_b, got_b, own, left, right, rest_sems, line_sems = scratch[:9]
    got_q, q_own, q_left, q_right, q_sems, q_line_sems, q_sum, route_sems = scratch[9:17]
    gain_sum, gain_got, gain_sems = scratch[17:]
    docs, me = lax.axis_index("docs"), lax.axis_index("seq")
    beside, over = (docs, flip(me, 2)), (1 - docs, me)
    greet([(docs, flip(me, bits)) for bits in range(15, 0, -1)] + [over])
    gains = Everywhere(gain_sum, gain_got, gain_sems)
    gain_sum[0] = gain_ref[...]
    gains.step()
    places = (3, 1, 2, 0)
    sent = []
    for place in places:
        far_a[place] = add_low(a_ref[4 + place], a_got_ref[4 + place])
        sent.append(remote(far_a.at[place], got_a.at[place], rest_sems, place, beside))
        sent[-1].start()
        far_b[place] = add_low(b_ref[1, place], b_got_ref[1, place])
        sent.append(remote(far_b.at[place], got_b.at[place], rest_sems, 4 + place, over))
        sent[-1].start()
    crossed = []
    for n, ref in enumerate((q0_ref, q1_ref)):
        crossed.append(remote(ref.at[1], got_q.at[n], q_sems, n, over))
        crossed[-1].start()
    rows = Collect(keep_ref, send_ref, *collect_scr)
    rows.begin()
    gains.step()
    line = Line(own, left, right, line_sems)
    for n, place in enumerate(places):
        sent[2 * n].wait_recv()
        near = add_full(a_ref[place], a_got_ref[place]) + got_a[place].astype(F32)
        own[place, :CUT] = near.astype(BF16)
        sent[2 * n + 1].wait_recv()
        near = add_full(b_ref[0, place], b_got_ref[0, place]) + got_b[place].astype(F32)
        own[place, CUT:] = near.astype(BF16)
        if place > 0:
            line.begin(Line.PLACE[place])
        if n == 0:
            rows.along_x()
            gains.step()
    line.forward(3, 1)
    line.forward(0, -1)
    gains.step()
    line.forward(2, 1)
    line.forward(1, -1)
    gains.step()
    q_line = Line(q_own, q_left, q_right, q_line_sems)
    for n, ref in enumerate((q0_ref, q1_ref)):
        crossed[n].wait_recv()
        for place in range(PLANES):
            q_own[place, 144 * n : 144 * n + 144] = add_low(ref[0, place], got_q[n, place])
    for place in places[:3]:
        q_line.begin(Line.PLACE[place])
    rows.along_z()
    q_line.forward(3, 1)
    q_line.forward(0, -1)
    q_line.forward(2, 1)
    q_line.forward(1, -1)
    line.arrived()
    line.total(rest_ref, slice(0, 432))
    q_line.arrived()
    for layer in range(LAYERS):
        for t in range(3):
            first = 144 * layer + 48 * t
            q_line.total(q_sum.at[t, layer], slice(first, first + 48))
    plane, group = me // 4, me % 4

    def routed(t, act_here, act_there):
        local = 3 * plane + t
        number = 16 * (local // 4) + 4 * group + local % 4
        owner, slot = number // 3, number % 3
        here = pltpu.make_async_copy(q_sum.at[t], qkv_ref.at[slot], route_sems.at[2, slot])
        there = pltpu.make_async_remote_copy(
            q_sum.at[t],
            qkv_ref.at[slot],
            route_sems.at[0, t],
            route_sems.at[1, slot],
            device_id=(docs, owner),
            device_id_type=MESH,
        )
        pl.when(owner == me)(lambda: act_here(here))
        pl.when(owner != me)(lambda: act_there(there))

    for t in range(3):
        routed(t, lambda copy: copy.start(), lambda copy: copy.start())
    gains.step()
    gain_out_ref[...] = gain_sum[5]
    rows.finish()
    rows_ref[...] = collect_scr[0][...]
    for t in range(3):
        routed(t, lambda copy: copy.wait(), lambda copy: copy.wait_send())
    for slot in range(3):
        number = 3 * me + slot
        local = 4 * (number // 16) + number % 4
        source = 4 * (local // 3) + (number % 16) // 4

        def arrived(slot=slot):
            pltpu.make_async_copy(
                qkv_ref.at[slot], qkv_ref.at[slot], route_sems.at[1, slot]
            ).wait()

        pl.when(source != me)(arrived)
    for copy in sent + crossed:
        copy.wait_send()
    for part in (line, q_line, gains):
        part.finish()


def close(keep, send, first, second, grad_qkv, gain_grads, number):
    width = keep.shape[-1]
    low = 432 - CUT

    def line(rows):
        return [pltpu.VMEM((PLANES, rows, 384), BF16) for _ in range(3)]

    sems = pltpu.SemaphoreType.DMA
    return pl.pallas_call(
        close_kernel,
        out_shape=(
            jax.ShapeDtypeStruct((PLANES, 64, width), BF16),
            jax.ShapeDtypeStruct((432, 384), F32),
            jax.ShapeDtypeStruct((3, LAYERS, 48, 384), F32),
            jax.ShapeDtypeStruct((8, width), F32),
        ),
        in_specs=[vmem() for _ in range(9)],
        out_specs=(vmem(), vmem(), hbm(), vmem()),
        scratch_shapes=collect_scratch(width)
        + [
            pltpu.VMEM((PLANES, CUT, 384), BF16),
            pltpu.VMEM((PLANES, CUT, 384), BF16),
            pltpu.VMEM((PLANES, low, 384), BF16),
            pltpu.VMEM((PLANES, low, 384), BF16),
            *line(432),
            sems((2, 8)),
            sems((2, 2, 4)),
            pltpu.VMEM((LAYERS, PLANES, 144, 384), BF16),
            *line(144 * LAYERS),
            sems((2, 2)),
            sems((2, 2, 4)),
            pltpu.VMEM((3, LAYERS, 48, 384), F32),
            sems((3, 3)),
            pltpu.VMEM((6, 8, width), F32),
            pltpu.VMEM((5, 8, width), F32),
            sems((2, 5)),
        ],
        compiler_params=pltpu.CompilerParams(
            collective_id=number, has_side_effects=True, vmem_limit_bytes=48 * 2**20
        ),
        name="close",
    )(keep, send, *first, *second, *grad_qkv, gain_grads)


class Transfer:
    def __init__(self, steps):
        self.steps = steps
        self.result = None
        self.pending = next(steps)

    def go_on(self, arrived):
        try:
            self.pending = self.steps.send(arrived)
        except StopIteration as end:
            self.pending = ()
            self.result = end.value


def beside(result, *transfers):
    live = [transfer for transfer in transfers if transfer.result is None]
    result, arrived = lax.optimization_barrier((result, [transfer.pending for transfer in live]))
    for transfer, values in zip(live, arrived):
        transfer.go_on(values)
    return result


def in_core_order(core, own, other):
    return jnp.where(
        core == 0,
        jnp.concatenate([own, other], axis=0),
        jnp.concatenate([other, own], axis=0),
    )


def pick(stack, index):
    return lax.dynamic_index_in_dim(stack, index, 0, keepdims=False)


def pack_qkv(shards, me, core):
    rows = shards.shape[1]
    parts = shards.reshape(LAYERS, rows, 3, GROUPS, GROUP_HEADS, HEAD)
    pairs = jnp.transpose(parts[:, :, 1:], (3, 0, 1, 4, 2, 5)).reshape(GROUPS, LAYERS, rows, 384)
    query = jnp.transpose(parts[:, :, 0], (2, 0, 1, 3, 4)).reshape(GROUPS, LAYERS, rows, 192)
    packed = jnp.concatenate([pairs, query], axis=3)
    group = me & 3
    got = [pick(packed, group)] + [swap(pick(packed, group ^ r), r) for r in range(1, 4)]

    def in_order(own, other):
        return jnp.where(
            core == 0,
            jnp.concatenate([own, other], axis=1),
            jnp.concatenate([other, own], axis=1),
        )

    here, there = in_order(got[0], got[1]), in_order(got[2], got[3])
    both = jnp.where(
        (me >> 1) & 1 == 0,
        jnp.stack([here, there], axis=1),
        jnp.stack([there, here], axis=1),
    )
    return [both[layer] for layer in range(LAYERS)]


def pack_rest(out_weight, up_weight, down_weight, core):
    def mine(shard, side):
        half = shard.shape[2] // 2
        return lax.dynamic_slice_in_dim(shard, side * half, half, axis=2)

    def both(side):
        return jnp.concatenate([mine(up_weight, side), mine(out_weight, side)], axis=2)

    own, got = both(core), swap(both(1 - core), 1)
    rows = jnp.where(
        core == 0,
        jnp.concatenate([own, got], axis=1),
        jnp.concatenate([got, own], axis=1),
    )
    parts = []
    for layer in range(LAYERS):
        up, out = rows[layer, :, :1536], rows[layer, :, 1536:]
        down = [down_weight[layer, :48], down_weight[layer, 48:]]
        if layer == 0:
            parts.append((up, jnp.concatenate(down + [out], axis=1)))
        else:
            parts.append((jnp.concatenate([up, down[0], out], axis=1), down[1]))
    return parts


def gather_rest(first, second):
    first, second, got_first, got_second = yield (
        first,
        second,
        swap(first, 2),
        swap_docs(second),
    )
    first = jnp.concatenate([first, got_first], axis=0)
    second = jnp.concatenate([second, got_second], axis=0)
    first, second, got_first, got_second = yield (
        first,
        second,
        swap_docs(first),
        swap(second, 2),
    )
    first = jnp.concatenate([first, got_first], axis=0)
    second = jnp.concatenate([second, got_second], axis=0)
    return (yield (first, swap(first, 1), second, swap(second, 1)))


def add_low(first, second):
    return (first.astype(F32) + second.astype(F32)).astype(BF16)


def add_full(first, second):
    return first.astype(F32) + second.astype(F32)


def reduce_part(keep, send, mover, then):
    total = add_low(*(yield (keep, mover(send))))
    if total.shape[0] == 8:
        near, far = total[:4], total[4:]
    else:
        near, far = total[0], total[1]
    near, got = yield (near, then(far))
    pieces = [add_low(near[n], got[n]) for n in range(PLANES)]
    moved = [pieces[0]] + [swap(pieces[n], (0, 8, 4, 12)[n]) for n in range(1, PLANES)]
    parts = yield moved
    total = parts[0].astype(F32)
    for part in parts[1:]:
        total = total + part.astype(F32)
    return total


def swap_x(value):
    return swap(value, 2)


def split_rest(total):
    down = total[240:].reshape(4, 48, 384)
    return (
        total[192:240].T,
        total[:192].T,
        jnp.transpose(down, (0, 2, 1)).reshape(1536, 48),
    )


def local_two_by_sixteen(
    tokens,
    qkv_weight,
    out_weight,
    up_weight,
    down_weight,
    norm_gains,
    doc_lengths,
    global_ids,
    random_ids,
    cotangent,
):
    docs_dev, block, width = tokens.shape
    me = lax.axis_index("seq").astype(jnp.int32)
    docs = lax.axis_index("docs").astype(jnp.int32)
    plane, core = me >> 2, me & 1
    chip = docs * 8 + (me >> 1)
    info = jnp.concatenate(
        [
            jnp.stack(
                [me, chip, pick(doc_lengths, plane), plane, docs, core, jnp.zeros_like(me), chip]
            ),
            doc_lengths,
        ]
    )
    features = key_features(
        lax.dynamic_index_in_dim(random_ids, plane, 1, keepdims=False),
        pick(global_ids, plane),
        pick(doc_lengths, plane),
    )

    wq = pack_qkv(qkv_weight, me, core)
    parts = pack_rest(out_weight, up_weight, down_weight, core)
    own_gains = jnp.pad(norm_gains.reshape(1, -1), ((0, 15), (0, 128 - norm_gains.size)))
    opened = open_layer(tokens, own_gains, wq, *parts, 0)
    x, up, down = opened[0], opened[4], opened[5]
    gain = opened[1].reshape(32, 16, 128)[:, 0, : norm_gains.size].reshape((32,) + norm_gains.shape)
    gain = jnp.transpose(gain, (1, 2, 0, 3)).reshape(LAYERS, 2, width).astype(F32)
    weights = [weight.reshape(CHIPS, 48, 576) for weight in opened[2:4]]
    rest_0 = (up.reshape(2, CHIPS, 48, -1), down.reshape(2, CHIPS, 48, -1))
    rest_1 = Transfer(gather_rest(*opened[6:]))
    qkv, o = beside(attend(features, x, weights[0]), rest_1)
    held = [(x, qkv)]
    o = exchange(o, 1)
    fed = feed(info, o, tokens, gain[0], rest_0)
    held[0] += (fed[:4],)
    x = spread(fed[5], 2)
    qkv, o = beside(attend(features, x, weights[1]), rest_1)
    o = beside(exchange(o, 3), rest_1)
    fed_1 = feed(info, o, fed[4], gain[1], rest_1.result)
    held.append((x, qkv, fed_1[:4]))
    base, grad_o, gain_1, *sums = feed_back(
        info, cotangent, None, gain[1], held[1][2], rest_1.result, 4
    )
    first_1 = Transfer(reduce_part(sums[0], sums[1], swap_docs, swap_x))
    grad_o = exchange(grad_o, 5)
    grad_o, sums = lax.optimization_barrier((grad_o, sums[2:]))
    second_1 = Transfer(reduce_part(sums[0], sums[1], swap_x, swap_docs))
    keep, send, qkv_1 = beside(
        attend_back(info, features, held[1][1], grad_o, held[1][0], weights[1]), second_1
    )
    extra = beside(collect(keep, send, 6), first_1, second_1)
    base, grad_o, gain_0, *sums = beside(
        feed_back(info, base, extra, gain[0], held[0][2], rest_0, 7), second_1
    )
    first = (sums[0], swap_docs(sums[1]))
    grad_o = beside(exchange(grad_o, 8), first_1)
    grad_o, sums = lax.optimization_barrier((grad_o, sums[2:]))
    second = (sums[0], swap_x(sums[1]))
    keep, send, qkv_0 = beside(
        attend_back(info, features, held[0][1], grad_o, held[0][0], weights[0]), first_1
    )
    gain_grads = jnp.concatenate([gain_0, gain_1, jnp.zeros((4, width), F32)], axis=0)
    extra, rest_grads, qkv_grads, gain_grads = close(
        keep, send, first, second, (qkv_0, qkv_1), gain_grads, 9
    )
    grad_tokens = base.reshape(docs_dev, block, width) + extra.astype(F32)
    share = width // 32
    gain_grads = lax.dynamic_slice_in_dim(gain_grads, (docs * 16 + me) * share, share, axis=1)
    rest = [
        split_rest(rest_grads),
        split_rest(jnp.concatenate([first_1.result, second_1.result], axis=0)),
    ]
    return (
        fed_1[4].astype(BF16).reshape(docs_dev, block, width),
        grad_tokens,
        jnp.transpose(qkv_grads, (1, 3, 0, 2)).reshape(LAYERS, 384, 144),
        *(jnp.stack(pair) for pair in zip(*rest)),
        gain_grads[:4].reshape(LAYERS, 2, share),
    )


def solution(mesh):
    def local(*args):
        docs_dev, _, width = args[0].shape
        if fits(mesh, docs_dev, width // HEAD):
            return local_two_by_sixteen(*args)
        return local_any_mesh(*args)

    return jax.shard_map(
        local,
        mesh=mesh,
        in_specs=(
            P("docs", "seq", None),
            P(None, ("docs", "seq"), None),
            P(None, ("docs", "seq"), None),
            P(None, ("docs", "seq"), None),
            P(None, ("docs", "seq"), None),
            P(None, None, ("docs", "seq")),
            P("docs"),
            P("docs", None),
            P(None, "docs", None),
            P("docs", "seq", None),
        ),
        out_specs=(
            P("docs", "seq", None),
            P("docs", "seq", None),
            P(None, "docs", "seq"),
            P(None, "docs", "seq"),
            P(None, "docs", "seq"),
            P(None, "docs", "seq"),
            P(None, None, ("docs", "seq")),
        ),
        check_vma=False,
    )
```

```python
import functools
import types

import jax
import jax.numpy as jnp
from jax import lax
from jax.experimental import pallas as pl
from jax.experimental.pallas import tpu as pltpu
from jax.sharding import PartitionSpec as P

HEAD = 64
RAND = 3
GLOB = 2
LAYERS = 2


NEGATIVE = -1e30
EPSILON = 1e-05


def with_halo(cells, sides, width):
    for axis, dim in sides:
        count = lax.axis_size(axis)
        head = lax.slice_in_dim(cells, 0, width, axis=dim)
        tail = lax.slice_in_dim(cells, cells.shape[dim] - width, cells.shape[dim], axis=dim)
        cells = jnp.concatenate(
            [
                lax.ppermute(tail, axis, [(i, (i + 1) % count) for i in range(count)]),
                cells,
                lax.ppermute(head, axis, [((i + 1) % count, i) for i in range(count)]),
            ],
            axis=dim,
        )
    return cells


def combined_all(value, axis, join):
    pieces = jax.tree.map(lambda part: lax.all_gather(part, axis), value)
    head = jax.tree.map(lambda part: part[0], pieces)
    tail = jax.tree.map(lambda part: part[1:], pieces)
    so_far, _ = lax.scan(lambda so_far, piece: (join(so_far, piece), None), head, tail)
    return so_far


def norm_rows(values, gain):
    centre = values - jnp.mean(values, axis=-1, keepdims=True)
    spread = jnp.mean(centre * centre, axis=-1, keepdims=True)
    return centre * lax.rsqrt(spread + EPSILON) * gain


def gelu_tanh(values):
    return jax.nn.gelu(values, approximate=True)


def earlier_equal(values):
    length = values.shape[-1]
    order = jnp.arange(length, dtype=jnp.int32)
    before = order[None, :] < order[:, None]
    same = values[..., :, None] == values[..., None, :]
    return jnp.sum(jnp.logical_and(same, before), axis=-1)


def merge_stats(first, second):
    highest = jnp.maximum(first[0], second[0])
    return (
        highest,
        first[1] * jnp.exp(first[0] - highest) + second[1] * jnp.exp(second[0] - highest),
    )


def sparse_probs(query, key_part, key_inside, scale):
    scores = (
        jnp.einsum("kbhd,kjhd->khbj", query, key_part, preferred_element_type=jnp.float32) * scale
    )
    scores = jnp.where(key_inside[:, None, None, :], scores, NEGATIVE)
    expo = jnp.exp(scores - jnp.max(scores, axis=-1, keepdims=True))
    return expo / jnp.sum(expo, axis=-1, keepdims=True)


def global_scores(global_query, local_keys, inside, scale):
    scores = (
        jnp.einsum(
            "ksbhd,kjhd->kshbj", global_query, local_keys, preferred_element_type=jnp.float32
        )
        * scale
    )
    return jnp.where(inside[:, None, None, None, :], scores, NEGATIVE)


def local_any_mesh(
    tokens,
    qkv_weight,
    out_weight,
    up_weight,
    down_weight,
    norm_gains,
    doc_lengths,
    global_ids,
    random_ids,
    cotangent,
):
    nseq = lax.axis_size("seq")
    device = lax.axis_index("seq")
    docs_dev, block, width = tokens.shape
    count = docs_dev * block
    heads = width // HEAD
    scale = HEAD ** (-0.5)
    capacity = max(2, (docs_dev * RAND + nseq - 1) // nseq)
    global_capacity = (docs_dev * GLOB + nseq - 1) // nseq
    entries = docs_dev * RAND
    global_entries = docs_dev * GLOB
    offsets = jnp.arange(block, dtype=jnp.int32)
    inside = (device * block + offsets)[None, :] < doc_lengths[:, None]
    live_rows = inside.reshape(count, 1)
    wanted = random_ids.reshape(nseq, entries)
    wanted_rank = earlier_equal(wanted)
    slot_ids = jnp.arange(capacity, dtype=jnp.int32)
    hits = jnp.logical_and((wanted == device)[:, :, None], wanted_rank[:, :, None] == slot_ids)
    hits = jnp.any(hits.reshape(nseq, docs_dev, RAND, capacity), axis=2)
    hits = jnp.transpose(hits, (0, 2, 1))
    doc_ids = jnp.arange(docs_dev, dtype=jnp.int32)
    send_doc = jnp.sum(jnp.where(hits, doc_ids, 0), axis=2)
    send_live = jnp.any(hits, axis=2)
    owner_pick = hits.astype(jnp.float32)
    listed_here = lax.dynamic_index_in_dim(wanted, device, 0, keepdims=False)
    listed_rank = lax.dynamic_index_in_dim(wanted_rank, device, 0, keepdims=False)
    fetch_slot = listed_here * capacity + listed_rank
    global_block = global_ids.reshape(global_entries)
    global_rank = earlier_equal(global_block)
    global_slot = global_block * global_capacity + global_rank
    own_entry = global_block == device
    owned = jnp.logical_and(
        own_entry[:, None], global_rank[:, None] == jnp.arange(global_capacity, dtype=jnp.int32)
    )
    entry_doc = jnp.arange(global_entries, dtype=jnp.int32) // GLOB
    global_send_doc = jnp.sum(jnp.where(owned, entry_doc[:, None], 0), axis=0)
    global_send_live = jnp.any(owned, axis=0)
    own_flag = jnp.any(own_entry.reshape(docs_dev, GLOB), axis=1)
    own_slot = jnp.sum(jnp.where(own_entry, global_rank, 0).reshape(docs_dev, GLOB), axis=1)
    neighbours = jnp.stack([(device - 1) % nseq, device, (device + 1) % nseq])
    key_blocks = jnp.concatenate(
        [
            jnp.broadcast_to(neighbours[None, :], (docs_dev, 3)),
            listed_here.reshape(docs_dev, RAND),
            global_ids,
        ],
        axis=1,
    )
    span = key_blocks.shape[1] * block
    key_inside = (key_blocks[:, :, None] * block + offsets < doc_lengths[:, None, None]).reshape(
        docs_dev, span
    )
    keep_local = inside[:, None, None, None, :]
    hidden = tokens.reshape(count, width).astype(jnp.float32)
    held = []
    for layer in range(LAYERS):
        weights = (
            lax.all_gather(qkv_weight[layer], ("docs", "seq"), axis=0, tiled=True),
            lax.all_gather(out_weight[layer], ("docs", "seq"), axis=0, tiled=True),
            lax.all_gather(up_weight[layer], ("docs", "seq"), axis=0, tiled=True),
            lax.all_gather(down_weight[layer], ("docs", "seq"), axis=0, tiled=True),
            lax.all_gather(norm_gains[layer], ("docs", "seq"), axis=1, tiled=True),
        )
        weight_qkv, weight_out, weight_up, weight_down, gain_pair = weights
        gain_pair = gain_pair.astype(jnp.float32)
        lowered = hidden.astype(jnp.bfloat16)
        projected = (
            jnp.dot(lowered, weight_qkv, preferred_element_type=jnp.float32)
            .astype(jnp.bfloat16)
            .reshape(docs_dev, block, 3 * width)
        )
        pairs = projected[:, :, width:]
        window = with_halo(pairs, (("seq", 1),), block)
        outgoing = jnp.where(
            send_live[:, :, None, None],
            jnp.take(pairs, send_doc, axis=0),
            jnp.zeros((), jnp.bfloat16),
        )
        incoming = lax.all_to_all(outgoing, "seq", split_axis=0, concat_axis=0, tiled=True)
        fetched = jnp.take(
            incoming.reshape(nseq * capacity, block, 2 * width), fetch_slot, axis=0
        ).reshape(docs_dev, RAND * block, 2 * width)
        global_send = jnp.where(
            global_send_live[:, None, None],
            jnp.take(projected, global_send_doc, axis=0),
            jnp.zeros((), jnp.bfloat16),
        )
        gathered = lax.all_gather(global_send, "seq", axis=0, tiled=True)
        global_picked = jnp.take(gathered, global_slot, axis=0).reshape(
            docs_dev, GLOB, block, 3 * width
        )
        global_query = global_picked[..., :width].reshape(docs_dev, GLOB, block, heads, HEAD)
        listed_pairs = jnp.concatenate(
            [
                window,
                fetched,
                global_picked[..., width:].reshape(docs_dev, GLOB * block, 2 * width),
            ],
            axis=1,
        )
        query = projected[:, :, :width].reshape(docs_dev, block, heads, HEAD)
        key_part = listed_pairs[:, :, :width].reshape(docs_dev, span, heads, HEAD)
        value_part = listed_pairs[:, :, width:].reshape(docs_dev, span, heads, HEAD)
        probs = sparse_probs(query, key_part, key_inside, scale)
        mixed = jnp.einsum(
            "khbj,kjhd->kbhd",
            probs.astype(jnp.bfloat16),
            value_part,
            preferred_element_type=jnp.float32,
        )
        local_keys = projected[:, :, width : 2 * width].reshape(docs_dev, block, heads, HEAD)
        local_values = projected[:, :, 2 * width :].reshape(docs_dev, block, heads, HEAD)
        wide_scores = global_scores(global_query, local_keys, inside, scale)
        global_top = jnp.max(wide_scores, axis=-1)
        global_total = jnp.sum(
            jnp.where(keep_local, jnp.exp(wide_scores - global_top[..., None]), 0.0), axis=-1
        )
        global_top, global_total = combined_all((global_top, global_total), "seq", merge_stats)
        wide_probs = (
            jnp.where(keep_local, jnp.exp(wide_scores - global_top[..., None]), 0.0)
            / global_total[..., None]
        )
        wide_part = jnp.einsum(
            "kshbj,kjhd->ksbhd",
            wide_probs.astype(jnp.bfloat16),
            local_values,
            preferred_element_type=jnp.float32,
        )
        wide_buffer = (
            jnp.zeros((nseq * global_capacity, block, width), jnp.float32)
            .at[global_slot]
            .set(wide_part.reshape(global_entries, block, width))
        )
        wide_sum = lax.psum_scatter(wide_buffer, "seq", scatter_dimension=0, tiled=True)
        attended = jnp.where(
            own_flag[:, None, None],
            jnp.take(wide_sum, own_slot, axis=0),
            mixed.reshape(docs_dev, block, width),
        )
        attended = attended.reshape(count, width).astype(jnp.bfloat16)
        after_attn = hidden + jnp.dot(attended, weight_out, preferred_element_type=jnp.float32)
        normed = norm_rows(after_attn, gain_pair[0])
        normed_low = normed.astype(jnp.bfloat16)
        up_values = jnp.dot(normed_low, weight_up, preferred_element_type=jnp.float32)
        activated = gelu_tanh(up_values).astype(jnp.bfloat16)
        after_ffn = normed + jnp.dot(activated, weight_down, preferred_element_type=jnp.float32)
        held.append(
            (
                weights,
                lowered,
                projected,
                listed_pairs,
                global_query,
                global_top,
                global_total,
                attended,
                after_attn,
                normed_low,
                up_values,
                activated,
                after_ffn,
            )
        )
        hidden = jnp.where(live_rows, norm_rows(after_ffn, gain_pair[1]), 0.0)
    gradient = cotangent.reshape(count, width).astype(jnp.float32)
    layer_grads = []
    for layer in reversed(range(LAYERS)):
        (
            weights,
            lowered,
            projected,
            listed_pairs,
            global_query,
            global_top,
            global_total,
            attended,
            after_attn,
            normed_low,
            up_values,
            activated,
            after_ffn,
        ) = held[layer]
        weights = (
            lax.all_gather(qkv_weight[layer], ("docs", "seq"), axis=0, tiled=True),
            lax.all_gather(out_weight[layer], ("docs", "seq"), axis=0, tiled=True),
            lax.all_gather(up_weight[layer], ("docs", "seq"), axis=0, tiled=True),
            lax.all_gather(down_weight[layer], ("docs", "seq"), axis=0, tiled=True),
            lax.all_gather(norm_gains[layer], ("docs", "seq"), axis=1, tiled=True),
        )
        weight_qkv, weight_out, weight_up, weight_down, gain_pair = weights
        gain_pair = gain_pair.astype(jnp.float32)
        gradient = jnp.where(live_rows, gradient, 0.0)
        grad_ffn, grad_gain_out = jax.vjp(norm_rows, after_ffn, gain_pair[1])[1](gradient)
        grad_down_low = grad_ffn.astype(jnp.bfloat16)
        grad_down_layer = jnp.einsum(
            "rf,rd->fd", activated, grad_down_low, preferred_element_type=jnp.float32
        )
        grad_activated = jnp.einsum(
            "rd,fd->rf", grad_down_low, weight_down, preferred_element_type=jnp.float32
        )
        grad_up_low = jax.vjp(gelu_tanh, up_values)[1](grad_activated)[0].astype(jnp.bfloat16)
        grad_up_layer = jnp.einsum(
            "rd,rf->df", normed_low, grad_up_low, preferred_element_type=jnp.float32
        )
        grad_normed = grad_ffn + jnp.einsum(
            "rf,df->rd", grad_up_low, weight_up, preferred_element_type=jnp.float32
        )
        grad_attn, grad_gain_mid = jax.vjp(norm_rows, after_attn, gain_pair[0])[1](grad_normed)
        grad_attn_low = grad_attn.astype(jnp.bfloat16)
        grad_out_layer = jnp.einsum(
            "rd,re->de", attended, grad_attn_low, preferred_element_type=jnp.float32
        )
        grad_mixed = (
            jnp.einsum("re,de->rd", grad_attn_low, weight_out, preferred_element_type=jnp.float32)
            .astype(jnp.bfloat16)
            .reshape(docs_dev, block, width)
        )
        query = projected[:, :, :width].reshape(docs_dev, block, heads, HEAD)
        key_part = listed_pairs[:, :, :width].reshape(docs_dev, span, heads, HEAD)
        value_part = listed_pairs[:, :, width:].reshape(docs_dev, span, heads, HEAD)
        probs = sparse_probs(query, key_part, key_inside, scale)
        grad_sparse = jnp.where(
            own_flag[:, None, None], jnp.zeros((), jnp.bfloat16), grad_mixed
        ).reshape(docs_dev, block, heads, HEAD)
        grad_probs = jnp.einsum(
            "kbhd,kjhd->khbj", grad_sparse, value_part, preferred_element_type=jnp.float32
        )
        delta = jnp.sum(probs * grad_probs, axis=-1, keepdims=True)
        grad_scores = (probs * (grad_probs - delta)).astype(jnp.bfloat16)
        grad_query = (
            jnp.einsum("khbj,kjhd->kbhd", grad_scores, key_part, preferred_element_type=jnp.float32)
            * scale
        )
        grad_key_part = (
            jnp.einsum("khbj,kbhd->kjhd", grad_scores, query, preferred_element_type=jnp.float32)
            * scale
        )
        grad_value_part = jnp.einsum(
            "khbj,kbhd->kjhd",
            probs.astype(jnp.bfloat16),
            grad_sparse,
            preferred_element_type=jnp.float32,
        )
        grad_listed = jnp.concatenate(
            [
                grad_key_part.reshape(docs_dev, span, width),
                grad_value_part.reshape(docs_dev, span, width),
            ],
            axis=2,
        )
        wide_out = jnp.where(
            global_send_live[:, None, None],
            jnp.take(grad_mixed, global_send_doc, axis=0),
            jnp.zeros((), jnp.bfloat16),
        )
        wide_all = lax.all_gather(wide_out, "seq", axis=0, tiled=True)
        wide_grad = jnp.take(wide_all, global_slot, axis=0).reshape(
            docs_dev, GLOB, block, heads, HEAD
        )
        local_keys = projected[:, :, width : 2 * width].reshape(docs_dev, block, heads, HEAD)
        local_values = projected[:, :, 2 * width :].reshape(docs_dev, block, heads, HEAD)
        wide_scores = global_scores(global_query, local_keys, inside, scale)
        wide_probs = (
            jnp.where(keep_local, jnp.exp(wide_scores - global_top[..., None]), 0.0)
            / global_total[..., None]
        )
        wide_grad_probs = jnp.einsum(
            "ksbhd,kjhd->kshbj", wide_grad, local_values, preferred_element_type=jnp.float32
        )
        wide_delta = lax.psum(jnp.sum(wide_probs * wide_grad_probs, axis=-1), "seq")
        wide_grad_scores = (wide_probs * (wide_grad_probs - wide_delta[..., None])).astype(
            jnp.bfloat16
        )
        wide_grad_query = (
            jnp.einsum(
                "kshbj,kjhd->ksbhd",
                wide_grad_scores,
                local_keys,
                preferred_element_type=jnp.float32,
            )
            * scale
        )
        wide_grad_keys = (
            jnp.einsum(
                "kshbj,ksbhd->kjhd",
                wide_grad_scores,
                global_query,
                preferred_element_type=jnp.float32,
            )
            * scale
        )
        wide_grad_values = jnp.einsum(
            "kshbj,ksbhd->kjhd",
            wide_probs.astype(jnp.bfloat16),
            wide_grad,
            preferred_element_type=jnp.float32,
        )
        global_grads = jnp.concatenate(
            [
                wide_grad_query.reshape(global_entries, block, width),
                grad_listed[:, (3 + RAND) * block :, :].reshape(global_entries, block, 2 * width),
            ],
            axis=2,
        )
        global_buffer = (
            jnp.zeros((nseq * global_capacity, block, 3 * width), jnp.float32)
            .at[global_slot]
            .set(global_grads)
        )
        global_share = lax.psum_scatter(global_buffer, "seq", scatter_dimension=0, tiled=True)
        global_mine = jnp.where(
            own_flag[:, None, None], jnp.take(global_share, own_slot, axis=0), 0.0
        )
        grad_fetched = grad_listed[:, 3 * block : (3 + RAND) * block, :].reshape(
            entries, block, 2 * width
        )
        back_out = (
            jnp.zeros((nseq * capacity, block, 2 * width), jnp.float32)
            .at[fetch_slot]
            .set(grad_fetched)
            .reshape(nseq, capacity, block, 2 * width)
        )
        back_in = lax.all_to_all(back_out, "seq", split_axis=0, concat_axis=0, tiled=True)
        grad_random = jnp.einsum(
            "dck,dcbf->kbf", owner_pick, back_in, precision=lax.Precision.HIGHEST
        )
        grad_window = grad_listed[:, : 3 * block, :]
        edges = jnp.concatenate([grad_window[:, :block], grad_window[:, 2 * block :]], axis=1)
        beside_all = with_halo(edges, (("seq", 1),), block)
        grad_pairs = (
            grad_window[:, block : 2 * block]
            + beside_all[:, :block]
            + beside_all[:, 3 * block :]
            + grad_random
            + global_mine[:, :, width:]
        )
        grad_pairs = grad_pairs + jnp.concatenate(
            [
                wide_grad_keys.reshape(docs_dev, block, width),
                wide_grad_values.reshape(docs_dev, block, width),
            ],
            axis=2,
        )
        grad_queries = grad_query.reshape(docs_dev, block, width) + global_mine[:, :, :width]
        grad_projected = (
            jnp.concatenate([grad_queries, grad_pairs], axis=2)
            .reshape(count, 3 * width)
            .astype(jnp.bfloat16)
        )
        grad_qkv_layer = jnp.einsum(
            "rd,re->de", lowered, grad_projected, preferred_element_type=jnp.float32
        )
        gradient = grad_attn + jnp.einsum(
            "re,de->rd", grad_projected, weight_qkv, preferred_element_type=jnp.float32
        )
        group_shares = (
            lax.psum_scatter(grad_qkv_layer, "docs", scatter_dimension=0, tiled=True),
            lax.psum_scatter(grad_out_layer, "docs", scatter_dimension=0, tiled=True),
            lax.psum_scatter(grad_up_layer, "docs", scatter_dimension=0, tiled=True),
            lax.psum_scatter(grad_down_layer, "docs", scatter_dimension=0, tiled=True),
            lax.psum_scatter(
                jnp.stack([grad_gain_mid, grad_gain_out]), "docs", scatter_dimension=1, tiled=True
            ),
        )
        shares = (
            lax.psum_scatter(group_shares[0], "seq", scatter_dimension=1, tiled=True),
            lax.psum_scatter(group_shares[1], "seq", scatter_dimension=1, tiled=True),
            lax.psum_scatter(group_shares[2], "seq", scatter_dimension=1, tiled=True),
            lax.psum_scatter(group_shares[3], "seq", scatter_dimension=1, tiled=True),
            lax.psum_scatter(group_shares[4], "seq", scatter_dimension=1, tiled=True),
        )
        layer_grads.insert(0, shares)
    stacked = [
        jnp.stack([layer_grads[number][member] for number in range(LAYERS)]) for member in range(5)
    ]
    return (
        hidden.astype(jnp.bfloat16).reshape(docs_dev, block, width),
        gradient.reshape(docs_dev, block, width),
        stacked[0],
        stacked[1],
        stacked[2],
        stacked[3],
        stacked[4],
    )


PLANES = 4
GROUPS = 4
CHIPS = 16
GROUP_HEADS = 3
CUT = 240
MESH = pl.DeviceIdType.MESH
F32 = jnp.float32
BF16 = jnp.bfloat16


def fits(mesh, docs_dev, heads):
    return (
        mesh.shape["docs"] == 2
        and mesh.shape["seq"] == 16
        and docs_dev == PLANES
        and heads == GROUPS * GROUP_HEADS
    )


def swap(value, bits):
    return lax.ppermute(value, "seq", [(i, i ^ bits) for i in range(16)])


def swap_docs(value):
    return lax.ppermute(value, "docs", [(0, 1), (1, 0)])


def dot(left, right):
    return lax.dot_general(left, right, (((1,), (0,)), ((), ())), preferred_element_type=F32)


def dot_nt(left, right):
    return lax.dot_general(left, right, (((1,), (1,)), ((), ())), preferred_element_type=F32)


def dot_tn(left, right):
    return lax.dot_general(left, right, (((0,), (0,)), ((), ())), preferred_element_type=F32)


def vmem():
    return pl.BlockSpec(memory_space=pltpu.VMEM)


def smem():
    return pl.BlockSpec(memory_space=pltpu.SMEM)


def hbm():
    return pl.BlockSpec(memory_space=pltpu.HBM)


def params():
    return pltpu.CompilerParams(vmem_limit_bytes=56 * 2**20)


QUERIES = 1024
BACK_QUERIES = 512


def key_features(own_random, own_global, length):
    block = jnp.arange(16, dtype=jnp.int32)
    window = jnp.stack([(block + 15) % 16, block, (block + 1) % 16], axis=1)
    ids = jnp.concatenate([window, own_random, jnp.broadcast_to(own_global, (16, GLOB))], axis=1)
    count = jnp.sum((ids[:, :, None] == block).astype(F32), axis=1).T
    special = jnp.any(own_global[None, :] == block[:, None], axis=1)
    count = jnp.where(special[None, :], 1.0, count)
    extra = jnp.where(count > 0, jnp.log(jnp.maximum(count, 1.0)), NEGATIVE)
    inside = jnp.arange(1024, dtype=jnp.int32)[:, None] < length
    extra = jnp.where(inside, jnp.repeat(extra, 64, axis=0), NEGATIVE)
    high = extra.astype(BF16)
    low = jnp.where(extra > 0, extra - high.astype(F32), 0.0).astype(BF16)
    return jnp.concatenate([high, low, jnp.zeros((1024, 32), BF16)], axis=1)


def halves_beside(rows):
    return jnp.concatenate([rows[:32], rows[32:]], axis=1)


def halves_below(rows):
    return jnp.concatenate([rows[:, :192], rows[:, 192:]], axis=0)


def spread_heads(qkv, feature_ref, key_scr, query_scr):
    row = lax.broadcasted_iota(jnp.int32, (1024, 64), 0) // 64
    lane = lax.broadcasted_iota(jnp.int32, (1024, 64), 1)
    place = jnp.where(jnp.logical_and(lane < 32, lane % 16 == row), 1.0, 0.0).astype(BF16)
    for h in range(GROUP_HEADS):
        key_scr[h] = jnp.concatenate([qkv[:, 128 * h : 128 * h + 64], feature_ref[...]], axis=1)
        query = qkv[:, 384 + 64 * h : 448 + 64 * h] * jnp.asarray(HEAD**-0.5, BF16)
        query_scr[h] = jnp.concatenate([query, place], axis=1)


def expo_columns(scores):
    expo = jnp.exp(scores - jnp.max(scores, axis=0, keepdims=True))
    return expo, 1.0 / jnp.sum(expo, axis=0, keepdims=True)


def attend_kernel(feature_ref, x_ref, w_ref, qkv_ref, o_ref, key_scr, query_scr, value_scr, o_scr):
    weight = w_ref[...].reshape(-1, 576)
    qkv = dot(x_ref[...].reshape(1024, x_ref.shape[-1]), weight).astype(BF16)
    qkv_ref[...] = qkv
    spread_heads(qkv, feature_ref, key_scr, query_scr)
    for h in range(GROUP_HEADS):
        value_scr[h] = qkv[:, 128 * h + 64 : 128 * h + 128].T

    def chunk(n, _):
        at = pl.multiple_of(n * QUERIES, QUERIES)
        for h in range(GROUP_HEADS):
            scores = dot_nt(key_scr[h], query_scr[h, pl.ds(at, QUERIES), :])
            expo, rate = expo_columns(scores)
            o_scr[n, 64 * h : 64 * h + 64, :] = dot(value_scr[h], (expo * rate).astype(BF16))
        rows = o_scr[n].T.astype(BF16)
        for m in range(QUERIES // 64):
            o_ref[n * (QUERIES // 64) + m] = halves_beside(rows[64 * m : 64 * m + 64])
        return 0

    lax.fori_loop(0, 1024 // QUERIES, chunk, 0)


def attend(features, x, weight):
    return pl.pallas_call(
        attend_kernel,
        out_shape=(
            jax.ShapeDtypeStruct((1024, 576), BF16),
            jax.ShapeDtypeStruct((16, 32, 384), BF16),
        ),
        in_specs=[vmem(), vmem(), vmem()],
        out_specs=(vmem(), vmem()),
        scratch_shapes=[
            pltpu.VMEM((3, 1024, 128), BF16),
            pltpu.VMEM((3, 1024, 128), BF16),
            pltpu.VMEM((3, 64, 1024), BF16),
            pltpu.VMEM((1024 // QUERIES, 192, QUERIES), F32),
        ],
        compiler_params=params(),
        cost_estimate=pl.CostEstimate(
            flops=3 * 10**9, bytes_accessed=6 * 10**6, transcendentals=3 * 10**6
        ),
        name="attend",
    )(features, x, weight)


def load_ordered(w_refs, wu, wd, wo, sems):
    up_ref, down_ref = w_refs
    pltpu.make_async_copy(down_ref.at[:, :, :, pl.ds(1536, 384)], wo, sems.at[0]).start()
    pltpu.make_async_copy(up_ref, wu, sems.at[1]).start()
    for plane in range(2):
        for part in range(2):
            source = down_ref.at[plane, :, :, pl.ds(768 * part, 768)]
            pltpu.make_async_copy(source, wd.at[:, plane, part], sems.at[2]).start()


def load_slots(w_refs, wu, wd, wo, sems):
    ao_ref, ar_ref, bo_ref, br_ref = w_refs
    docs, me = lax.axis_index("docs"), lax.axis_index("seq")
    x, core = (me // 2) % 2, me % 2

    def one(j, _):
        over, z, across = j // 8, (j // 2) % 4, j % 2
        over, across = over + docs - 2 * over * docs, across + x - 2 * across * x
        at_a, at_b = 8 * over + 4 * across + z, 8 * across + 4 * over + z
        for plane, a, b in ((core, ao_ref, bo_ref), (1 - core, ar_ref, br_ref)):
            a, b = a.at[at_a], b.at[at_b]
            pltpu.make_async_copy(a.at[:, pl.ds(2304, 384)], wo.at[plane, j], sems.at[0]).start()
            pltpu.make_async_copy(a.at[:, pl.ds(0, 1536)], wu.at[plane, j], sems.at[1]).start()
            for part, source in enumerate((a.at[:, pl.ds(1536, 768)], b)):
                pltpu.make_async_copy(source, wd.at[j, plane, part], sems.at[2]).start()
        return 0

    lax.fori_loop(0, CHIPS, one, 0)


def load_weights(w_refs, *scratch):
    if len(w_refs) == 2:
        load_ordered(w_refs, *scratch)
    else:
        load_slots(w_refs, *scratch)


def wait_weight(scr, sem):
    pltpu.make_async_copy(scr, scr, sem).wait()


def inside_rows(info):
    row = lax.broadcasted_iota(jnp.int32, (256, 1), 0)
    length = jnp.zeros_like(row)
    for k in range(PLANES):
        length = jnp.where(row // 64 == k, info[8 + k], length)
    return info[0] * 64 + row % 64 < length


def norm_parts(values):
    centre = values - jnp.mean(values, axis=-1, keepdims=True)
    spread = jnp.mean(centre * centre, axis=-1, keepdims=True)
    rate = lax.rsqrt(spread + EPSILON)
    return centre * rate, rate


def norm_back(unit, rate, gain, grad):
    scaled = grad * gain
    inner = jnp.mean(scaled * unit, axis=-1, keepdims=True)
    outer = jnp.mean(scaled, axis=-1, keepdims=True)
    return rate * (scaled - outer - unit * inner), jnp.sum(grad * unit, axis=0, keepdims=True)


CURVE = 0.7978845608028654


def gelu_parts(values):
    square = values * values
    bend = jnp.tanh(CURVE * (values + 0.044715 * (square * values)))
    return 0.5 * values * (1.0 + bend), bend, square


def gelu_slope(values, bend, square):
    return 0.5 * (1.0 + bend) + 0.5 * values * (1.0 - bend * bend) * (
        CURVE * (1.0 + 3 * 0.044715 * square)
    )


def feed_kernel(pieces, info, o_ref, h_ref, gain_ref, *refs):
    w_refs, refs = refs[:pieces], refs[pieces:]
    mixed_ref, h1_ref, up_ref, h2_ref, next_ref, low_ref, wu, wd, wo, act_scr, sems = refs
    load_weights(w_refs, wu, wd, wo, sems)
    for k in range(PLANES):
        mixed_ref[64 * k : 64 * k + 64, :] = jnp.concatenate(
            [halves_below(o_ref[4 * k + g]) for g in range(GROUPS)], axis=1
        )
    mixed = mixed_ref[...]
    wait_weight(wo, sems.at[0])
    attended = jnp.concatenate([dot(mixed, wo[side].reshape(768, 384)) for side in range(2)], axis=1)
    h1 = h_ref[...].reshape(256, 768).astype(F32) + attended
    h1_ref[...] = h1
    x1 = norm_parts(h1)[0] * gain_ref[0:1, :]
    x1_low = x1.astype(BF16)
    wait_weight(wu, sems.at[1])
    for side in range(2):
        for part in range(3):
            at = 1536 * side + 512 * part
            up = dot(x1_low, wu[side, :, :, 512 * part : 512 * part + 512].reshape(768, 512))
            up_ref[:, at : at + 512] = up
            act_scr[:, at : at + 512] = gelu_parts(up)[0].astype(BF16)
    wait_weight(wd, sems.at[2])
    h2 = x1 + dot(act_scr[...], wd[...].reshape(3072, 768))
    h2_ref[...] = h2
    out = jnp.where(inside_rows(info), norm_parts(h2)[0] * gain_ref[1:2, :], 0.0)
    next_ref[...] = out
    low = out.astype(BF16)
    for k in range(PLANES):
        low_ref[k] = low[64 * k : 64 * k + 64]


WEIGHT_SCRATCH = [
    pltpu.VMEM((2, 16, 48, 1536), BF16),
    pltpu.VMEM((16, 2, 2, 48, 768), BF16),
    pltpu.VMEM((2, 16, 48, 384), BF16),
]


def feed(info, o, hidden, gains, weights):
    return pl.pallas_call(
        functools.partial(feed_kernel, len(weights)),
        out_shape=(
            jax.ShapeDtypeStruct((256, 768), BF16),
            jax.ShapeDtypeStruct((256, 768), F32),
            jax.ShapeDtypeStruct((256, 3072), F32),
            jax.ShapeDtypeStruct((256, 768), F32),
            jax.ShapeDtypeStruct((256, 768), F32),
            jax.ShapeDtypeStruct((4, 64, 768), BF16),
        ),
        in_specs=[smem(), vmem(), vmem(), vmem()] + [hbm() for _ in weights],
        out_specs=tuple(vmem() for _ in range(6)),
        scratch_shapes=WEIGHT_SCRATCH
        + [pltpu.VMEM((256, 3072), BF16), pltpu.SemaphoreType.DMA((3,))],
        compiler_params=params(),
        cost_estimate=pl.CostEstimate(
            flops=3 * 10**9, bytes_accessed=20 * 10**6, transcendentals=10**6
        ),
        name="feed",
    )(info, o, hidden, gains, *weights)


def feed_back_kernel(
    pieces,
    has_extra,
    info,
    base_ref,
    extra_ref,
    gain_ref,
    mixed_ref,
    h1_ref,
    up_ref,
    h2_ref,
    *refs,
):
    w_refs, refs = refs[:pieces], refs[pieces:]
    dh1_ref, do_ref, dgain_ref, *sum_refs, wu, wd, wo, gu, gd, go, got, sems, pair_sems, out_sems = refs
    load_weights(w_refs, wu, wd, wo, sems)
    docs, me = lax.axis_index("docs"), lax.axis_index("seq")
    mate = (docs, flip(me, 1))
    greet([mate])
    units = [(ry, place) for ry in range(2) for place in range(8)]

    def other_docs(ry):
        return docs if ry == 0 else 1 - docs

    def owner(place, rc):
        return flip(me, (place % 2) * 8 + (place // 2 % 2) * 4 + (place // 4) * 2 + rc)

    def exchange_units(scr, first, count, n):
        copies = []
        for ry, place in units:
            copies.append(
                pltpu.make_async_remote_copy(
                    scr.at[other_docs(ry), owner(place, 1)],
                    got.at[ry, place, pl.ds(first, count)],
                    pair_sems.at[0, n],
                    pair_sems.at[1, n],
                    device_id=mate,
                    device_id_type=MESH,
                )
            )
            copies[-1].start()
        return copies
    if has_extra:
        parts = [
            base_ref[64 * k : 64 * k + 64, :] + extra_ref[k].astype(F32)
            for k in range(PLANES)
        ]
        grad = jnp.concatenate(parts, axis=0)
    else:
        grad = base_ref[...].reshape(256, 768).astype(F32)
    grad = jnp.where(inside_rows(info), grad, 0.0)
    unit2, rate2 = norm_parts(h2_ref[...])
    dh2, dgain1 = norm_back(unit2, rate2, gain_ref[1:2, :], grad)
    dgain_ref[1:2, :] = dgain1
    df = dh2.astype(BF16)
    unit1, rate1 = norm_parts(h1_ref[...])
    x1_low = (unit1 * gain_ref[0:1, :]).astype(BF16)
    wait_weight(wd, sems.at[2])
    wait_weight(wu, sems.at[1])
    dx1 = dh2
    for part in range(8):
        at = 384 * part
        d_act = dot_nt(df, wd[2 * part : 2 * part + 2].reshape(384, 768))
        up = up_ref[:, at : at + 384]
        act, bend, square = gelu_parts(up)
        act = act.astype(BF16)
        dup = (gelu_slope(up, bend, square) * d_act).astype(BF16)
        side, start = part // 4, 384 * (part % 4)
        dx1 += dot_nt(dup, wu[side, :, :, start : start + 384].reshape(768, 384))
        gt_up = dot_tn(dup, x1_low).astype(BF16)
        for n in range(2):
            for half in range(2):
                gu[half, 2 * part + n] = gt_up[
                    192 * n : 192 * n + 192, 384 * half : 384 * half + 384
                ]
        gt_down = dot_tn(df, act).astype(BF16)
        row = 48 * (part % 4)
        for s in range(16):
            gd[part // 4, s, row : row + 48, :] = gt_down[48 * s : 48 * s + 48]
    exchange_units(gu, 0, 192, 0)
    exchange_units(gd, 240, 192, 1)
    dh1, dgain0 = norm_back(unit1, rate1, gain_ref[0:1, :], dx1)
    dgain_ref[0:1, :] = dgain0
    dh1_ref[...] = dh1
    da = dh1.astype(BF16)
    gt_out = dot_tn(da, mixed_ref[...]).astype(BF16)
    for s in range(16):
        for half in range(2):
            go[half, s] = gt_out[48 * s : 48 * s + 48, 384 * half : 384 * half + 384]
    exchange_units(go, 192, 48, 2)
    wait_weight(wo, sems.at[0])
    do = dot_nt(da[:, 0:384], wo[0].reshape(768, 384))
    do += dot_nt(da[:, 384:768], wo[1].reshape(768, 384))
    do = do.astype(BF16)
    for k in range(PLANES):
        for g in range(GROUPS):
            do_ref[4 * k + g] = halves_beside(do[64 * k : 64 * k + 64, 192 * g : 192 * g + 192])
    for n, (first, count) in enumerate(((0, 192), (240, 192), (192, 48))):
        part = got.at[:, :, pl.ds(first, count)]
        pltpu.make_async_copy(part, part, pair_sems.at[1, n]).wait()
    copies = []
    for ry, place in units:
        for scr, first, count in ((gu, 0, 192), (go, 192, 48), (gd, 240, 192)):
            span = slice(first, first + count)
            own = scr[other_docs(ry), owner(place, 0)].astype(F32)
            got[ry, place, span] = (own + got[ry, place, span].astype(F32)).astype(BF16)
        for ref, source in (
            (sum_refs[ry].at[place], got.at[ry, place, pl.ds(0, CUT)]),
            (sum_refs[2 + place // 4].at[ry, place % 4], got.at[ry, place, pl.ds(CUT, 432 - CUT)]),
        ):
            copies.append(pltpu.make_async_copy(source, ref, out_sems.at[len(copies)]))
            copies[-1].start()
    for n, scr in enumerate((gu, gd, go)):
        half = scr.at[:, pl.ds(0, 8)]
        pltpu.make_async_copy(half, half, pair_sems.at[0, n]).wait()
    for copy in copies:
        copy.wait()


def feed_back(info, base, extra, gains, saved, weights, number):
    mixed, h1, up, h2 = saved
    has_extra = extra is not None
    if not has_extra:
        extra = jnp.zeros((8, 128), BF16)
    return pl.pallas_call(
        functools.partial(feed_back_kernel, len(weights), has_extra),
        out_shape=(
            jax.ShapeDtypeStruct((256, 768), F32),
            jax.ShapeDtypeStruct((16, 32, 384), BF16),
            jax.ShapeDtypeStruct((2, 768), F32),
            jax.ShapeDtypeStruct((8, CUT, 384), BF16),
            jax.ShapeDtypeStruct((8, CUT, 384), BF16),
            jax.ShapeDtypeStruct((2, 4, 432 - CUT, 384), BF16),
            jax.ShapeDtypeStruct((2, 4, 432 - CUT, 384), BF16),
        ),
        in_specs=[smem()] + [vmem()] * 7 + [hbm() for _ in weights],
        out_specs=(vmem(), vmem(), vmem(), hbm(), hbm(), hbm(), hbm()),
        scratch_shapes=WEIGHT_SCRATCH
        + [
            pltpu.VMEM((2, 16, 192, 384), BF16),
            pltpu.VMEM((2, 16, 192, 384), BF16),
            pltpu.VMEM((2, 16, 48, 384), BF16),
            pltpu.VMEM((2, 8, 432, 384), BF16),
            pltpu.SemaphoreType.DMA((3,)),
            pltpu.SemaphoreType.DMA((2, 3)),
            pltpu.SemaphoreType.DMA((32,)),
        ],
        compiler_params=pltpu.CompilerParams(
            collective_id=number, has_side_effects=True, vmem_limit_bytes=56 * 2**20
        ),
        cost_estimate=pl.CostEstimate(
            flops=6 * 10**9, bytes_accessed=40 * 10**6, transcendentals=10**6
        ),
        name="feed_back",
    )(info, base, extra, gains, mixed, h1, up, h2, *weights)


def flip(index, bits):
    for bit in (1, 2, 4, 8):
        if bits & bit:
            index = index + bit - 2 * bit * ((index // bit) % 2)
    return index


def greet(peers):
    barrier = pltpu.get_barrier_semaphore()
    for peer in peers:
        pl.semaphore_signal(barrier, inc=1, device_id=peer, device_id_type=MESH)
    pl.semaphore_wait(barrier, len(peers))


def remote(source, target, sems, n, peer):
    return pltpu.make_async_remote_copy(
        source, target, sems.at[0, n], sems.at[1, n], device_id=peer, device_id_type=MESH
    )


def comm_params(number):
    return pltpu.CompilerParams(
        collective_id=number, has_side_effects=True, vmem_limit_bytes=16 * 2**20
    )


class Spread:
    def __init__(self, low_ref, x_ref, sems, own_sem):
        self.low_ref, self.x_ref, self.sems = low_ref, x_ref, sems
        self.docs, self.me = lax.axis_index("docs"), lax.axis_index("seq")
        self.own = pltpu.make_async_copy(low_ref.at[self.me // 4], x_ref.at[self.me], own_sem)
        self.hops, self.across, self.mates = [], [], []

    def send(self, source, slot, n, bits):
        peer = (self.docs, flip(self.me, bits))
        copy = remote(source, self.x_ref.at[slot], self.sems, n, peer)
        copy.start()
        return copy

    def begin(self):
        for rz in range(1, 4):
            source = self.low_ref.at[flip(self.me, 4 * rz) // 4]
            self.hops.append(self.send(source, self.me, rz, 4 * rz))
        self.own.start()
        source = self.low_ref.at[self.me // 4]
        self.across.append(self.send(source, self.me, 4, 2))
        self.mates.append(self.send(source, self.me, 8, 1))

    def forward(self, rz):
        self.hops[rz - 1].wait_recv()
        slot = flip(self.me, 4 * rz)
        self.across.append(self.send(self.x_ref.at[slot], slot, 4 + rz, 2))
        self.mates.append(self.send(self.x_ref.at[slot], slot, 8 + rz, 1))

    def from_beside(self):
        for rz in range(4):
            self.across[rz].wait_recv()
            slot = flip(flip(self.me, 4 * rz), 2)
            self.mates.append(self.send(self.x_ref.at[slot], slot, 12 + rz, 1))

    def finish(self):
        for copy in self.mates:
            copy.wait_recv()
        for copy in self.hops + self.across + self.mates:
            copy.wait_send()
        self.own.wait()


def spread_peers():
    docs, me = lax.axis_index("docs"), lax.axis_index("seq")
    return [(docs, flip(me, bits)) for bits in (4, 8, 12, 2, 1)]


def spread_kernel(low_ref, x_ref, sems, own_sem):
    greet(spread_peers())
    rows = Spread(low_ref, x_ref, sems, own_sem)
    rows.begin()
    for rz in range(1, 4):
        rows.forward(rz)
    rows.from_beside()
    rows.finish()


def spread(low, number):
    return pl.pallas_call(
        spread_kernel,
        out_shape=jax.ShapeDtypeStruct((16, 64, low.shape[-1]), BF16),
        in_specs=[hbm()],
        out_specs=hbm(),
        scratch_shapes=[pltpu.SemaphoreType.DMA((2, 16)), pltpu.SemaphoreType.DMA],
        compiler_params=comm_params(number),
        name="spread",
    )(low)


class Slabs:
    def __init__(self, source, w_ref, sems, own_sem, docs_first=False, z_only=False):
        self.source, self.w_ref, self.sems, self.z_only = source, w_ref, sems, z_only
        self.docs, self.me = lax.axis_index("docs"), lax.axis_index("seq")
        self.plane, self.x, self.core = self.me // 4, (self.me // 2) % 2, self.me % 2
        beside, over = (self.docs, flip(self.me, 2)), (1 - self.docs, self.me)
        self.peers = (over, beside) if docs_first else (beside, over)
        if docs_first:
            self.near = ((self.docs, self.x), (1 - self.docs, self.x))
            self.far = ((self.docs, 1 - self.x), (1 - self.docs, 1 - self.x))
        else:
            self.near = ((self.docs, self.x), (self.docs, 1 - self.x))
            self.far = ((1 - self.docs, self.x), (1 - self.docs, 1 - self.x))
        self.mate = (self.docs, flip(self.me, 1))
        self.own = pltpu.make_async_copy(source, self.slot(self.near[0], self.plane), own_sem)

    def slot(self, at, z):
        return self.w_ref.at[z] if self.z_only else self.w_ref.at[self.core, at[0], z, at[1]]

    def copy(self, at, z, own, send, recv, peer):
        slot = self.slot(at, z)
        return pltpu.make_async_remote_copy(
            self.source if own else slot,
            slot,
            self.sems.at[0, send],
            self.sems.at[1, recv],
            device_id=peer,
            device_id_type=MESH,
        )

    def line(self, z, own, step):
        peer = (self.docs, self.me + 4 * step)
        return self.copy(self.near[0], z, own, z + (0 if step > 0 else 4), z, peer)

    def first(self, z, own=False):
        return self.copy(self.near[0], z, own, 8 + z, 8 + z, self.peers[0])

    def second(self, z, n, own=False):
        return self.copy(self.near[n], z, own, 12 + 4 * n + z, 12 + 4 * n + z, self.peers[1])

    def core_copy(self, at, n, z, own=False):
        return self.copy(at, z, own, 20 + 4 * n + z, 20 + 4 * n + z, self.mate)

    def begin(self):
        self.own.start()
        for step in (1, -1):
            pl.when(self.has(self.plane + step))(self.line(self.plane, True, step).start)
        if not self.z_only:
            self.first(self.plane, True).start()
            self.core_copy(self.near[0], 0, self.plane, True).start()

    def has(self, z):
        return jnp.logical_and(z >= 0, z < PLANES)

    def each(self, distance, act):
        if distance == 0:
            act(self.plane, 0)
            return
        for step in (1, -1):
            z = self.plane - step * distance
            pl.when(self.has(z))(functools.partial(act, z, step))

    def from_line(self, distance):
        def act(z, step):
            self.line(z, False, step).wait_recv()
            pl.when(self.has(self.plane + step))(self.line(z, False, step).start)
            if not self.z_only:
                self.first(z).start()
                self.core_copy(self.near[0], 0, z).start()

        self.each(distance, act)

    def from_first(self, distance):
        def act(z, step):
            self.first(z).wait_recv()
            self.second(z, 0, distance == 0).start()
            self.second(z, 1).start()
            self.core_copy(self.near[1], 1, z).start()

        self.each(distance, act)

    def from_second(self, distance):
        def act(z, step):
            for n in range(2):
                self.second(z, n).wait_recv()
                self.core_copy(self.far[n], 2 + n, z).start()

        self.each(distance, act)

    def finish(self):
        for z in range(PLANES):
            for step in (1, -1):
                sent = jnp.logical_and(
                    (self.plane - z) * step >= 0, self.has(self.plane + step)
                )
                pl.when(sent)(self.line(z, False, step).wait_send)
            if not self.z_only:
                self.first(z).wait_send()
                for n, at in enumerate(self.near + self.far):
                    if n < 2:
                        self.second(z, n).wait_send()
                    self.core_copy(at, n, z).wait()
        self.own.wait()


class Rows:
    def __init__(self, source, w_ref, sems, own_sem):
        self.source, self.w_ref, self.sems = source, w_ref, sems
        self.docs, self.me = lax.axis_index("docs"), lax.axis_index("seq")
        self.over = (1 - self.docs, self.me)
        self.own = pltpu.make_async_copy(source, w_ref.at[self.docs, self.me // 4], own_sem)
        self.hops, self.moved = [], []

    def begin(self):
        target = self.w_ref.at[self.docs, self.me // 4]
        for rz in range(1, 4):
            peer = (self.docs, flip(self.me, 4 * rz))
            self.hops.append(remote(self.source, target, self.sems, rz, peer))
            self.hops[-1].start()
        self.own.start()
        self.moved.append(remote(self.source, target, self.sems, 4, self.over))
        self.moved[0].start()

    def forward(self, rz):
        self.hops[rz - 1].wait_recv()
        slot = self.w_ref.at[self.docs, flip(self.me, 4 * rz) // 4]
        self.moved.append(remote(slot, slot, self.sems, 4 + rz, self.over))
        self.moved[-1].start()

    def finish(self):
        for copy in self.moved:
            copy.wait_recv()
        for copy in self.hops + self.moved:
            copy.wait_send()
        self.own.wait()


class Tiles:
    def __init__(self, source, w_ref, sems, own_sem):
        self.source, self.w_ref, self.sems = source, w_ref, sems
        self.docs, self.me = lax.axis_index("docs"), lax.axis_index("seq")
        self.place = (self.docs, self.me // 4, (self.me // 2) % 2, self.me % 2)
        self.own = pltpu.make_async_copy(source, w_ref.at[self.place], own_sem)
        self.sent, self.last = [], []

    def send(self, part, n, peer):
        self.last.append(remote(part, part, self.sems, n, peer))
        self.last[-1].start()
        self.sent.append(self.last[-1])

    def arrived(self):
        for copy in self.last:
            copy.wait_recv()
        self.last = []

    def begin(self):
        self.own.start()
        self.own.wait()
        self.send(self.w_ref.at[self.place], 0, (self.docs, flip(self.me, 1)))

    def along_x(self):
        self.arrived()
        self.send(self.w_ref.at[self.place[:3]], 1, (self.docs, flip(self.me, 2)))

    def along_z(self):
        self.arrived()
        for rz in range(1, 4):
            self.send(self.w_ref.at[self.place[:2]], 1 + rz, (self.docs, flip(self.me, 4 * rz)))

    def along_docs(self):
        self.arrived()
        self.send(self.w_ref.at[self.docs], 5, (1 - self.docs, self.me))

    def finish(self):
        self.arrived()
        for copy in self.sent:
            copy.wait_send()


def open_kernel(*refs):
    low_ref, gain_ref, wq_ref, wq_1_ref, up_ref, down_ref, up_1_ref, down_1_ref = refs[:8]
    x_ref, gains_ref, w_ref, w_1_ref, wu_ref, wd_ref, wu_1_ref, wd_1_ref = refs[8:16]
    sems, gain_sems, own_sems, w_sems, w_1_sems, up_sems, down_sems, up_1_sems, down_1_sems = refs[16:]
    docs, me = lax.axis_index("docs"), lax.axis_index("seq")
    greet(spread_peers() + [(1 - docs, me)])
    gains = Tiles(gain_ref, gains_ref, gain_sems, own_sems.at[7])
    qkv = Rows(wq_ref, w_ref, w_sems, own_sems.at[0])
    qkv_1 = Rows(wq_1_ref, w_1_ref, w_1_sems, own_sems.at[1])
    whole = [
        Slabs(up_ref, wu_ref, up_sems, own_sems.at[2]),
        Slabs(down_ref, wd_ref, down_sems, own_sems.at[3], docs_first=True),
    ]
    lines = [
        Slabs(up_1_ref, wu_1_ref, up_1_sems, own_sems.at[4], z_only=True),
        Slabs(down_1_ref, wd_1_ref, down_1_sems, own_sems.at[5], z_only=True),
    ]
    rows = Spread(low_ref, x_ref, sems, own_sems.at[6])

    def every(parts, step, *arguments):
        for part in parts:
            getattr(part, step)(*arguments)

    every(whole, "begin")
    gains.begin()
    every(whole, "from_line", 1)
    every(whole, "from_first", 0)
    gains.along_x()
    rows.begin()
    qkv.begin()
    every(whole, "from_line", 2)
    every(whole, "from_first", 1)
    gains.along_z()
    every(whole, "from_line", 3)
    every(whole, "from_first", 2)
    every([rows], "forward", 1)
    every([rows], "forward", 2)
    every([rows], "forward", 3)
    gains.along_docs()
    qkv_1.begin()
    every(lines, "begin")
    every(whole, "from_first", 3)
    every(whole, "from_second", 0)
    for rz in range(1, 4):
        qkv.forward(rz)
    rows.from_beside()
    for rz in range(1, 4):
        qkv_1.forward(rz)
    for distance in range(1, 4):
        every(lines, "from_line", distance)
        every(whole, "from_second", distance)
    every([rows, gains, qkv, qkv_1] + whole + lines, "finish")


def open_layer(low, gain, wq, first, second, number):
    def whole(part):
        return jax.ShapeDtypeStruct((2, 2, PLANES, 2) + part.shape, BF16)

    def line(part):
        return jax.ShapeDtypeStruct((PLANES,) + part.shape, BF16)

    sems = pltpu.SemaphoreType.DMA
    return pl.pallas_call(
        open_kernel,
        out_shape=(
            jax.ShapeDtypeStruct((16, 64, low.shape[-1]), BF16),
            jax.ShapeDtypeStruct((2, PLANES, 2, 2) + gain.shape, BF16),
            jax.ShapeDtypeStruct((2, PLANES) + wq[0].shape, BF16),
            jax.ShapeDtypeStruct((2, PLANES) + wq[1].shape, BF16),
            whole(first[0]),
            whole(first[1]),
            line(second[0]),
            line(second[1]),
        ),
        in_specs=[hbm() for _ in range(8)],
        out_specs=tuple(hbm() for _ in range(8)),
        scratch_shapes=[
            sems((2, 16)),
            sems((2, 6)),
            sems((8,)),
            sems((2, 8)),
            sems((2, 8)),
            sems((2, 36)),
            sems((2, 36)),
            sems((2, 8)),
            sems((2, 8)),
        ],
        compiler_params=comm_params(number),
        name="open_layer",
    )(low, gain, *wq, *first, *second)


def exchange_kernel(x_ref, o_ref, sems, own_sem):
    docs, me = lax.axis_index("docs"), lax.axis_index("seq")
    order = list(range(15, 0, -1))
    greet([(docs, flip(me, bits)) for bits in order])
    copies = []
    for bits in order:
        peer = flip(me, bits)
        copies.append(remote(x_ref.at[peer], o_ref.at[me], sems, bits, (docs, peer)))
        copies[-1].start()
    own = pltpu.make_async_copy(x_ref.at[me], o_ref.at[me], own_sem)
    own.start()
    for copy in copies:
        copy.wait_recv()
    for copy in copies:
        copy.wait_send()
    own.wait()


def exchange(x, number):
    return pl.pallas_call(
        exchange_kernel,
        out_shape=jax.ShapeDtypeStruct(x.shape, x.dtype),
        in_specs=[hbm()],
        out_specs=hbm(),
        scratch_shapes=[pltpu.SemaphoreType.DMA((2, 16)), pltpu.SemaphoreType.DMA],
        compiler_params=comm_params(number),
        name="exchange",
    )(x)


class Collect:
    def __init__(self, keep_ref, send_ref, land, got_core, got_x, sum_x, near, sums, sems):
        self.keep_ref, self.send_ref, self.land, self.got_core = keep_ref, send_ref, land, got_core
        self.got_x, self.sum_x, self.near, self.sums, self.sems = got_x, sum_x, near, sums, sems
        self.docs, self.me = lax.axis_index("docs"), lax.axis_index("seq")
        self.order = (3, 2, 1, 0)
        self.first, self.across, self.hops = {}, {}, []

    def begin(self):
        mate = (self.docs, flip(self.me, 1))
        for rz in self.order:
            for n in (2 * rz + 1, 2 * rz):
                self.first[n] = remote(
                    self.send_ref.at[n], self.got_core.at[n], self.sems, n, mate
                )
                self.first[n].start()

    def along_x(self):
        beside = (self.docs, flip(self.me, 2))
        for rz in self.order:
            n = 2 * rz + 1
            self.first[n].wait_recv()
            self.sum_x[rz] = add_low(self.keep_ref[n], self.got_core[n])
            self.across[rz] = remote(
                self.sum_x.at[rz], self.got_x.at[rz], self.sems, 8 + rz, beside
            )
            self.across[rz].start()
            n = 2 * rz
            self.first[n].wait_recv()
            self.near[rz] = add_full(self.keep_ref[n], self.got_core[n])

    def along_z(self):
        plane = self.me // 4
        for rz in self.order:
            self.across[rz].wait_recv()
            total = add_low(self.near[rz], self.got_x[rz])
            if rz == 0:
                self.land[plane] = total
            else:
                self.sums[rz] = total
                peer = (self.docs, flip(self.me, 4 * rz))
                copy = remote(self.sums.at[rz], self.land.at[plane], self.sems, 12 + rz, peer)
                copy.start()
                self.hops.append(copy)

    def finish(self):
        for copy in self.hops:
            copy.wait_recv()
        for copy in list(self.first.values()) + list(self.across.values()) + self.hops:
            copy.wait_send()


def collect_scratch(width):
    return [
        pltpu.VMEM((4, 64, width), BF16),
        pltpu.VMEM((8, 64, width), BF16),
        pltpu.VMEM((4, 64, width), BF16),
        pltpu.VMEM((4, 64, width), BF16),
        pltpu.VMEM((4, 64, width), F32),
        pltpu.VMEM((4, 64, width), BF16),
        pltpu.SemaphoreType.DMA((2, 16)),
    ]


class Exchange:
    def __init__(self, source, land, sems, own_sem):
        docs, me = lax.axis_index("docs"), lax.axis_index("seq")
        self.copies = []
        for bits in range(15, 0, -1):
            peer = flip(me, bits)
            self.copies.append(remote(source.at[peer], land.at[me], sems, bits, (docs, peer)))
        self.own = pltpu.make_async_copy(source.at[me], land.at[me], own_sem)

    def begin(self):
        for copy in self.copies:
            copy.start()
        self.own.start()

    def arrived(self):
        for copy in self.copies:
            copy.wait_recv()
        self.own.wait()

    def finish(self):
        for copy in self.copies:
            copy.wait_send()


class Line:
    PLACE = (0, 2, 1, 3)

    def __init__(self, own, from_left, from_right, sems):
        self.own, self.landing, self.sems = own, (from_left, from_right), sems
        self.docs, self.me = lax.axis_index("docs"), lax.axis_index("seq")
        self.plane = self.me // 4

    def copy(self, place, target, step):
        side = 0 if step > 0 else 1
        return pltpu.make_async_remote_copy(
            self.own.at[place],
            self.landing[side].at[target],
            self.sems.at[0, side, target],
            self.sems.at[1, side, target],
            device_id=(self.docs, self.me + 4 * step),
            device_id_type=MESH,
        )

    def at(self, plane, act):
        pl.when(self.plane == plane)(act)

    def begin(self, rz):
        for plane, step in ((0, 1), (3, -1)):
            self.at(plane, self.copy(self.PLACE[rz], plane ^ rz, step).start)

    def hop(self, number):
        for plane, target, step in (
            ((1, 3, 1), (2, 0, -1)),
            ((1, 0, -1), (2, 3, 1)),
            ((1, 2, 1), (2, 1, -1)),
        )[number]:
            place, side = self.PLACE[plane ^ target], 0 if step > 0 else 1

            def act(place=place, side=side, target=target, step=step):
                copy = self.copy(place, target, step)
                copy.wait_recv()
                self.own[place] = add_low(self.own[place], self.landing[side][target])
                copy.start()

            self.at(plane, act)

    def total(self, out_ref, rows):
        for plane in range(PLANES):

            def act(plane=plane):
                total = self.own[0, rows].astype(F32)
                for side, step in ((0, 1), (1, -1)):
                    if 0 <= plane - step < PLANES:
                        total = total + self.landing[side][plane, rows].astype(F32)
                out_ref[...] = total

            self.at(plane, act)

    def arrived(self):
        for plane in range(PLANES):

            def act(plane=plane):
                for step in (1, -1):
                    if 0 <= plane - step < PLANES:
                        self.copy(0, plane, step).wait_recv()

            self.at(plane, act)

    def finish(self):
        for plane in range(PLANES):

            def act(plane=plane):
                for target in range(PLANES):
                    step = 1 if target > plane else -1
                    if target != plane:
                        self.copy(self.PLACE[plane ^ target], target, step).wait_send()

            self.at(plane, act)


class Everywhere:
    def __init__(self, total, got, sems):
        self.total, self.got, self.sems = total, got, sems
        docs, me = lax.axis_index("docs"), lax.axis_index("seq")
        self.peers = [(docs, flip(me, bits)) for bits in (1, 2, 4, 8)] + [(1 - docs, me)]
        self.copies = []

    def step(self):
        n = len(self.copies)
        if n > 0:
            self.copies[-1].wait_recv()
            self.total[n] = self.total[n - 1] + self.got[n - 1]
        if n < len(self.peers):
            copy = remote(self.total.at[n], self.got.at[n], self.sems, n, self.peers[n])
            copy.start()
            self.copies.append(copy)

    def finish(self):
        for copy in self.copies:
            copy.wait_send()


class Rest:
    ORDER = (3, 1, 2, 0)

    def __init__(self, a_keep, a_send, b_keep, b_send, scr):
        self.a_keep, self.a_send, self.b_keep, self.b_send = a_keep, a_send, b_keep, b_send
        self.scr = scr
        docs, me = lax.axis_index("docs"), lax.axis_index("seq")
        self.beside, self.over = (docs, flip(me, 2)), (1 - docs, me)
        self.line = Line(scr.own, scr.left, scr.right, scr.line_sems)
        self.sent = []

    def copy(self, n, place):
        scr = self.scr
        source, target, peer = (
            (self.a_send.at[4 + place], scr.a_got.at[4 + place], self.over),
            (self.b_send.at[1, place], scr.b_got.at[1, place], self.beside),
            (self.a_send.at[place], scr.a_got.at[place], self.over),
            (self.b_send.at[0, place], scr.b_got.at[0, place], self.beside),
            (scr.a_far.at[place], scr.a_far_got.at[place], self.beside),
            (scr.b_far.at[place], scr.b_far_got.at[place], self.over),
        )[n]
        return remote(source, target, scr.rest_sems, 4 * n + place, peer)

    def start(self, n, place):
        self.sent.append(self.copy(n, place))
        self.sent[-1].start()

    def first(self, place):
        for n in range(4):
            self.start(n, place)

    def second(self, place):
        scr = self.scr
        self.copy(0, place).wait_recv()
        scr.a_far[place] = add_low(self.a_keep[4 + place], scr.a_got[4 + place])
        self.start(4, place)
        self.copy(1, place).wait_recv()
        scr.b_far[place] = add_low(self.b_keep[1, place], scr.b_got[1, place])
        self.start(5, place)

    def third(self, place):
        scr = self.scr
        self.copy(2, place).wait_recv()
        self.copy(4, place).wait_recv()
        near = add_full(self.a_keep[place], scr.a_got[place]) + scr.a_far_got[place].astype(F32)
        scr.own[place, :CUT] = near.astype(BF16)
        self.copy(3, place).wait_recv()
        self.copy(5, place).wait_recv()
        near = add_full(self.b_keep[0, place], scr.b_got[0, place])
        near = near + scr.b_far_got[place].astype(F32)
        scr.own[place, CUT:] = near.astype(BF16)
        if place > 0:
            self.line.begin(Line.PLACE[place])

    def finish(self):
        for copy in self.sent:
            copy.wait_send()
        self.line.finish()


class Route:
    def __init__(self, source, out_ref, sems):
        self.source, self.out_ref, self.sems = source, out_ref, sems
        self.docs, self.me = lax.axis_index("docs"), lax.axis_index("seq")

    def each(self, act_here, act_there):
        for t in range(3):
            local = 3 * (self.me // 4) + t
            number = 16 * (local // 4) + 4 * (self.me % 4) + local % 4
            owner, slot = number // 3, number % 3
            target = self.out_ref.at[slot]
            here = pltpu.make_async_copy(self.source.at[t], target, self.sems.at[2, slot])
            there = pltpu.make_async_remote_copy(
                self.source.at[t],
                target,
                self.sems.at[0, t],
                self.sems.at[1, slot],
                device_id=(self.docs, owner),
                device_id_type=MESH,
            )
            pl.when(owner == self.me)(functools.partial(act_here, here))
            pl.when(owner != self.me)(functools.partial(act_there, there))

    def begin(self):
        self.each(lambda copy: copy.start(), lambda copy: copy.start())

    def finish(self):
        self.each(lambda copy: copy.wait(), lambda copy: copy.wait_send())
        for slot in range(3):
            number = 3 * self.me + slot
            local = 4 * (number // 16) + number % 4
            source = 4 * (local // 3) + (number % 16) // 4
            target = self.out_ref.at[slot]
            wait = pltpu.make_async_copy(target, target, self.sems.at[1, slot]).wait
            pl.when(source != self.me)(wait)


def back_scratch(width):
    low = 432 - CUT
    sems = pltpu.SemaphoreType.DMA

    def vm(*shape, dtype=BF16):
        return pltpu.VMEM(shape, dtype)

    return dict(
        qkv=vm(1024, 576),
        weight=vm(CHIPS, 48, 576),
        x=vm(16, 64, width),
        a_keep=vm(8, CUT, 384),
        b_keep=vm(2, 4, low, 384),
        load_sems=sems((5,)),
        do=vm(16, 32, 384),
        do_sems=sems((2, 16)),
        do_own=sems,
        key=vm(3, 1024, 128),
        query=vm(3, 1024, 128),
        value=vm(3, 1024, 64),
        turned=vm(3, 64, 1024),
        side=vm(2, 3, 1024, 128),
        dkv=vm(3, 1024, 128, dtype=F32),
        dq=vm(1024 // BACK_QUERIES, 192, BACK_QUERIES, dtype=F32),
        dqkv=vm(1024, 576),
        rows=vm(2, 8, 64, width),
        land=vm(4, 64, width),
        got_core=vm(8, 64, width),
        got_x=vm(4, 64, width),
        sum_x=vm(4, 64, width),
        near=vm(4, 64, width, dtype=F32),
        sums=vm(4, 64, width),
        row_sems=sems((2, 16)),
        a_got=vm(8, CUT, 384),
        b_got=vm(2, 4, low, 384),
        a_far=vm(4, CUT, 384),
        a_far_got=vm(4, CUT, 384),
        b_far=vm(4, low, 384),
        b_far_got=vm(4, low, 384),
        rest_sems=sems((2, 24)),
        own=vm(4, 432, 384),
        left=vm(4, 432, 384),
        right=vm(4, 432, 384),
        line_sems=sems((2, 2, 4)),
        q_grad=vm(2, 4, 144, 384),
        q_got=vm(4, 144, 384),
        q_own=vm(4, 144, 384),
        q_land=vm(4, 144, 384),
        q_sems=sems((2, 4)),
        q_sum=vm(3, 48, 384, dtype=F32),
        route_sems=sems((3, 3)),
        gain_sum=vm(6, 8, width, dtype=F32),
        gain_got=vm(5, 8, width, dtype=F32),
        gain_sems=sems((2, 5)),
    )


def attend_back_kernel(names, last, *refs):
    feature_ref, qkv_ref, do_ref, x_ref, w_ref, a_keep, a_send, b_keep, b_send = refs[:9]
    gain_ref, rows_ref, rest_ref, out_ref, gain_out_ref = refs[9:14]
    scr = types.SimpleNamespace(**dict(zip(names, refs[14:])))
    docs, me = lax.axis_index("docs"), lax.axis_index("seq")
    plane = me // 4
    over = (1 - docs, me)
    loads = {}
    for n, (name, ref) in enumerate(
        dict(qkv=qkv_ref, weight=w_ref, a_keep=a_keep, b_keep=b_keep, x=x_ref).items()
    ):
        loads[name] = pltpu.make_async_copy(ref, getattr(scr, name), scr.load_sems.at[n])
        loads[name].start()
    greet([(docs, flip(me, bits)) for bits in range(15, 0, -1)] + [over])
    exchange = Exchange(do_ref, scr.do, scr.do_sems, scr.do_own)
    exchange.begin()
    rest = Rest(scr.a_keep, a_send, scr.b_keep, b_send, scr)
    rest.first(3)
    rest.first(1)
    gains = Everywhere(scr.gain_sum, scr.gain_got, scr.gain_sems)
    if last:
        scr.gain_sum[0] = gain_ref[...]
        gains.step()

    loads["qkv"].wait()
    qkv = scr.qkv[...]
    spread_heads(qkv, feature_ref, scr.key, scr.query)
    zero = jnp.zeros((1024, 64), BF16)
    for h in range(GROUP_HEADS):
        scr.value[h] = qkv[:, 128 * h + 64 : 128 * h + 128]
        scr.turned[h] = qkv[:, 128 * h : 128 * h + 64].T
        scr.side[0, h] = jnp.concatenate([scr.query[h, :, :64], zero], axis=1)
    loads["a_keep"].wait()
    loads["b_keep"].wait()
    exchange.arrived()
    grad_o = jnp.concatenate([halves_below(scr.do[n]) for n in range(16)], axis=0)
    for h in range(GROUP_HEADS):
        scr.side[1, h] = jnp.concatenate([zero, grad_o[:, 64 * h : 64 * h + 64]], axis=1)

    def part(n, h):
        at = slice(BACK_QUERIES * n, BACK_QUERIES * n + BACK_QUERIES)
        expo, rate = expo_columns(dot_nt(scr.key[h], scr.query[h, at, :]))
        probs = expo * rate
        grad_probs = dot_nt(scr.value[h], scr.side[1, h, at, :][:, 64:])
        delta = jnp.sum(probs * grad_probs, axis=0, keepdims=True)
        grad_scores = (probs * (grad_probs - delta)).astype(BF16)
        scr.dq[n, 64 * h : 64 * h + 64, :] = dot(scr.turned[h], grad_scores) * (HEAD**-0.5)
        dkv = dot(grad_scores, scr.side[0, h, at, :])
        dkv += dot(probs.astype(BF16), scr.side[1, h, at, :])
        if n == 0:
            scr.dkv[h] = dkv
        else:
            scr.dqkv[:, 128 * h : 128 * h + 128] = (scr.dkv[h] + dkv).astype(BF16)

    part(0, 0)
    rest.second(3)
    rest.first(2)
    part(0, 1)
    if last:
        gains.step()
    part(0, 2)
    rest.second(1)
    scr.dqkv[0:512, 384:576] = scr.dq[0].T.astype(BF16)
    part(1, 0)
    rest.third(3)
    part(1, 1)
    rest.second(2)
    part(1, 2)
    rest.third(1)
    rest.line.hop(0)
    if last:
        gains.step()
    scr.dqkv[512:1024, 384:576] = scr.dq[1].T.astype(BF16)
    loads["x"].wait()
    grad = dot_tn(scr.dqkv[...], scr.x[...].reshape(1024, scr.x.shape[-1]))
    order = [6, 7, 8, 0, 2, 4, 1, 3, 5]
    grad = jnp.concatenate([grad[64 * n : 64 * n + 64] for n in order], axis=0).astype(BF16)
    for quarter in range(PLANES):
        apart = flip(plane, quarter)
        place = (apart % 2) * 2 + apart // 2
        for side in range(2):
            at = docs if side == 0 else 1 - docs
            scr.q_grad[at, place] = grad[
                144 * quarter : 144 * quarter + 144, 384 * side : 384 * side + 384
            ]
    crossed = remote(scr.q_grad.at[1], scr.q_got, scr.q_sems, 0, over)
    crossed.start()
    rest.first(0)
    loads["weight"].wait()
    rows = Collect(
        scr.rows.at[0],
        scr.rows.at[1],
        scr.land,
        scr.got_core,
        scr.got_x,
        scr.sum_x,
        scr.near,
        scr.sums,
        scr.row_sems,
    )
    for half in (1, 0):
        part_rows = []
        for n in range(8):
            block = flip(me, (n // 2) * 4 + (n % 2) * 2 + half)
            part_rows.append(scr.dqkv[pl.ds(pl.multiple_of(block * 64, 64), 64), :])
        product = dot_nt(jnp.concatenate(part_rows, axis=0), scr.weight[...].reshape(-1, 576))
        scr.rows[half] = product.astype(BF16).reshape(scr.rows.shape[1:])
        if half == 1:
            rows.begin()
    rest.third(2)
    rest.line.hop(1)
    rows.along_x()
    if last:
        gains.step()
    crossed.wait_recv()
    turned = []
    for place in Rest.ORDER:
        rz = Line.PLACE[place]
        scr.q_own[place] = add_low(scr.q_grad[0, place], scr.q_got[place])
        if rz > 0:
            peer = (docs, flip(me, 4 * rz))
            turned.append(
                remote(scr.q_own.at[place], scr.q_land.at[place], scr.q_sems, place, peer)
            )
            turned[-1].start()
    rest.line.hop(2)
    rest.second(0)
    rows.along_z()
    if last:
        gains.step()
    for copy in turned:
        copy.wait_recv()
    total = scr.q_own[0].astype(F32)
    for place in range(1, PLANES):
        total = total + scr.q_land[place].astype(F32)
    scr.q_sum[...] = total.reshape(scr.q_sum.shape)
    route = Route(scr.q_sum, out_ref, scr.route_sems)
    route.begin()
    rest.third(0)
    if last:
        gains.step()
        gain_out_ref[...] = scr.gain_sum[5]
        gains.finish()
    else:
        gain_out_ref[...] = gain_ref[...]
    rest.line.arrived()
    rest.line.total(rest_ref, slice(0, 432))
    rows.finish()
    rows_ref[...] = scr.land[...]
    for piece in (exchange, rest, route):
        piece.finish()
    for copy in turned + [crossed]:
        copy.wait_send()


def attend_back(features, qkv, grad_o, x, weight, sums, gain_grads, last, number):
    width = x.shape[-1]
    scratch = back_scratch(width)
    return pl.pallas_call(
        functools.partial(attend_back_kernel, tuple(scratch), last),
        out_shape=(
            jax.ShapeDtypeStruct((PLANES, 64, width), BF16),
            jax.ShapeDtypeStruct((432, 384), F32),
            jax.ShapeDtypeStruct((3, 48, 384), F32),
            jax.ShapeDtypeStruct((8, width), F32),
        ),
        in_specs=[vmem()] + [hbm()] * 8 + [vmem()],
        out_specs=(vmem(), vmem(), hbm(), vmem()),
        scratch_shapes=list(scratch.values()),
        compiler_params=pltpu.CompilerParams(
            collective_id=number, has_side_effects=True, vmem_limit_bytes=56 * 2**20
        ),
        cost_estimate=pl.CostEstimate(
            flops=8 * 10**9, bytes_accessed=10 * 10**6, transcendentals=3 * 10**6
        ),
        name="attend_back",
    )(features, qkv, grad_o, x, weight, *sums, gain_grads)


class Transfer:
    def __init__(self, steps):
        self.steps = steps
        self.result = None
        self.pending = next(steps)

    def go_on(self, arrived):
        try:
            self.pending = self.steps.send(arrived)
        except StopIteration as end:
            self.pending = ()
            self.result = end.value


def beside(result, *transfers):
    live = [transfer for transfer in transfers if transfer.result is None]
    result, arrived = lax.optimization_barrier((result, [transfer.pending for transfer in live]))
    for transfer, values in zip(live, arrived):
        transfer.go_on(values)
    return result


def in_core_order(core, own, other):
    return jnp.where(
        core == 0,
        jnp.concatenate([own, other], axis=0),
        jnp.concatenate([other, own], axis=0),
    )


def pick(stack, index):
    return lax.dynamic_index_in_dim(stack, index, 0, keepdims=False)


def pack_qkv(shards, me, core):
    rows = shards.shape[1]
    parts = shards.reshape(LAYERS, rows, 3, GROUPS, GROUP_HEADS, HEAD)
    pairs = jnp.transpose(parts[:, :, 1:], (3, 0, 1, 4, 2, 5)).reshape(GROUPS, LAYERS, rows, 384)
    query = jnp.transpose(parts[:, :, 0], (2, 0, 1, 3, 4)).reshape(GROUPS, LAYERS, rows, 192)
    packed = jnp.concatenate([pairs, query], axis=3)
    group = me & 3
    got = [pick(packed, group)] + [swap(pick(packed, group ^ r), r) for r in range(1, 4)]

    def in_order(own, other):
        return jnp.where(
            core == 0,
            jnp.concatenate([own, other], axis=1),
            jnp.concatenate([other, own], axis=1),
        )

    here, there = in_order(got[0], got[1]), in_order(got[2], got[3])
    both = jnp.where(
        (me >> 1) & 1 == 0,
        jnp.stack([here, there], axis=1),
        jnp.stack([there, here], axis=1),
    )
    return [both[layer] for layer in range(LAYERS)]


def pack_rest(out_weight, up_weight, down_weight, core):
    def mine(shard, side):
        half = shard.shape[2] // 2
        return lax.dynamic_slice_in_dim(shard, side * half, half, axis=2)

    def both(side):
        return jnp.concatenate([mine(up_weight, side), mine(out_weight, side)], axis=2)

    own, got = both(core), swap(both(1 - core), 1)
    rows = jnp.where(
        core == 0,
        jnp.concatenate([own, got], axis=1),
        jnp.concatenate([got, own], axis=1),
    )
    parts = []
    for layer in range(LAYERS):
        up, out = rows[layer, :, :1536], rows[layer, :, 1536:]
        down = [down_weight[layer, :48], down_weight[layer, 48:]]
        if layer == 0:
            parts.append((up, jnp.concatenate(down + [out], axis=1)))
        else:
            parts.append((jnp.concatenate([up, down[0], out], axis=1), down[1]))
    return parts


def gather_rest(first, second):
    first, second, got_first, got_second = yield (
        first,
        second,
        swap(first, 2),
        swap_docs(second),
    )
    first = jnp.concatenate([first, got_first], axis=0)
    second = jnp.concatenate([second, got_second], axis=0)
    first, second, got_first, got_second = yield (
        first,
        second,
        swap_docs(first),
        swap(second, 2),
    )
    first = jnp.concatenate([first, got_first], axis=0)
    second = jnp.concatenate([second, got_second], axis=0)
    return (yield (first, swap(first, 1), second, swap(second, 1)))


def add_low(first, second):
    return (first.astype(F32) + second.astype(F32)).astype(BF16)


def add_full(first, second):
    return first.astype(F32) + second.astype(F32)


def split_rest(total):
    down = total[240:].reshape(4, 48, 384)
    return (
        total[192:240].T,
        total[:192].T,
        jnp.transpose(down, (0, 2, 1)).reshape(1536, 48),
    )


def local_two_by_sixteen(
    tokens,
    qkv_weight,
    out_weight,
    up_weight,
    down_weight,
    norm_gains,
    doc_lengths,
    global_ids,
    random_ids,
    cotangent,
):
    docs_dev, block, width = tokens.shape
    me = lax.axis_index("seq").astype(jnp.int32)
    docs = lax.axis_index("docs").astype(jnp.int32)
    plane, core = me >> 2, me & 1
    chip = docs * 8 + (me >> 1)
    info = jnp.concatenate(
        [
            jnp.stack(
                [me, chip, pick(doc_lengths, plane), plane, docs, core, jnp.zeros_like(me), chip]
            ),
            doc_lengths,
        ]
    )
    features = key_features(
        lax.dynamic_index_in_dim(random_ids, plane, 1, keepdims=False),
        pick(global_ids, plane),
        pick(doc_lengths, plane),
    )

    wq = pack_qkv(qkv_weight, me, core)
    parts = pack_rest(out_weight, up_weight, down_weight, core)
    own_gains = jnp.pad(norm_gains.reshape(1, -1), ((0, 15), (0, 128 - norm_gains.size)))
    opened = open_layer(tokens, own_gains, wq, *parts, 0)
    x, up, down = opened[0], opened[4], opened[5]
    gain = opened[1].reshape(32, 16, 128)[:, 0, : norm_gains.size].reshape((32,) + norm_gains.shape)
    gain = jnp.transpose(gain, (1, 2, 0, 3)).reshape(LAYERS, 2, width).astype(F32)
    weights = [weight.reshape(CHIPS, 48, 576) for weight in opened[2:4]]
    rest_0 = (up.reshape(2, CHIPS, 48, -1), down.reshape(2, CHIPS, 48, -1))
    rest_1 = Transfer(gather_rest(*opened[6:]))
    qkv, o = beside(attend(features, x, weights[0]), rest_1)
    held = [(x, qkv)]
    o = exchange(o, 1)
    fed = feed(info, o, tokens, gain[0], rest_0)
    held[0] += (fed[:4],)
    x = spread(fed[5], 2)
    qkv, o = beside(attend(features, x, weights[1]), rest_1)
    o = beside(exchange(o, 3), rest_1)
    fed_1 = feed(info, o, fed[4], gain[1], rest_1.result)
    held.append((x, qkv, fed_1[:4]))
    base, grad_o, gain_1, *sums = feed_back(
        info, cotangent, None, gain[1], held[1][2], rest_1.result, 4
    )
    extra, rest_grads_1, qkv_1, gain_1 = attend_back(
        features,
        held[1][1],
        grad_o,
        held[1][0],
        weights[1],
        sums,
        jnp.pad(gain_1, ((2, 4), (0, 0))),
        False,
        5,
    )
    base, grad_o, gain_0, *sums = feed_back(info, base, extra, gain[0], held[0][2], rest_0, 6)
    extra, rest_grads, qkv_0, gain_grads = attend_back(
        features,
        held[0][1],
        grad_o,
        held[0][0],
        weights[0],
        sums,
        gain_1 + jnp.pad(gain_0, ((0, 6), (0, 0))),
        True,
        7,
    )
    grad_tokens = base.reshape(docs_dev, block, width) + extra.astype(F32)
    share = width // 32
    gain_grads = lax.dynamic_slice_in_dim(gain_grads, (docs * 16 + me) * share, share, axis=1)
    rest = [split_rest(rest_grads), split_rest(rest_grads_1)]
    qkv_grads = jnp.stack([qkv_0, qkv_1])
    return (
        fed_1[4].astype(BF16).reshape(docs_dev, block, width),
        grad_tokens,
        jnp.transpose(qkv_grads, (0, 3, 1, 2)).reshape(LAYERS, 384, 144),
        *(jnp.stack(pair) for pair in zip(*rest)),
        gain_grads[:4].reshape(LAYERS, 2, share),
    )


def solution(mesh):
    def local(*args):
        docs_dev, _, width = args[0].shape
        if fits(mesh, docs_dev, width // HEAD):
            return local_two_by_sixteen(*args)
        return local_any_mesh(*args)

    return jax.shard_map(
        local,
        mesh=mesh,
        in_specs=(
            P("docs", "seq", None),
            P(None, ("docs", "seq"), None),
            P(None, ("docs", "seq"), None),
            P(None, ("docs", "seq"), None),
            P(None, ("docs", "seq"), None),
            P(None, None, ("docs", "seq")),
            P("docs"),
            P("docs", None),
            P(None, "docs", None),
            P("docs", "seq", None),
        ),
        out_specs=(
            P("docs", "seq", None),
            P("docs", "seq", None),
            P(None, "docs", "seq"),
            P(None, "docs", "seq"),
            P(None, "docs", "seq"),
            P(None, "docs", "seq"),
            P(None, None, ("docs", "seq")),
        ),
        check_vma=False,
    )
```

```python
import functools
import types

import jax
import jax.numpy as jnp
from jax import lax
from jax.experimental import pallas as pl
from jax.experimental.pallas import tpu as pltpu
from jax.sharding import PartitionSpec as P

HEAD = 64
RAND = 3
GLOB = 2
LAYERS = 2


NEGATIVE = -1e30
EPSILON = 1e-05


def with_halo(cells, sides, width):
    for axis, dim in sides:
        count = lax.axis_size(axis)
        head = lax.slice_in_dim(cells, 0, width, axis=dim)
        tail = lax.slice_in_dim(cells, cells.shape[dim] - width, cells.shape[dim], axis=dim)
        cells = jnp.concatenate(
            [
                lax.ppermute(tail, axis, [(i, (i + 1) % count) for i in range(count)]),
                cells,
                lax.ppermute(head, axis, [((i + 1) % count, i) for i in range(count)]),
            ],
            axis=dim,
        )
    return cells


def combined_all(value, axis, join):
    pieces = jax.tree.map(lambda part: lax.all_gather(part, axis), value)
    head = jax.tree.map(lambda part: part[0], pieces)
    tail = jax.tree.map(lambda part: part[1:], pieces)
    so_far, _ = lax.scan(lambda so_far, piece: (join(so_far, piece), None), head, tail)
    return so_far


def norm_rows(values, gain):
    centre = values - jnp.mean(values, axis=-1, keepdims=True)
    spread = jnp.mean(centre * centre, axis=-1, keepdims=True)
    return centre * lax.rsqrt(spread + EPSILON) * gain


def gelu_tanh(values):
    return jax.nn.gelu(values, approximate=True)


def earlier_equal(values):
    length = values.shape[-1]
    order = jnp.arange(length, dtype=jnp.int32)
    before = order[None, :] < order[:, None]
    same = values[..., :, None] == values[..., None, :]
    return jnp.sum(jnp.logical_and(same, before), axis=-1)


def merge_stats(first, second):
    highest = jnp.maximum(first[0], second[0])
    return (
        highest,
        first[1] * jnp.exp(first[0] - highest) + second[1] * jnp.exp(second[0] - highest),
    )


def sparse_probs(query, key_part, key_inside, scale):
    scores = (
        jnp.einsum("kbhd,kjhd->khbj", query, key_part, preferred_element_type=jnp.float32) * scale
    )
    scores = jnp.where(key_inside[:, None, None, :], scores, NEGATIVE)
    expo = jnp.exp(scores - jnp.max(scores, axis=-1, keepdims=True))
    return expo / jnp.sum(expo, axis=-1, keepdims=True)


def global_scores(global_query, local_keys, inside, scale):
    scores = (
        jnp.einsum(
            "ksbhd,kjhd->kshbj", global_query, local_keys, preferred_element_type=jnp.float32
        )
        * scale
    )
    return jnp.where(inside[:, None, None, None, :], scores, NEGATIVE)


def local_any_mesh(
    tokens,
    qkv_weight,
    out_weight,
    up_weight,
    down_weight,
    norm_gains,
    doc_lengths,
    global_ids,
    random_ids,
    cotangent,
):
    nseq = lax.axis_size("seq")
    device = lax.axis_index("seq")
    docs_dev, block, width = tokens.shape
    count = docs_dev * block
    heads = width // HEAD
    scale = HEAD ** (-0.5)
    capacity = max(2, (docs_dev * RAND + nseq - 1) // nseq)
    global_capacity = (docs_dev * GLOB + nseq - 1) // nseq
    entries = docs_dev * RAND
    global_entries = docs_dev * GLOB
    offsets = jnp.arange(block, dtype=jnp.int32)
    inside = (device * block + offsets)[None, :] < doc_lengths[:, None]
    live_rows = inside.reshape(count, 1)
    wanted = random_ids.reshape(nseq, entries)
    wanted_rank = earlier_equal(wanted)
    slot_ids = jnp.arange(capacity, dtype=jnp.int32)
    hits = jnp.logical_and((wanted == device)[:, :, None], wanted_rank[:, :, None] == slot_ids)
    hits = jnp.any(hits.reshape(nseq, docs_dev, RAND, capacity), axis=2)
    hits = jnp.transpose(hits, (0, 2, 1))
    doc_ids = jnp.arange(docs_dev, dtype=jnp.int32)
    send_doc = jnp.sum(jnp.where(hits, doc_ids, 0), axis=2)
    send_live = jnp.any(hits, axis=2)
    owner_pick = hits.astype(jnp.float32)
    listed_here = lax.dynamic_index_in_dim(wanted, device, 0, keepdims=False)
    listed_rank = lax.dynamic_index_in_dim(wanted_rank, device, 0, keepdims=False)
    fetch_slot = listed_here * capacity + listed_rank
    global_block = global_ids.reshape(global_entries)
    global_rank = earlier_equal(global_block)
    global_slot = global_block * global_capacity + global_rank
    own_entry = global_block == device
    owned = jnp.logical_and(
        own_entry[:, None], global_rank[:, None] == jnp.arange(global_capacity, dtype=jnp.int32)
    )
    entry_doc = jnp.arange(global_entries, dtype=jnp.int32) // GLOB
    global_send_doc = jnp.sum(jnp.where(owned, entry_doc[:, None], 0), axis=0)
    global_send_live = jnp.any(owned, axis=0)
    own_flag = jnp.any(own_entry.reshape(docs_dev, GLOB), axis=1)
    own_slot = jnp.sum(jnp.where(own_entry, global_rank, 0).reshape(docs_dev, GLOB), axis=1)
    neighbours = jnp.stack([(device - 1) % nseq, device, (device + 1) % nseq])
    key_blocks = jnp.concatenate(
        [
            jnp.broadcast_to(neighbours[None, :], (docs_dev, 3)),
            listed_here.reshape(docs_dev, RAND),
            global_ids,
        ],
        axis=1,
    )
    span = key_blocks.shape[1] * block
    key_inside = (key_blocks[:, :, None] * block + offsets < doc_lengths[:, None, None]).reshape(
        docs_dev, span
    )
    keep_local = inside[:, None, None, None, :]
    hidden = tokens.reshape(count, width).astype(jnp.float32)
    held = []
    for layer in range(LAYERS):
        weights = (
            lax.all_gather(qkv_weight[layer], ("docs", "seq"), axis=0, tiled=True),
            lax.all_gather(out_weight[layer], ("docs", "seq"), axis=0, tiled=True),
            lax.all_gather(up_weight[layer], ("docs", "seq"), axis=0, tiled=True),
            lax.all_gather(down_weight[layer], ("docs", "seq"), axis=0, tiled=True),
            lax.all_gather(norm_gains[layer], ("docs", "seq"), axis=1, tiled=True),
        )
        weight_qkv, weight_out, weight_up, weight_down, gain_pair = weights
        gain_pair = gain_pair.astype(jnp.float32)
        lowered = hidden.astype(jnp.bfloat16)
        projected = (
            jnp.dot(lowered, weight_qkv, preferred_element_type=jnp.float32)
            .astype(jnp.bfloat16)
            .reshape(docs_dev, block, 3 * width)
        )
        pairs = projected[:, :, width:]
        window = with_halo(pairs, (("seq", 1),), block)
        outgoing = jnp.where(
            send_live[:, :, None, None],
            jnp.take(pairs, send_doc, axis=0),
            jnp.zeros((), jnp.bfloat16),
        )
        incoming = lax.all_to_all(outgoing, "seq", split_axis=0, concat_axis=0, tiled=True)
        fetched = jnp.take(
            incoming.reshape(nseq * capacity, block, 2 * width), fetch_slot, axis=0
        ).reshape(docs_dev, RAND * block, 2 * width)
        global_send = jnp.where(
            global_send_live[:, None, None],
            jnp.take(projected, global_send_doc, axis=0),
            jnp.zeros((), jnp.bfloat16),
        )
        gathered = lax.all_gather(global_send, "seq", axis=0, tiled=True)
        global_picked = jnp.take(gathered, global_slot, axis=0).reshape(
            docs_dev, GLOB, block, 3 * width
        )
        global_query = global_picked[..., :width].reshape(docs_dev, GLOB, block, heads, HEAD)
        listed_pairs = jnp.concatenate(
            [
                window,
                fetched,
                global_picked[..., width:].reshape(docs_dev, GLOB * block, 2 * width),
            ],
            axis=1,
        )
        query = projected[:, :, :width].reshape(docs_dev, block, heads, HEAD)
        key_part = listed_pairs[:, :, :width].reshape(docs_dev, span, heads, HEAD)
        value_part = listed_pairs[:, :, width:].reshape(docs_dev, span, heads, HEAD)
        probs = sparse_probs(query, key_part, key_inside, scale)
        mixed = jnp.einsum(
            "khbj,kjhd->kbhd",
            probs.astype(jnp.bfloat16),
            value_part,
            preferred_element_type=jnp.float32,
        )
        local_keys = projected[:, :, width : 2 * width].reshape(docs_dev, block, heads, HEAD)
        local_values = projected[:, :, 2 * width :].reshape(docs_dev, block, heads, HEAD)
        wide_scores = global_scores(global_query, local_keys, inside, scale)
        global_top = jnp.max(wide_scores, axis=-1)
        global_total = jnp.sum(
            jnp.where(keep_local, jnp.exp(wide_scores - global_top[..., None]), 0.0), axis=-1
        )
        global_top, global_total = combined_all((global_top, global_total), "seq", merge_stats)
        wide_probs = (
            jnp.where(keep_local, jnp.exp(wide_scores - global_top[..., None]), 0.0)
            / global_total[..., None]
        )
        wide_part = jnp.einsum(
            "kshbj,kjhd->ksbhd",
            wide_probs.astype(jnp.bfloat16),
            local_values,
            preferred_element_type=jnp.float32,
        )
        wide_buffer = (
            jnp.zeros((nseq * global_capacity, block, width), jnp.float32)
            .at[global_slot]
            .set(wide_part.reshape(global_entries, block, width))
        )
        wide_sum = lax.psum_scatter(wide_buffer, "seq", scatter_dimension=0, tiled=True)
        attended = jnp.where(
            own_flag[:, None, None],
            jnp.take(wide_sum, own_slot, axis=0),
            mixed.reshape(docs_dev, block, width),
        )
        attended = attended.reshape(count, width).astype(jnp.bfloat16)
        after_attn = hidden + jnp.dot(attended, weight_out, preferred_element_type=jnp.float32)
        normed = norm_rows(after_attn, gain_pair[0])
        normed_low = normed.astype(jnp.bfloat16)
        up_values = jnp.dot(normed_low, weight_up, preferred_element_type=jnp.float32)
        activated = gelu_tanh(up_values).astype(jnp.bfloat16)
        after_ffn = normed + jnp.dot(activated, weight_down, preferred_element_type=jnp.float32)
        held.append(
            (
                weights,
                lowered,
                projected,
                listed_pairs,
                global_query,
                global_top,
                global_total,
                attended,
                after_attn,
                normed_low,
                up_values,
                activated,
                after_ffn,
            )
        )
        hidden = jnp.where(live_rows, norm_rows(after_ffn, gain_pair[1]), 0.0)
    gradient = cotangent.reshape(count, width).astype(jnp.float32)
    layer_grads = []
    for layer in reversed(range(LAYERS)):
        (
            weights,
            lowered,
            projected,
            listed_pairs,
            global_query,
            global_top,
            global_total,
            attended,
            after_attn,
            normed_low,
            up_values,
            activated,
            after_ffn,
        ) = held[layer]
        weights = (
            lax.all_gather(qkv_weight[layer], ("docs", "seq"), axis=0, tiled=True),
            lax.all_gather(out_weight[layer], ("docs", "seq"), axis=0, tiled=True),
            lax.all_gather(up_weight[layer], ("docs", "seq"), axis=0, tiled=True),
            lax.all_gather(down_weight[layer], ("docs", "seq"), axis=0, tiled=True),
            lax.all_gather(norm_gains[layer], ("docs", "seq"), axis=1, tiled=True),
        )
        weight_qkv, weight_out, weight_up, weight_down, gain_pair = weights
        gain_pair = gain_pair.astype(jnp.float32)
        gradient = jnp.where(live_rows, gradient, 0.0)
        grad_ffn, grad_gain_out = jax.vjp(norm_rows, after_ffn, gain_pair[1])[1](gradient)
        grad_down_low = grad_ffn.astype(jnp.bfloat16)
        grad_down_layer = jnp.einsum(
            "rf,rd->fd", activated, grad_down_low, preferred_element_type=jnp.float32
        )
        grad_activated = jnp.einsum(
            "rd,fd->rf", grad_down_low, weight_down, preferred_element_type=jnp.float32
        )
        grad_up_low = jax.vjp(gelu_tanh, up_values)[1](grad_activated)[0].astype(jnp.bfloat16)
        grad_up_layer = jnp.einsum(
            "rd,rf->df", normed_low, grad_up_low, preferred_element_type=jnp.float32
        )
        grad_normed = grad_ffn + jnp.einsum(
            "rf,df->rd", grad_up_low, weight_up, preferred_element_type=jnp.float32
        )
        grad_attn, grad_gain_mid = jax.vjp(norm_rows, after_attn, gain_pair[0])[1](grad_normed)
        grad_attn_low = grad_attn.astype(jnp.bfloat16)
        grad_out_layer = jnp.einsum(
            "rd,re->de", attended, grad_attn_low, preferred_element_type=jnp.float32
        )
        grad_mixed = (
            jnp.einsum("re,de->rd", grad_attn_low, weight_out, preferred_element_type=jnp.float32)
            .astype(jnp.bfloat16)
            .reshape(docs_dev, block, width)
        )
        query = projected[:, :, :width].reshape(docs_dev, block, heads, HEAD)
        key_part = listed_pairs[:, :, :width].reshape(docs_dev, span, heads, HEAD)
        value_part = listed_pairs[:, :, width:].reshape(docs_dev, span, heads, HEAD)
        probs = sparse_probs(query, key_part, key_inside, scale)
        grad_sparse = jnp.where(
            own_flag[:, None, None], jnp.zeros((), jnp.bfloat16), grad_mixed
        ).reshape(docs_dev, block, heads, HEAD)
        grad_probs = jnp.einsum(
            "kbhd,kjhd->khbj", grad_sparse, value_part, preferred_element_type=jnp.float32
        )
        delta = jnp.sum(probs * grad_probs, axis=-1, keepdims=True)
        grad_scores = (probs * (grad_probs - delta)).astype(jnp.bfloat16)
        grad_query = (
            jnp.einsum("khbj,kjhd->kbhd", grad_scores, key_part, preferred_element_type=jnp.float32)
            * scale
        )
        grad_key_part = (
            jnp.einsum("khbj,kbhd->kjhd", grad_scores, query, preferred_element_type=jnp.float32)
            * scale
        )
        grad_value_part = jnp.einsum(
            "khbj,kbhd->kjhd",
            probs.astype(jnp.bfloat16),
            grad_sparse,
            preferred_element_type=jnp.float32,
        )
        grad_listed = jnp.concatenate(
            [
                grad_key_part.reshape(docs_dev, span, width),
                grad_value_part.reshape(docs_dev, span, width),
            ],
            axis=2,
        )
        wide_out = jnp.where(
            global_send_live[:, None, None],
            jnp.take(grad_mixed, global_send_doc, axis=0),
            jnp.zeros((), jnp.bfloat16),
        )
        wide_all = lax.all_gather(wide_out, "seq", axis=0, tiled=True)
        wide_grad = jnp.take(wide_all, global_slot, axis=0).reshape(
            docs_dev, GLOB, block, heads, HEAD
        )
        local_keys = projected[:, :, width : 2 * width].reshape(docs_dev, block, heads, HEAD)
        local_values = projected[:, :, 2 * width :].reshape(docs_dev, block, heads, HEAD)
        wide_scores = global_scores(global_query, local_keys, inside, scale)
        wide_probs = (
            jnp.where(keep_local, jnp.exp(wide_scores - global_top[..., None]), 0.0)
            / global_total[..., None]
        )
        wide_grad_probs = jnp.einsum(
            "ksbhd,kjhd->kshbj", wide_grad, local_values, preferred_element_type=jnp.float32
        )
        wide_delta = lax.psum(jnp.sum(wide_probs * wide_grad_probs, axis=-1), "seq")
        wide_grad_scores = (wide_probs * (wide_grad_probs - wide_delta[..., None])).astype(
            jnp.bfloat16
        )
        wide_grad_query = (
            jnp.einsum(
                "kshbj,kjhd->ksbhd",
                wide_grad_scores,
                local_keys,
                preferred_element_type=jnp.float32,
            )
            * scale
        )
        wide_grad_keys = (
            jnp.einsum(
                "kshbj,ksbhd->kjhd",
                wide_grad_scores,
                global_query,
                preferred_element_type=jnp.float32,
            )
            * scale
        )
        wide_grad_values = jnp.einsum(
            "kshbj,ksbhd->kjhd",
            wide_probs.astype(jnp.bfloat16),
            wide_grad,
            preferred_element_type=jnp.float32,
        )
        global_grads = jnp.concatenate(
            [
                wide_grad_query.reshape(global_entries, block, width),
                grad_listed[:, (3 + RAND) * block :, :].reshape(global_entries, block, 2 * width),
            ],
            axis=2,
        )
        global_buffer = (
            jnp.zeros((nseq * global_capacity, block, 3 * width), jnp.float32)
            .at[global_slot]
            .set(global_grads)
        )
        global_share = lax.psum_scatter(global_buffer, "seq", scatter_dimension=0, tiled=True)
        global_mine = jnp.where(
            own_flag[:, None, None], jnp.take(global_share, own_slot, axis=0), 0.0
        )
        grad_fetched = grad_listed[:, 3 * block : (3 + RAND) * block, :].reshape(
            entries, block, 2 * width
        )
        back_out = (
            jnp.zeros((nseq * capacity, block, 2 * width), jnp.float32)
            .at[fetch_slot]
            .set(grad_fetched)
            .reshape(nseq, capacity, block, 2 * width)
        )
        back_in = lax.all_to_all(back_out, "seq", split_axis=0, concat_axis=0, tiled=True)
        grad_random = jnp.einsum(
            "dck,dcbf->kbf", owner_pick, back_in, precision=lax.Precision.HIGHEST
        )
        grad_window = grad_listed[:, : 3 * block, :]
        edges = jnp.concatenate([grad_window[:, :block], grad_window[:, 2 * block :]], axis=1)
        beside_all = with_halo(edges, (("seq", 1),), block)
        grad_pairs = (
            grad_window[:, block : 2 * block]
            + beside_all[:, :block]
            + beside_all[:, 3 * block :]
            + grad_random
            + global_mine[:, :, width:]
        )
        grad_pairs = grad_pairs + jnp.concatenate(
            [
                wide_grad_keys.reshape(docs_dev, block, width),
                wide_grad_values.reshape(docs_dev, block, width),
            ],
            axis=2,
        )
        grad_queries = grad_query.reshape(docs_dev, block, width) + global_mine[:, :, :width]
        grad_projected = (
            jnp.concatenate([grad_queries, grad_pairs], axis=2)
            .reshape(count, 3 * width)
            .astype(jnp.bfloat16)
        )
        grad_qkv_layer = jnp.einsum(
            "rd,re->de", lowered, grad_projected, preferred_element_type=jnp.float32
        )
        gradient = grad_attn + jnp.einsum(
            "re,de->rd", grad_projected, weight_qkv, preferred_element_type=jnp.float32
        )
        group_shares = (
            lax.psum_scatter(grad_qkv_layer, "docs", scatter_dimension=0, tiled=True),
            lax.psum_scatter(grad_out_layer, "docs", scatter_dimension=0, tiled=True),
            lax.psum_scatter(grad_up_layer, "docs", scatter_dimension=0, tiled=True),
            lax.psum_scatter(grad_down_layer, "docs", scatter_dimension=0, tiled=True),
            lax.psum_scatter(
                jnp.stack([grad_gain_mid, grad_gain_out]), "docs", scatter_dimension=1, tiled=True
            ),
        )
        shares = (
            lax.psum_scatter(group_shares[0], "seq", scatter_dimension=1, tiled=True),
            lax.psum_scatter(group_shares[1], "seq", scatter_dimension=1, tiled=True),
            lax.psum_scatter(group_shares[2], "seq", scatter_dimension=1, tiled=True),
            lax.psum_scatter(group_shares[3], "seq", scatter_dimension=1, tiled=True),
            lax.psum_scatter(group_shares[4], "seq", scatter_dimension=1, tiled=True),
        )
        layer_grads.insert(0, shares)
    stacked = [
        jnp.stack([layer_grads[number][member] for number in range(LAYERS)]) for member in range(5)
    ]
    return (
        hidden.astype(jnp.bfloat16).reshape(docs_dev, block, width),
        gradient.reshape(docs_dev, block, width),
        stacked[0],
        stacked[1],
        stacked[2],
        stacked[3],
        stacked[4],
    )


PLANES = 4
GROUPS = 4
CHIPS = 16
GROUP_HEADS = 3
CUT = 240
MESH = pl.DeviceIdType.MESH
F32 = jnp.float32
BF16 = jnp.bfloat16


def fits(mesh, docs_dev, heads):
    return (
        mesh.shape["docs"] == 2
        and mesh.shape["seq"] == 16
        and docs_dev == PLANES
        and heads == GROUPS * GROUP_HEADS
    )


def swap(value, bits):
    return lax.ppermute(value, "seq", [(i, i ^ bits) for i in range(16)])


def swap_docs(value):
    return lax.ppermute(value, "docs", [(0, 1), (1, 0)])


def dot(left, right):
    return lax.dot_general(left, right, (((1,), (0,)), ((), ())), preferred_element_type=F32)


def dot_nt(left, right):
    return lax.dot_general(left, right, (((1,), (1,)), ((), ())), preferred_element_type=F32)


def dot_tn(left, right):
    return lax.dot_general(left, right, (((0,), (0,)), ((), ())), preferred_element_type=F32)


def vmem():
    return pl.BlockSpec(memory_space=pltpu.VMEM)


def smem():
    return pl.BlockSpec(memory_space=pltpu.SMEM)


def hbm():
    return pl.BlockSpec(memory_space=pltpu.HBM)


def params():
    return pltpu.CompilerParams(vmem_limit_bytes=56 * 2**20)


QUERIES = 512
BACK_QUERIES = 512


def key_features(own_random, own_global, length):
    block = jnp.arange(16, dtype=jnp.int32)
    window = jnp.stack([(block + 15) % 16, block, (block + 1) % 16], axis=1)
    ids = jnp.concatenate([window, own_random, jnp.broadcast_to(own_global, (16, GLOB))], axis=1)
    count = jnp.sum((ids[:, :, None] == block).astype(F32), axis=1).T
    special = jnp.any(own_global[None, :] == block[:, None], axis=1)
    count = jnp.where(special[None, :], 1.0, count)
    extra = jnp.where(count > 0, jnp.log(jnp.maximum(count, 1.0)), NEGATIVE)
    inside = jnp.arange(1024, dtype=jnp.int32)[:, None] < length
    extra = jnp.where(inside, jnp.repeat(extra, 64, axis=0), NEGATIVE)
    high = extra.astype(BF16)
    low = jnp.where(extra > 0, extra - high.astype(F32), 0.0).astype(BF16)
    return jnp.concatenate([high, low, jnp.zeros((1024, 32), BF16)], axis=1)


def halves_beside(rows):
    return jnp.concatenate([rows[:32], rows[32:]], axis=1)


def halves_below(rows):
    return jnp.concatenate([rows[:, :192], rows[:, 192:]], axis=0)


def spread_heads(qkv, feature_ref, key_scr, query_scr):
    row = lax.broadcasted_iota(jnp.int32, (1024, 64), 0) // 64
    lane = lax.broadcasted_iota(jnp.int32, (1024, 64), 1)
    place = jnp.where(jnp.logical_and(lane < 32, lane % 16 == row), 1.0, 0.0).astype(BF16)
    for h in range(GROUP_HEADS):
        key_scr[h] = jnp.concatenate([qkv[:, 128 * h : 128 * h + 64], feature_ref[...]], axis=1)
        query = qkv[:, 384 + 64 * h : 448 + 64 * h] * jnp.asarray(HEAD**-0.5, BF16)
        query_scr[h] = jnp.concatenate([query, place], axis=1)


def expo_columns(scores):
    expo = jnp.exp(scores - jnp.max(scores, axis=0, keepdims=True))
    return expo, 1.0 / jnp.sum(expo, axis=0, keepdims=True)


def load_ordered(w_refs, wu, wd, wo, sems):
    up_ref, down_ref = w_refs
    pltpu.make_async_copy(down_ref.at[:, :, :, pl.ds(1536, 384)], wo, sems.at[0]).start()
    pltpu.make_async_copy(up_ref, wu, sems.at[1]).start()
    for plane in range(2):
        for part in range(2):
            source = down_ref.at[plane, :, :, pl.ds(768 * part, 768)]
            pltpu.make_async_copy(source, wd.at[:, plane, part], sems.at[2]).start()


def wait_weight(scr, sem):
    pltpu.make_async_copy(scr, scr, sem).wait()


def inside_rows(info):
    row = lax.broadcasted_iota(jnp.int32, (256, 1), 0)
    length = jnp.zeros_like(row)
    for k in range(PLANES):
        length = jnp.where(row // 64 == k, info[8 + k], length)
    return info[0] * 64 + row % 64 < length


def norm_parts(values):
    centre = values - jnp.mean(values, axis=-1, keepdims=True)
    spread = jnp.mean(centre * centre, axis=-1, keepdims=True)
    rate = lax.rsqrt(spread + EPSILON)
    return centre * rate, rate


def norm_back(unit, rate, gain, grad):
    scaled = grad * gain
    inner = jnp.mean(scaled * unit, axis=-1, keepdims=True)
    outer = jnp.mean(scaled, axis=-1, keepdims=True)
    return rate * (scaled - outer - unit * inner), jnp.sum(grad * unit, axis=0, keepdims=True)


CURVE = 0.7978845608028654


def gelu_parts(values):
    square = values * values
    bend = jnp.tanh(CURVE * (values + 0.044715 * (square * values)))
    return 0.5 * values * (1.0 + bend), bend, square


def gelu_slope(values, bend, square):
    return 0.5 * (1.0 + bend) + 0.5 * values * (1.0 - bend * bend) * (
        CURVE * (1.0 + 3 * 0.044715 * square)
    )


WEIGHT_SCRATCH = [
    pltpu.VMEM((2, 16, 48, 1536), BF16),
    pltpu.VMEM((16, 2, 2, 48, 768), BF16),
    pltpu.VMEM((2, 16, 48, 384), BF16),
]


def feed_back_kernel(
    pieces,
    has_extra,
    info,
    base_ref,
    extra_ref,
    gain_ref,
    mixed_ref,
    h1_ref,
    up_ref,
    h2_ref,
    *refs,
):
    w_refs, refs = refs[:pieces], refs[pieces:]
    dh1_ref, do_ref, dgain_ref, *sum_refs, wu, wd, wo, gu, gd, go, got, sems, pair_sems, out_sems = refs
    load_ordered(w_refs, wu, wd, wo, sems)
    docs, me = lax.axis_index("docs"), lax.axis_index("seq")
    mate = (docs, flip(me, 1))
    greet([mate])
    units = [(ry, place) for ry in range(2) for place in range(8)]

    def other_docs(ry):
        return docs if ry == 0 else 1 - docs

    def owner(place, rc):
        return flip(me, (place % 2) * 8 + (place // 2 % 2) * 4 + (place // 4) * 2 + rc)

    def exchange_units(scr, first, count, n):
        copies = []
        for ry, place in units:
            copies.append(
                pltpu.make_async_remote_copy(
                    scr.at[other_docs(ry), owner(place, 1)],
                    got.at[ry, place, pl.ds(first, count)],
                    pair_sems.at[0, n],
                    pair_sems.at[1, n],
                    device_id=mate,
                    device_id_type=MESH,
                )
            )
            copies[-1].start()
        return copies
    if has_extra:
        parts = [
            base_ref[64 * k : 64 * k + 64, :] + extra_ref[k].astype(F32)
            for k in range(PLANES)
        ]
        grad = jnp.concatenate(parts, axis=0)
    else:
        grad = base_ref[...].reshape(256, 768).astype(F32)
    grad = jnp.where(inside_rows(info), grad, 0.0)
    unit2, rate2 = norm_parts(h2_ref[...])
    dh2, dgain1 = norm_back(unit2, rate2, gain_ref[1:2, :], grad)
    dgain_ref[1:2, :] = dgain1
    df = dh2.astype(BF16)
    unit1, rate1 = norm_parts(h1_ref[...])
    x1_low = (unit1 * gain_ref[0:1, :]).astype(BF16)
    wait_weight(wd, sems.at[2])
    wait_weight(wu, sems.at[1])
    dx1 = dh2
    for part in range(8):
        at = 384 * part
        d_act = dot_nt(df, wd[2 * part : 2 * part + 2].reshape(384, 768))
        up = up_ref[:, at : at + 384]
        act, bend, square = gelu_parts(up)
        act = act.astype(BF16)
        dup = (gelu_slope(up, bend, square) * d_act).astype(BF16)
        side, start = part // 4, 384 * (part % 4)
        dx1 += dot_nt(dup, wu[side, :, :, start : start + 384].reshape(768, 384))
        gt_up = dot_tn(dup, x1_low).astype(BF16)
        for n in range(2):
            for half in range(2):
                gu[half, 2 * part + n] = gt_up[
                    192 * n : 192 * n + 192, 384 * half : 384 * half + 384
                ]
        gt_down = dot_tn(df, act).astype(BF16)
        row = 48 * (part % 4)
        for s in range(16):
            gd[part // 4, s, row : row + 48, :] = gt_down[48 * s : 48 * s + 48]
    exchange_units(gu, 0, 192, 0)
    exchange_units(gd, 240, 192, 1)
    dh1, dgain0 = norm_back(unit1, rate1, gain_ref[0:1, :], dx1)
    dgain_ref[0:1, :] = dgain0
    dh1_ref[...] = dh1
    da = dh1.astype(BF16)
    gt_out = dot_tn(da, mixed_ref[...]).astype(BF16)
    for s in range(16):
        for half in range(2):
            go[half, s] = gt_out[48 * s : 48 * s + 48, 384 * half : 384 * half + 384]
    exchange_units(go, 192, 48, 2)
    wait_weight(wo, sems.at[0])
    do = dot_nt(da[:, 0:384], wo[0].reshape(768, 384))
    do += dot_nt(da[:, 384:768], wo[1].reshape(768, 384))
    do = do.astype(BF16)
    for k in range(PLANES):
        for g in range(GROUPS):
            do_ref[4 * k + g] = halves_beside(do[64 * k : 64 * k + 64, 192 * g : 192 * g + 192])
    for n, (first, count) in enumerate(((0, 192), (240, 192), (192, 48))):
        part = got.at[:, :, pl.ds(first, count)]
        pltpu.make_async_copy(part, part, pair_sems.at[1, n]).wait()
    copies = []
    for ry, place in units:
        for scr, first, count in ((gu, 0, 192), (go, 192, 48), (gd, 240, 192)):
            span = slice(first, first + count)
            own = scr[other_docs(ry), owner(place, 0)].astype(F32)
            got[ry, place, span] = (own + got[ry, place, span].astype(F32)).astype(BF16)
        for ref, source in (
            (sum_refs[ry].at[place], got.at[ry, place, pl.ds(0, CUT)]),
            (sum_refs[2 + place // 4].at[ry, place % 4], got.at[ry, place, pl.ds(CUT, 432 - CUT)]),
        ):
            copies.append(pltpu.make_async_copy(source, ref, out_sems.at[len(copies)]))
            copies[-1].start()
    for n, scr in enumerate((gu, gd, go)):
        half = scr.at[:, pl.ds(0, 8)]
        pltpu.make_async_copy(half, half, pair_sems.at[0, n]).wait()
    for copy in copies:
        copy.wait()


def feed_back(info, base, extra, gains, saved, weights, number):
    mixed, h1, up, h2 = saved
    has_extra = extra is not None
    if not has_extra:
        extra = jnp.zeros((8, 128), BF16)
    return pl.pallas_call(
        functools.partial(feed_back_kernel, len(weights), has_extra),
        out_shape=(
            jax.ShapeDtypeStruct((256, 768), F32),
            jax.ShapeDtypeStruct((16, 32, 384), BF16),
            jax.ShapeDtypeStruct((2, 768), F32),
            jax.ShapeDtypeStruct((8, CUT, 384), BF16),
            jax.ShapeDtypeStruct((8, CUT, 384), BF16),
            jax.ShapeDtypeStruct((2, 4, 432 - CUT, 384), BF16),
            jax.ShapeDtypeStruct((2, 4, 432 - CUT, 384), BF16),
        ),
        in_specs=[smem()] + [vmem()] * 7 + [hbm() for _ in weights],
        out_specs=(vmem(), vmem(), vmem(), hbm(), hbm(), hbm(), hbm()),
        scratch_shapes=WEIGHT_SCRATCH
        + [
            pltpu.VMEM((2, 16, 192, 384), BF16),
            pltpu.VMEM((2, 16, 192, 384), BF16),
            pltpu.VMEM((2, 16, 48, 384), BF16),
            pltpu.VMEM((2, 8, 432, 384), BF16),
            pltpu.SemaphoreType.DMA((3,)),
            pltpu.SemaphoreType.DMA((2, 3)),
            pltpu.SemaphoreType.DMA((32,)),
        ],
        compiler_params=pltpu.CompilerParams(
            collective_id=number, has_side_effects=True, vmem_limit_bytes=56 * 2**20
        ),
        cost_estimate=pl.CostEstimate(
            flops=6 * 10**9, bytes_accessed=40 * 10**6, transcendentals=10**6
        ),
        name="feed_back",
    )(info, base, extra, gains, mixed, h1, up, h2, *weights)


def flip(index, bits):
    for bit in (1, 2, 4, 8):
        if bits & bit:
            index = index + bit - 2 * bit * ((index // bit) % 2)
    return index


def greet(peers):
    barrier = pltpu.get_barrier_semaphore()
    for peer in peers:
        pl.semaphore_signal(barrier, inc=1, device_id=peer, device_id_type=MESH)
    pl.semaphore_wait(barrier, len(peers))


def remote(source, target, sems, n, peer):
    return pltpu.make_async_remote_copy(
        source, target, sems.at[0, n], sems.at[1, n], device_id=peer, device_id_type=MESH
    )


def comm_params(number):
    return pltpu.CompilerParams(
        collective_id=number, has_side_effects=True, vmem_limit_bytes=16 * 2**20
    )


class Spread:
    def __init__(self, low_ref, x_ref, sems, own_sem):
        self.low_ref, self.x_ref, self.sems = low_ref, x_ref, sems
        self.docs, self.me = lax.axis_index("docs"), lax.axis_index("seq")
        self.own = pltpu.make_async_copy(low_ref.at[self.me // 4], x_ref.at[self.me], own_sem)
        self.hops, self.across, self.mates = [], [], []

    def send(self, source, slot, n, bits):
        peer = (self.docs, flip(self.me, bits))
        copy = remote(source, self.x_ref.at[slot], self.sems, n, peer)
        copy.start()
        return copy

    def begin(self):
        for rz in range(1, 4):
            source = self.low_ref.at[flip(self.me, 4 * rz) // 4]
            self.hops.append(self.send(source, self.me, rz, 4 * rz))
        self.own.start()
        source = self.low_ref.at[self.me // 4]
        self.across.append(self.send(source, self.me, 4, 2))
        self.mates.append(self.send(source, self.me, 8, 1))

    def forward(self, rz):
        self.hops[rz - 1].wait_recv()
        slot = flip(self.me, 4 * rz)
        self.across.append(self.send(self.x_ref.at[slot], slot, 4 + rz, 2))
        self.mates.append(self.send(self.x_ref.at[slot], slot, 8 + rz, 1))

    def from_beside(self):
        for rz in range(4):
            self.across[rz].wait_recv()
            slot = flip(flip(self.me, 4 * rz), 2)
            self.mates.append(self.send(self.x_ref.at[slot], slot, 12 + rz, 1))

    def arrived(self):
        for copy in self.mates:
            copy.wait_recv()
        self.own.wait()

    def finish(self):
        for copy in self.hops + self.across + self.mates:
            copy.wait_send()


class Slabs:
    def __init__(self, source, w_ref, sems, own_sem, docs_first=False):
        self.source, self.w_ref, self.sems = source, w_ref, sems
        self.docs, self.me = lax.axis_index("docs"), lax.axis_index("seq")
        self.plane, self.x, self.core = self.me // 4, (self.me // 2) % 2, self.me % 2
        beside, over = (self.docs, flip(self.me, 2)), (1 - self.docs, self.me)
        self.peers = (over, beside) if docs_first else (beside, over)
        if docs_first:
            self.near = ((self.docs, self.x), (1 - self.docs, self.x))
            self.far = ((self.docs, 1 - self.x), (1 - self.docs, 1 - self.x))
        else:
            self.near = ((self.docs, self.x), (self.docs, 1 - self.x))
            self.far = ((1 - self.docs, self.x), (1 - self.docs, 1 - self.x))
        self.mate = (self.docs, flip(self.me, 1))
        self.own = pltpu.make_async_copy(source, self.slot(self.near[0], self.plane), own_sem)

    def slot(self, at, z):
        return self.w_ref.at[self.core, 8 * at[0] + 2 * z + at[1]]

    def copy(self, at, z, own, send, recv, peer):
        slot = self.slot(at, z)
        return pltpu.make_async_remote_copy(
            self.source if own else slot,
            slot,
            self.sems.at[0, send],
            self.sems.at[1, recv],
            device_id=peer,
            device_id_type=MESH,
        )

    def line(self, z, own, step):
        peer = (self.docs, self.me + 4 * step)
        return self.copy(self.near[0], z, own, z + (0 if step > 0 else 4), z, peer)

    def first(self, z, own=False):
        return self.copy(self.near[0], z, own, 8 + z, 8 + z, self.peers[0])

    def second(self, z, n, own=False):
        return self.copy(self.near[n], z, own, 12 + 4 * n + z, 12 + 4 * n + z, self.peers[1])

    def core_copy(self, at, n, z, own=False):
        return self.copy(at, z, own, 20 + 4 * n + z, 20 + 4 * n + z, self.mate)

    def begin(self):
        self.own.start()
        for step in (1, -1):
            pl.when(self.has(self.plane + step))(self.line(self.plane, True, step).start)
        self.first(self.plane, True).start()
        self.core_copy(self.near[0], 0, self.plane, True).start()

    def has(self, z):
        return jnp.logical_and(z >= 0, z < PLANES)

    def each(self, distance, act):
        if distance == 0:
            act(self.plane, 0)
            return
        for step in (1, -1):
            z = self.plane - step * distance
            pl.when(self.has(z))(functools.partial(act, z, step))

    def from_line(self, distance):
        def act(z, step):
            self.line(z, False, step).wait_recv()
            pl.when(self.has(self.plane + step))(self.line(z, False, step).start)
            self.first(z).start()
            self.core_copy(self.near[0], 0, z).start()

        self.each(distance, act)

    def from_first(self, distance):
        def act(z, step):
            self.first(z).wait_recv()
            self.second(z, 0, distance == 0).start()
            self.second(z, 1).start()
            self.core_copy(self.near[1], 1, z).start()

        self.each(distance, act)

    def from_second(self, distance):
        def act(z, step):
            for n in range(2):
                self.second(z, n).wait_recv()
                self.core_copy(self.far[n], 2 + n, z).start()

        self.each(distance, act)

    def arrived(self):
        for z in range(PLANES):
            for n, at in enumerate(self.near + self.far):
                self.core_copy(at, n, z).wait_recv()
        self.own.wait()

    def finish(self):
        for z in range(PLANES):
            for step in (1, -1):
                sent = jnp.logical_and(
                    (self.plane - z) * step >= 0, self.has(self.plane + step)
                )
                pl.when(sent)(self.line(z, False, step).wait_send)
            self.first(z).wait_send()
            for n, at in enumerate(self.near + self.far):
                if n < 2:
                    self.second(z, n).wait_send()
                self.core_copy(at, n, z).wait_send()


class Rows:
    def __init__(self, source, w_ref, sems, own_sem):
        self.source, self.w_ref, self.sems = source, w_ref, sems
        self.docs, self.me = lax.axis_index("docs"), lax.axis_index("seq")
        self.over = (1 - self.docs, self.me)
        self.own = pltpu.make_async_copy(source, self.slot(self.me // 4), own_sem)
        self.hops, self.moved = [], []

    def slot(self, z):
        return self.w_ref.at[pl.ds(8 * self.docs + 2 * z, 2)]

    def begin(self):
        target = self.slot(self.me // 4)
        for rz in range(1, 4):
            peer = (self.docs, flip(self.me, 4 * rz))
            self.hops.append(remote(self.source, target, self.sems, rz, peer))
            self.hops[-1].start()
        self.own.start()
        self.moved.append(remote(self.source, target, self.sems, 4, self.over))
        self.moved[0].start()

    def forward(self, rz):
        self.hops[rz - 1].wait_recv()
        slot = self.slot(flip(self.me, 4 * rz) // 4)
        self.moved.append(remote(slot, slot, self.sems, 4 + rz, self.over))
        self.moved[-1].start()

    def arrived(self):
        for copy in self.moved:
            copy.wait_recv()
        self.own.wait()

    def finish(self):
        for copy in self.hops + self.moved:
            copy.wait_send()


class Collect:
    def __init__(self, keep_ref, send_ref, land, got_core, got_x, sum_x, near, sums, sems):
        self.keep_ref, self.send_ref, self.land, self.got_core = keep_ref, send_ref, land, got_core
        self.got_x, self.sum_x, self.near, self.sums, self.sems = got_x, sum_x, near, sums, sems
        self.docs, self.me = lax.axis_index("docs"), lax.axis_index("seq")
        self.order = (3, 2, 1, 0)
        self.first, self.across, self.hops = {}, {}, []

    def begin(self):
        mate = (self.docs, flip(self.me, 1))
        for rz in self.order:
            for n in (2 * rz + 1, 2 * rz):
                self.first[n] = remote(
                    self.send_ref.at[n], self.got_core.at[n], self.sems, n, mate
                )
                self.first[n].start()

    def along_x(self):
        beside = (self.docs, flip(self.me, 2))
        for rz in self.order:
            n = 2 * rz + 1
            self.first[n].wait_recv()
            self.sum_x[rz] = add_low(self.keep_ref[n], self.got_core[n])
            self.across[rz] = remote(
                self.sum_x.at[rz], self.got_x.at[rz], self.sems, 8 + rz, beside
            )
            self.across[rz].start()
            n = 2 * rz
            self.first[n].wait_recv()
            self.near[rz] = add_full(self.keep_ref[n], self.got_core[n])

    def along_z(self):
        plane = self.me // 4
        for rz in self.order:
            self.across[rz].wait_recv()
            total = add_low(self.near[rz], self.got_x[rz])
            if rz == 0:
                self.land[plane] = total
            else:
                self.sums[rz] = total
                peer = (self.docs, flip(self.me, 4 * rz))
                copy = remote(self.sums.at[rz], self.land.at[plane], self.sems, 12 + rz, peer)
                copy.start()
                self.hops.append(copy)

    def finish(self):
        for copy in self.hops:
            copy.wait_recv()
        for copy in list(self.first.values()) + list(self.across.values()) + self.hops:
            copy.wait_send()


class Exchange:
    def __init__(self, source, land, sems, own_sem):
        docs, me = lax.axis_index("docs"), lax.axis_index("seq")
        self.copies = []
        for bits in range(15, 0, -1):
            peer = flip(me, bits)
            self.copies.append(remote(source.at[peer], land.at[me], sems, bits, (docs, peer)))
        self.own = pltpu.make_async_copy(source.at[me], land.at[me], own_sem)

    def begin(self):
        for copy in self.copies:
            copy.start()
        self.own.start()

    def arrived(self):
        for copy in self.copies:
            copy.wait_recv()
        self.own.wait()

    def finish(self):
        for copy in self.copies:
            copy.wait_send()


class Line:
    PLACE = (0, 2, 1, 3)

    def __init__(self, own, from_left, from_right, sems):
        self.own, self.landing, self.sems = own, (from_left, from_right), sems
        self.docs, self.me = lax.axis_index("docs"), lax.axis_index("seq")
        self.plane = self.me // 4

    def copy(self, place, target, step):
        side = 0 if step > 0 else 1
        return pltpu.make_async_remote_copy(
            self.own.at[place],
            self.landing[side].at[target],
            self.sems.at[0, side, target],
            self.sems.at[1, side, target],
            device_id=(self.docs, self.me + 4 * step),
            device_id_type=MESH,
        )

    def at(self, plane, act):
        pl.when(self.plane == plane)(act)

    def begin(self, rz):
        for plane, step in ((0, 1), (3, -1)):
            self.at(plane, self.copy(self.PLACE[rz], plane ^ rz, step).start)

    def hop(self, number):
        for plane, target, step in (
            ((1, 3, 1), (2, 0, -1)),
            ((1, 0, -1), (2, 3, 1)),
            ((1, 2, 1), (2, 1, -1)),
        )[number]:
            place, side = self.PLACE[plane ^ target], 0 if step > 0 else 1

            def act(place=place, side=side, target=target, step=step):
                copy = self.copy(place, target, step)
                copy.wait_recv()
                self.own[place] = add_low(self.own[place], self.landing[side][target])
                copy.start()

            self.at(plane, act)

    def total(self, out_ref, rows):
        for plane in range(PLANES):

            def act(plane=plane):
                total = self.own[0, rows].astype(F32)
                for side, step in ((0, 1), (1, -1)):
                    if 0 <= plane - step < PLANES:
                        total = total + self.landing[side][plane, rows].astype(F32)
                out_ref[...] = total

            self.at(plane, act)

    def arrived(self):
        for plane in range(PLANES):

            def act(plane=plane):
                for step in (1, -1):
                    if 0 <= plane - step < PLANES:
                        self.copy(0, plane, step).wait_recv()

            self.at(plane, act)

    def finish(self):
        for plane in range(PLANES):

            def act(plane=plane):
                for target in range(PLANES):
                    step = 1 if target > plane else -1
                    if target != plane:
                        self.copy(self.PLACE[plane ^ target], target, step).wait_send()

            self.at(plane, act)


class Everywhere:
    def __init__(self, total, got, sems):
        self.total, self.got, self.sems = total, got, sems
        docs, me = lax.axis_index("docs"), lax.axis_index("seq")
        self.peers = [(docs, flip(me, bits)) for bits in (1, 2, 4, 8)] + [(1 - docs, me)]
        self.copies = []

    def step(self):
        n = len(self.copies)
        if n > 0:
            self.copies[-1].wait_recv()
            self.total[n] = self.total[n - 1] + self.got[n - 1]
        if n < len(self.peers):
            copy = remote(self.total.at[n], self.got.at[n], self.sems, n, self.peers[n])
            copy.start()
            self.copies.append(copy)

    def finish(self):
        for copy in self.copies:
            copy.wait_send()


class Rest:
    ORDER = (3, 1, 2, 0)

    def __init__(self, a_keep, a_send, b_keep, b_send, scr):
        self.a_keep, self.a_send, self.b_keep, self.b_send = a_keep, a_send, b_keep, b_send
        self.scr = scr
        docs, me = lax.axis_index("docs"), lax.axis_index("seq")
        self.beside, self.over = (docs, flip(me, 2)), (1 - docs, me)
        self.line = Line(scr.own, scr.left, scr.right, scr.line_sems)
        self.sent = []

    def copy(self, n, place):
        scr = self.scr
        source, target, peer = (
            (self.a_send.at[4 + place], scr.a_got.at[4 + place], self.over),
            (self.b_send.at[1, place], scr.b_got.at[1, place], self.beside),
            (self.a_send.at[place], scr.a_got.at[place], self.over),
            (self.b_send.at[0, place], scr.b_got.at[0, place], self.beside),
            (scr.a_far.at[place], scr.a_far_got.at[place], self.beside),
            (scr.b_far.at[place], scr.b_far_got.at[place], self.over),
        )[n]
        return remote(source, target, scr.rest_sems, 4 * n + place, peer)

    def start(self, n, place):
        self.sent.append(self.copy(n, place))
        self.sent[-1].start()

    def first(self, place):
        for n in range(4):
            self.start(n, place)

    def second(self, place):
        scr = self.scr
        self.copy(0, place).wait_recv()
        scr.a_far[place] = add_low(self.a_keep[4 + place], scr.a_got[4 + place])
        self.start(4, place)
        self.copy(1, place).wait_recv()
        scr.b_far[place] = add_low(self.b_keep[1, place], scr.b_got[1, place])
        self.start(5, place)

    def third(self, place):
        scr = self.scr
        self.copy(2, place).wait_recv()
        self.copy(4, place).wait_recv()
        near = add_full(self.a_keep[place], scr.a_got[place]) + scr.a_far_got[place].astype(F32)
        scr.own[place, :CUT] = near.astype(BF16)
        self.copy(3, place).wait_recv()
        self.copy(5, place).wait_recv()
        near = add_full(self.b_keep[0, place], scr.b_got[0, place])
        near = near + scr.b_far_got[place].astype(F32)
        scr.own[place, CUT:] = near.astype(BF16)
        if place > 0:
            self.line.begin(Line.PLACE[place])

    def finish(self):
        for copy in self.sent:
            copy.wait_send()
        self.line.finish()


class Route:
    def __init__(self, source, out_ref, sems):
        self.source, self.out_ref, self.sems = source, out_ref, sems
        self.docs, self.me = lax.axis_index("docs"), lax.axis_index("seq")

    def each(self, act_here, act_there):
        for t in range(3):
            local = 3 * (self.me // 4) + t
            number = 16 * (local // 4) + 4 * (self.me % 4) + local % 4
            owner, slot = number // 3, number % 3
            target = self.out_ref.at[slot]
            here = pltpu.make_async_copy(self.source.at[t], target, self.sems.at[2, slot])
            there = pltpu.make_async_remote_copy(
                self.source.at[t],
                target,
                self.sems.at[0, t],
                self.sems.at[1, slot],
                device_id=(self.docs, owner),
                device_id_type=MESH,
            )
            pl.when(owner == self.me)(functools.partial(act_here, here))
            pl.when(owner != self.me)(functools.partial(act_there, there))

    def begin(self):
        self.each(lambda copy: copy.start(), lambda copy: copy.start())

    def finish(self):
        self.each(lambda copy: copy.wait(), lambda copy: copy.wait_send())
        for slot in range(3):
            number = 3 * self.me + slot
            local = 4 * (number // 16) + number % 4
            source = 4 * (local // 3) + (number % 16) // 4
            target = self.out_ref.at[slot]
            wait = pltpu.make_async_copy(target, target, self.sems.at[1, slot]).wait
            pl.when(source != self.me)(wait)


def back_scratch(width):
    low = 432 - CUT
    sems = pltpu.SemaphoreType.DMA

    def vm(*shape, dtype=BF16):
        return pltpu.VMEM(shape, dtype)

    return dict(
        qkv=vm(1024, 576),
        weight=vm(CHIPS, 48, 576),
        x=vm(16, 64, width),
        a_keep=vm(8, CUT, 384),
        b_keep=vm(2, 4, low, 384),
        load_sems=sems((5,)),
        do=vm(16, 32, 384),
        do_sems=sems((2, 16)),
        do_own=sems,
        key=vm(3, 1024, 128),
        query=vm(3, 1024, 128),
        value=vm(3, 1024, 64),
        turned=vm(3, 64, 1024),
        side=vm(2, 3, 1024, 128),
        dkv=vm(3, 1024, 128, dtype=F32),
        dq=vm(1024 // BACK_QUERIES, 192, BACK_QUERIES, dtype=F32),
        dqkv=vm(1024, 576),
        rows=vm(2, 8, 64, width),
        land=vm(4, 64, width),
        got_core=vm(8, 64, width),
        got_x=vm(4, 64, width),
        sum_x=vm(4, 64, width),
        near=vm(4, 64, width, dtype=F32),
        sums=vm(4, 64, width),
        row_sems=sems((2, 16)),
        a_got=vm(8, CUT, 384),
        b_got=vm(2, 4, low, 384),
        a_far=vm(4, CUT, 384),
        a_far_got=vm(4, CUT, 384),
        b_far=vm(4, low, 384),
        b_far_got=vm(4, low, 384),
        rest_sems=sems((2, 24)),
        own=vm(4, 432, 384),
        left=vm(4, 432, 384),
        right=vm(4, 432, 384),
        line_sems=sems((2, 2, 4)),
        q_grad=vm(2, 4, 144, 384),
        q_got=vm(4, 144, 384),
        q_own=vm(4, 144, 384),
        q_land=vm(4, 144, 384),
        q_sems=sems((2, 4)),
        q_sum=vm(3, 48, 384, dtype=F32),
        route_sems=sems((3, 3)),
        gain_sum=vm(6, 8, width, dtype=F32),
        gain_got=vm(5, 8, width, dtype=F32),
        gain_sems=sems((2, 5)),
    )


def attend_back_kernel(names, last, *refs):
    feature_ref, qkv_ref, do_ref, x_ref, w_ref, a_keep, a_send, b_keep, b_send = refs[:9]
    gain_ref, rows_ref, rest_ref, out_ref, gain_out_ref = refs[9:14]
    scr = types.SimpleNamespace(**dict(zip(names, refs[14:])))
    docs, me = lax.axis_index("docs"), lax.axis_index("seq")
    plane = me // 4
    over = (1 - docs, me)
    loads = {}
    for n, (name, ref) in enumerate(
        dict(qkv=qkv_ref, weight=w_ref, a_keep=a_keep, b_keep=b_keep, x=x_ref).items()
    ):
        loads[name] = pltpu.make_async_copy(ref, getattr(scr, name), scr.load_sems.at[n])
        loads[name].start()
    greet([(docs, flip(me, bits)) for bits in range(15, 0, -1)] + [over])
    exchange = Exchange(do_ref, scr.do, scr.do_sems, scr.do_own)
    exchange.begin()
    rest = Rest(scr.a_keep, a_send, scr.b_keep, b_send, scr)
    rest.first(3)
    rest.first(1)
    gains = Everywhere(scr.gain_sum, scr.gain_got, scr.gain_sems)
    if last:
        scr.gain_sum[0] = gain_ref[...]
        gains.step()

    loads["qkv"].wait()
    qkv = scr.qkv[...]
    spread_heads(qkv, feature_ref, scr.key, scr.query)
    zero = jnp.zeros((1024, 64), BF16)
    for h in range(GROUP_HEADS):
        scr.value[h] = qkv[:, 128 * h + 64 : 128 * h + 128]
        scr.turned[h] = qkv[:, 128 * h : 128 * h + 64].T
        scr.side[0, h] = jnp.concatenate([scr.query[h, :, :64], zero], axis=1)
    loads["a_keep"].wait()
    loads["b_keep"].wait()
    exchange.arrived()
    grad_o = jnp.concatenate([halves_below(scr.do[n]) for n in range(16)], axis=0)
    for h in range(GROUP_HEADS):
        scr.side[1, h] = jnp.concatenate([zero, grad_o[:, 64 * h : 64 * h + 64]], axis=1)

    def part(n, h):
        at = slice(BACK_QUERIES * n, BACK_QUERIES * n + BACK_QUERIES)
        expo, rate = expo_columns(dot_nt(scr.key[h], scr.query[h, at, :]))
        probs = expo * rate
        grad_probs = dot_nt(scr.value[h], scr.side[1, h, at, :][:, 64:])
        delta = jnp.sum(probs * grad_probs, axis=0, keepdims=True)
        grad_scores = (probs * (grad_probs - delta)).astype(BF16)
        scr.dq[n, 64 * h : 64 * h + 64, :] = dot(scr.turned[h], grad_scores) * (HEAD**-0.5)
        dkv = dot(grad_scores, scr.side[0, h, at, :])
        dkv += dot(probs.astype(BF16), scr.side[1, h, at, :])
        if n == 0:
            scr.dkv[h] = dkv
        else:
            scr.dqkv[:, 128 * h : 128 * h + 128] = (scr.dkv[h] + dkv).astype(BF16)

    part(0, 0)
    rest.second(3)
    rest.first(2)
    part(0, 1)
    if last:
        gains.step()
    part(0, 2)
    rest.second(1)
    scr.dqkv[0:512, 384:576] = scr.dq[0].T.astype(BF16)
    part(1, 0)
    rest.third(3)
    part(1, 1)
    rest.second(2)
    part(1, 2)
    rest.third(1)
    rest.line.hop(0)
    if last:
        gains.step()
    scr.dqkv[512:1024, 384:576] = scr.dq[1].T.astype(BF16)
    loads["x"].wait()
    grad = dot_tn(scr.dqkv[...], scr.x[...].reshape(1024, scr.x.shape[-1]))
    order = [6, 7, 8, 0, 2, 4, 1, 3, 5]
    grad = jnp.concatenate([grad[64 * n : 64 * n + 64] for n in order], axis=0).astype(BF16)
    for quarter in range(PLANES):
        apart = flip(plane, quarter)
        place = (apart % 2) * 2 + apart // 2
        for side in range(2):
            at = docs if side == 0 else 1 - docs
            scr.q_grad[at, place] = grad[
                144 * quarter : 144 * quarter + 144, 384 * side : 384 * side + 384
            ]
    crossed = remote(scr.q_grad.at[1], scr.q_got, scr.q_sems, 0, over)
    crossed.start()
    rest.first(0)
    loads["weight"].wait()
    rows = Collect(
        scr.rows.at[0],
        scr.rows.at[1],
        scr.land,
        scr.got_core,
        scr.got_x,
        scr.sum_x,
        scr.near,
        scr.sums,
        scr.row_sems,
    )
    for half in (1, 0):
        part_rows = []
        for n in range(8):
            block = flip(me, (n // 2) * 4 + (n % 2) * 2 + half)
            part_rows.append(scr.dqkv[pl.ds(pl.multiple_of(block * 64, 64), 64), :])
        product = dot_nt(jnp.concatenate(part_rows, axis=0), scr.weight[...].reshape(-1, 576))
        scr.rows[half] = product.astype(BF16).reshape(scr.rows.shape[1:])
        if half == 1:
            rows.begin()
    rest.third(2)
    rest.line.hop(1)
    rows.along_x()
    if last:
        gains.step()
    crossed.wait_recv()
    turned = []
    for place in Rest.ORDER:
        rz = Line.PLACE[place]
        scr.q_own[place] = add_low(scr.q_grad[0, place], scr.q_got[place])
        if rz > 0:
            peer = (docs, flip(me, 4 * rz))
            turned.append(
                remote(scr.q_own.at[place], scr.q_land.at[place], scr.q_sems, place, peer)
            )
            turned[-1].start()
    rest.line.hop(2)
    rest.second(0)
    rows.along_z()
    if last:
        gains.step()
    for copy in turned:
        copy.wait_recv()
    total = scr.q_own[0].astype(F32)
    for place in range(1, PLANES):
        total = total + scr.q_land[place].astype(F32)
    scr.q_sum[...] = total.reshape(scr.q_sum.shape)
    route = Route(scr.q_sum, out_ref, scr.route_sems)
    route.begin()
    rest.third(0)
    if last:
        gains.step()
        gain_out_ref[...] = scr.gain_sum[5]
        gains.finish()
    else:
        gain_out_ref[...] = gain_ref[...]
    rest.line.arrived()
    rest.line.total(rest_ref, slice(0, 432))
    rows.finish()
    rows_ref[...] = scr.land[...]
    for piece in (exchange, rest, route):
        piece.finish()
    for copy in turned + [crossed]:
        copy.wait_send()


def attend_back(features, qkv, grad_o, x, weight, sums, gain_grads, last, number):
    width = x.shape[-1]
    scratch = back_scratch(width)
    return pl.pallas_call(
        functools.partial(attend_back_kernel, tuple(scratch), last),
        out_shape=(
            jax.ShapeDtypeStruct((PLANES, 64, width), BF16),
            jax.ShapeDtypeStruct((432, 384), F32),
            jax.ShapeDtypeStruct((3, 48, 384), F32),
            jax.ShapeDtypeStruct((8, width), F32),
        ),
        in_specs=[vmem()] + [hbm()] * 8 + [vmem()],
        out_specs=(vmem(), vmem(), hbm(), vmem()),
        scratch_shapes=list(scratch.values()),
        compiler_params=pltpu.CompilerParams(
            collective_id=number, has_side_effects=True, vmem_limit_bytes=56 * 2**20
        ),
        cost_estimate=pl.CostEstimate(
            flops=8 * 10**9, bytes_accessed=10 * 10**6, transcendentals=3 * 10**6
        ),
        name="attend_back",
    )(features, qkv, grad_o, x, weight, *sums, gain_grads)


def forward_scratch(width):
    sems = pltpu.SemaphoreType.DMA

    def vm(*shape, dtype=BF16):
        return pltpu.VMEM(shape, dtype)

    scratch = dict(
        x=vm(16, 64, width),
        weight=vm(CHIPS, 48, 576),
        qkv=vm(1024, 576),
        key=vm(3, 1024, 128),
        query=vm(3, 1024, 128),
        value=vm(3, 64, 1024),
        turned=vm(192, 1024, dtype=F32),
        o=vm(LAYERS, 16, 32, 384),
        o_got=vm(LAYERS, 16, 32, 384),
        mixed=vm(256, width),
        h1=vm(256, width, dtype=F32),
        up=vm(256, 4 * width, dtype=F32),
        h2=vm(256, width, dtype=F32),
        hidden=vm(256, width, dtype=F32),
        low=vm(4, 64, width),
        act=vm(256, 4 * width),
        wu=WEIGHT_SCRATCH[0],
        wd=WEIGHT_SCRATCH[1],
        wo=WEIGHT_SCRATCH[2],
        weight_sems=sems((3,)),
        load_sems=sems((3,)),
        gain_sum=vm(6, 8, width, dtype=F32),
        gain_got=vm(5, 8, width, dtype=F32),
        gain_sems=sems((2, 5)),
        own_sems=sems((2, 5)),
        save_sems=sems((2, 5)),
    )
    for layer in range(LAYERS):
        scratch[f"row_sems_{layer}"] = sems((2, 16))
        scratch[f"qkv_sems_{layer}"] = sems((2, 8))
        scratch[f"o_sems_{layer}"] = sems((2, 16))
        scratch[f"up_sems_{layer}"] = sems((2, 36))
        scratch[f"down_sems_{layer}"] = sems((2, 36))
    return scratch


def forward_kernel(names, *refs):
    info, feature_ref, tokens_ref, gain_ref = refs[:4]
    wq_refs, up_refs, down_refs = refs[4:6], refs[6:8], refs[8:10]
    saved_refs = (refs[10:16], refs[16:22])
    w_refs, wu_refs, wd_refs, gains_ref, result_ref = refs[22:24], refs[24:26], refs[26:28], refs[28], refs[29]
    scr = types.SimpleNamespace(**dict(zip(names, refs[30:])))
    docs, me = lax.axis_index("docs"), lax.axis_index("seq")
    pltpu.make_async_copy(tokens_ref, scr.low, scr.load_sems.at[2]).start()
    greet([(docs, flip(me, bits)) for bits in range(15, 0, -1)] + [(1 - docs, me)])
    gains = Everywhere(scr.gain_sum, scr.gain_got, scr.gain_sems)
    scr.gain_sum[0] = gain_ref[...]

    def sems(name, layer):
        return getattr(scr, f"{name}_sems_{layer}")

    qkvs, slabs = [], []
    for layer in range(LAYERS):
        own = scr.own_sems.at[layer]
        qkvs.append(Rows(wq_refs[layer], w_refs[layer], sems("qkv", layer), own.at[0]))
        slabs.append(
            [
                Slabs(up_refs[layer], wu_refs[layer], sems("up", layer), own.at[1]),
                Slabs(down_refs[layer], wd_refs[layer], sems("down", layer), own.at[2], True),
            ]
        )

    def spread(layer, source):
        x_ref = saved_refs[layer][0]
        return Spread(source, x_ref, sems("row", layer), scr.own_sems.at[layer, 3])

    def every(parts, step, *arguments):
        for part in parts:
            getattr(part, step)(*arguments)

    def move(layer, *steps):
        for step in steps:
            name = {"l": "from_line", "f": "from_first", "s": "from_second"}[step[0]]
            every(slabs[layer], name, int(step[1]))

    def save(layer, n, source):
        copy = pltpu.make_async_copy(source, saved_refs[layer][n + 1], scr.save_sems.at[layer, n])
        copy.start()
        return copy

    saves = []

    def attend(layer, rows, ticks):
        qkvs[layer].arrived()
        rows.arrived()
        load_x = pltpu.make_async_copy(saved_refs[layer][0], scr.x, scr.load_sems.at[0])
        load_w = pltpu.make_async_copy(
            w_refs[layer], scr.weight, scr.load_sems.at[1]
        )
        load_x.start()
        load_w.start()
        while saves:
            saves.pop().wait()
        load_x.wait()
        load_w.wait()
        scr.qkv[...] = dot(
            scr.x[...].reshape(1024, scr.x.shape[-1]), scr.weight[...].reshape(-1, 576)
        ).astype(BF16)
        saves.append(save(layer, 0, scr.qkv))
        qkv = scr.qkv[...]
        spread_heads(qkv, feature_ref, scr.key, scr.query)
        for h in range(GROUP_HEADS):
            scr.value[h] = qkv[:, 128 * h + 64 : 128 * h + 128].T
        exchange = Exchange(
            scr.o.at[layer], scr.o_got.at[layer], sems("o", layer), scr.own_sems.at[layer, 4]
        )
        for n in range(1024 // QUERIES):
            at = slice(QUERIES * n, QUERIES * n + QUERIES)
            for h in range(GROUP_HEADS):
                expo, rate = expo_columns(dot_nt(scr.key[h], scr.query[h, at, :]))
                scr.turned[64 * h : 64 * h + 64, at] = dot(
                    scr.value[h], (expo * rate).astype(BF16)
                )
                ticks.pop(0)()
            rows_o = scr.turned[:, at].T.astype(BF16)
            for m in range(QUERIES // 64):
                scr.o[layer, n * (QUERIES // 64) + m] = halves_beside(rows_o[64 * m : 64 * m + 64])
        exchange.begin()
        return exchange

    def feed(layer, exchange, ticks):
        exchange.arrived()
        every(slabs[layer], "arrived")
        load_ordered(
            (wu_refs[layer], wd_refs[layer]), scr.wu, scr.wd, scr.wo, scr.weight_sems
        )
        for k in range(PLANES):
            scr.mixed[64 * k : 64 * k + 64, :] = jnp.concatenate(
                [halves_below(scr.o_got[layer, 4 * k + g]) for g in range(GROUPS)], axis=1
            )
        saves.append(save(layer, 1, scr.mixed))
        mixed = scr.mixed[...]
        gain = scr.gain_sum[5, 2 * layer : 2 * layer + 2]
        ticks.pop(0)()
        wait_weight(scr.wo, scr.weight_sems.at[0])
        attended = jnp.concatenate(
            [dot(mixed, scr.wo[side].reshape(768, 384)) for side in range(2)], axis=1
        )
        before = scr.low[...].reshape(256, -1).astype(F32) if layer == 0 else scr.hidden[...]
        h1 = before + attended
        scr.h1[...] = h1
        saves.append(save(layer, 2, scr.h1))
        x1 = norm_parts(h1)[0] * gain[0:1, :]
        x1_low = x1.astype(BF16)
        wait_weight(scr.wu, scr.weight_sems.at[1])
        for side in range(2):
            for part in range(3):
                at = 1536 * side + 512 * part
                up = dot(x1_low, scr.wu[side, :, :, 512 * part : 512 * part + 512].reshape(768, 512))
                scr.up[:, at : at + 512] = up
                scr.act[:, at : at + 512] = gelu_parts(up)[0].astype(BF16)
            ticks.pop(0)()
        saves.append(save(layer, 3, scr.up))
        wait_weight(scr.wd, scr.weight_sems.at[2])
        h2 = x1 + dot(scr.act[...], scr.wd[...].reshape(3072, 768))
        scr.h2[...] = h2
        saves.append(save(layer, 4, scr.h2))
        out = jnp.where(inside_rows(info), norm_parts(h2)[0] * gain[1:2, :], 0.0)
        low = out.astype(BF16)
        if layer == 0:
            scr.hidden[...] = out
            scr.low[...] = low.reshape(scr.low.shape)
        else:
            result_ref[...] = low.reshape(result_ref.shape)

    every(slabs[0], "begin")
    gains.step()
    move(0, "l1", "f0")
    rows_0 = spread(0, tokens_ref)
    rows_0.begin()
    qkvs[0].begin()
    gains.step()
    move(0, "l2", "f1")
    for rz in range(1, 4):
        rows_0.forward(rz)
    for rz in range(1, 4):
        qkvs[0].forward(rz)
    rows_0.from_beside()
    gains.step()
    pltpu.make_async_copy(tokens_ref, scr.low, scr.load_sems.at[2]).wait()

    def begin_second():
        every(slabs[1], "begin")
        qkvs[1].begin()

    def nothing():
        pass

    exchange_0 = attend(
        0,
        rows_0,
        [
            lambda: move(0, "l3"),
            lambda: move(0, "f2"),
            lambda: move(0, "s0"),
            lambda: move(0, "f3"),
            gains.step,
            begin_second,
        ],
    )
    move(0, "s1")
    gains.step()
    move(0, "s2")
    move(1, "l1")
    move(0, "s3")
    gains.step()
    gains_ref[...] = scr.gain_sum[5]
    feed(0, exchange_0, [lambda: move(1, "f0"), nothing, lambda: move(1, "l2")])
    rows_1 = spread(1, scr.low)
    rows_1.begin()
    for rz in range(1, 4):
        qkvs[1].forward(rz)
    move(1, "f1")
    for rz in range(1, 4):
        rows_1.forward(rz)
    move(1, "l3")
    rows_1.from_beside()
    exchange_1 = attend(
        1,
        rows_1,
        [
            lambda: move(1, "f2"),
            lambda: move(1, "s0"),
            lambda: move(1, "f3"),
            nothing,
            lambda: move(1, "s1"),
            nothing,
        ],
    )
    move(1, "s2", "s3")
    feed(1, exchange_1, [nothing] * 3)
    for copy in saves:
        copy.wait()
    every([rows_0, rows_1, exchange_0, exchange_1, gains] + qkvs + slabs[0] + slabs[1], "finish")


def forward(info, features, tokens, gain, wq, parts, number):
    width = tokens.shape[-1]
    scratch = forward_scratch(width)

    def out(*shape, dtype=BF16):
        return jax.ShapeDtypeStruct(shape, dtype)

    saved = [
        out(16, 64, width),
        out(1024, 576),
        out(256, width),
        out(256, width, dtype=F32),
        out(256, 4 * width, dtype=F32),
        out(256, width, dtype=F32),
    ]
    shapes = saved + saved + [out(CHIPS, 48, 576)] * 2
    shapes += [out(2, CHIPS, 48, 1536)] * 2 + [out(2, CHIPS, 48, 1920)] * 2
    shapes += [out(8, width, dtype=F32), out(PLANES, 64, width)]
    return pl.pallas_call(
        functools.partial(forward_kernel, tuple(scratch)),
        out_shape=tuple(shapes),
        in_specs=[smem(), vmem(), hbm(), vmem()] + [hbm()] * 6,
        out_specs=tuple([hbm()] * (len(shapes) - 2) + [vmem(), vmem()]),
        scratch_shapes=list(scratch.values()),
        compiler_params=pltpu.CompilerParams(
            collective_id=number, has_side_effects=True, vmem_limit_bytes=58 * 2**20
        ),
        name="forward",
    )(info, features, tokens, gain, *wq, *(part[0] for part in parts), *(part[1] for part in parts))


def pick(stack, index):
    return lax.dynamic_index_in_dim(stack, index, 0, keepdims=False)


def pack_qkv(shards, me, core):
    rows = shards.shape[1]
    parts = shards.reshape(LAYERS, rows, 3, GROUPS, GROUP_HEADS, HEAD)
    pairs = jnp.transpose(parts[:, :, 1:], (3, 0, 1, 4, 2, 5)).reshape(GROUPS, LAYERS, rows, 384)
    query = jnp.transpose(parts[:, :, 0], (2, 0, 1, 3, 4)).reshape(GROUPS, LAYERS, rows, 192)
    packed = jnp.concatenate([pairs, query], axis=3)
    group = me & 3
    got = [pick(packed, group)] + [swap(pick(packed, group ^ r), r) for r in range(1, 4)]

    def in_order(own, other):
        return jnp.where(
            core == 0,
            jnp.concatenate([own, other], axis=1),
            jnp.concatenate([other, own], axis=1),
        )

    here, there = in_order(got[0], got[1]), in_order(got[2], got[3])
    both = jnp.where(
        (me >> 1) & 1 == 0,
        jnp.stack([here, there], axis=1),
        jnp.stack([there, here], axis=1),
    )
    return [both[layer] for layer in range(LAYERS)]


def pack_rest(out_weight, up_weight, down_weight, core):
    def mine(shard, side):
        half = shard.shape[2] // 2
        return lax.dynamic_slice_in_dim(shard, side * half, half, axis=2)

    def both(side):
        return jnp.concatenate([mine(up_weight, side), mine(out_weight, side)], axis=2)

    own, got = both(core), swap(both(1 - core), 1)
    rows = jnp.where(
        core == 0,
        jnp.concatenate([own, got], axis=1),
        jnp.concatenate([got, own], axis=1),
    )
    parts = []
    for layer in range(LAYERS):
        up, out = rows[layer, :, :1536], rows[layer, :, 1536:]
        down = [down_weight[layer, :48], down_weight[layer, 48:], out]
        parts.append((up, jnp.concatenate(down, axis=1)))
    return parts


def add_low(first, second):
    return (first.astype(F32) + second.astype(F32)).astype(BF16)


def add_full(first, second):
    return first.astype(F32) + second.astype(F32)


def split_rest(total):
    down = total[240:].reshape(4, 48, 384)
    return (
        total[192:240].T,
        total[:192].T,
        jnp.transpose(down, (0, 2, 1)).reshape(1536, 48),
    )


def local_two_by_sixteen(
    tokens,
    qkv_weight,
    out_weight,
    up_weight,
    down_weight,
    norm_gains,
    doc_lengths,
    global_ids,
    random_ids,
    cotangent,
):
    docs_dev, block, width = tokens.shape
    me = lax.axis_index("seq").astype(jnp.int32)
    docs = lax.axis_index("docs").astype(jnp.int32)
    plane, core = me >> 2, me & 1
    chip = docs * 8 + (me >> 1)
    info = jnp.concatenate(
        [
            jnp.stack(
                [me, chip, pick(doc_lengths, plane), plane, docs, core, jnp.zeros_like(me), chip]
            ),
            doc_lengths,
        ]
    )
    features = key_features(
        lax.dynamic_index_in_dim(random_ids, plane, 1, keepdims=False),
        pick(global_ids, plane),
        pick(doc_lengths, plane),
    )

    wq = pack_qkv(qkv_weight, me, core)
    parts = pack_rest(out_weight, up_weight, down_weight, core)
    share = width // 32
    own_gains = lax.dynamic_update_slice(
        jnp.zeros((8, width), F32),
        norm_gains.reshape(2 * LAYERS, share).astype(F32),
        (jnp.zeros((), jnp.int32), (docs * 16 + me) * share),
    )
    made = forward(info, features, tokens, own_gains, wq, parts, 0)
    held, weights = (made[:6], made[6:12]), made[12:14]
    rest = list(zip(made[14:16], made[16:18]))
    gain = (made[18][0:2], made[18][2:4])
    base, grad_o, gain_1, *sums = feed_back(
        info, cotangent, None, gain[1], held[1][2:], rest[1], 1
    )
    extra, rest_grads_1, qkv_1, gain_1 = attend_back(
        features,
        held[1][1],
        grad_o,
        held[1][0],
        weights[1],
        sums,
        jnp.pad(gain_1, ((2, 4), (0, 0))),
        False,
        2,
    )
    base, grad_o, gain_0, *sums = feed_back(info, base, extra, gain[0], held[0][2:], rest[0], 3)
    extra, rest_grads, qkv_0, gain_grads = attend_back(
        features,
        held[0][1],
        grad_o,
        held[0][0],
        weights[0],
        sums,
        gain_1 + jnp.pad(gain_0, ((0, 6), (0, 0))),
        True,
        4,
    )
    grad_tokens = base.reshape(docs_dev, block, width) + extra.astype(F32)
    gain_grads = lax.dynamic_slice_in_dim(gain_grads, (docs * 16 + me) * share, share, axis=1)
    rest = [split_rest(part) for part in (rest_grads, rest_grads_1)]
    qkv_grads = jnp.stack([qkv_0, qkv_1])
    return (
        made[19],
        grad_tokens,
        jnp.transpose(qkv_grads, (0, 3, 1, 2)).reshape(LAYERS, 384, 144),
        *(jnp.stack(pair) for pair in zip(*rest)),
        gain_grads[:4].reshape(LAYERS, 2, share),
    )


def solution(mesh):
    def local(*args):
        docs_dev, _, width = args[0].shape
        if fits(mesh, docs_dev, width // HEAD):
            return local_two_by_sixteen(*args)
        return local_any_mesh(*args)

    return jax.shard_map(
        local,
        mesh=mesh,
        in_specs=(
            P("docs", "seq", None),
            P(None, ("docs", "seq"), None),
            P(None, ("docs", "seq"), None),
            P(None, ("docs", "seq"), None),
            P(None, ("docs", "seq"), None),
            P(None, None, ("docs", "seq")),
            P("docs"),
            P("docs", None),
            P(None, "docs", None),
            P("docs", "seq", None),
        ),
        out_specs=(
            P("docs", "seq", None),
            P("docs", "seq", None),
            P(None, "docs", "seq"),
            P(None, "docs", "seq"),
            P(None, "docs", "seq"),
            P(None, "docs", "seq"),
            P(None, None, ("docs", "seq")),
        ),
        check_vma=False,
    )
```

```python
import functools
import types

import jax
import jax.numpy as jnp
from jax import lax
from jax.experimental import pallas as pl
from jax.experimental.pallas import tpu as pltpu
from jax.sharding import PartitionSpec as P

HEAD = 64
RAND = 3
GLOB = 2
LAYERS = 2


NEGATIVE = -1e30
EPSILON = 1e-05


def with_halo(cells, sides, width):
    for axis, dim in sides:
        count = lax.axis_size(axis)
        head = lax.slice_in_dim(cells, 0, width, axis=dim)
        tail = lax.slice_in_dim(cells, cells.shape[dim] - width, cells.shape[dim], axis=dim)
        cells = jnp.concatenate(
            [
                lax.ppermute(tail, axis, [(i, (i + 1) % count) for i in range(count)]),
                cells,
                lax.ppermute(head, axis, [((i + 1) % count, i) for i in range(count)]),
            ],
            axis=dim,
        )
    return cells


def combined_all(value, axis, join):
    pieces = jax.tree.map(lambda part: lax.all_gather(part, axis), value)
    head = jax.tree.map(lambda part: part[0], pieces)
    tail = jax.tree.map(lambda part: part[1:], pieces)
    so_far, _ = lax.scan(lambda so_far, piece: (join(so_far, piece), None), head, tail)
    return so_far


def norm_rows(values, gain):
    centre = values - jnp.mean(values, axis=-1, keepdims=True)
    spread = jnp.mean(centre * centre, axis=-1, keepdims=True)
    return centre * lax.rsqrt(spread + EPSILON) * gain


def gelu_tanh(values):
    return jax.nn.gelu(values, approximate=True)


def earlier_equal(values):
    length = values.shape[-1]
    order = jnp.arange(length, dtype=jnp.int32)
    before = order[None, :] < order[:, None]
    same = values[..., :, None] == values[..., None, :]
    return jnp.sum(jnp.logical_and(same, before), axis=-1)


def merge_stats(first, second):
    highest = jnp.maximum(first[0], second[0])
    return (
        highest,
        first[1] * jnp.exp(first[0] - highest) + second[1] * jnp.exp(second[0] - highest),
    )


def sparse_probs(query, key_part, key_inside, scale):
    scores = (
        jnp.einsum("kbhd,kjhd->khbj", query, key_part, preferred_element_type=jnp.float32) * scale
    )
    scores = jnp.where(key_inside[:, None, None, :], scores, NEGATIVE)
    expo = jnp.exp(scores - jnp.max(scores, axis=-1, keepdims=True))
    return expo / jnp.sum(expo, axis=-1, keepdims=True)


def global_scores(global_query, local_keys, inside, scale):
    scores = (
        jnp.einsum(
            "ksbhd,kjhd->kshbj", global_query, local_keys, preferred_element_type=jnp.float32
        )
        * scale
    )
    return jnp.where(inside[:, None, None, None, :], scores, NEGATIVE)


def local_any_mesh(
    tokens,
    qkv_weight,
    out_weight,
    up_weight,
    down_weight,
    norm_gains,
    doc_lengths,
    global_ids,
    random_ids,
    cotangent,
):
    nseq = lax.axis_size("seq")
    device = lax.axis_index("seq")
    docs_dev, block, width = tokens.shape
    count = docs_dev * block
    heads = width // HEAD
    scale = HEAD ** (-0.5)
    capacity = max(2, (docs_dev * RAND + nseq - 1) // nseq)
    global_capacity = (docs_dev * GLOB + nseq - 1) // nseq
    entries = docs_dev * RAND
    global_entries = docs_dev * GLOB
    offsets = jnp.arange(block, dtype=jnp.int32)
    inside = (device * block + offsets)[None, :] < doc_lengths[:, None]
    live_rows = inside.reshape(count, 1)
    wanted = random_ids.reshape(nseq, entries)
    wanted_rank = earlier_equal(wanted)
    slot_ids = jnp.arange(capacity, dtype=jnp.int32)
    hits = jnp.logical_and((wanted == device)[:, :, None], wanted_rank[:, :, None] == slot_ids)
    hits = jnp.any(hits.reshape(nseq, docs_dev, RAND, capacity), axis=2)
    hits = jnp.transpose(hits, (0, 2, 1))
    doc_ids = jnp.arange(docs_dev, dtype=jnp.int32)
    send_doc = jnp.sum(jnp.where(hits, doc_ids, 0), axis=2)
    send_live = jnp.any(hits, axis=2)
    owner_pick = hits.astype(jnp.float32)
    listed_here = lax.dynamic_index_in_dim(wanted, device, 0, keepdims=False)
    listed_rank = lax.dynamic_index_in_dim(wanted_rank, device, 0, keepdims=False)
    fetch_slot = listed_here * capacity + listed_rank
    global_block = global_ids.reshape(global_entries)
    global_rank = earlier_equal(global_block)
    global_slot = global_block * global_capacity + global_rank
    own_entry = global_block == device
    owned = jnp.logical_and(
        own_entry[:, None], global_rank[:, None] == jnp.arange(global_capacity, dtype=jnp.int32)
    )
    entry_doc = jnp.arange(global_entries, dtype=jnp.int32) // GLOB
    global_send_doc = jnp.sum(jnp.where(owned, entry_doc[:, None], 0), axis=0)
    global_send_live = jnp.any(owned, axis=0)
    own_flag = jnp.any(own_entry.reshape(docs_dev, GLOB), axis=1)
    own_slot = jnp.sum(jnp.where(own_entry, global_rank, 0).reshape(docs_dev, GLOB), axis=1)
    neighbours = jnp.stack([(device - 1) % nseq, device, (device + 1) % nseq])
    key_blocks = jnp.concatenate(
        [
            jnp.broadcast_to(neighbours[None, :], (docs_dev, 3)),
            listed_here.reshape(docs_dev, RAND),
            global_ids,
        ],
        axis=1,
    )
    span = key_blocks.shape[1] * block
    key_inside = (key_blocks[:, :, None] * block + offsets < doc_lengths[:, None, None]).reshape(
        docs_dev, span
    )
    keep_local = inside[:, None, None, None, :]
    hidden = tokens.reshape(count, width).astype(jnp.float32)
    held = []
    for layer in range(LAYERS):
        weights = (
            lax.all_gather(qkv_weight[layer], ("docs", "seq"), axis=0, tiled=True),
            lax.all_gather(out_weight[layer], ("docs", "seq"), axis=0, tiled=True),
            lax.all_gather(up_weight[layer], ("docs", "seq"), axis=0, tiled=True),
            lax.all_gather(down_weight[layer], ("docs", "seq"), axis=0, tiled=True),
            lax.all_gather(norm_gains[layer], ("docs", "seq"), axis=1, tiled=True),
        )
        weight_qkv, weight_out, weight_up, weight_down, gain_pair = weights
        gain_pair = gain_pair.astype(jnp.float32)
        lowered = hidden.astype(jnp.bfloat16)
        projected = (
            jnp.dot(lowered, weight_qkv, preferred_element_type=jnp.float32)
            .astype(jnp.bfloat16)
            .reshape(docs_dev, block, 3 * width)
        )
        pairs = projected[:, :, width:]
        window = with_halo(pairs, (("seq", 1),), block)
        outgoing = jnp.where(
            send_live[:, :, None, None],
            jnp.take(pairs, send_doc, axis=0),
            jnp.zeros((), jnp.bfloat16),
        )
        incoming = lax.all_to_all(outgoing, "seq", split_axis=0, concat_axis=0, tiled=True)
        fetched = jnp.take(
            incoming.reshape(nseq * capacity, block, 2 * width), fetch_slot, axis=0
        ).reshape(docs_dev, RAND * block, 2 * width)
        global_send = jnp.where(
            global_send_live[:, None, None],
            jnp.take(projected, global_send_doc, axis=0),
            jnp.zeros((), jnp.bfloat16),
        )
        gathered = lax.all_gather(global_send, "seq", axis=0, tiled=True)
        global_picked = jnp.take(gathered, global_slot, axis=0).reshape(
            docs_dev, GLOB, block, 3 * width
        )
        global_query = global_picked[..., :width].reshape(docs_dev, GLOB, block, heads, HEAD)
        listed_pairs = jnp.concatenate(
            [
                window,
                fetched,
                global_picked[..., width:].reshape(docs_dev, GLOB * block, 2 * width),
            ],
            axis=1,
        )
        query = projected[:, :, :width].reshape(docs_dev, block, heads, HEAD)
        key_part = listed_pairs[:, :, :width].reshape(docs_dev, span, heads, HEAD)
        value_part = listed_pairs[:, :, width:].reshape(docs_dev, span, heads, HEAD)
        probs = sparse_probs(query, key_part, key_inside, scale)
        mixed = jnp.einsum(
            "khbj,kjhd->kbhd",
            probs.astype(jnp.bfloat16),
            value_part,
            preferred_element_type=jnp.float32,
        )
        local_keys = projected[:, :, width : 2 * width].reshape(docs_dev, block, heads, HEAD)
        local_values = projected[:, :, 2 * width :].reshape(docs_dev, block, heads, HEAD)
        wide_scores = global_scores(global_query, local_keys, inside, scale)
        global_top = jnp.max(wide_scores, axis=-1)
        global_total = jnp.sum(
            jnp.where(keep_local, jnp.exp(wide_scores - global_top[..., None]), 0.0), axis=-1
        )
        global_top, global_total = combined_all((global_top, global_total), "seq", merge_stats)
        wide_probs = (
            jnp.where(keep_local, jnp.exp(wide_scores - global_top[..., None]), 0.0)
            / global_total[..., None]
        )
        wide_part = jnp.einsum(
            "kshbj,kjhd->ksbhd",
            wide_probs.astype(jnp.bfloat16),
            local_values,
            preferred_element_type=jnp.float32,
        )
        wide_buffer = (
            jnp.zeros((nseq * global_capacity, block, width), jnp.float32)
            .at[global_slot]
            .set(wide_part.reshape(global_entries, block, width))
        )
        wide_sum = lax.psum_scatter(wide_buffer, "seq", scatter_dimension=0, tiled=True)
        attended = jnp.where(
            own_flag[:, None, None],
            jnp.take(wide_sum, own_slot, axis=0),
            mixed.reshape(docs_dev, block, width),
        )
        attended = attended.reshape(count, width).astype(jnp.bfloat16)
        after_attn = hidden + jnp.dot(attended, weight_out, preferred_element_type=jnp.float32)
        normed = norm_rows(after_attn, gain_pair[0])
        normed_low = normed.astype(jnp.bfloat16)
        up_values = jnp.dot(normed_low, weight_up, preferred_element_type=jnp.float32)
        activated = gelu_tanh(up_values).astype(jnp.bfloat16)
        after_ffn = normed + jnp.dot(activated, weight_down, preferred_element_type=jnp.float32)
        held.append(
            (
                weights,
                lowered,
                projected,
                listed_pairs,
                global_query,
                global_top,
                global_total,
                attended,
                after_attn,
                normed_low,
                up_values,
                activated,
                after_ffn,
            )
        )
        hidden = jnp.where(live_rows, norm_rows(after_ffn, gain_pair[1]), 0.0)
    gradient = cotangent.reshape(count, width).astype(jnp.float32)
    layer_grads = []
    for layer in reversed(range(LAYERS)):
        (
            weights,
            lowered,
            projected,
            listed_pairs,
            global_query,
            global_top,
            global_total,
            attended,
            after_attn,
            normed_low,
            up_values,
            activated,
            after_ffn,
        ) = held[layer]
        weights = (
            lax.all_gather(qkv_weight[layer], ("docs", "seq"), axis=0, tiled=True),
            lax.all_gather(out_weight[layer], ("docs", "seq"), axis=0, tiled=True),
            lax.all_gather(up_weight[layer], ("docs", "seq"), axis=0, tiled=True),
            lax.all_gather(down_weight[layer], ("docs", "seq"), axis=0, tiled=True),
            lax.all_gather(norm_gains[layer], ("docs", "seq"), axis=1, tiled=True),
        )
        weight_qkv, weight_out, weight_up, weight_down, gain_pair = weights
        gain_pair = gain_pair.astype(jnp.float32)
        gradient = jnp.where(live_rows, gradient, 0.0)
        grad_ffn, grad_gain_out = jax.vjp(norm_rows, after_ffn, gain_pair[1])[1](gradient)
        grad_down_low = grad_ffn.astype(jnp.bfloat16)
        grad_down_layer = jnp.einsum(
            "rf,rd->fd", activated, grad_down_low, preferred_element_type=jnp.float32
        )
        grad_activated = jnp.einsum(
            "rd,fd->rf", grad_down_low, weight_down, preferred_element_type=jnp.float32
        )
        grad_up_low = jax.vjp(gelu_tanh, up_values)[1](grad_activated)[0].astype(jnp.bfloat16)
        grad_up_layer = jnp.einsum(
            "rd,rf->df", normed_low, grad_up_low, preferred_element_type=jnp.float32
        )
        grad_normed = grad_ffn + jnp.einsum(
            "rf,df->rd", grad_up_low, weight_up, preferred_element_type=jnp.float32
        )
        grad_attn, grad_gain_mid = jax.vjp(norm_rows, after_attn, gain_pair[0])[1](grad_normed)
        grad_attn_low = grad_attn.astype(jnp.bfloat16)
        grad_out_layer = jnp.einsum(
            "rd,re->de", attended, grad_attn_low, preferred_element_type=jnp.float32
        )
        grad_mixed = (
            jnp.einsum("re,de->rd", grad_attn_low, weight_out, preferred_element_type=jnp.float32)
            .astype(jnp.bfloat16)
            .reshape(docs_dev, block, width)
        )
        query = projected[:, :, :width].reshape(docs_dev, block, heads, HEAD)
        key_part = listed_pairs[:, :, :width].reshape(docs_dev, span, heads, HEAD)
        value_part = listed_pairs[:, :, width:].reshape(docs_dev, span, heads, HEAD)
        probs = sparse_probs(query, key_part, key_inside, scale)
        grad_sparse = jnp.where(
            own_flag[:, None, None], jnp.zeros((), jnp.bfloat16), grad_mixed
        ).reshape(docs_dev, block, heads, HEAD)
        grad_probs = jnp.einsum(
            "kbhd,kjhd->khbj", grad_sparse, value_part, preferred_element_type=jnp.float32
        )
        delta = jnp.sum(probs * grad_probs, axis=-1, keepdims=True)
        grad_scores = (probs * (grad_probs - delta)).astype(jnp.bfloat16)
        grad_query = (
            jnp.einsum("khbj,kjhd->kbhd", grad_scores, key_part, preferred_element_type=jnp.float32)
            * scale
        )
        grad_key_part = (
            jnp.einsum("khbj,kbhd->kjhd", grad_scores, query, preferred_element_type=jnp.float32)
            * scale
        )
        grad_value_part = jnp.einsum(
            "khbj,kbhd->kjhd",
            probs.astype(jnp.bfloat16),
            grad_sparse,
            preferred_element_type=jnp.float32,
        )
        grad_listed = jnp.concatenate(
            [
                grad_key_part.reshape(docs_dev, span, width),
                grad_value_part.reshape(docs_dev, span, width),
            ],
            axis=2,
        )
        wide_out = jnp.where(
            global_send_live[:, None, None],
            jnp.take(grad_mixed, global_send_doc, axis=0),
            jnp.zeros((), jnp.bfloat16),
        )
        wide_all = lax.all_gather(wide_out, "seq", axis=0, tiled=True)
        wide_grad = jnp.take(wide_all, global_slot, axis=0).reshape(
            docs_dev, GLOB, block, heads, HEAD
        )
        local_keys = projected[:, :, width : 2 * width].reshape(docs_dev, block, heads, HEAD)
        local_values = projected[:, :, 2 * width :].reshape(docs_dev, block, heads, HEAD)
        wide_scores = global_scores(global_query, local_keys, inside, scale)
        wide_probs = (
            jnp.where(keep_local, jnp.exp(wide_scores - global_top[..., None]), 0.0)
            / global_total[..., None]
        )
        wide_grad_probs = jnp.einsum(
            "ksbhd,kjhd->kshbj", wide_grad, local_values, preferred_element_type=jnp.float32
        )
        wide_delta = lax.psum(jnp.sum(wide_probs * wide_grad_probs, axis=-1), "seq")
        wide_grad_scores = (wide_probs * (wide_grad_probs - wide_delta[..., None])).astype(
            jnp.bfloat16
        )
        wide_grad_query = (
            jnp.einsum(
                "kshbj,kjhd->ksbhd",
                wide_grad_scores,
                local_keys,
                preferred_element_type=jnp.float32,
            )
            * scale
        )
        wide_grad_keys = (
            jnp.einsum(
                "kshbj,ksbhd->kjhd",
                wide_grad_scores,
                global_query,
                preferred_element_type=jnp.float32,
            )
            * scale
        )
        wide_grad_values = jnp.einsum(
            "kshbj,ksbhd->kjhd",
            wide_probs.astype(jnp.bfloat16),
            wide_grad,
            preferred_element_type=jnp.float32,
        )
        global_grads = jnp.concatenate(
            [
                wide_grad_query.reshape(global_entries, block, width),
                grad_listed[:, (3 + RAND) * block :, :].reshape(global_entries, block, 2 * width),
            ],
            axis=2,
        )
        global_buffer = (
            jnp.zeros((nseq * global_capacity, block, 3 * width), jnp.float32)
            .at[global_slot]
            .set(global_grads)
        )
        global_share = lax.psum_scatter(global_buffer, "seq", scatter_dimension=0, tiled=True)
        global_mine = jnp.where(
            own_flag[:, None, None], jnp.take(global_share, own_slot, axis=0), 0.0
        )
        grad_fetched = grad_listed[:, 3 * block : (3 + RAND) * block, :].reshape(
            entries, block, 2 * width
        )
        back_out = (
            jnp.zeros((nseq * capacity, block, 2 * width), jnp.float32)
            .at[fetch_slot]
            .set(grad_fetched)
            .reshape(nseq, capacity, block, 2 * width)
        )
        back_in = lax.all_to_all(back_out, "seq", split_axis=0, concat_axis=0, tiled=True)
        grad_random = jnp.einsum(
            "dck,dcbf->kbf", owner_pick, back_in, precision=lax.Precision.HIGHEST
        )
        grad_window = grad_listed[:, : 3 * block, :]
        edges = jnp.concatenate([grad_window[:, :block], grad_window[:, 2 * block :]], axis=1)
        beside_all = with_halo(edges, (("seq", 1),), block)
        grad_pairs = (
            grad_window[:, block : 2 * block]
            + beside_all[:, :block]
            + beside_all[:, 3 * block :]
            + grad_random
            + global_mine[:, :, width:]
        )
        grad_pairs = grad_pairs + jnp.concatenate(
            [
                wide_grad_keys.reshape(docs_dev, block, width),
                wide_grad_values.reshape(docs_dev, block, width),
            ],
            axis=2,
        )
        grad_queries = grad_query.reshape(docs_dev, block, width) + global_mine[:, :, :width]
        grad_projected = (
            jnp.concatenate([grad_queries, grad_pairs], axis=2)
            .reshape(count, 3 * width)
            .astype(jnp.bfloat16)
        )
        grad_qkv_layer = jnp.einsum(
            "rd,re->de", lowered, grad_projected, preferred_element_type=jnp.float32
        )
        gradient = grad_attn + jnp.einsum(
            "re,de->rd", grad_projected, weight_qkv, preferred_element_type=jnp.float32
        )
        group_shares = (
            lax.psum_scatter(grad_qkv_layer, "docs", scatter_dimension=0, tiled=True),
            lax.psum_scatter(grad_out_layer, "docs", scatter_dimension=0, tiled=True),
            lax.psum_scatter(grad_up_layer, "docs", scatter_dimension=0, tiled=True),
            lax.psum_scatter(grad_down_layer, "docs", scatter_dimension=0, tiled=True),
            lax.psum_scatter(
                jnp.stack([grad_gain_mid, grad_gain_out]), "docs", scatter_dimension=1, tiled=True
            ),
        )
        shares = (
            lax.psum_scatter(group_shares[0], "seq", scatter_dimension=1, tiled=True),
            lax.psum_scatter(group_shares[1], "seq", scatter_dimension=1, tiled=True),
            lax.psum_scatter(group_shares[2], "seq", scatter_dimension=1, tiled=True),
            lax.psum_scatter(group_shares[3], "seq", scatter_dimension=1, tiled=True),
            lax.psum_scatter(group_shares[4], "seq", scatter_dimension=1, tiled=True),
        )
        layer_grads.insert(0, shares)
    stacked = [
        jnp.stack([layer_grads[number][member] for number in range(LAYERS)]) for member in range(5)
    ]
    return (
        hidden.astype(jnp.bfloat16).reshape(docs_dev, block, width),
        gradient.reshape(docs_dev, block, width),
        stacked[0],
        stacked[1],
        stacked[2],
        stacked[3],
        stacked[4],
    )


PLANES = 4
GROUPS = 4
CHIPS = 16
GROUP_HEADS = 3
CUT = 240
MESH = pl.DeviceIdType.MESH
F32 = jnp.float32
BF16 = jnp.bfloat16


def fits(mesh, docs_dev, heads):
    return (
        mesh.shape["docs"] == 2
        and mesh.shape["seq"] == 16
        and docs_dev == PLANES
        and heads == GROUPS * GROUP_HEADS
    )


def swap(value, bits):
    return lax.ppermute(value, "seq", [(i, i ^ bits) for i in range(16)])


def swap_docs(value):
    return lax.ppermute(value, "docs", [(0, 1), (1, 0)])


def dot(left, right):
    return lax.dot_general(left, right, (((1,), (0,)), ((), ())), preferred_element_type=F32)


def dot_nt(left, right):
    return lax.dot_general(left, right, (((1,), (1,)), ((), ())), preferred_element_type=F32)


def dot_tn(left, right):
    return lax.dot_general(left, right, (((0,), (0,)), ((), ())), preferred_element_type=F32)


def vmem():
    return pl.BlockSpec(memory_space=pltpu.VMEM)


def smem():
    return pl.BlockSpec(memory_space=pltpu.SMEM)


def hbm():
    return pl.BlockSpec(memory_space=pltpu.HBM)


def params():
    return pltpu.CompilerParams(vmem_limit_bytes=56 * 2**20)


QUERIES = 512
BACK_QUERIES = 512


def key_features(own_random, own_global, length):
    block = jnp.arange(16, dtype=jnp.int32)
    window = jnp.stack([(block + 15) % 16, block, (block + 1) % 16], axis=1)
    ids = jnp.concatenate([window, own_random, jnp.broadcast_to(own_global, (16, GLOB))], axis=1)
    count = jnp.sum((ids[:, :, None] == block).astype(F32), axis=1).T
    special = jnp.any(own_global[None, :] == block[:, None], axis=1)
    count = jnp.where(special[None, :], 1.0, count)
    extra = jnp.where(count > 0, jnp.log(jnp.maximum(count, 1.0)), NEGATIVE)
    inside = jnp.arange(1024, dtype=jnp.int32)[:, None] < length
    extra = jnp.where(inside, jnp.repeat(extra, 64, axis=0), NEGATIVE)
    high = extra.astype(BF16)
    low = jnp.where(extra > 0, extra - high.astype(F32), 0.0).astype(BF16)
    return jnp.concatenate([high, low, jnp.zeros((1024, 32), BF16)], axis=1)


def halves_beside(rows):
    return jnp.concatenate([rows[:32], rows[32:]], axis=1)


def halves_below(rows):
    return jnp.concatenate([rows[:, :192], rows[:, 192:]], axis=0)


def spread_heads(qkv, feature_ref, key_scr, query_scr):
    row = lax.broadcasted_iota(jnp.int32, (1024, 64), 0) // 64
    lane = lax.broadcasted_iota(jnp.int32, (1024, 64), 1)
    place = jnp.where(jnp.logical_and(lane < 32, lane % 16 == row), 1.0, 0.0).astype(BF16)
    for h in range(GROUP_HEADS):
        key_scr[h] = jnp.concatenate([qkv[:, 128 * h : 128 * h + 64], feature_ref[...]], axis=1)
        query = qkv[:, 384 + 64 * h : 448 + 64 * h] * jnp.asarray(HEAD**-0.5, BF16)
        query_scr[h] = jnp.concatenate([query, place], axis=1)


def expo_columns(scores):
    expo = jnp.exp(scores - jnp.max(scores, axis=0, keepdims=True))
    return expo, 1.0 / jnp.sum(expo, axis=0, keepdims=True)


def load_up(up_ref, wu, wo, sems):
    pltpu.make_async_copy(up_ref.at[:, :, :, pl.ds(1536, 384)], wo, sems.at[0]).start()
    pltpu.make_async_copy(up_ref.at[:, :, :, pl.ds(0, 1536)], wu, sems.at[1]).start()


def load_down(down_ref, wd, sems):
    for plane in range(2):
        for part in range(2):
            source = down_ref.at[plane, :, :, pl.ds(768 * part, 768)]
            pltpu.make_async_copy(source, wd.at[:, plane, part], sems.at[2]).start()


def wait_weight(scr, sem):
    pltpu.make_async_copy(scr, scr, sem).wait()


def inside_rows(info):
    row = lax.broadcasted_iota(jnp.int32, (256, 1), 0)
    length = jnp.zeros_like(row)
    for k in range(PLANES):
        length = jnp.where(row // 64 == k, info[8 + k], length)
    return info[0] * 64 + row % 64 < length


def norm_parts(values):
    centre = values - jnp.mean(values, axis=-1, keepdims=True)
    spread = jnp.mean(centre * centre, axis=-1, keepdims=True)
    rate = lax.rsqrt(spread + EPSILON)
    return centre * rate, rate


def norm_back(unit, rate, gain, grad):
    scaled = grad * gain
    inner = jnp.mean(scaled * unit, axis=-1, keepdims=True)
    outer = jnp.mean(scaled, axis=-1, keepdims=True)
    return rate * (scaled - outer - unit * inner), jnp.sum(grad * unit, axis=0, keepdims=True)


CURVE = 0.7978845608028654


def gelu_parts(values):
    square = values * values
    bend = jnp.tanh(CURVE * (values + 0.044715 * (square * values)))
    return 0.5 * values * (1.0 + bend), bend, square


def gelu_slope(values, bend, square):
    return 0.5 * (1.0 + bend) + 0.5 * values * (1.0 - bend * bend) * (
        CURVE * (1.0 + 3 * 0.044715 * square)
    )


WEIGHT_SCRATCH = [
    pltpu.VMEM((2, 16, 48, 1536), BF16),
    pltpu.VMEM((16, 2, 2, 48, 768), BF16),
    pltpu.VMEM((2, 16, 48, 384), BF16),
]


def feed_back_kernel(
    pieces,
    has_extra,
    info,
    base_ref,
    extra_ref,
    gain_ref,
    mixed_ref,
    h1_ref,
    up_ref,
    h2_ref,
    *refs,
):
    w_refs, refs = refs[:pieces], refs[pieces:]
    dh1_ref, do_ref, dgain_ref, *sum_refs, wu, wd, wo, gu, gd, go, got, sems, pair_sems, out_sems = refs
    load_down(w_refs[1], wd, sems)
    load_up(w_refs[0], wu, wo, sems)
    docs, me = lax.axis_index("docs"), lax.axis_index("seq")
    mate = (docs, flip(me, 1))
    greet([mate])
    units = [(ry, place) for ry in range(2) for place in range(8)]

    def other_docs(ry):
        return docs if ry == 0 else 1 - docs

    def owner(place, rc):
        return flip(me, (place % 2) * 8 + (place // 2 % 2) * 4 + (place // 4) * 2 + rc)

    def to_mate(source, ry, place, first, count, n):
        pltpu.make_async_remote_copy(
            source,
            got.at[ry, place, pl.ds(first, count)],
            pair_sems.at[0, n],
            pair_sems.at[1, n],
            device_id=mate,
            device_id_type=MESH,
        ).start()

    def up_to_mate(part):
        x, z = (me // 2) % 2, me // 4
        across = x if part % 2 == 0 else 1 - x
        low = z % 2 if part // 2 % 2 == 0 else 1 - z % 2
        high = z // 2 if part // 4 == 0 else 1 - z // 2
        for half in range(2):
            source = gu.at[half, 2 * part + 1 - me % 2]
            to_mate(source, other_docs(half), 4 * across + 2 * low + high, 0, 192, 0)

    if has_extra:
        parts = [
            base_ref[64 * k : 64 * k + 64, :] + extra_ref[k].astype(F32)
            for k in range(PLANES)
        ]
        grad = jnp.concatenate(parts, axis=0)
    else:
        grad = base_ref[...].reshape(256, 768).astype(F32)
    grad = jnp.where(inside_rows(info), grad, 0.0)
    unit2, rate2 = norm_parts(h2_ref[...])
    dh2, dgain1 = norm_back(unit2, rate2, gain_ref[1:2, :], grad)
    dgain_ref[1:2, :] = dgain1
    df = dh2.astype(BF16)
    df_turned = df.T
    unit1, rate1 = norm_parts(h1_ref[...])
    x1_low = (unit1 * gain_ref[0:1, :]).astype(BF16)
    wait_weight(wd, sems.at[2])
    wait_weight(wu, sems.at[1])
    dx1 = dh2
    for part in range(8):
        at = 384 * part
        d_act = dot_nt(df, wd[2 * part : 2 * part + 2].reshape(384, 768))
        up = up_ref[:, at : at + 384]
        act, bend, square = gelu_parts(up)
        act = act.astype(BF16)
        dup = (gelu_slope(up, bend, square) * d_act).astype(BF16)
        side, start = part // 4, 384 * (part % 4)
        dx1 += dot_nt(dup, wu[side, :, :, start : start + 384].reshape(768, 384))
        gt_up = dot_tn(dup, x1_low).astype(BF16)
        for n in range(2):
            for half in range(2):
                gu[half, 2 * part + n] = gt_up[
                    192 * n : 192 * n + 192, 384 * half : 384 * half + 384
                ]
        gt_down = dot(df_turned, act).astype(BF16)
        row = 48 * (part % 4)
        for s in range(16):
            gd[part // 4, s, row : row + 48, :] = gt_down[48 * s : 48 * s + 48]
        up_to_mate(part)
        if part % 4 == 3:
            for place in range(8):
                source = gd.at[part // 4, owner(place, 1)]
                to_mate(source, other_docs(part // 4), place, 240, 192, 1)
    dh1, dgain0 = norm_back(unit1, rate1, gain_ref[0:1, :], dx1)
    dgain_ref[0:1, :] = dgain0
    dh1_ref[...] = dh1
    da = dh1.astype(BF16)
    gt_out = dot_tn(da, mixed_ref[...]).astype(BF16)
    for s in range(16):
        for half in range(2):
            go[half, s] = gt_out[48 * s : 48 * s + 48, 384 * half : 384 * half + 384]
    for ry, place in units:
        to_mate(go.at[other_docs(ry), owner(place, 1)], ry, place, 192, 48, 2)
    wait_weight(wo, sems.at[0])
    do = dot_nt(da[:, 0:384], wo[0].reshape(768, 384))
    do += dot_nt(da[:, 384:768], wo[1].reshape(768, 384))
    do = do.astype(BF16)
    for k in range(PLANES):
        for g in range(GROUPS):
            do_ref[4 * k + g] = halves_beside(do[64 * k : 64 * k + 64, 192 * g : 192 * g + 192])
    for n, (first, count) in enumerate(((0, 192), (240, 192), (192, 48))):
        part = got.at[:, :, pl.ds(first, count)]
        pltpu.make_async_copy(part, part, pair_sems.at[1, n]).wait()
    copies = []
    for ry, place in units:
        for scr, first, count in ((gu, 0, 192), (go, 192, 48), (gd, 240, 192)):
            span = slice(first, first + count)
            own = scr[other_docs(ry), owner(place, 0)].astype(F32)
            got[ry, place, span] = (own + got[ry, place, span].astype(F32)).astype(BF16)
        for ref, source in (
            (sum_refs[ry].at[place], got.at[ry, place, pl.ds(0, CUT)]),
            (sum_refs[2 + place // 4].at[ry, place % 4], got.at[ry, place, pl.ds(CUT, 432 - CUT)]),
        ):
            copies.append(pltpu.make_async_copy(source, ref, out_sems.at[len(copies)]))
            copies[-1].start()
    for n, scr in enumerate((gu, gd, go)):
        half = scr.at[:, pl.ds(0, 8)]
        pltpu.make_async_copy(half, half, pair_sems.at[0, n]).wait()
    for copy in copies:
        copy.wait()


def feed_back(info, base, extra, gains, saved, weights, number):
    mixed, h1, up, h2 = saved
    has_extra = extra is not None
    if not has_extra:
        extra = jnp.zeros((8, 128), BF16)
    return pl.pallas_call(
        functools.partial(feed_back_kernel, len(weights), has_extra),
        out_shape=(
            jax.ShapeDtypeStruct((256, 768), F32),
            jax.ShapeDtypeStruct((16, 32, 384), BF16),
            jax.ShapeDtypeStruct((2, 768), F32),
            jax.ShapeDtypeStruct((8, CUT, 384), BF16),
            jax.ShapeDtypeStruct((8, CUT, 384), BF16),
            jax.ShapeDtypeStruct((2, 4, 432 - CUT, 384), BF16),
            jax.ShapeDtypeStruct((2, 4, 432 - CUT, 384), BF16),
        ),
        in_specs=[smem()] + [vmem()] * 7 + [hbm() for _ in weights],
        out_specs=(vmem(), vmem(), vmem(), hbm(), hbm(), hbm(), hbm()),
        scratch_shapes=WEIGHT_SCRATCH
        + [
            pltpu.VMEM((2, 16, 192, 384), BF16),
            pltpu.VMEM((2, 16, 192, 384), BF16),
            pltpu.VMEM((2, 16, 48, 384), BF16),
            pltpu.VMEM((2, 8, 432, 384), BF16),
            pltpu.SemaphoreType.DMA((3,)),
            pltpu.SemaphoreType.DMA((2, 3)),
            pltpu.SemaphoreType.DMA((32,)),
        ],
        compiler_params=pltpu.CompilerParams(
            collective_id=number, has_side_effects=True, vmem_limit_bytes=56 * 2**20
        ),
        cost_estimate=pl.CostEstimate(
            flops=6 * 10**9, bytes_accessed=40 * 10**6, transcendentals=10**6
        ),
        name="feed_back",
    )(info, base, extra, gains, mixed, h1, up, h2, *weights)


def flip(index, bits):
    for bit in (1, 2, 4, 8):
        if bits & bit:
            index = index + bit - 2 * bit * ((index // bit) % 2)
    return index


def greet(peers):
    barrier = pltpu.get_barrier_semaphore()
    for peer in peers:
        pl.semaphore_signal(barrier, inc=1, device_id=peer, device_id_type=MESH)
    pl.semaphore_wait(barrier, len(peers))


def remote(source, target, sems, n, peer):
    return pltpu.make_async_remote_copy(
        source, target, sems.at[0, n], sems.at[1, n], device_id=peer, device_id_type=MESH
    )


def comm_params(number):
    return pltpu.CompilerParams(
        collective_id=number, has_side_effects=True, vmem_limit_bytes=16 * 2**20
    )


class Spread:
    def __init__(self, low_ref, x_ref, sems, own_sem):
        self.low_ref, self.x_ref, self.sems = low_ref, x_ref, sems
        self.docs, self.me = lax.axis_index("docs"), lax.axis_index("seq")
        self.own = pltpu.make_async_copy(low_ref.at[self.me // 4], x_ref.at[self.me], own_sem)
        self.hops, self.across, self.mates = [], [], []

    def send(self, source, slot, n, bits):
        peer = (self.docs, flip(self.me, bits))
        copy = remote(source, self.x_ref.at[slot], self.sems, n, peer)
        copy.start()
        return copy

    def begin(self):
        for rz in range(1, 4):
            source = self.low_ref.at[flip(self.me, 4 * rz) // 4]
            self.hops.append(self.send(source, self.me, rz, 4 * rz))
        self.own.start()
        source = self.low_ref.at[self.me // 4]
        self.across.append(self.send(source, self.me, 4, 2))
        self.mates.append(self.send(source, self.me, 8, 1))

    def forward(self, rz):
        self.hops[rz - 1].wait_recv()
        slot = flip(self.me, 4 * rz)
        self.across.append(self.send(self.x_ref.at[slot], slot, 4 + rz, 2))
        self.mates.append(self.send(self.x_ref.at[slot], slot, 8 + rz, 1))

    def from_beside(self):
        for rz in range(4):
            self.across[rz].wait_recv()
            slot = flip(flip(self.me, 4 * rz), 2)
            self.mates.append(self.send(self.x_ref.at[slot], slot, 12 + rz, 1))

    def arrived(self):
        for copy in self.mates:
            copy.wait_recv()
        self.own.wait()

    def finish(self):
        for copy in self.hops + self.across + self.mates:
            copy.wait_send()


class Slabs:
    def __init__(self, source, w_ref, sems, own_sem, docs_first=False):
        self.source, self.w_ref, self.sems = source, w_ref, sems
        self.docs, self.me = lax.axis_index("docs"), lax.axis_index("seq")
        self.plane, self.x, self.core = self.me // 4, (self.me // 2) % 2, self.me % 2
        beside, over = (self.docs, flip(self.me, 2)), (1 - self.docs, self.me)
        self.peers = (over, beside) if docs_first else (beside, over)
        if docs_first:
            self.near = ((self.docs, self.x), (1 - self.docs, self.x))
            self.far = ((self.docs, 1 - self.x), (1 - self.docs, 1 - self.x))
        else:
            self.near = ((self.docs, self.x), (self.docs, 1 - self.x))
            self.far = ((1 - self.docs, self.x), (1 - self.docs, 1 - self.x))
        self.mate = (self.docs, flip(self.me, 1))
        self.own = pltpu.make_async_copy(source, self.slot(self.near[0], self.plane), own_sem)

    def slot(self, at, z):
        return self.w_ref.at[self.core, 8 * at[0] + 2 * z + at[1]]

    def copy(self, at, z, own, send, recv, peer):
        slot = self.slot(at, z)
        return pltpu.make_async_remote_copy(
            self.source if own else slot,
            slot,
            self.sems.at[0, send],
            self.sems.at[1, recv],
            device_id=peer,
            device_id_type=MESH,
        )

    def line(self, z, own, step):
        peer = (self.docs, self.me + 4 * step)
        return self.copy(self.near[0], z, own, z + (0 if step > 0 else 4), z, peer)

    def first(self, z, own=False):
        return self.copy(self.near[0], z, own, 8 + z, 8 + z, self.peers[0])

    def second(self, z, n, own=False):
        return self.copy(self.near[n], z, own, 12 + 4 * n + z, 12 + 4 * n + z, self.peers[1])

    def core_copy(self, at, n, z, own=False):
        return self.copy(at, z, own, 20 + 4 * n + z, 20 + 4 * n + z, self.mate)

    def begin(self):
        self.own.start()
        for step in (1, -1):
            pl.when(self.has(self.plane + step))(self.line(self.plane, True, step).start)
        self.first(self.plane, True).start()
        self.core_copy(self.near[0], 0, self.plane, True).start()

    def has(self, z):
        return jnp.logical_and(z >= 0, z < PLANES)

    def each(self, distance, act):
        if distance == 0:
            act(self.plane, 0)
            return
        for step in (1, -1):
            z = self.plane - step * distance
            pl.when(self.has(z))(functools.partial(act, z, step))

    def from_line(self, distance):
        def act(z, step):
            self.line(z, False, step).wait_recv()
            pl.when(self.has(self.plane + step))(self.line(z, False, step).start)
            self.first(z).start()
            self.core_copy(self.near[0], 0, z).start()

        self.each(distance, act)

    def from_first(self, distance):
        def act(z, step):
            self.first(z).wait_recv()
            self.second(z, 0, distance == 0).start()
            self.second(z, 1).start()
            self.core_copy(self.near[1], 1, z).start()

        self.each(distance, act)

    def from_second(self, distance):
        def act(z, step):
            for n in range(2):
                self.second(z, n).wait_recv()
                self.core_copy(self.far[n], 2 + n, z).start()

        self.each(distance, act)

    def arrived(self):
        for z in range(PLANES):
            for n, at in enumerate(self.near + self.far):
                self.core_copy(at, n, z).wait_recv()
        self.own.wait()

    def finish(self):
        for z in range(PLANES):
            for step in (1, -1):
                sent = jnp.logical_and(
                    (self.plane - z) * step >= 0, self.has(self.plane + step)
                )
                pl.when(sent)(self.line(z, False, step).wait_send)
            self.first(z).wait_send()
            for n, at in enumerate(self.near + self.far):
                if n < 2:
                    self.second(z, n).wait_send()
                self.core_copy(at, n, z).wait_send()


class Rows:
    def __init__(self, source, w_ref, sems, own_sem):
        self.source, self.w_ref, self.sems = source, w_ref, sems
        self.docs, self.me = lax.axis_index("docs"), lax.axis_index("seq")
        self.over = (1 - self.docs, self.me)
        self.own = pltpu.make_async_copy(source, self.slot(self.me // 4), own_sem)
        self.hops, self.moved = [], []

    def slot(self, z):
        return self.w_ref.at[pl.ds(8 * self.docs + 2 * z, 2)]

    def begin(self):
        target = self.slot(self.me // 4)
        for rz in range(1, 4):
            peer = (self.docs, flip(self.me, 4 * rz))
            self.hops.append(remote(self.source, target, self.sems, rz, peer))
            self.hops[-1].start()
        self.own.start()
        self.moved.append(remote(self.source, target, self.sems, 4, self.over))
        self.moved[0].start()

    def forward(self, rz):
        self.hops[rz - 1].wait_recv()
        slot = self.slot(flip(self.me, 4 * rz) // 4)
        self.moved.append(remote(slot, slot, self.sems, 4 + rz, self.over))
        self.moved[-1].start()

    def arrived(self):
        for copy in self.moved:
            copy.wait_recv()
        self.own.wait()

    def finish(self):
        for copy in self.hops + self.moved:
            copy.wait_send()


class Collect:
    def __init__(self, keep_ref, send_ref, land, got_core, got_x, sum_x, near, sums, sems):
        self.keep_ref, self.send_ref, self.land, self.got_core = keep_ref, send_ref, land, got_core
        self.got_x, self.sum_x, self.near, self.sums, self.sems = got_x, sum_x, near, sums, sems
        self.docs, self.me = lax.axis_index("docs"), lax.axis_index("seq")
        self.order = (3, 2, 1, 0)
        self.first, self.across, self.hops = {}, {}, []

    def begin(self):
        mate = (self.docs, flip(self.me, 1))
        for rz in self.order:
            for n in (2 * rz + 1, 2 * rz):
                self.first[n] = remote(
                    self.send_ref.at[n], self.got_core.at[n], self.sems, n, mate
                )
                self.first[n].start()

    def along_x(self):
        beside = (self.docs, flip(self.me, 2))
        for rz in self.order:
            n = 2 * rz + 1
            self.first[n].wait_recv()
            self.sum_x[rz] = add_low(self.keep_ref[n], self.got_core[n])
            self.across[rz] = remote(
                self.sum_x.at[rz], self.got_x.at[rz], self.sems, 8 + rz, beside
            )
            self.across[rz].start()
            n = 2 * rz
            self.first[n].wait_recv()
            self.near[rz] = add_full(self.keep_ref[n], self.got_core[n])

    def along_z(self):
        plane = self.me // 4
        for rz in self.order:
            self.across[rz].wait_recv()
            total = add_low(self.near[rz], self.got_x[rz])
            if rz == 0:
                self.land[plane] = total
            else:
                self.sums[rz] = total
                peer = (self.docs, flip(self.me, 4 * rz))
                copy = remote(self.sums.at[rz], self.land.at[plane], self.sems, 12 + rz, peer)
                copy.start()
                self.hops.append(copy)

    def finish(self):
        for copy in self.hops:
            copy.wait_recv()
        for copy in list(self.first.values()) + list(self.across.values()) + self.hops:
            copy.wait_send()


class Exchange:
    def __init__(self, source, land, sems, own_sem):
        docs, me = lax.axis_index("docs"), lax.axis_index("seq")
        self.copies = []
        for bits in range(15, 0, -1):
            peer = flip(me, bits)
            self.copies.append(remote(source.at[peer], land.at[me], sems, bits, (docs, peer)))
        self.own = pltpu.make_async_copy(source.at[me], land.at[me], own_sem)

    def begin(self):
        for copy in self.copies:
            copy.start()
        self.own.start()

    def arrived(self):
        for copy in self.copies:
            copy.wait_recv()
        self.own.wait()

    def finish(self):
        for copy in self.copies:
            copy.wait_send()


class Line:
    PLACE = (0, 2, 1, 3)

    def __init__(self, own, from_left, from_right, sems):
        self.own, self.landing, self.sems = own, (from_left, from_right), sems
        self.docs, self.me = lax.axis_index("docs"), lax.axis_index("seq")
        self.plane = self.me // 4

    def copy(self, place, target, step):
        side = 0 if step > 0 else 1
        return pltpu.make_async_remote_copy(
            self.own.at[place],
            self.landing[side].at[target],
            self.sems.at[0, side, target],
            self.sems.at[1, side, target],
            device_id=(self.docs, self.me + 4 * step),
            device_id_type=MESH,
        )

    def at(self, plane, act):
        pl.when(self.plane == plane)(act)

    def begin(self, rz):
        for plane, step in ((0, 1), (3, -1)):
            self.at(plane, self.copy(self.PLACE[rz], plane ^ rz, step).start)

    def hop(self, number):
        for plane, target, step in (
            ((1, 3, 1), (2, 0, -1)),
            ((1, 0, -1), (2, 3, 1)),
            ((1, 2, 1), (2, 1, -1)),
        )[number]:
            place, side = self.PLACE[plane ^ target], 0 if step > 0 else 1

            def act(place=place, side=side, target=target, step=step):
                copy = self.copy(place, target, step)
                copy.wait_recv()
                self.own[place] = add_low(self.own[place], self.landing[side][target])
                copy.start()

            self.at(plane, act)

    def total(self, out_ref, rows):
        for plane in range(PLANES):

            def act(plane=plane):
                total = self.own[0, rows].astype(F32)
                for side, step in ((0, 1), (1, -1)):
                    if 0 <= plane - step < PLANES:
                        total = total + self.landing[side][plane, rows].astype(F32)
                out_ref[...] = total

            self.at(plane, act)

    def arrived(self):
        for plane in range(PLANES):

            def act(plane=plane):
                for step in (1, -1):
                    if 0 <= plane - step < PLANES:
                        self.copy(0, plane, step).wait_recv()

            self.at(plane, act)

    def finish(self):
        for plane in range(PLANES):

            def act(plane=plane):
                for target in range(PLANES):
                    step = 1 if target > plane else -1
                    if target != plane:
                        self.copy(self.PLACE[plane ^ target], target, step).wait_send()

            self.at(plane, act)


class Everywhere:
    def __init__(self, total, got, sems):
        self.total, self.got, self.sems = total, got, sems
        docs, me = lax.axis_index("docs"), lax.axis_index("seq")
        self.peers = [(docs, flip(me, bits)) for bits in (1, 2, 4, 8)] + [(1 - docs, me)]
        self.copies = []

    def step(self):
        n = len(self.copies)
        if n > 0:
            self.copies[-1].wait_recv()
            self.total[n] = self.total[n - 1] + self.got[n - 1]
        if n < len(self.peers):
            copy = remote(self.total.at[n], self.got.at[n], self.sems, n, self.peers[n])
            copy.start()
            self.copies.append(copy)

    def finish(self):
        for copy in self.copies:
            copy.wait_send()


class Rest:
    ORDER = (3, 1, 2, 0)

    def __init__(self, a_keep, a_send, b_keep, b_send, scr):
        self.a_keep, self.a_send, self.b_keep, self.b_send = a_keep, a_send, b_keep, b_send
        self.scr = scr
        docs, me = lax.axis_index("docs"), lax.axis_index("seq")
        self.beside, self.over = (docs, flip(me, 2)), (1 - docs, me)
        self.line = Line(scr.own, scr.left, scr.right, scr.line_sems)
        self.sent = []

    def copy(self, n, place):
        scr = self.scr
        source, target, peer = (
            (self.a_send.at[4 + place], scr.a_got.at[4 + place], self.over),
            (self.b_send.at[1, place], scr.b_got.at[1, place], self.beside),
            (self.a_send.at[place], scr.a_got.at[place], self.over),
            (self.b_send.at[0, place], scr.b_got.at[0, place], self.beside),
            (scr.a_far.at[place], scr.a_far_got.at[place], self.beside),
            (scr.b_far.at[place], scr.b_far_got.at[place], self.over),
        )[n]
        return remote(source, target, scr.rest_sems, 4 * n + place, peer)

    def start(self, n, place):
        self.sent.append(self.copy(n, place))
        self.sent[-1].start()

    def first(self, place):
        for n in range(4):
            self.start(n, place)

    def second(self, place):
        scr = self.scr
        self.copy(0, place).wait_recv()
        scr.a_far[place] = add_low(self.a_keep[4 + place], scr.a_got[4 + place])
        self.start(4, place)
        self.copy(1, place).wait_recv()
        scr.b_far[place] = add_low(self.b_keep[1, place], scr.b_got[1, place])
        self.start(5, place)

    def third(self, place):
        scr = self.scr
        self.copy(2, place).wait_recv()
        self.copy(4, place).wait_recv()
        near = add_full(self.a_keep[place], scr.a_got[place]) + scr.a_far_got[place].astype(F32)
        scr.own[place, :CUT] = near.astype(BF16)
        self.copy(3, place).wait_recv()
        self.copy(5, place).wait_recv()
        near = add_full(self.b_keep[0, place], scr.b_got[0, place])
        near = near + scr.b_far_got[place].astype(F32)
        scr.own[place, CUT:] = near.astype(BF16)
        if place > 0:
            self.line.begin(Line.PLACE[place])

    def finish(self):
        for copy in self.sent:
            copy.wait_send()
        self.line.finish()


class Route:
    def __init__(self, source, out_ref, sems):
        self.source, self.out_ref, self.sems = source, out_ref, sems
        self.docs, self.me = lax.axis_index("docs"), lax.axis_index("seq")

    def each(self, act_here, act_there):
        for t in range(3):
            local = 3 * (self.me // 4) + t
            number = 16 * (local // 4) + 4 * (self.me % 4) + local % 4
            owner, slot = number // 3, number % 3
            target = self.out_ref.at[slot]
            here = pltpu.make_async_copy(self.source.at[t], target, self.sems.at[2, slot])
            there = pltpu.make_async_remote_copy(
                self.source.at[t],
                target,
                self.sems.at[0, t],
                self.sems.at[1, slot],
                device_id=(self.docs, owner),
                device_id_type=MESH,
            )
            pl.when(owner == self.me)(functools.partial(act_here, here))
            pl.when(owner != self.me)(functools.partial(act_there, there))

    def begin(self):
        self.each(lambda copy: copy.start(), lambda copy: copy.start())

    def finish(self):
        self.each(lambda copy: copy.wait(), lambda copy: copy.wait_send())
        for slot in range(3):
            number = 3 * self.me + slot
            local = 4 * (number // 16) + number % 4
            source = 4 * (local // 3) + (number % 16) // 4
            target = self.out_ref.at[slot]
            wait = pltpu.make_async_copy(target, target, self.sems.at[1, slot]).wait
            pl.when(source != self.me)(wait)


def back_scratch(width):
    low = 432 - CUT
    sems = pltpu.SemaphoreType.DMA

    def vm(*shape, dtype=BF16):
        return pltpu.VMEM(shape, dtype)

    return dict(
        qkv=vm(1024, 576),
        weight=vm(CHIPS, 48, 640),
        x=vm(16, 64, width),
        a_keep=vm(8, CUT, 384),
        b_keep=vm(2, 4, low, 384),
        load_sems=sems((5,)),
        do=vm(16, 32, 384),
        do_sems=sems((2, 16)),
        do_own=sems,
        key=vm(3, 1024, 128),
        query=vm(3, 1024, 128),
        value=vm(3, 1024, 64),
        turned=vm(3, 64, 1024),
        side=vm(2, 3, 1024, 128),
        dkv=vm(3, 1024, 128, dtype=F32),
        dq=vm(1024 // BACK_QUERIES, 192, BACK_QUERIES, dtype=F32),
        dqkv=vm(1024, 576),
        rows=vm(2, 8, 64, width),
        land=vm(4, 64, width),
        got_core=vm(8, 64, width),
        got_x=vm(4, 64, width),
        sum_x=vm(4, 64, width),
        near=vm(4, 64, width, dtype=F32),
        sums=vm(4, 64, width),
        row_sems=sems((2, 16)),
        a_got=vm(8, CUT, 384),
        b_got=vm(2, 4, low, 384),
        a_far=vm(4, CUT, 384),
        a_far_got=vm(4, CUT, 384),
        b_far=vm(4, low, 384),
        b_far_got=vm(4, low, 384),
        rest_sems=sems((2, 24)),
        own=vm(4, 432, 384),
        left=vm(4, 432, 384),
        right=vm(4, 432, 384),
        line_sems=sems((2, 2, 4)),
        q_grad=vm(2, 4, 144, 384),
        q_got=vm(4, 144, 384),
        q_own=vm(4, 144, 384),
        q_land=vm(4, 144, 384),
        q_sems=sems((2, 4)),
        q_sum=vm(3, 48, 384, dtype=F32),
        route_sems=sems((3, 3)),
        gain_sum=vm(6, 8, width, dtype=F32),
        gain_got=vm(5, 8, width, dtype=F32),
        gain_sems=sems((2, 5)),
    )


def attend_back_kernel(names, last, *refs):
    feature_ref, qkv_ref, do_ref, x_ref, w_ref, a_keep, a_send, b_keep, b_send = refs[:9]
    gain_ref, rows_ref, rest_ref, out_ref, gain_out_ref = refs[9:14]
    scr = types.SimpleNamespace(**dict(zip(names, refs[14:])))
    docs, me = lax.axis_index("docs"), lax.axis_index("seq")
    plane = me // 4
    over = (1 - docs, me)
    loads = {}
    for n, (name, ref) in enumerate(
        dict(qkv=qkv_ref, weight=w_ref, a_keep=a_keep, b_keep=b_keep, x=x_ref).items()
    ):
        loads[name] = pltpu.make_async_copy(ref, getattr(scr, name), scr.load_sems.at[n])
        loads[name].start()
    greet([(docs, flip(me, bits)) for bits in range(15, 0, -1)] + [over])
    exchange = Exchange(do_ref, scr.do, scr.do_sems, scr.do_own)
    exchange.begin()
    rest = Rest(scr.a_keep, a_send, scr.b_keep, b_send, scr)
    rest.first(3)
    rest.first(1)
    gains = Everywhere(scr.gain_sum, scr.gain_got, scr.gain_sems)
    if last:
        scr.gain_sum[0] = gain_ref[...]
        gains.step()

    loads["qkv"].wait()
    qkv = scr.qkv[...]
    spread_heads(qkv, feature_ref, scr.key, scr.query)
    zero = jnp.zeros((1024, 64), BF16)
    for h in range(GROUP_HEADS):
        scr.value[h] = qkv[:, 128 * h + 64 : 128 * h + 128]
        scr.turned[h] = qkv[:, 128 * h : 128 * h + 64].T
        scr.side[0, h] = jnp.concatenate([scr.query[h, :, :64], zero], axis=1)
    loads["a_keep"].wait()
    loads["b_keep"].wait()
    exchange.arrived()
    grad_o = jnp.concatenate([halves_below(scr.do[n]) for n in range(16)], axis=0)
    for h in range(GROUP_HEADS):
        scr.side[1, h] = jnp.concatenate([zero, grad_o[:, 64 * h : 64 * h + 64]], axis=1)

    def part(n, h):
        at = slice(BACK_QUERIES * n, BACK_QUERIES * n + BACK_QUERIES)
        expo, rate = expo_columns(dot_nt(scr.key[h], scr.query[h, at, :]))
        probs = expo * rate
        grad_probs = dot_nt(scr.value[h], scr.side[1, h, at, :][:, 64:])
        delta = jnp.sum(probs * grad_probs, axis=0, keepdims=True)
        grad_scores = (probs * (grad_probs - delta)).astype(BF16)
        scr.dq[n, 64 * h : 64 * h + 64, :] = dot(scr.turned[h], grad_scores) * (HEAD**-0.5)
        dkv = dot(grad_scores, scr.side[0, h, at, :])
        dkv += dot(probs.astype(BF16), scr.side[1, h, at, :])
        if n == 0:
            scr.dkv[h] = dkv
        else:
            scr.dqkv[:, 128 * h : 128 * h + 128] = (scr.dkv[h] + dkv).astype(BF16)

    part(0, 0)
    rest.second(3)
    rest.first(2)
    part(0, 1)
    if last:
        gains.step()
    part(0, 2)
    rest.second(1)
    scr.dqkv[0:512, 384:576] = scr.dq[0].T.astype(BF16)
    part(1, 0)
    rest.third(3)
    part(1, 1)
    rest.second(2)
    part(1, 2)
    rest.third(1)
    rest.line.hop(0)
    if last:
        gains.step()
    scr.dqkv[512:1024, 384:576] = scr.dq[1].T.astype(BF16)
    loads["x"].wait()
    grad = dot_tn(scr.dqkv[...], scr.x[...].reshape(1024, scr.x.shape[-1]))
    order = [6, 7, 8, 0, 2, 4, 1, 3, 5]
    grad = jnp.concatenate([grad[64 * n : 64 * n + 64] for n in order], axis=0).astype(BF16)
    for quarter in range(PLANES):
        apart = flip(plane, quarter)
        place = (apart % 2) * 2 + apart // 2
        for side in range(2):
            at = docs if side == 0 else 1 - docs
            scr.q_grad[at, place] = grad[
                144 * quarter : 144 * quarter + 144, 384 * side : 384 * side + 384
            ]
    crossed = remote(scr.q_grad.at[1], scr.q_got, scr.q_sems, 0, over)
    crossed.start()
    rest.first(0)
    loads["weight"].wait()
    rows = Collect(
        scr.rows.at[0],
        scr.rows.at[1],
        scr.land,
        scr.got_core,
        scr.got_x,
        scr.sum_x,
        scr.near,
        scr.sums,
        scr.row_sems,
    )
    for half in (1, 0):
        part_rows = []
        for n in range(8):
            block = flip(me, (n // 2) * 4 + (n % 2) * 2 + half)
            part_rows.append(scr.dqkv[pl.ds(pl.multiple_of(block * 64, 64), 64), :])
        product = dot_nt(jnp.concatenate(part_rows, axis=0), scr.weight[:, :, :576].reshape(-1, 576))
        scr.rows[half] = product.astype(BF16).reshape(scr.rows.shape[1:])
        if half == 1:
            rows.begin()
    rest.third(2)
    rest.line.hop(1)
    rows.along_x()
    if last:
        gains.step()
    crossed.wait_recv()
    turned = []
    for place in Rest.ORDER:
        rz = Line.PLACE[place]
        scr.q_own[place] = add_low(scr.q_grad[0, place], scr.q_got[place])
        if rz > 0:
            peer = (docs, flip(me, 4 * rz))
            turned.append(
                remote(scr.q_own.at[place], scr.q_land.at[place], scr.q_sems, place, peer)
            )
            turned[-1].start()
    rest.line.hop(2)
    rest.second(0)
    rows.along_z()
    if last:
        gains.step()
    for copy in turned:
        copy.wait_recv()
    total = scr.q_own[0].astype(F32)
    for place in range(1, PLANES):
        total = total + scr.q_land[place].astype(F32)
    scr.q_sum[...] = total.reshape(scr.q_sum.shape)
    route = Route(scr.q_sum, out_ref, scr.route_sems)
    route.begin()
    rest.third(0)
    if last:
        gains.step()
        gain_out_ref[...] = scr.gain_sum[5]
        gains.finish()
    else:
        gain_out_ref[...] = gain_ref[...]
    rest.line.arrived()
    rest.line.total(rest_ref, slice(0, 432))
    rows.finish()
    rows_ref[...] = scr.land[...]
    for piece in (exchange, rest, route):
        piece.finish()
    for copy in turned + [crossed]:
        copy.wait_send()


def attend_back(features, qkv, grad_o, x, weight, sums, gain_grads, last, number):
    width = x.shape[-1]
    scratch = back_scratch(width)
    return pl.pallas_call(
        functools.partial(attend_back_kernel, tuple(scratch), last),
        out_shape=(
            jax.ShapeDtypeStruct((PLANES, 64, width), BF16),
            jax.ShapeDtypeStruct((432, 384), F32),
            jax.ShapeDtypeStruct((3, 48, 384), F32),
            jax.ShapeDtypeStruct((8, width), F32),
        ),
        in_specs=[vmem()] + [hbm()] * 8 + [vmem()],
        out_specs=(vmem(), vmem(), hbm(), vmem()),
        scratch_shapes=list(scratch.values()),
        compiler_params=pltpu.CompilerParams(
            collective_id=number, has_side_effects=True, vmem_limit_bytes=56 * 2**20
        ),
        cost_estimate=pl.CostEstimate(
            flops=8 * 10**9, bytes_accessed=10 * 10**6, transcendentals=3 * 10**6
        ),
        name="attend_back",
    )(features, qkv, grad_o, x, weight, *sums, gain_grads)


def forward_scratch(width):
    sems = pltpu.SemaphoreType.DMA

    def vm(*shape, dtype=BF16):
        return pltpu.VMEM(shape, dtype)

    scratch = dict(
        x=vm(16, 64, width),
        weight=vm(CHIPS, 48, 640),
        qkv=vm(1024, 576),
        key=vm(3, 1024, 128),
        query=vm(3, 1024, 128),
        value=vm(3, 64, 1024),
        turned=vm(192, 1024, dtype=F32),
        o=vm(LAYERS, 16, 32, 384),
        o_got=vm(LAYERS, 16, 32, 384),
        mixed=vm(256, width),
        h1=vm(256, width, dtype=F32),
        up=vm(256, 4 * width, dtype=F32),
        h2=vm(256, width, dtype=F32),
        hidden=vm(256, width, dtype=F32),
        low=vm(4, 64, width),
        act=vm(256, 4 * width),
        wu=WEIGHT_SCRATCH[0],
        wd=WEIGHT_SCRATCH[1],
        wo=WEIGHT_SCRATCH[2],
        weight_sems=sems((3,)),
        load_sems=sems((3,)),
        own_sems=sems((2, 5)),
        save_sems=sems((2, 5)),
    )
    for layer in range(LAYERS):
        scratch[f"row_sems_{layer}"] = sems((2, 16))
        scratch[f"qkv_sems_{layer}"] = sems((2, 8))
        scratch[f"o_sems_{layer}"] = sems((2, 16))
        scratch[f"up_sems_{layer}"] = sems((2, 36))
        scratch[f"down_sems_{layer}"] = sems((2, 36))
    return scratch


def forward_kernel(names, *refs):
    info, feature_ref, tokens_ref = refs[:3]
    wq_refs, up_refs, down_refs = refs[3:5], refs[5:7], refs[7:9]
    saved_refs = (refs[9:15], refs[15:21])
    w_refs, wu_refs, wd_refs, gains_ref, result_ref = refs[21:23], refs[23:25], refs[25:27], refs[27], refs[28]
    scr = types.SimpleNamespace(**dict(zip(names, refs[29:])))
    docs, me = lax.axis_index("docs"), lax.axis_index("seq")
    pltpu.make_async_copy(tokens_ref, scr.low, scr.load_sems.at[2]).start()
    greet([(docs, flip(me, bits)) for bits in range(15, 0, -1)] + [(1 - docs, me)])

    def sems(name, layer):
        return getattr(scr, f"{name}_sems_{layer}")

    qkvs, slabs = [], []
    for layer in range(LAYERS):
        own = scr.own_sems.at[layer]
        qkvs.append(Rows(wq_refs[layer], w_refs[layer], sems("qkv", layer), own.at[0]))
        slabs.append(
            [
                Slabs(up_refs[layer], wu_refs[layer], sems("up", layer), own.at[1]),
                Slabs(down_refs[layer], wd_refs[layer], sems("down", layer), own.at[2], True),
            ]
        )

    def spread(layer, source):
        x_ref = saved_refs[layer][0]
        return Spread(source, x_ref, sems("row", layer), scr.own_sems.at[layer, 3])

    def every(parts, step, *arguments):
        for part in parts:
            getattr(part, step)(*arguments)

    def move(layer, *steps):
        for step in steps:
            name = {"l": "from_line", "f": "from_first", "s": "from_second"}[step[0]]
            every(slabs[layer], name, int(step[1]))

    def save(layer, n, source):
        copy = pltpu.make_async_copy(source, saved_refs[layer][n + 1], scr.save_sems.at[layer, n])
        copy.start()
        return copy

    saves = []

    def attend(layer, rows, ticks):
        qkvs[layer].arrived()
        rows.arrived()
        load_x = pltpu.make_async_copy(saved_refs[layer][0], scr.x, scr.load_sems.at[0])
        load_w = pltpu.make_async_copy(
            w_refs[layer], scr.weight, scr.load_sems.at[1]
        )
        load_x.start()
        load_w.start()
        while saves:
            saves.pop().wait()
        load_x.wait()
        load_w.wait()
        scr.qkv[...] = dot(
            scr.x[...].reshape(1024, scr.x.shape[-1]), scr.weight[:, :, :576].reshape(-1, 576)
        ).astype(BF16)
        if layer == 0:
            share = scr.x.shape[-1] // 32
            shares = [
                scr.weight[chip, 24 * core : 24 * core + 4, 576 : 576 + share]
                for chip in range(CHIPS)
                for core in range(2)
            ]
            gains_ref[0:4] = jnp.concatenate(shares, axis=1).astype(F32)
        saves.append(save(layer, 0, scr.qkv))
        qkv = scr.qkv[...]
        spread_heads(qkv, feature_ref, scr.key, scr.query)
        for h in range(GROUP_HEADS):
            scr.value[h] = qkv[:, 128 * h + 64 : 128 * h + 128].T
        exchange = Exchange(
            scr.o.at[layer], scr.o_got.at[layer], sems("o", layer), scr.own_sems.at[layer, 4]
        )
        for n in range(1024 // QUERIES):
            at = slice(QUERIES * n, QUERIES * n + QUERIES)
            for h in range(GROUP_HEADS):
                expo, rate = expo_columns(dot_nt(scr.key[h], scr.query[h, at, :]))
                scr.turned[64 * h : 64 * h + 64, at] = dot(
                    scr.value[h], (expo * rate).astype(BF16)
                )
                ticks.pop(0)()
            rows_o = scr.turned[:, at].T.astype(BF16)
            for m in range(QUERIES // 64):
                scr.o[layer, n * (QUERIES // 64) + m] = halves_beside(rows_o[64 * m : 64 * m + 64])
        exchange.begin()
        return exchange

    def feed(layer, exchange, ticks):
        exchange.arrived()
        slabs[layer][0].arrived()
        load_up(wu_refs[layer], scr.wu, scr.wo, scr.weight_sems)
        for k in range(PLANES):
            scr.mixed[64 * k : 64 * k + 64, :] = jnp.concatenate(
                [halves_below(scr.o_got[layer, 4 * k + g]) for g in range(GROUPS)], axis=1
            )
        saves.append(save(layer, 1, scr.mixed))
        mixed = scr.mixed[...]
        gain = gains_ref[2 * layer : 2 * layer + 2]
        ticks.pop(0)()
        wait_weight(scr.wo, scr.weight_sems.at[0])
        attended = jnp.concatenate(
            [dot(mixed, scr.wo[side].reshape(768, 384)) for side in range(2)], axis=1
        )
        before = scr.low[...].reshape(256, -1).astype(F32) if layer == 0 else scr.hidden[...]
        h1 = before + attended
        scr.h1[...] = h1
        saves.append(save(layer, 2, scr.h1))
        x1 = norm_parts(h1)[0] * gain[0:1, :]
        x1_low = x1.astype(BF16)
        wait_weight(scr.wu, scr.weight_sems.at[1])
        for side in range(2):
            for part in range(3):
                at = 1536 * side + 512 * part
                up = dot(x1_low, scr.wu[side, :, :, 512 * part : 512 * part + 512].reshape(768, 512))
                scr.up[:, at : at + 512] = up
                scr.act[:, at : at + 512] = gelu_parts(up)[0].astype(BF16)
            ticks.pop(0)()
        saves.append(save(layer, 3, scr.up))
        slabs[layer][1].arrived()
        load_down(wd_refs[layer], scr.wd, scr.weight_sems)
        wait_weight(scr.wd, scr.weight_sems.at[2])
        h2 = x1 + dot(scr.act[...], scr.wd[...].reshape(3072, 768))
        scr.h2[...] = h2
        saves.append(save(layer, 4, scr.h2))
        out = jnp.where(inside_rows(info), norm_parts(h2)[0] * gain[1:2, :], 0.0)
        low = out.astype(BF16)
        if layer == 0:
            scr.hidden[...] = out
            scr.low[...] = low.reshape(scr.low.shape)
        else:
            result_ref[...] = low.reshape(result_ref.shape)

    def nothing():
        pass

    def step(layer, *steps):
        return lambda: move(layer, *steps)

    rows_0 = spread(0, tokens_ref)
    rows_0.begin()
    qkvs[0].begin()
    every(slabs[0], "begin")
    for rz in range(1, 4):
        rows_0.forward(rz)
        qkvs[0].forward(rz)
        if rz == 1:
            move(0, "f0")
    rows_0.from_beside()
    pltpu.make_async_copy(tokens_ref, scr.low, scr.load_sems.at[2]).wait()
    exchange_0 = attend(
        0,
        rows_0,
        [
            step(0, "l1"),
            nothing,
            step(0, "f1"),
            step(0, "l2"),
            lambda: every(slabs[1], "begin"),
            step(0, "s0"),
        ],
    )
    move(0, "l3", "f2", "s1", "f3")
    move(1, "l1")
    move(0, "s2")
    move(1, "l2")
    qkvs[1].begin()
    move(0, "s3")
    feed(0, exchange_0, [step(1, "l3"), step(1, "f0"), nothing])
    rows_1 = spread(1, scr.low)
    rows_1.begin()
    for rz in range(1, 4):
        rows_1.forward(rz)
    for rz in range(1, 4):
        qkvs[1].forward(rz)
    rows_1.from_beside()
    move(1, "f1", "f2")
    exchange_1 = attend(
        1,
        rows_1,
        [nothing, step(1, "f3"), nothing, step(1, "s0"), nothing, step(1, "s1")],
    )
    move(1, "s2", "s3")
    feed(1, exchange_1, [nothing] * 3)
    for copy in saves:
        copy.wait()
    every([rows_0, rows_1, exchange_0, exchange_1] + qkvs + slabs[0] + slabs[1], "finish")


def forward(info, features, tokens, wq, parts, number):
    width = tokens.shape[-1]
    scratch = forward_scratch(width)

    def out(*shape, dtype=BF16):
        return jax.ShapeDtypeStruct(shape, dtype)

    saved = [
        out(16, 64, width),
        out(1024, 576),
        out(256, width),
        out(256, width, dtype=F32),
        out(256, 4 * width, dtype=F32),
        out(256, width, dtype=F32),
    ]
    shapes = saved + saved + [out(CHIPS, 48, 640)] * 2
    shapes += [out(2, CHIPS, 48, 1920)] * 2 + [out(2, CHIPS, 48, 1536)] * 2
    shapes += [out(4, width, dtype=F32), out(PLANES, 64, width)]
    return pl.pallas_call(
        functools.partial(forward_kernel, tuple(scratch)),
        out_shape=tuple(shapes),
        in_specs=[smem(), vmem(), hbm()] + [hbm()] * 6,
        out_specs=tuple([hbm()] * (len(shapes) - 2) + [vmem(), vmem()]),
        scratch_shapes=list(scratch.values()),
        compiler_params=pltpu.CompilerParams(
            collective_id=number, has_side_effects=True, vmem_limit_bytes=58 * 2**20
        ),
        name="forward",
    )(info, features, tokens, *wq, *(part[0] for part in parts), *(part[1] for part in parts))


def pick(stack, index):
    return lax.dynamic_index_in_dim(stack, index, 0, keepdims=False)


def pack_qkv(shards, gains, me, core):
    rows = shards.shape[1]
    parts = shards.reshape(LAYERS, rows, 3, GROUPS, GROUP_HEADS, HEAD)
    pairs = jnp.transpose(parts[:, :, 1:], (3, 0, 1, 4, 2, 5)).reshape(GROUPS, LAYERS, rows, 384)
    query = jnp.transpose(parts[:, :, 0], (2, 0, 1, 3, 4)).reshape(GROUPS, LAYERS, rows, 192)
    share = gains.shape[-1]
    beside = jnp.pad(gains.reshape(2 * LAYERS, share), ((0, rows - 2 * LAYERS), (0, 64 - share)))
    beside = jnp.broadcast_to(beside, (GROUPS, LAYERS, rows, 64))
    packed = jnp.concatenate([pairs, query, beside], axis=3)
    group = me & 3
    got = [pick(packed, group)] + [swap(pick(packed, group ^ r), r) for r in range(1, 4)]

    def in_order(own, other):
        return jnp.where(
            core == 0,
            jnp.concatenate([own, other], axis=1),
            jnp.concatenate([other, own], axis=1),
        )

    here, there = in_order(got[0], got[1]), in_order(got[2], got[3])
    both = jnp.where(
        (me >> 1) & 1 == 0,
        jnp.stack([here, there], axis=1),
        jnp.stack([there, here], axis=1),
    )
    return [both[layer] for layer in range(LAYERS)]


def pack_rest(out_weight, up_weight, down_weight, core):
    def mine(shard, side):
        half = shard.shape[2] // 2
        return lax.dynamic_slice_in_dim(shard, side * half, half, axis=2)

    def both(side):
        return jnp.concatenate([mine(up_weight, side), mine(out_weight, side)], axis=2)

    own, got = both(core), swap(both(1 - core), 1)
    rows = jnp.where(
        core == 0,
        jnp.concatenate([own, got], axis=1),
        jnp.concatenate([got, own], axis=1),
    )
    parts = []
    for layer in range(LAYERS):
        down = [down_weight[layer, :48], down_weight[layer, 48:]]
        parts.append((rows[layer], jnp.concatenate(down, axis=1)))
    return parts


def add_low(first, second):
    return (first.astype(F32) + second.astype(F32)).astype(BF16)


def add_full(first, second):
    return first.astype(F32) + second.astype(F32)


def split_rest(total):
    down = total[240:].reshape(4, 48, 384)
    return (
        total[192:240].T,
        total[:192].T,
        jnp.transpose(down, (0, 2, 1)).reshape(1536, 48),
    )


def local_two_by_sixteen(
    tokens,
    qkv_weight,
    out_weight,
    up_weight,
    down_weight,
    norm_gains,
    doc_lengths,
    global_ids,
    random_ids,
    cotangent,
):
    docs_dev, block, width = tokens.shape
    me = lax.axis_index("seq").astype(jnp.int32)
    docs = lax.axis_index("docs").astype(jnp.int32)
    plane, core = me >> 2, me & 1
    chip = docs * 8 + (me >> 1)
    info = jnp.concatenate(
        [
            jnp.stack(
                [me, chip, pick(doc_lengths, plane), plane, docs, core, jnp.zeros_like(me), chip]
            ),
            doc_lengths,
        ]
    )
    features = key_features(
        lax.dynamic_index_in_dim(random_ids, plane, 1, keepdims=False),
        pick(global_ids, plane),
        pick(doc_lengths, plane),
    )

    wq = pack_qkv(qkv_weight, norm_gains, me, core)
    parts = pack_rest(out_weight, up_weight, down_weight, core)
    share = width // 32
    made = forward(info, features, tokens, wq, parts, 0)
    held, weights = (made[:6], made[6:12]), made[12:14]
    rest = list(zip(made[14:16], made[16:18]))
    gain = (made[18][0:2], made[18][2:4])
    base, grad_o, gain_1, *sums = feed_back(
        info, cotangent, None, gain[1], held[1][2:], rest[1], 1
    )
    extra, rest_grads_1, qkv_1, gain_1 = attend_back(
        features,
        held[1][1],
        grad_o,
        held[1][0],
        weights[1],
        sums,
        jnp.pad(gain_1, ((2, 4), (0, 0))),
        False,
        2,
    )
    base, grad_o, gain_0, *sums = feed_back(info, base, extra, gain[0], held[0][2:], rest[0], 3)
    extra, rest_grads, qkv_0, gain_grads = attend_back(
        features,
        held[0][1],
        grad_o,
        held[0][0],
        weights[0],
        sums,
        gain_1 + jnp.pad(gain_0, ((0, 6), (0, 0))),
        True,
        4,
    )
    grad_tokens = base.reshape(docs_dev, block, width) + extra.astype(F32)
    gain_grads = lax.dynamic_slice_in_dim(gain_grads, (docs * 16 + me) * share, share, axis=1)
    rest = [split_rest(part) for part in (rest_grads, rest_grads_1)]
    qkv_grads = jnp.stack([qkv_0, qkv_1])
    return (
        made[19],
        grad_tokens,
        jnp.transpose(qkv_grads, (0, 3, 1, 2)).reshape(LAYERS, 384, 144),
        *(jnp.stack(pair) for pair in zip(*rest)),
        gain_grads[:4].reshape(LAYERS, 2, share),
    )


def solution(mesh):
    def local(*args):
        docs_dev, _, width = args[0].shape
        if fits(mesh, docs_dev, width // HEAD):
            return local_two_by_sixteen(*args)
        return local_any_mesh(*args)

    return jax.shard_map(
        local,
        mesh=mesh,
        in_specs=(
            P("docs", "seq", None),
            P(None, ("docs", "seq"), None),
            P(None, ("docs", "seq"), None),
            P(None, ("docs", "seq"), None),
            P(None, ("docs", "seq"), None),
            P(None, None, ("docs", "seq")),
            P("docs"),
            P("docs", None),
            P(None, "docs", None),
            P("docs", "seq", None),
        ),
        out_specs=(
            P("docs", "seq", None),
            P("docs", "seq", None),
            P(None, "docs", "seq"),
            P(None, "docs", "seq"),
            P(None, "docs", "seq"),
            P(None, "docs", "seq"),
            P(None, None, ("docs", "seq")),
        ),
        check_vma=False,
    )
```

```python
import functools
import types

import jax
import jax.numpy as jnp
from jax import lax
from jax.experimental import pallas as pl
from jax.experimental.pallas import tpu as pltpu
from jax.sharding import PartitionSpec as P

HEAD = 64
RAND = 3
GLOB = 2
LAYERS = 2


NEGATIVE = -1e30
EPSILON = 1e-05


def with_halo(cells, sides, width):
    for axis, dim in sides:
        count = lax.axis_size(axis)
        head = lax.slice_in_dim(cells, 0, width, axis=dim)
        tail = lax.slice_in_dim(cells, cells.shape[dim] - width, cells.shape[dim], axis=dim)
        cells = jnp.concatenate(
            [
                lax.ppermute(tail, axis, [(i, (i + 1) % count) for i in range(count)]),
                cells,
                lax.ppermute(head, axis, [((i + 1) % count, i) for i in range(count)]),
            ],
            axis=dim,
        )
    return cells


def combined_all(value, axis, join):
    pieces = jax.tree.map(lambda part: lax.all_gather(part, axis), value)
    head = jax.tree.map(lambda part: part[0], pieces)
    tail = jax.tree.map(lambda part: part[1:], pieces)
    so_far, _ = lax.scan(lambda so_far, piece: (join(so_far, piece), None), head, tail)
    return so_far


def norm_rows(values, gain):
    centre = values - jnp.mean(values, axis=-1, keepdims=True)
    spread = jnp.mean(centre * centre, axis=-1, keepdims=True)
    return centre * lax.rsqrt(spread + EPSILON) * gain


def gelu_tanh(values):
    return jax.nn.gelu(values, approximate=True)


def earlier_equal(values):
    length = values.shape[-1]
    order = jnp.arange(length, dtype=jnp.int32)
    before = order[None, :] < order[:, None]
    same = values[..., :, None] == values[..., None, :]
    return jnp.sum(jnp.logical_and(same, before), axis=-1)


def merge_stats(first, second):
    highest = jnp.maximum(first[0], second[0])
    return (
        highest,
        first[1] * jnp.exp(first[0] - highest) + second[1] * jnp.exp(second[0] - highest),
    )


def sparse_probs(query, key_part, key_inside, scale):
    scores = (
        jnp.einsum("kbhd,kjhd->khbj", query, key_part, preferred_element_type=jnp.float32) * scale
    )
    scores = jnp.where(key_inside[:, None, None, :], scores, NEGATIVE)
    expo = jnp.exp(scores - jnp.max(scores, axis=-1, keepdims=True))
    return expo / jnp.sum(expo, axis=-1, keepdims=True)


def global_scores(global_query, local_keys, inside, scale):
    scores = (
        jnp.einsum(
            "ksbhd,kjhd->kshbj", global_query, local_keys, preferred_element_type=jnp.float32
        )
        * scale
    )
    return jnp.where(inside[:, None, None, None, :], scores, NEGATIVE)


def local_any_mesh(
    tokens,
    qkv_weight,
    out_weight,
    up_weight,
    down_weight,
    norm_gains,
    doc_lengths,
    global_ids,
    random_ids,
    cotangent,
):
    nseq = lax.axis_size("seq")
    device = lax.axis_index("seq")
    docs_dev, block, width = tokens.shape
    count = docs_dev * block
    heads = width // HEAD
    scale = HEAD ** (-0.5)
    capacity = max(2, (docs_dev * RAND + nseq - 1) // nseq)
    global_capacity = (docs_dev * GLOB + nseq - 1) // nseq
    entries = docs_dev * RAND
    global_entries = docs_dev * GLOB
    offsets = jnp.arange(block, dtype=jnp.int32)
    inside = (device * block + offsets)[None, :] < doc_lengths[:, None]
    live_rows = inside.reshape(count, 1)
    wanted = random_ids.reshape(nseq, entries)
    wanted_rank = earlier_equal(wanted)
    slot_ids = jnp.arange(capacity, dtype=jnp.int32)
    hits = jnp.logical_and((wanted == device)[:, :, None], wanted_rank[:, :, None] == slot_ids)
    hits = jnp.any(hits.reshape(nseq, docs_dev, RAND, capacity), axis=2)
    hits = jnp.transpose(hits, (0, 2, 1))
    doc_ids = jnp.arange(docs_dev, dtype=jnp.int32)
    send_doc = jnp.sum(jnp.where(hits, doc_ids, 0), axis=2)
    send_live = jnp.any(hits, axis=2)
    owner_pick = hits.astype(jnp.float32)
    listed_here = lax.dynamic_index_in_dim(wanted, device, 0, keepdims=False)
    listed_rank = lax.dynamic_index_in_dim(wanted_rank, device, 0, keepdims=False)
    fetch_slot = listed_here * capacity + listed_rank
    global_block = global_ids.reshape(global_entries)
    global_rank = earlier_equal(global_block)
    global_slot = global_block * global_capacity + global_rank
    own_entry = global_block == device
    owned = jnp.logical_and(
        own_entry[:, None], global_rank[:, None] == jnp.arange(global_capacity, dtype=jnp.int32)
    )
    entry_doc = jnp.arange(global_entries, dtype=jnp.int32) // GLOB
    global_send_doc = jnp.sum(jnp.where(owned, entry_doc[:, None], 0), axis=0)
    global_send_live = jnp.any(owned, axis=0)
    own_flag = jnp.any(own_entry.reshape(docs_dev, GLOB), axis=1)
    own_slot = jnp.sum(jnp.where(own_entry, global_rank, 0).reshape(docs_dev, GLOB), axis=1)
    neighbours = jnp.stack([(device - 1) % nseq, device, (device + 1) % nseq])
    key_blocks = jnp.concatenate(
        [
            jnp.broadcast_to(neighbours[None, :], (docs_dev, 3)),
            listed_here.reshape(docs_dev, RAND),
            global_ids,
        ],
        axis=1,
    )
    span = key_blocks.shape[1] * block
    key_inside = (key_blocks[:, :, None] * block + offsets < doc_lengths[:, None, None]).reshape(
        docs_dev, span
    )
    keep_local = inside[:, None, None, None, :]
    hidden = tokens.reshape(count, width).astype(jnp.float32)
    held = []
    for layer in range(LAYERS):
        weights = (
            lax.all_gather(qkv_weight[layer], ("docs", "seq"), axis=0, tiled=True),
            lax.all_gather(out_weight[layer], ("docs", "seq"), axis=0, tiled=True),
            lax.all_gather(up_weight[layer], ("docs", "seq"), axis=0, tiled=True),
            lax.all_gather(down_weight[layer], ("docs", "seq"), axis=0, tiled=True),
            lax.all_gather(norm_gains[layer], ("docs", "seq"), axis=1, tiled=True),
        )
        weight_qkv, weight_out, weight_up, weight_down, gain_pair = weights
        gain_pair = gain_pair.astype(jnp.float32)
        lowered = hidden.astype(jnp.bfloat16)
        projected = (
            jnp.dot(lowered, weight_qkv, preferred_element_type=jnp.float32)
            .astype(jnp.bfloat16)
            .reshape(docs_dev, block, 3 * width)
        )
        pairs = projected[:, :, width:]
        window = with_halo(pairs, (("seq", 1),), block)
        outgoing = jnp.where(
            send_live[:, :, None, None],
            jnp.take(pairs, send_doc, axis=0),
            jnp.zeros((), jnp.bfloat16),
        )
        incoming = lax.all_to_all(outgoing, "seq", split_axis=0, concat_axis=0, tiled=True)
        fetched = jnp.take(
            incoming.reshape(nseq * capacity, block, 2 * width), fetch_slot, axis=0
        ).reshape(docs_dev, RAND * block, 2 * width)
        global_send = jnp.where(
            global_send_live[:, None, None],
            jnp.take(projected, global_send_doc, axis=0),
            jnp.zeros((), jnp.bfloat16),
        )
        gathered = lax.all_gather(global_send, "seq", axis=0, tiled=True)
        global_picked = jnp.take(gathered, global_slot, axis=0).reshape(
            docs_dev, GLOB, block, 3 * width
        )
        global_query = global_picked[..., :width].reshape(docs_dev, GLOB, block, heads, HEAD)
        listed_pairs = jnp.concatenate(
            [
                window,
                fetched,
                global_picked[..., width:].reshape(docs_dev, GLOB * block, 2 * width),
            ],
            axis=1,
        )
        query = projected[:, :, :width].reshape(docs_dev, block, heads, HEAD)
        key_part = listed_pairs[:, :, :width].reshape(docs_dev, span, heads, HEAD)
        value_part = listed_pairs[:, :, width:].reshape(docs_dev, span, heads, HEAD)
        probs = sparse_probs(query, key_part, key_inside, scale)
        mixed = jnp.einsum(
            "khbj,kjhd->kbhd",
            probs.astype(jnp.bfloat16),
            value_part,
            preferred_element_type=jnp.float32,
        )
        local_keys = projected[:, :, width : 2 * width].reshape(docs_dev, block, heads, HEAD)
        local_values = projected[:, :, 2 * width :].reshape(docs_dev, block, heads, HEAD)
        wide_scores = global_scores(global_query, local_keys, inside, scale)
        global_top = jnp.max(wide_scores, axis=-1)
        global_total = jnp.sum(
            jnp.where(keep_local, jnp.exp(wide_scores - global_top[..., None]), 0.0), axis=-1
        )
        global_top, global_total = combined_all((global_top, global_total), "seq", merge_stats)
        wide_probs = (
            jnp.where(keep_local, jnp.exp(wide_scores - global_top[..., None]), 0.0)
            / global_total[..., None]
        )
        wide_part = jnp.einsum(
            "kshbj,kjhd->ksbhd",
            wide_probs.astype(jnp.bfloat16),
            local_values,
            preferred_element_type=jnp.float32,
        )
        wide_buffer = (
            jnp.zeros((nseq * global_capacity, block, width), jnp.float32)
            .at[global_slot]
            .set(wide_part.reshape(global_entries, block, width))
        )
        wide_sum = lax.psum_scatter(wide_buffer, "seq", scatter_dimension=0, tiled=True)
        attended = jnp.where(
            own_flag[:, None, None],
            jnp.take(wide_sum, own_slot, axis=0),
            mixed.reshape(docs_dev, block, width),
        )
        attended = attended.reshape(count, width).astype(jnp.bfloat16)
        after_attn = hidden + jnp.dot(attended, weight_out, preferred_element_type=jnp.float32)
        normed = norm_rows(after_attn, gain_pair[0])
        normed_low = normed.astype(jnp.bfloat16)
        up_values = jnp.dot(normed_low, weight_up, preferred_element_type=jnp.float32)
        activated = gelu_tanh(up_values).astype(jnp.bfloat16)
        after_ffn = normed + jnp.dot(activated, weight_down, preferred_element_type=jnp.float32)
        held.append(
            (
                weights,
                lowered,
                projected,
                listed_pairs,
                global_query,
                global_top,
                global_total,
                attended,
                after_attn,
                normed_low,
                up_values,
                activated,
                after_ffn,
            )
        )
        hidden = jnp.where(live_rows, norm_rows(after_ffn, gain_pair[1]), 0.0)
    gradient = cotangent.reshape(count, width).astype(jnp.float32)
    layer_grads = []
    for layer in reversed(range(LAYERS)):
        (
            weights,
            lowered,
            projected,
            listed_pairs,
            global_query,
            global_top,
            global_total,
            attended,
            after_attn,
            normed_low,
            up_values,
            activated,
            after_ffn,
        ) = held[layer]
        weights = (
            lax.all_gather(qkv_weight[layer], ("docs", "seq"), axis=0, tiled=True),
            lax.all_gather(out_weight[layer], ("docs", "seq"), axis=0, tiled=True),
            lax.all_gather(up_weight[layer], ("docs", "seq"), axis=0, tiled=True),
            lax.all_gather(down_weight[layer], ("docs", "seq"), axis=0, tiled=True),
            lax.all_gather(norm_gains[layer], ("docs", "seq"), axis=1, tiled=True),
        )
        weight_qkv, weight_out, weight_up, weight_down, gain_pair = weights
        gain_pair = gain_pair.astype(jnp.float32)
        gradient = jnp.where(live_rows, gradient, 0.0)
        grad_ffn, grad_gain_out = jax.vjp(norm_rows, after_ffn, gain_pair[1])[1](gradient)
        grad_down_low = grad_ffn.astype(jnp.bfloat16)
        grad_down_layer = jnp.einsum(
            "rf,rd->fd", activated, grad_down_low, preferred_element_type=jnp.float32
        )
        grad_activated = jnp.einsum(
            "rd,fd->rf", grad_down_low, weight_down, preferred_element_type=jnp.float32
        )
        grad_up_low = jax.vjp(gelu_tanh, up_values)[1](grad_activated)[0].astype(jnp.bfloat16)
        grad_up_layer = jnp.einsum(
            "rd,rf->df", normed_low, grad_up_low, preferred_element_type=jnp.float32
        )
        grad_normed = grad_ffn + jnp.einsum(
            "rf,df->rd", grad_up_low, weight_up, preferred_element_type=jnp.float32
        )
        grad_attn, grad_gain_mid = jax.vjp(norm_rows, after_attn, gain_pair[0])[1](grad_normed)
        grad_attn_low = grad_attn.astype(jnp.bfloat16)
        grad_out_layer = jnp.einsum(
            "rd,re->de", attended, grad_attn_low, preferred_element_type=jnp.float32
        )
        grad_mixed = (
            jnp.einsum("re,de->rd", grad_attn_low, weight_out, preferred_element_type=jnp.float32)
            .astype(jnp.bfloat16)
            .reshape(docs_dev, block, width)
        )
        query = projected[:, :, :width].reshape(docs_dev, block, heads, HEAD)
        key_part = listed_pairs[:, :, :width].reshape(docs_dev, span, heads, HEAD)
        value_part = listed_pairs[:, :, width:].reshape(docs_dev, span, heads, HEAD)
        probs = sparse_probs(query, key_part, key_inside, scale)
        grad_sparse = jnp.where(
            own_flag[:, None, None], jnp.zeros((), jnp.bfloat16), grad_mixed
        ).reshape(docs_dev, block, heads, HEAD)
        grad_probs = jnp.einsum(
            "kbhd,kjhd->khbj", grad_sparse, value_part, preferred_element_type=jnp.float32
        )
        delta = jnp.sum(probs * grad_probs, axis=-1, keepdims=True)
        grad_scores = (probs * (grad_probs - delta)).astype(jnp.bfloat16)
        grad_query = (
            jnp.einsum("khbj,kjhd->kbhd", grad_scores, key_part, preferred_element_type=jnp.float32)
            * scale
        )
        grad_key_part = (
            jnp.einsum("khbj,kbhd->kjhd", grad_scores, query, preferred_element_type=jnp.float32)
            * scale
        )
        grad_value_part = jnp.einsum(
            "khbj,kbhd->kjhd",
            probs.astype(jnp.bfloat16),
            grad_sparse,
            preferred_element_type=jnp.float32,
        )
        grad_listed = jnp.concatenate(
            [
                grad_key_part.reshape(docs_dev, span, width),
                grad_value_part.reshape(docs_dev, span, width),
            ],
            axis=2,
        )
        wide_out = jnp.where(
            global_send_live[:, None, None],
            jnp.take(grad_mixed, global_send_doc, axis=0),
            jnp.zeros((), jnp.bfloat16),
        )
        wide_all = lax.all_gather(wide_out, "seq", axis=0, tiled=True)
        wide_grad = jnp.take(wide_all, global_slot, axis=0).reshape(
            docs_dev, GLOB, block, heads, HEAD
        )
        local_keys = projected[:, :, width : 2 * width].reshape(docs_dev, block, heads, HEAD)
        local_values = projected[:, :, 2 * width :].reshape(docs_dev, block, heads, HEAD)
        wide_scores = global_scores(global_query, local_keys, inside, scale)
        wide_probs = (
            jnp.where(keep_local, jnp.exp(wide_scores - global_top[..., None]), 0.0)
            / global_total[..., None]
        )
        wide_grad_probs = jnp.einsum(
            "ksbhd,kjhd->kshbj", wide_grad, local_values, preferred_element_type=jnp.float32
        )
        wide_delta = lax.psum(jnp.sum(wide_probs * wide_grad_probs, axis=-1), "seq")
        wide_grad_scores = (wide_probs * (wide_grad_probs - wide_delta[..., None])).astype(
            jnp.bfloat16
        )
        wide_grad_query = (
            jnp.einsum(
                "kshbj,kjhd->ksbhd",
                wide_grad_scores,
                local_keys,
                preferred_element_type=jnp.float32,
            )
            * scale
        )
        wide_grad_keys = (
            jnp.einsum(
                "kshbj,ksbhd->kjhd",
                wide_grad_scores,
                global_query,
                preferred_element_type=jnp.float32,
            )
            * scale
        )
        wide_grad_values = jnp.einsum(
            "kshbj,ksbhd->kjhd",
            wide_probs.astype(jnp.bfloat16),
            wide_grad,
            preferred_element_type=jnp.float32,
        )
        global_grads = jnp.concatenate(
            [
                wide_grad_query.reshape(global_entries, block, width),
                grad_listed[:, (3 + RAND) * block :, :].reshape(global_entries, block, 2 * width),
            ],
            axis=2,
        )
        global_buffer = (
            jnp.zeros((nseq * global_capacity, block, 3 * width), jnp.float32)
            .at[global_slot]
            .set(global_grads)
        )
        global_share = lax.psum_scatter(global_buffer, "seq", scatter_dimension=0, tiled=True)
        global_mine = jnp.where(
            own_flag[:, None, None], jnp.take(global_share, own_slot, axis=0), 0.0
        )
        grad_fetched = grad_listed[:, 3 * block : (3 + RAND) * block, :].reshape(
            entries, block, 2 * width
        )
        back_out = (
            jnp.zeros((nseq * capacity, block, 2 * width), jnp.float32)
            .at[fetch_slot]
            .set(grad_fetched)
            .reshape(nseq, capacity, block, 2 * width)
        )
        back_in = lax.all_to_all(back_out, "seq", split_axis=0, concat_axis=0, tiled=True)
        grad_random = jnp.einsum(
            "dck,dcbf->kbf", owner_pick, back_in, precision=lax.Precision.HIGHEST
        )
        grad_window = grad_listed[:, : 3 * block, :]
        edges = jnp.concatenate([grad_window[:, :block], grad_window[:, 2 * block :]], axis=1)
        beside_all = with_halo(edges, (("seq", 1),), block)
        grad_pairs = (
            grad_window[:, block : 2 * block]
            + beside_all[:, :block]
            + beside_all[:, 3 * block :]
            + grad_random
            + global_mine[:, :, width:]
        )
        grad_pairs = grad_pairs + jnp.concatenate(
            [
                wide_grad_keys.reshape(docs_dev, block, width),
                wide_grad_values.reshape(docs_dev, block, width),
            ],
            axis=2,
        )
        grad_queries = grad_query.reshape(docs_dev, block, width) + global_mine[:, :, :width]
        grad_projected = (
            jnp.concatenate([grad_queries, grad_pairs], axis=2)
            .reshape(count, 3 * width)
            .astype(jnp.bfloat16)
        )
        grad_qkv_layer = jnp.einsum(
            "rd,re->de", lowered, grad_projected, preferred_element_type=jnp.float32
        )
        gradient = grad_attn + jnp.einsum(
            "re,de->rd", grad_projected, weight_qkv, preferred_element_type=jnp.float32
        )
        group_shares = (
            lax.psum_scatter(grad_qkv_layer, "docs", scatter_dimension=0, tiled=True),
            lax.psum_scatter(grad_out_layer, "docs", scatter_dimension=0, tiled=True),
            lax.psum_scatter(grad_up_layer, "docs", scatter_dimension=0, tiled=True),
            lax.psum_scatter(grad_down_layer, "docs", scatter_dimension=0, tiled=True),
            lax.psum_scatter(
                jnp.stack([grad_gain_mid, grad_gain_out]), "docs", scatter_dimension=1, tiled=True
            ),
        )
        shares = (
            lax.psum_scatter(group_shares[0], "seq", scatter_dimension=1, tiled=True),
            lax.psum_scatter(group_shares[1], "seq", scatter_dimension=1, tiled=True),
            lax.psum_scatter(group_shares[2], "seq", scatter_dimension=1, tiled=True),
            lax.psum_scatter(group_shares[3], "seq", scatter_dimension=1, tiled=True),
            lax.psum_scatter(group_shares[4], "seq", scatter_dimension=1, tiled=True),
        )
        layer_grads.insert(0, shares)
    stacked = [
        jnp.stack([layer_grads[number][member] for number in range(LAYERS)]) for member in range(5)
    ]
    return (
        hidden.astype(jnp.bfloat16).reshape(docs_dev, block, width),
        gradient.reshape(docs_dev, block, width),
        stacked[0],
        stacked[1],
        stacked[2],
        stacked[3],
        stacked[4],
    )


PLANES = 4
GROUPS = 4
CHIPS = 16
GROUP_HEADS = 3
CUT = 240
MESH = pl.DeviceIdType.MESH
F32 = jnp.float32
BF16 = jnp.bfloat16


def fits(mesh, docs_dev, heads):
    return (
        mesh.shape["docs"] == 2
        and mesh.shape["seq"] == 16
        and docs_dev == PLANES
        and heads == GROUPS * GROUP_HEADS
    )


def swap(value, bits):
    return lax.ppermute(value, "seq", [(i, i ^ bits) for i in range(16)])


def swap_docs(value):
    return lax.ppermute(value, "docs", [(0, 1), (1, 0)])


def dot(left, right):
    return lax.dot_general(left, right, (((1,), (0,)), ((), ())), preferred_element_type=F32)


def dot_nt(left, right):
    return lax.dot_general(left, right, (((1,), (1,)), ((), ())), preferred_element_type=F32)


def dot_tn(left, right):
    return lax.dot_general(left, right, (((0,), (0,)), ((), ())), preferred_element_type=F32)


def vmem():
    return pl.BlockSpec(memory_space=pltpu.VMEM)


def smem():
    return pl.BlockSpec(memory_space=pltpu.SMEM)


def hbm():
    return pl.BlockSpec(memory_space=pltpu.HBM)


def params():
    return pltpu.CompilerParams(vmem_limit_bytes=56 * 2**20)


QUERIES = 512
BACK_QUERIES = 512


def key_features(own_random, own_global, length):
    block = jnp.arange(16, dtype=jnp.int32)
    window = jnp.stack([(block + 15) % 16, block, (block + 1) % 16], axis=1)
    ids = jnp.concatenate([window, own_random, jnp.broadcast_to(own_global, (16, GLOB))], axis=1)
    count = jnp.sum((ids[:, :, None] == block).astype(F32), axis=1).T
    special = jnp.any(own_global[None, :] == block[:, None], axis=1)
    count = jnp.where(special[None, :], 1.0, count)
    extra = jnp.where(count > 0, jnp.log(jnp.maximum(count, 1.0)), NEGATIVE)
    inside = jnp.arange(1024, dtype=jnp.int32)[:, None] < length
    extra = jnp.where(inside, jnp.repeat(extra, 64, axis=0), NEGATIVE)
    high = extra.astype(BF16)
    low = jnp.where(extra > 0, extra - high.astype(F32), 0.0).astype(BF16)
    return jnp.concatenate([high, low, jnp.zeros((1024, 32), BF16)], axis=1)


def halves_beside(rows):
    return jnp.concatenate([rows[:32], rows[32:]], axis=1)


def halves_below(rows):
    return jnp.concatenate([rows[:, :192], rows[:, 192:]], axis=0)


def spread_heads(qkv, feature_ref, key_scr, query_scr):
    row = lax.broadcasted_iota(jnp.int32, (1024, 64), 0) // 64
    lane = lax.broadcasted_iota(jnp.int32, (1024, 64), 1)
    place = jnp.where(jnp.logical_and(lane < 32, lane % 16 == row), 1.0, 0.0).astype(BF16)
    for h in range(GROUP_HEADS):
        key_scr[h] = jnp.concatenate([qkv[:, 128 * h : 128 * h + 64], feature_ref[...]], axis=1)
        query = qkv[:, 384 + 64 * h : 448 + 64 * h] * jnp.asarray(HEAD**-0.5, BF16)
        query_scr[h] = jnp.concatenate([query, place], axis=1)


def expo_columns(scores):
    expo = jnp.exp(scores - jnp.max(scores, axis=0, keepdims=True))
    return expo, 1.0 / jnp.sum(expo, axis=0, keepdims=True)


def load_up(up_ref, wu, wo, sems):
    pltpu.make_async_copy(up_ref.at[:, :, :, pl.ds(1536, 384)], wo, sems.at[0]).start()
    pltpu.make_async_copy(up_ref.at[:, :, :, pl.ds(0, 1536)], wu, sems.at[1]).start()


def load_down(down_ref, wd, sems):
    for plane in range(2):
        for part in range(2):
            source = down_ref.at[plane, :, :, pl.ds(768 * part, 768)]
            pltpu.make_async_copy(source, wd.at[:, plane, part], sems.at[2]).start()


def wait_weight(scr, sem):
    pltpu.make_async_copy(scr, scr, sem).wait()


def inside_rows(info):
    row = lax.broadcasted_iota(jnp.int32, (256, 1), 0)
    length = jnp.zeros_like(row)
    for k in range(PLANES):
        length = jnp.where(row // 64 == k, info[8 + k], length)
    return info[0] * 64 + row % 64 < length


def norm_parts(values):
    centre = values - jnp.mean(values, axis=-1, keepdims=True)
    spread = jnp.mean(centre * centre, axis=-1, keepdims=True)
    rate = lax.rsqrt(spread + EPSILON)
    return centre * rate, rate


def norm_back(unit, rate, gain, grad):
    scaled = grad * gain
    inner = jnp.mean(scaled * unit, axis=-1, keepdims=True)
    outer = jnp.mean(scaled, axis=-1, keepdims=True)
    return rate * (scaled - outer - unit * inner), jnp.sum(grad * unit, axis=0, keepdims=True)


CURVE = 0.7978845608028654


def gelu_parts(values):
    square = values * values
    bend = jnp.tanh(CURVE * (values + 0.044715 * (square * values)))
    return 0.5 * values * (1.0 + bend), bend, square


def gelu_slope(values, bend, square):
    return 0.5 * (1.0 + bend) + 0.5 * values * (1.0 - bend * bend) * (
        CURVE * (1.0 + 3 * 0.044715 * square)
    )


WEIGHT_SCRATCH = [
    pltpu.VMEM((2, 16, 48, 1536), BF16),
    pltpu.VMEM((16, 2, 2, 48, 768), BF16),
    pltpu.VMEM((2, 16, 48, 384), BF16),
]


def feed_back_kernel(
    pieces,
    layer,
    info,
    base_ref,
    extra_ref,
    gain_ref,
    gain_sum_ref,
    mixed_ref,
    h1_ref,
    up_ref,
    h2_ref,
    *refs,
):
    w_refs, refs = refs[:pieces], refs[pieces:]
    dh1_ref, do_ref, dgain_ref, *sum_refs, wu, wd, wo, gu, gd, go, got, sems, pair_sems, out_sems = refs
    load_down(w_refs[1], wd, sems)
    load_up(w_refs[0], wu, wo, sems)
    docs, me = lax.axis_index("docs"), lax.axis_index("seq")
    mate = (docs, flip(me, 1))
    greet([mate])
    units = [(ry, place) for ry in range(2) for place in range(8)]

    def other_docs(ry):
        return docs if ry == 0 else 1 - docs

    def owner(place, rc):
        return flip(me, (place % 2) * 8 + (place // 2 % 2) * 4 + (place // 4) * 2 + rc)

    def to_mate(source, ry, place, first, count, n):
        pltpu.make_async_remote_copy(
            source,
            got.at[ry, place, pl.ds(first, count)],
            pair_sems.at[0, n],
            pair_sems.at[1, n],
            device_id=mate,
            device_id_type=MESH,
        ).start()

    def up_to_mate(part):
        x, z = (me // 2) % 2, me // 4
        across = x if part % 2 == 0 else 1 - x
        low = z % 2 if part // 2 % 2 == 0 else 1 - z % 2
        high = z // 2 if part // 4 == 0 else 1 - z // 2
        for half in range(2):
            source = gu.at[half, 2 * part + 1 - me % 2]
            to_mate(source, other_docs(half), 4 * across + 2 * low + high, 0, 192, 0)

    if layer == 0:
        parts = [
            base_ref[64 * k : 64 * k + 64, :] + extra_ref[k].astype(F32)
            for k in range(PLANES)
        ]
        grad = jnp.concatenate(parts, axis=0)
    else:
        grad = base_ref[...].reshape(256, 768).astype(F32)
    grad = jnp.where(inside_rows(info), grad, 0.0)
    unit2, rate2 = norm_parts(h2_ref[...])
    dh2, dgain1 = norm_back(unit2, rate2, gain_ref[2 * layer + 1 : 2 * layer + 2, :], grad)
    dgain_ref[...] = gain_sum_ref[...] if layer == 0 else jnp.zeros_like(dgain_ref)
    dgain_ref[2 * layer + 1 : 2 * layer + 2, :] = dgain1
    df = dh2.astype(BF16)
    df_turned = df.T
    unit1, rate1 = norm_parts(h1_ref[...])
    x1_low = (unit1 * gain_ref[2 * layer : 2 * layer + 1, :]).astype(BF16)
    wait_weight(wd, sems.at[2])
    wait_weight(wu, sems.at[1])
    dx1 = dh2
    for part in range(8):
        at = 384 * part
        d_act = dot_nt(df, wd[2 * part : 2 * part + 2].reshape(384, 768))
        up = up_ref[:, at : at + 384]
        act, bend, square = gelu_parts(up)
        act = act.astype(BF16)
        dup = (gelu_slope(up, bend, square) * d_act).astype(BF16)
        side, start = part // 4, 384 * (part % 4)
        dx1 += dot_nt(dup, wu[side, :, :, start : start + 384].reshape(768, 384))
        gt_up = dot_tn(dup, x1_low).astype(BF16)
        for n in range(2):
            for half in range(2):
                gu[half, 2 * part + n] = gt_up[
                    192 * n : 192 * n + 192, 384 * half : 384 * half + 384
                ]
        gt_down = dot(df_turned, act).astype(BF16)
        row = 48 * (part % 4)
        for s in range(16):
            gd[part // 4, s, row : row + 48, :] = gt_down[48 * s : 48 * s + 48]
        up_to_mate(part)
        if part % 4 == 3:
            for place in range(8):
                source = gd.at[part // 4, owner(place, 1)]
                to_mate(source, other_docs(part // 4), place, 240, 192, 1)
    dh1, dgain0 = norm_back(unit1, rate1, gain_ref[2 * layer : 2 * layer + 1, :], dx1)
    dgain_ref[2 * layer : 2 * layer + 1, :] = dgain0
    dh1_ref[...] = dh1
    da = dh1.astype(BF16)
    gt_out = dot_tn(da, mixed_ref[...]).astype(BF16)
    for s in range(16):
        for half in range(2):
            go[half, s] = gt_out[48 * s : 48 * s + 48, 384 * half : 384 * half + 384]
    for ry, place in units:
        to_mate(go.at[other_docs(ry), owner(place, 1)], ry, place, 192, 48, 2)
    wait_weight(wo, sems.at[0])
    do = dot_nt(da[:, 0:384], wo[0].reshape(768, 384))
    do += dot_nt(da[:, 384:768], wo[1].reshape(768, 384))
    do = do.astype(BF16)
    for k in range(PLANES):
        for g in range(GROUPS):
            do_ref[4 * k + g] = halves_beside(do[64 * k : 64 * k + 64, 192 * g : 192 * g + 192])
    copies = []
    for n, (scr, first, count) in enumerate(((gu, 0, 192), (gd, 240, 192), (go, 192, 48))):
        part = got.at[:, :, pl.ds(first, count)]
        pltpu.make_async_copy(part, part, pair_sems.at[1, n]).wait()
        for ry, place in units:
            span = slice(first, first + count)
            own = scr[other_docs(ry), owner(place, 0)].astype(F32)
            got[ry, place, span] = (own + got[ry, place, span].astype(F32)).astype(BF16)
            if n == 1:
                source, ref = got.at[ry, place, pl.ds(CUT, 432 - CUT)], sum_refs[2 + place // 4]
                target = ref.at[ry, place % 4]
            elif n == 2:
                source, target = got.at[ry, place, pl.ds(0, CUT)], sum_refs[ry].at[place]
            if n > 0:
                copies.append(pltpu.make_async_copy(source, target, out_sems.at[len(copies)]))
                copies[-1].start()
    for n, scr in enumerate((gu, gd, go)):
        half = scr.at[:, pl.ds(0, 8)]
        pltpu.make_async_copy(half, half, pair_sems.at[0, n]).wait()
    for copy in copies:
        copy.wait()


def feed_back(layer, info, base, extra, gains, gain_sum, saved, weights, number):
    mixed, h1, up, h2 = saved
    return pl.pallas_call(
        functools.partial(feed_back_kernel, len(weights), layer),
        out_shape=(
            jax.ShapeDtypeStruct((256, 768), F32),
            jax.ShapeDtypeStruct((16, 32, 384), BF16),
            jax.ShapeDtypeStruct((8, 768), F32),
            jax.ShapeDtypeStruct((8, CUT, 384), BF16),
            jax.ShapeDtypeStruct((8, CUT, 384), BF16),
            jax.ShapeDtypeStruct((2, 4, 432 - CUT, 384), BF16),
            jax.ShapeDtypeStruct((2, 4, 432 - CUT, 384), BF16),
        ),
        in_specs=[smem()] + [vmem()] * 8 + [hbm() for _ in weights],
        out_specs=(vmem(), vmem(), vmem(), hbm(), hbm(), hbm(), hbm()),
        scratch_shapes=WEIGHT_SCRATCH
        + [
            pltpu.VMEM((2, 16, 192, 384), BF16),
            pltpu.VMEM((2, 16, 192, 384), BF16),
            pltpu.VMEM((2, 16, 48, 384), BF16),
            pltpu.VMEM((2, 8, 432, 384), BF16),
            pltpu.SemaphoreType.DMA((3,)),
            pltpu.SemaphoreType.DMA((2, 3)),
            pltpu.SemaphoreType.DMA((32,)),
        ],
        compiler_params=pltpu.CompilerParams(
            collective_id=number, has_side_effects=True, vmem_limit_bytes=56 * 2**20
        ),
        cost_estimate=pl.CostEstimate(
            flops=6 * 10**9, bytes_accessed=40 * 10**6, transcendentals=10**6
        ),
        name="feed_back",
    )(info, base, extra, gains, gain_sum, mixed, h1, up, h2, *weights)


def flip(index, bits):
    for bit in (1, 2, 4, 8):
        if bits & bit:
            index = index + bit - 2 * bit * ((index // bit) % 2)
    return index


def greet(peers):
    barrier = pltpu.get_barrier_semaphore()
    for peer in peers:
        pl.semaphore_signal(barrier, inc=1, device_id=peer, device_id_type=MESH)
    pl.semaphore_wait(barrier, len(peers))


def remote(source, target, sems, n, peer):
    return pltpu.make_async_remote_copy(
        source, target, sems.at[0, n], sems.at[1, n], device_id=peer, device_id_type=MESH
    )


def comm_params(number):
    return pltpu.CompilerParams(
        collective_id=number, has_side_effects=True, vmem_limit_bytes=16 * 2**20
    )


class Spread:
    def __init__(self, low_ref, x_ref, sems, own_sem):
        self.low_ref, self.x_ref, self.sems = low_ref, x_ref, sems
        self.docs, self.me = lax.axis_index("docs"), lax.axis_index("seq")
        self.own = pltpu.make_async_copy(low_ref.at[self.me // 4], x_ref.at[self.me], own_sem)
        self.hops, self.across, self.mates = [], [], []

    def send(self, source, slot, n, bits):
        peer = (self.docs, flip(self.me, bits))
        copy = remote(source, self.x_ref.at[slot], self.sems, n, peer)
        copy.start()
        return copy

    def begin(self):
        for rz in range(1, 4):
            source = self.low_ref.at[flip(self.me, 4 * rz) // 4]
            self.hops.append(self.send(source, self.me, rz, 4 * rz))
        self.own.start()
        source = self.low_ref.at[self.me // 4]
        self.across.append(self.send(source, self.me, 4, 2))
        self.mates.append(self.send(source, self.me, 8, 1))

    def forward(self, rz):
        self.hops[rz - 1].wait_recv()
        slot = flip(self.me, 4 * rz)
        self.across.append(self.send(self.x_ref.at[slot], slot, 4 + rz, 2))
        self.mates.append(self.send(self.x_ref.at[slot], slot, 8 + rz, 1))

    def from_beside(self):
        for rz in range(4):
            self.across[rz].wait_recv()
            slot = flip(flip(self.me, 4 * rz), 2)
            self.mates.append(self.send(self.x_ref.at[slot], slot, 12 + rz, 1))

    def arrived(self):
        for copy in self.mates:
            copy.wait_recv()
        self.own.wait()

    def finish(self):
        for copy in self.hops + self.across + self.mates:
            copy.wait_send()


class Slabs:
    def __init__(self, source, w_ref, sems, own_sem, docs_first=False):
        self.source, self.w_ref, self.sems = source, w_ref, sems
        self.docs, self.me = lax.axis_index("docs"), lax.axis_index("seq")
        self.plane, self.x, self.core = self.me // 4, (self.me // 2) % 2, self.me % 2
        beside, over = (self.docs, flip(self.me, 2)), (1 - self.docs, self.me)
        self.peers = (over, beside) if docs_first else (beside, over)
        if docs_first:
            self.near = ((self.docs, self.x), (1 - self.docs, self.x))
            self.far = ((self.docs, 1 - self.x), (1 - self.docs, 1 - self.x))
        else:
            self.near = ((self.docs, self.x), (self.docs, 1 - self.x))
            self.far = ((1 - self.docs, self.x), (1 - self.docs, 1 - self.x))
        self.mate = (self.docs, flip(self.me, 1))
        self.own = pltpu.make_async_copy(source, self.slot(self.near[0], self.plane), own_sem)

    def slot(self, at, z):
        return self.w_ref.at[self.core, 8 * at[0] + 2 * z + at[1]]

    def copy(self, at, z, own, send, recv, peer):
        slot = self.slot(at, z)
        return pltpu.make_async_remote_copy(
            self.source if own else slot,
            slot,
            self.sems.at[0, send],
            self.sems.at[1, recv],
            device_id=peer,
            device_id_type=MESH,
        )

    def line(self, z, own, step):
        peer = (self.docs, self.me + 4 * step)
        return self.copy(self.near[0], z, own, z + (0 if step > 0 else 4), z, peer)

    def first(self, z, own=False):
        return self.copy(self.near[0], z, own, 8 + z, 8 + z, self.peers[0])

    def second(self, z, n, own=False):
        return self.copy(self.near[n], z, own, 12 + 4 * n + z, 12 + 4 * n + z, self.peers[1])

    def core_copy(self, at, n, z, own=False):
        return self.copy(at, z, own, 20 + 4 * n + z, 20 + 4 * n + z, self.mate)

    def begin(self):
        self.own.start()
        for step in (1, -1):
            pl.when(self.has(self.plane + step))(self.line(self.plane, True, step).start)
        self.first(self.plane, True).start()
        self.core_copy(self.near[0], 0, self.plane, True).start()

    def has(self, z):
        return jnp.logical_and(z >= 0, z < PLANES)

    def each(self, distance, act):
        if distance == 0:
            act(self.plane, 0)
            return
        for step in (1, -1):
            z = self.plane - step * distance
            pl.when(self.has(z))(functools.partial(act, z, step))

    def from_line(self, distance):
        def act(z, step):
            self.line(z, False, step).wait_recv()
            pl.when(self.has(self.plane + step))(self.line(z, False, step).start)
            self.first(z).start()
            self.core_copy(self.near[0], 0, z).start()

        self.each(distance, act)

    def from_first(self, distance):
        def act(z, step):
            self.first(z).wait_recv()
            self.second(z, 0, distance == 0).start()
            self.second(z, 1).start()
            self.core_copy(self.near[1], 1, z).start()

        self.each(distance, act)

    def from_second(self, distance):
        def act(z, step):
            for n in range(2):
                self.second(z, n).wait_recv()
                self.core_copy(self.far[n], 2 + n, z).start()

        self.each(distance, act)

    def arrived(self):
        for z in range(PLANES):
            for n, at in enumerate(self.near + self.far):
                self.core_copy(at, n, z).wait_recv()
        self.own.wait()

    def finish(self):
        for z in range(PLANES):
            for step in (1, -1):
                sent = jnp.logical_and(
                    (self.plane - z) * step >= 0, self.has(self.plane + step)
                )
                pl.when(sent)(self.line(z, False, step).wait_send)
            self.first(z).wait_send()
            for n, at in enumerate(self.near + self.far):
                if n < 2:
                    self.second(z, n).wait_send()
                self.core_copy(at, n, z).wait_send()


class Rows:
    def __init__(self, source, w_ref, sems, own_sem):
        self.source, self.w_ref, self.sems = source, w_ref, sems
        self.docs, self.me = lax.axis_index("docs"), lax.axis_index("seq")
        self.over = (1 - self.docs, self.me)
        self.own = pltpu.make_async_copy(source, self.slot(self.me // 4), own_sem)
        self.hops, self.moved = [], []

    def slot(self, z):
        return self.w_ref.at[pl.ds(8 * self.docs + 2 * z, 2)]

    def begin(self):
        target = self.slot(self.me // 4)
        for rz in range(1, 4):
            peer = (self.docs, flip(self.me, 4 * rz))
            self.hops.append(remote(self.source, target, self.sems, rz, peer))
            self.hops[-1].start()
        self.own.start()
        self.moved.append(remote(self.source, target, self.sems, 4, self.over))
        self.moved[0].start()

    def forward(self, rz):
        self.hops[rz - 1].wait_recv()
        slot = self.slot(flip(self.me, 4 * rz) // 4)
        self.moved.append(remote(slot, slot, self.sems, 4 + rz, self.over))
        self.moved[-1].start()

    def arrived(self):
        for copy in self.moved:
            copy.wait_recv()
        self.own.wait()

    def finish(self):
        for copy in self.hops + self.moved:
            copy.wait_send()


class Collect:
    def __init__(self, keep_ref, send_ref, land, got_core, got_x, sum_x, near, sums, sems):
        self.keep_ref, self.send_ref, self.land, self.got_core = keep_ref, send_ref, land, got_core
        self.got_x, self.sum_x, self.near, self.sums, self.sems = got_x, sum_x, near, sums, sems
        self.docs, self.me = lax.axis_index("docs"), lax.axis_index("seq")
        self.order = (3, 2, 1, 0)
        self.first, self.across, self.hops = {}, {}, []

    def begin(self):
        mate = (self.docs, flip(self.me, 1))
        for rz in self.order:
            for n in (2 * rz + 1, 2 * rz):
                self.first[n] = remote(
                    self.send_ref.at[n], self.got_core.at[n], self.sems, n, mate
                )
                self.first[n].start()

    def along_x(self):
        beside = (self.docs, flip(self.me, 2))
        for rz in self.order:
            n = 2 * rz + 1
            self.first[n].wait_recv()
            self.sum_x[rz] = add_low(self.keep_ref[n], self.got_core[n])
            self.across[rz] = remote(
                self.sum_x.at[rz], self.got_x.at[rz], self.sems, 8 + rz, beside
            )
            self.across[rz].start()
            n = 2 * rz
            self.first[n].wait_recv()
            self.near[rz] = add_full(self.keep_ref[n], self.got_core[n])

    def along_z(self):
        plane = self.me // 4
        for rz in self.order:
            self.across[rz].wait_recv()
            total = add_low(self.near[rz], self.got_x[rz])
            if rz == 0:
                self.land[plane] = total
            else:
                self.sums[rz] = total
                peer = (self.docs, flip(self.me, 4 * rz))
                copy = remote(self.sums.at[rz], self.land.at[plane], self.sems, 12 + rz, peer)
                copy.start()
                self.hops.append(copy)

    def finish(self):
        for copy in self.hops:
            copy.wait_recv()
        for copy in list(self.first.values()) + list(self.across.values()) + self.hops:
            copy.wait_send()


class Exchange:
    def __init__(self, source, land, sems, own_sem):
        docs, me = lax.axis_index("docs"), lax.axis_index("seq")
        self.copies = []
        for bits in range(15, 0, -1):
            peer = flip(me, bits)
            self.copies.append(remote(source.at[peer], land.at[me], sems, bits, (docs, peer)))
        self.own = pltpu.make_async_copy(source.at[me], land.at[me], own_sem)

    def begin(self):
        for copy in self.copies:
            copy.start()
        self.own.start()

    def arrived(self):
        for copy in self.copies:
            copy.wait_recv()
        self.own.wait()

    def finish(self):
        for copy in self.copies:
            copy.wait_send()


class Line:
    PLACE = (0, 2, 1, 3)

    def __init__(self, own, from_left, from_right, sems):
        self.own, self.landing, self.sems = own, (from_left, from_right), sems
        self.docs, self.me = lax.axis_index("docs"), lax.axis_index("seq")
        self.plane = self.me // 4

    def copy(self, place, target, step):
        side = 0 if step > 0 else 1
        return pltpu.make_async_remote_copy(
            self.own.at[place],
            self.landing[side].at[target],
            self.sems.at[0, side, target],
            self.sems.at[1, side, target],
            device_id=(self.docs, self.me + 4 * step),
            device_id_type=MESH,
        )

    def at(self, plane, act):
        pl.when(self.plane == plane)(act)

    def begin(self, rz):
        for plane, step in ((0, 1), (3, -1)):
            self.at(plane, self.copy(self.PLACE[rz], plane ^ rz, step).start)

    def hop(self, number):
        for plane, target, step in (
            ((1, 3, 1), (2, 0, -1)),
            ((1, 0, -1), (2, 3, 1)),
            ((1, 2, 1), (2, 1, -1)),
        )[number]:
            place, side = self.PLACE[plane ^ target], 0 if step > 0 else 1

            def act(place=place, side=side, target=target, step=step):
                copy = self.copy(place, target, step)
                copy.wait_recv()
                self.own[place] = add_low(self.own[place], self.landing[side][target])
                copy.start()

            self.at(plane, act)

    def total(self, out_ref, rows):
        for plane in range(PLANES):

            def act(plane=plane):
                total = self.own[0, rows].astype(F32)
                for side, step in ((0, 1), (1, -1)):
                    if 0 <= plane - step < PLANES:
                        total = total + self.landing[side][plane, rows].astype(F32)
                out_ref[...] = total

            self.at(plane, act)

    def arrived(self):
        for plane in range(PLANES):

            def act(plane=plane):
                for step in (1, -1):
                    if 0 <= plane - step < PLANES:
                        self.copy(0, plane, step).wait_recv()

            self.at(plane, act)

    def finish(self):
        for plane in range(PLANES):

            def act(plane=plane):
                for target in range(PLANES):
                    step = 1 if target > plane else -1
                    if target != plane:
                        self.copy(self.PLACE[plane ^ target], target, step).wait_send()

            self.at(plane, act)


class Everywhere:
    def __init__(self, total, got, sems):
        self.total, self.got, self.sems = total, got, sems
        docs, me = lax.axis_index("docs"), lax.axis_index("seq")
        self.peers = [(docs, flip(me, bits)) for bits in (1, 2, 4, 8)] + [(1 - docs, me)]
        self.copies = []

    def step(self):
        n = len(self.copies)
        if n > 0:
            self.copies[-1].wait_recv()
            self.total[n] = self.total[n - 1] + self.got[n - 1]
        if n < len(self.peers):
            copy = remote(self.total.at[n], self.got.at[n], self.sems, n, self.peers[n])
            copy.start()
            self.copies.append(copy)

    def finish(self):
        for copy in self.copies:
            copy.wait_send()


class Rest:
    ORDER = (3, 1, 2, 0)

    def __init__(self, a_keep, a_send, b_keep, b_send, scr):
        self.a_keep, self.a_send, self.b_keep, self.b_send = a_keep, a_send, b_keep, b_send
        self.scr = scr
        docs, me = lax.axis_index("docs"), lax.axis_index("seq")
        self.beside, self.over = (docs, flip(me, 2)), (1 - docs, me)
        self.line = Line(scr.own, scr.left, scr.right, scr.line_sems)
        self.sent = []

    def copy(self, n, place):
        scr = self.scr
        source, target, peer = (
            (self.a_send.at[4 + place], scr.a_got.at[4 + place], self.over),
            (self.b_send.at[1, place], scr.b_got.at[1, place], self.beside),
            (self.a_send.at[place], scr.a_got.at[place], self.over),
            (self.b_send.at[0, place], scr.b_got.at[0, place], self.beside),
            (scr.a_far.at[place], scr.a_far_got.at[place], self.beside),
            (scr.b_far.at[place], scr.b_far_got.at[place], self.over),
        )[n]
        return remote(source, target, scr.rest_sems, 4 * n + place, peer)

    def start(self, n, place):
        self.sent.append(self.copy(n, place))
        self.sent[-1].start()

    def first(self, place):
        for n in range(4):
            self.start(n, place)

    def second(self, place):
        scr = self.scr
        self.copy(0, place).wait_recv()
        scr.a_far[place] = add_low(self.a_keep[4 + place], scr.a_got[4 + place])
        self.start(4, place)
        self.copy(1, place).wait_recv()
        scr.b_far[place] = add_low(self.b_keep[1, place], scr.b_got[1, place])
        self.start(5, place)

    def third(self, place):
        scr = self.scr
        self.copy(2, place).wait_recv()
        self.copy(4, place).wait_recv()
        near = add_full(self.a_keep[place], scr.a_got[place]) + scr.a_far_got[place].astype(F32)
        scr.own[place, :CUT] = near.astype(BF16)
        self.copy(3, place).wait_recv()
        self.copy(5, place).wait_recv()
        near = add_full(self.b_keep[0, place], scr.b_got[0, place])
        near = near + scr.b_far_got[place].astype(F32)
        scr.own[place, CUT:] = near.astype(BF16)
        if place > 0:
            self.line.begin(Line.PLACE[place])

    def finish(self):
        for copy in self.sent:
            copy.wait_send()
        self.line.finish()


class Route:
    def __init__(self, source, out_ref, sems):
        self.source, self.out_ref, self.sems = source, out_ref, sems
        self.docs, self.me = lax.axis_index("docs"), lax.axis_index("seq")

    def each(self, act_here, act_there):
        for t in range(3):
            local = 3 * (self.me // 4) + t
            number = 16 * (local // 4) + 4 * (self.me % 4) + local % 4
            owner, slot = number // 3, number % 3
            target = self.out_ref.at[slot]
            here = pltpu.make_async_copy(self.source.at[t], target, self.sems.at[2, slot])
            there = pltpu.make_async_remote_copy(
                self.source.at[t],
                target,
                self.sems.at[0, t],
                self.sems.at[1, slot],
                device_id=(self.docs, owner),
                device_id_type=MESH,
            )
            pl.when(owner == self.me)(functools.partial(act_here, here))
            pl.when(owner != self.me)(functools.partial(act_there, there))

    def begin(self):
        self.each(lambda copy: copy.start(), lambda copy: copy.start())

    def finish(self):
        self.each(lambda copy: copy.wait(), lambda copy: copy.wait_send())
        for slot in range(3):
            number = 3 * self.me + slot
            local = 4 * (number // 16) + number % 4
            source = 4 * (local // 3) + (number % 16) // 4
            target = self.out_ref.at[slot]
            wait = pltpu.make_async_copy(target, target, self.sems.at[1, slot]).wait
            pl.when(source != self.me)(wait)


def back_scratch(width):
    low = 432 - CUT
    sems = pltpu.SemaphoreType.DMA

    def vm(*shape, dtype=BF16):
        return pltpu.VMEM(shape, dtype)

    return dict(
        qkv=vm(1024, 576),
        weight=vm(CHIPS, 48, 640),
        x=vm(16, 64, width),
        a_keep=vm(8, CUT, 384),
        b_keep=vm(2, 4, low, 384),
        load_sems=sems((5,)),
        do=vm(16, 32, 384),
        do_sems=sems((2, 16)),
        do_own=sems,
        key=vm(3, 1024, 128),
        query=vm(3, 1024, 128),
        value=vm(3, 1024, 64),
        turned=vm(3, 64, 1024),
        side=vm(2, 3, 1024, 128),
        dkv=vm(3, 1024, 128, dtype=F32),
        dq=vm(1024 // BACK_QUERIES, 192, BACK_QUERIES, dtype=F32),
        dqkv=vm(1024, 576),
        rows=vm(2, 8, 64, width),
        land=vm(4, 64, width),
        got_core=vm(8, 64, width),
        got_x=vm(4, 64, width),
        sum_x=vm(4, 64, width),
        near=vm(4, 64, width, dtype=F32),
        sums=vm(4, 64, width),
        row_sems=sems((2, 16)),
        a_got=vm(8, CUT, 384),
        b_got=vm(2, 4, low, 384),
        a_far=vm(4, CUT, 384),
        a_far_got=vm(4, CUT, 384),
        b_far=vm(4, low, 384),
        b_far_got=vm(4, low, 384),
        rest_sems=sems((2, 24)),
        own=vm(4, 432, 384),
        left=vm(4, 432, 384),
        right=vm(4, 432, 384),
        line_sems=sems((2, 2, 4)),
        q_grad=vm(2, 4, 144, 384),
        q_got=vm(4, 144, 384),
        q_own=vm(4, 144, 384),
        q_land=vm(4, 144, 384),
        q_sems=sems((2, 4)),
        q_sum=vm(3, 48, 384, dtype=F32),
        route_sems=sems((3, 3)),
        gain_sum=vm(6, 8, width, dtype=F32),
        gain_got=vm(5, 8, width, dtype=F32),
        gain_sems=sems((2, 5)),
    )


def attend_back_kernel(names, last, *refs):
    feature_ref, qkv_ref, do_ref, x_ref, w_ref, a_keep, a_send, b_keep, b_send = refs[:9]
    gain_ref, rows_ref, rest_ref, out_ref, gain_out_ref = refs[9:14]
    scr = types.SimpleNamespace(**dict(zip(names, refs[14:])))
    docs, me = lax.axis_index("docs"), lax.axis_index("seq")
    plane = me // 4
    over = (1 - docs, me)
    loads = {}
    for n, (name, ref) in enumerate(
        dict(qkv=qkv_ref, weight=w_ref, a_keep=a_keep, b_keep=b_keep, x=x_ref).items()
    ):
        loads[name] = pltpu.make_async_copy(ref, getattr(scr, name), scr.load_sems.at[n])
        loads[name].start()
    greet([(docs, flip(me, bits)) for bits in range(15, 0, -1)] + [over])
    exchange = Exchange(do_ref, scr.do, scr.do_sems, scr.do_own)
    exchange.begin()
    rest = Rest(scr.a_keep, a_send, scr.b_keep, b_send, scr)
    rest.first(3)
    rest.first(1)
    gains = Everywhere(scr.gain_sum, scr.gain_got, scr.gain_sems)
    if last:
        scr.gain_sum[0] = gain_ref[...]
        gains.step()

    loads["qkv"].wait()
    qkv = scr.qkv[...]
    spread_heads(qkv, feature_ref, scr.key, scr.query)
    zero = jnp.zeros((1024, 64), BF16)
    for h in range(GROUP_HEADS):
        scr.value[h] = qkv[:, 128 * h + 64 : 128 * h + 128]
        scr.turned[h] = qkv[:, 128 * h : 128 * h + 64].T
        scr.side[0, h] = jnp.concatenate([scr.query[h, :, :64], zero], axis=1)
    loads["a_keep"].wait()
    loads["b_keep"].wait()
    exchange.arrived()
    grad_o = jnp.concatenate([halves_below(scr.do[n]) for n in range(16)], axis=0)
    for h in range(GROUP_HEADS):
        scr.side[1, h] = jnp.concatenate([zero, grad_o[:, 64 * h : 64 * h + 64]], axis=1)

    def part(n, h):
        at = slice(BACK_QUERIES * n, BACK_QUERIES * n + BACK_QUERIES)
        expo, rate = expo_columns(dot_nt(scr.key[h], scr.query[h, at, :]))
        probs = expo * rate
        grad_probs = dot_nt(scr.value[h], scr.side[1, h, at, :][:, 64:])
        delta = jnp.sum(probs * grad_probs, axis=0, keepdims=True)
        grad_scores = (probs * (grad_probs - delta)).astype(BF16)
        scr.dq[n, 64 * h : 64 * h + 64, :] = dot(scr.turned[h], grad_scores) * (HEAD**-0.5)
        dkv = dot(grad_scores, scr.side[0, h, at, :])
        dkv += dot(probs.astype(BF16), scr.side[1, h, at, :])
        if n == 0:
            scr.dkv[h] = dkv
        else:
            scr.dqkv[:, 128 * h : 128 * h + 128] = (scr.dkv[h] + dkv).astype(BF16)

    part(0, 0)
    rest.second(3)
    rest.first(2)
    part(0, 1)
    if last:
        gains.step()
    part(0, 2)
    rest.second(1)
    scr.dqkv[0:512, 384:576] = scr.dq[0].T.astype(BF16)
    part(1, 0)
    rest.third(3)
    part(1, 1)
    rest.second(2)
    part(1, 2)
    rest.third(1)
    rest.line.hop(0)
    if last:
        gains.step()
    scr.dqkv[512:1024, 384:576] = scr.dq[1].T.astype(BF16)
    loads["x"].wait()
    grad = dot_tn(scr.dqkv[...], scr.x[...].reshape(1024, scr.x.shape[-1]))
    order = [6, 7, 8, 0, 2, 4, 1, 3, 5]
    grad = jnp.concatenate([grad[64 * n : 64 * n + 64] for n in order], axis=0).astype(BF16)
    for quarter in range(PLANES):
        apart = flip(plane, quarter)
        place = (apart % 2) * 2 + apart // 2
        for side in range(2):
            at = docs if side == 0 else 1 - docs
            scr.q_grad[at, place] = grad[
                144 * quarter : 144 * quarter + 144, 384 * side : 384 * side + 384
            ]
    crossed = remote(scr.q_grad.at[1], scr.q_got, scr.q_sems, 0, over)
    crossed.start()
    rest.first(0)
    loads["weight"].wait()
    rows = Collect(
        scr.rows.at[0],
        scr.rows.at[1],
        scr.land,
        scr.got_core,
        scr.got_x,
        scr.sum_x,
        scr.near,
        scr.sums,
        scr.row_sems,
    )
    for half in (1, 0):
        part_rows = []
        for n in range(8):
            block = flip(me, (n // 2) * 4 + (n % 2) * 2 + half)
            part_rows.append(scr.dqkv[pl.ds(pl.multiple_of(block * 64, 64), 64), :])
        product = dot_nt(jnp.concatenate(part_rows, axis=0), scr.weight[:, :, :576].reshape(-1, 576))
        scr.rows[half] = product.astype(BF16).reshape(scr.rows.shape[1:])
        if half == 1:
            rows.begin()
    rest.third(2)
    rest.line.hop(1)
    rows.along_x()
    if last:
        gains.step()
    crossed.wait_recv()
    turned = []
    for place in Rest.ORDER:
        rz = Line.PLACE[place]
        scr.q_own[place] = add_low(scr.q_grad[0, place], scr.q_got[place])
        if rz > 0:
            peer = (docs, flip(me, 4 * rz))
            turned.append(
                remote(scr.q_own.at[place], scr.q_land.at[place], scr.q_sems, place, peer)
            )
            turned[-1].start()
    rest.line.hop(2)
    rest.second(0)
    rows.along_z()
    if last:
        gains.step()
    for copy in turned:
        copy.wait_recv()
    total = scr.q_own[0].astype(F32)
    for place in range(1, PLANES):
        total = total + scr.q_land[place].astype(F32)
    scr.q_sum[...] = total.reshape(scr.q_sum.shape)
    route = Route(scr.q_sum, out_ref, scr.route_sems)
    route.begin()
    rest.third(0)
    if last:
        gains.step()
        gain_out_ref[...] = scr.gain_sum[5]
        gains.finish()
    else:
        gain_out_ref[...] = gain_ref[...]
    rest.line.arrived()
    rest.line.total(rest_ref, slice(0, 432))
    rows.finish()
    rows_ref[...] = scr.land[...]
    for piece in (exchange, rest, route):
        piece.finish()
    for copy in turned + [crossed]:
        copy.wait_send()


def attend_back(features, qkv, grad_o, x, weight, sums, gain_grads, last, number):
    width = x.shape[-1]
    scratch = back_scratch(width)
    return pl.pallas_call(
        functools.partial(attend_back_kernel, tuple(scratch), last),
        out_shape=(
            jax.ShapeDtypeStruct((PLANES, 64, width), BF16),
            jax.ShapeDtypeStruct((432, 384), F32),
            jax.ShapeDtypeStruct((3, 48, 384), F32),
            jax.ShapeDtypeStruct((8, width), F32),
        ),
        in_specs=[vmem()] + [hbm()] * 8 + [vmem()],
        out_specs=(vmem(), vmem(), hbm(), vmem()),
        scratch_shapes=list(scratch.values()),
        compiler_params=pltpu.CompilerParams(
            collective_id=number, has_side_effects=True, vmem_limit_bytes=56 * 2**20
        ),
        cost_estimate=pl.CostEstimate(
            flops=8 * 10**9, bytes_accessed=10 * 10**6, transcendentals=3 * 10**6
        ),
        name="attend_back",
    )(features, qkv, grad_o, x, weight, *sums, gain_grads)


def forward_scratch(width):
    sems = pltpu.SemaphoreType.DMA

    def vm(*shape, dtype=BF16):
        return pltpu.VMEM(shape, dtype)

    scratch = dict(
        x=vm(16, 64, width),
        weight=vm(CHIPS, 48, 640),
        qkv=vm(1024, 576),
        key=vm(3, 1024, 128),
        query=vm(3, 1024, 128),
        value=vm(3, 64, 1024),
        turned=vm(192, 1024, dtype=F32),
        o=vm(LAYERS, 16, 32, 384),
        o_got=vm(LAYERS, 16, 32, 384),
        mixed=vm(256, width),
        h1=vm(256, width, dtype=F32),
        up=vm(256, 4 * width, dtype=F32),
        h2=vm(256, width, dtype=F32),
        hidden=vm(256, width, dtype=F32),
        low=vm(4, 64, width),
        act=vm(256, 4 * width),
        wu=WEIGHT_SCRATCH[0],
        wd=WEIGHT_SCRATCH[1],
        wo=WEIGHT_SCRATCH[2],
        weight_sems=sems((3,)),
        load_sems=sems((3,)),
        own_sems=sems((2, 5)),
        save_sems=sems((2, 5)),
    )
    for layer in range(LAYERS):
        scratch[f"row_sems_{layer}"] = sems((2, 16))
        scratch[f"qkv_sems_{layer}"] = sems((2, 8))
        scratch[f"o_sems_{layer}"] = sems((2, 16))
        scratch[f"up_sems_{layer}"] = sems((2, 36))
        scratch[f"down_sems_{layer}"] = sems((2, 36))
    return scratch


def forward_kernel(names, *refs):
    info, feature_ref, tokens_ref = refs[:3]
    wq_refs, up_refs, down_refs = (
        [ref.at[layer] for layer in range(LAYERS)] for ref in refs[3:6]
    )
    saved_refs = (refs[6:12], refs[12:18])
    w_refs, wu_refs, wd_refs, gains_ref, result_ref = refs[18:20], refs[20:22], refs[22:24], refs[24], refs[25]
    scr = types.SimpleNamespace(**dict(zip(names, refs[26:])))
    docs, me = lax.axis_index("docs"), lax.axis_index("seq")
    pltpu.make_async_copy(tokens_ref, scr.low, scr.load_sems.at[2]).start()
    greet([(docs, flip(me, bits)) for bits in range(15, 0, -1)] + [(1 - docs, me)])

    def sems(name, layer):
        return getattr(scr, f"{name}_sems_{layer}")

    qkvs, slabs = [], []
    for layer in range(LAYERS):
        own = scr.own_sems.at[layer]
        qkvs.append(Rows(wq_refs[layer], w_refs[layer], sems("qkv", layer), own.at[0]))
        slabs.append(
            [
                Slabs(up_refs[layer], wu_refs[layer], sems("up", layer), own.at[1]),
                Slabs(down_refs[layer], wd_refs[layer], sems("down", layer), own.at[2], True),
            ]
        )

    def spread(layer, source):
        x_ref = saved_refs[layer][0]
        return Spread(source, x_ref, sems("row", layer), scr.own_sems.at[layer, 3])

    def every(parts, step, *arguments):
        for part in parts:
            getattr(part, step)(*arguments)

    def move(layer, *steps):
        for step in steps:
            name = {"l": "from_line", "f": "from_first", "s": "from_second"}[step[0]]
            every(slabs[layer], name, int(step[1]))

    def save(layer, n, source):
        copy = pltpu.make_async_copy(source, saved_refs[layer][n + 1], scr.save_sems.at[layer, n])
        copy.start()
        return copy

    saves = []

    def attend(layer, rows, ticks):
        qkvs[layer].arrived()
        rows.arrived()
        load_x = pltpu.make_async_copy(saved_refs[layer][0], scr.x, scr.load_sems.at[0])
        load_w = pltpu.make_async_copy(
            w_refs[layer], scr.weight, scr.load_sems.at[1]
        )
        load_x.start()
        load_w.start()
        while saves:
            saves.pop().wait()
        load_x.wait()
        load_w.wait()
        scr.qkv[...] = dot(
            scr.x[...].reshape(1024, scr.x.shape[-1]), scr.weight[:, :, :576].reshape(-1, 576)
        ).astype(BF16)
        if layer == 0:
            share = scr.x.shape[-1] // 32
            shares = [
                scr.weight[chip, 24 * core : 24 * core + 4, 576 : 576 + share]
                for chip in range(CHIPS)
                for core in range(2)
            ]
            gains_ref[0:4] = jnp.concatenate(shares, axis=1).astype(F32)
        saves.append(save(layer, 0, scr.qkv))
        qkv = scr.qkv[...]
        spread_heads(qkv, feature_ref, scr.key, scr.query)
        for h in range(GROUP_HEADS):
            scr.value[h] = qkv[:, 128 * h + 64 : 128 * h + 128].T
        exchange = Exchange(
            scr.o.at[layer], scr.o_got.at[layer], sems("o", layer), scr.own_sems.at[layer, 4]
        )
        for n in range(1024 // QUERIES):
            at = slice(QUERIES * n, QUERIES * n + QUERIES)
            for h in range(GROUP_HEADS):
                expo, rate = expo_columns(dot_nt(scr.key[h], scr.query[h, at, :]))
                scr.turned[64 * h : 64 * h + 64, at] = dot(
                    scr.value[h], (expo * rate).astype(BF16)
                )
                ticks.pop(0)()
            rows_o = scr.turned[:, at].T.astype(BF16)
            for m in range(QUERIES // 64):
                scr.o[layer, n * (QUERIES // 64) + m] = halves_beside(rows_o[64 * m : 64 * m + 64])
        exchange.begin()
        return exchange

    def feed(layer, exchange, ticks):
        exchange.arrived()
        slabs[layer][0].arrived()
        load_up(wu_refs[layer], scr.wu, scr.wo, scr.weight_sems)
        for k in range(PLANES):
            scr.mixed[64 * k : 64 * k + 64, :] = jnp.concatenate(
                [halves_below(scr.o_got[layer, 4 * k + g]) for g in range(GROUPS)], axis=1
            )
        saves.append(save(layer, 1, scr.mixed))
        mixed = scr.mixed[...]
        gain = gains_ref[2 * layer : 2 * layer + 2]
        ticks.pop(0)()
        wait_weight(scr.wo, scr.weight_sems.at[0])
        attended = jnp.concatenate(
            [dot(mixed, scr.wo[side].reshape(768, 384)) for side in range(2)], axis=1
        )
        before = scr.low[...].reshape(256, -1).astype(F32) if layer == 0 else scr.hidden[...]
        h1 = before + attended
        scr.h1[...] = h1
        saves.append(save(layer, 2, scr.h1))
        x1 = norm_parts(h1)[0] * gain[0:1, :]
        x1_low = x1.astype(BF16)
        wait_weight(scr.wu, scr.weight_sems.at[1])
        for side in range(2):
            for part in range(3):
                at = 1536 * side + 512 * part
                up = dot(x1_low, scr.wu[side, :, :, 512 * part : 512 * part + 512].reshape(768, 512))
                scr.up[:, at : at + 512] = up
                scr.act[:, at : at + 512] = gelu_parts(up)[0].astype(BF16)
            ticks.pop(0)()
        saves.append(save(layer, 3, scr.up))
        slabs[layer][1].arrived()
        load_down(wd_refs[layer], scr.wd, scr.weight_sems)
        wait_weight(scr.wd, scr.weight_sems.at[2])
        h2 = x1 + dot(scr.act[...], scr.wd[...].reshape(3072, 768))
        scr.h2[...] = h2
        saves.append(save(layer, 4, scr.h2))
        out = jnp.where(inside_rows(info), norm_parts(h2)[0] * gain[1:2, :], 0.0)
        low = out.astype(BF16)
        if layer == 0:
            scr.hidden[...] = out
            scr.low[...] = low.reshape(scr.low.shape)
        else:
            result_ref[...] = low.reshape(result_ref.shape)

    def nothing():
        pass

    def step(layer, *steps):
        return lambda: move(layer, *steps)

    rows_0 = spread(0, tokens_ref)
    rows_0.begin()
    qkvs[0].begin()
    every(slabs[0], "begin")
    for rz in range(1, 4):
        rows_0.forward(rz)
        qkvs[0].forward(rz)
        if rz == 1:
            move(0, "f0")
    rows_0.from_beside()
    pltpu.make_async_copy(tokens_ref, scr.low, scr.load_sems.at[2]).wait()
    exchange_0 = attend(
        0,
        rows_0,
        [
            step(0, "l1"),
            nothing,
            step(0, "f1"),
            step(0, "l2"),
            lambda: every(slabs[1], "begin"),
            step(0, "s0"),
        ],
    )
    move(0, "l3", "f2", "s1", "f3")
    move(1, "l1")
    move(0, "s2")
    move(1, "l2")
    qkvs[1].begin()
    move(0, "s3")
    feed(0, exchange_0, [step(1, "l3"), step(1, "f0"), nothing])
    rows_1 = spread(1, scr.low)
    rows_1.begin()
    for rz in range(1, 4):
        rows_1.forward(rz)
    for rz in range(1, 4):
        qkvs[1].forward(rz)
    rows_1.from_beside()
    move(1, "f1", "f2")
    exchange_1 = attend(
        1,
        rows_1,
        [nothing, step(1, "f3"), nothing, step(1, "s0"), nothing, step(1, "s1")],
    )
    move(1, "s2", "s3")
    feed(1, exchange_1, [nothing] * 3)
    for copy in saves:
        copy.wait()
    every([rows_0, rows_1, exchange_0, exchange_1] + qkvs + slabs[0] + slabs[1], "finish")


def forward(info, features, tokens, wq, up, down, number):
    width = tokens.shape[-1]
    scratch = forward_scratch(width)

    def out(*shape, dtype=BF16):
        return jax.ShapeDtypeStruct(shape, dtype)

    saved = [
        out(16, 64, width),
        out(1024, 576),
        out(256, width),
        out(256, width, dtype=F32),
        out(256, 4 * width, dtype=F32),
        out(256, width, dtype=F32),
    ]
    shapes = saved + saved + [out(CHIPS, 48, 640)] * 2
    shapes += [out(2, CHIPS, 48, 1920)] * 2 + [out(2, CHIPS, 48, 1536)] * 2
    shapes += [out(4, width, dtype=F32), out(PLANES, 64, width)]
    return pl.pallas_call(
        functools.partial(forward_kernel, tuple(scratch)),
        out_shape=tuple(shapes),
        in_specs=[smem(), vmem()] + [hbm()] * 4,
        out_specs=tuple([hbm()] * (len(shapes) - 2) + [vmem(), vmem()]),
        scratch_shapes=list(scratch.values()),
        compiler_params=pltpu.CompilerParams(
            collective_id=number, has_side_effects=True, vmem_limit_bytes=58 * 2**20
        ),
        name="forward",
    )(info, features, tokens, wq, up, down)


def pick(stack, index):
    return lax.dynamic_index_in_dim(stack, index, 0, keepdims=False)


def pack_qkv(shards, gains, me, core):
    rows = shards.shape[1]
    parts = shards.reshape(LAYERS, rows, 3, GROUPS, GROUP_HEADS, HEAD)
    pairs = jnp.transpose(parts[:, :, 1:], (3, 0, 1, 4, 2, 5)).reshape(GROUPS, LAYERS, rows, 384)
    query = jnp.transpose(parts[:, :, 0], (2, 0, 1, 3, 4)).reshape(GROUPS, LAYERS, rows, 192)
    share = gains.shape[-1]
    beside = jnp.pad(gains.reshape(2 * LAYERS, share), ((0, rows - 2 * LAYERS), (0, 64 - share)))
    beside = jnp.broadcast_to(beside, (GROUPS, LAYERS, rows, 64))
    packed = jnp.concatenate([pairs, query, beside], axis=3)
    group = me & 3
    got = [pick(packed, group)] + [swap(pick(packed, group ^ r), r) for r in range(1, 4)]

    def in_order(own, other):
        return jnp.where(
            core == 0,
            jnp.concatenate([own, other], axis=1),
            jnp.concatenate([other, own], axis=1),
        )

    here, there = in_order(got[0], got[1]), in_order(got[2], got[3])
    both = jnp.where(
        (me >> 1) & 1 == 0,
        jnp.stack([here, there], axis=1),
        jnp.stack([there, here], axis=1),
    )
    return both


def pack_rest(out_weight, up_weight, down_weight, core):
    def mine(shard, side):
        half = shard.shape[2] // 2
        return lax.dynamic_slice_in_dim(shard, side * half, half, axis=2)

    def both(side):
        return jnp.concatenate([mine(up_weight, side), mine(out_weight, side)], axis=2)

    own, got = both(core), swap(both(1 - core), 1)
    rows = jnp.where(
        core == 0,
        jnp.concatenate([own, got], axis=1),
        jnp.concatenate([got, own], axis=1),
    )
    return rows, jnp.concatenate([down_weight[:, :48], down_weight[:, 48:]], axis=2)


def add_low(first, second):
    return (first.astype(F32) + second.astype(F32)).astype(BF16)


def add_full(first, second):
    return first.astype(F32) + second.astype(F32)


def split_rest(total):
    down = total[240:].reshape(4, 48, 384)
    return (
        total[192:240].T,
        total[:192].T,
        jnp.transpose(down, (0, 2, 1)).reshape(1536, 48),
    )


def local_two_by_sixteen(
    tokens,
    qkv_weight,
    out_weight,
    up_weight,
    down_weight,
    norm_gains,
    doc_lengths,
    global_ids,
    random_ids,
    cotangent,
):
    docs_dev, block, width = tokens.shape
    me = lax.axis_index("seq").astype(jnp.int32)
    docs = lax.axis_index("docs").astype(jnp.int32)
    plane, core = me >> 2, me & 1
    chip = docs * 8 + (me >> 1)
    info = jnp.concatenate(
        [
            jnp.stack(
                [me, chip, pick(doc_lengths, plane), plane, docs, core, jnp.zeros_like(me), chip]
            ),
            doc_lengths,
        ]
    )
    features = key_features(
        lax.dynamic_index_in_dim(random_ids, plane, 1, keepdims=False),
        pick(global_ids, plane),
        pick(doc_lengths, plane),
    )

    wq = pack_qkv(qkv_weight, norm_gains, me, core)
    up, down = pack_rest(out_weight, up_weight, down_weight, core)
    share = width // 32
    made = forward(info, features, tokens, wq, up, down, 0)
    held, weights = (made[:6], made[6:12]), made[12:14]
    rest = list(zip(made[14:16], made[16:18]))
    gain = made[18]
    base, grad_o, gain_grads, *sums = feed_back(
        1, info, cotangent, gain, gain, gain, held[1][2:], rest[1], 1
    )
    extra, rest_grads_1, qkv_1, gain_grads = attend_back(
        features, held[1][1], grad_o, held[1][0], weights[1], sums, gain_grads, False, 2
    )
    base, grad_o, gain_grads, *sums = feed_back(
        0, info, base, extra, gain, gain_grads, held[0][2:], rest[0], 3
    )
    extra, rest_grads, qkv_0, gain_grads = attend_back(
        features, held[0][1], grad_o, held[0][0], weights[0], sums, gain_grads, True, 4
    )
    grad_tokens = base.reshape(docs_dev, block, width) + extra.astype(F32)
    gain_grads = lax.dynamic_slice_in_dim(gain_grads, (docs * 16 + me) * share, share, axis=1)
    rest = [split_rest(part) for part in (rest_grads, rest_grads_1)]
    qkv_grads = jnp.stack([qkv_0, qkv_1])
    return (
        made[19],
        grad_tokens,
        jnp.transpose(qkv_grads, (0, 3, 1, 2)).reshape(LAYERS, 384, 144),
        *(jnp.stack(pair) for pair in zip(*rest)),
        gain_grads[:4].reshape(LAYERS, 2, share),
    )


def solution(mesh):
    def local(*args):
        docs_dev, _, width = args[0].shape
        if fits(mesh, docs_dev, width // HEAD):
            return local_two_by_sixteen(*args)
        return local_any_mesh(*args)

    return jax.shard_map(
        local,
        mesh=mesh,
        in_specs=(
            P("docs", "seq", None),
            P(None, ("docs", "seq"), None),
            P(None, ("docs", "seq"), None),
            P(None, ("docs", "seq"), None),
            P(None, ("docs", "seq"), None),
            P(None, None, ("docs", "seq")),
            P("docs"),
            P("docs", None),
            P(None, "docs", None),
            P("docs", "seq", None),
        ),
        out_specs=(
            P("docs", "seq", None),
            P("docs", "seq", None),
            P(None, "docs", "seq"),
            P(None, "docs", "seq"),
            P(None, "docs", "seq"),
            P(None, "docs", "seq"),
            P(None, None, ("docs", "seq")),
        ),
        check_vma=False,
    )
```

```python
import functools
import types

import jax
import jax.numpy as jnp
from jax import lax
from jax.experimental import pallas as pl
from jax.experimental.pallas import tpu as pltpu
from jax.sharding import PartitionSpec as P

HEAD = 64
RAND = 3
GLOB = 2
LAYERS = 2


NEGATIVE = -1e30
EPSILON = 1e-05


def with_halo(cells, sides, width):
    for axis, dim in sides:
        count = lax.axis_size(axis)
        head = lax.slice_in_dim(cells, 0, width, axis=dim)
        tail = lax.slice_in_dim(cells, cells.shape[dim] - width, cells.shape[dim], axis=dim)
        cells = jnp.concatenate(
            [
                lax.ppermute(tail, axis, [(i, (i + 1) % count) for i in range(count)]),
                cells,
                lax.ppermute(head, axis, [((i + 1) % count, i) for i in range(count)]),
            ],
            axis=dim,
        )
    return cells


def combined_all(value, axis, join):
    pieces = jax.tree.map(lambda part: lax.all_gather(part, axis), value)
    head = jax.tree.map(lambda part: part[0], pieces)
    tail = jax.tree.map(lambda part: part[1:], pieces)
    so_far, _ = lax.scan(lambda so_far, piece: (join(so_far, piece), None), head, tail)
    return so_far


def norm_rows(values, gain):
    centre = values - jnp.mean(values, axis=-1, keepdims=True)
    spread = jnp.mean(centre * centre, axis=-1, keepdims=True)
    return centre * lax.rsqrt(spread + EPSILON) * gain


def gelu_tanh(values):
    return jax.nn.gelu(values, approximate=True)


def earlier_equal(values):
    length = values.shape[-1]
    order = jnp.arange(length, dtype=jnp.int32)
    before = order[None, :] < order[:, None]
    same = values[..., :, None] == values[..., None, :]
    return jnp.sum(jnp.logical_and(same, before), axis=-1)


def merge_stats(first, second):
    highest = jnp.maximum(first[0], second[0])
    return (
        highest,
        first[1] * jnp.exp(first[0] - highest) + second[1] * jnp.exp(second[0] - highest),
    )


def sparse_probs(query, key_part, key_inside, scale):
    scores = (
        jnp.einsum("kbhd,kjhd->khbj", query, key_part, preferred_element_type=jnp.float32) * scale
    )
    scores = jnp.where(key_inside[:, None, None, :], scores, NEGATIVE)
    expo = jnp.exp(scores - jnp.max(scores, axis=-1, keepdims=True))
    return expo / jnp.sum(expo, axis=-1, keepdims=True)


def global_scores(global_query, local_keys, inside, scale):
    scores = (
        jnp.einsum(
            "ksbhd,kjhd->kshbj", global_query, local_keys, preferred_element_type=jnp.float32
        )
        * scale
    )
    return jnp.where(inside[:, None, None, None, :], scores, NEGATIVE)


def local_any_mesh(
    tokens,
    qkv_weight,
    out_weight,
    up_weight,
    down_weight,
    norm_gains,
    doc_lengths,
    global_ids,
    random_ids,
    cotangent,
):
    nseq = lax.axis_size("seq")
    device = lax.axis_index("seq")
    docs_dev, block, width = tokens.shape
    count = docs_dev * block
    heads = width // HEAD
    scale = HEAD ** (-0.5)
    capacity = max(2, (docs_dev * RAND + nseq - 1) // nseq)
    global_capacity = (docs_dev * GLOB + nseq - 1) // nseq
    entries = docs_dev * RAND
    global_entries = docs_dev * GLOB
    offsets = jnp.arange(block, dtype=jnp.int32)
    inside = (device * block + offsets)[None, :] < doc_lengths[:, None]
    live_rows = inside.reshape(count, 1)
    wanted = random_ids.reshape(nseq, entries)
    wanted_rank = earlier_equal(wanted)
    slot_ids = jnp.arange(capacity, dtype=jnp.int32)
    hits = jnp.logical_and((wanted == device)[:, :, None], wanted_rank[:, :, None] == slot_ids)
    hits = jnp.any(hits.reshape(nseq, docs_dev, RAND, capacity), axis=2)
    hits = jnp.transpose(hits, (0, 2, 1))
    doc_ids = jnp.arange(docs_dev, dtype=jnp.int32)
    send_doc = jnp.sum(jnp.where(hits, doc_ids, 0), axis=2)
    send_live = jnp.any(hits, axis=2)
    owner_pick = hits.astype(jnp.float32)
    listed_here = lax.dynamic_index_in_dim(wanted, device, 0, keepdims=False)
    listed_rank = lax.dynamic_index_in_dim(wanted_rank, device, 0, keepdims=False)
    fetch_slot = listed_here * capacity + listed_rank
    global_block = global_ids.reshape(global_entries)
    global_rank = earlier_equal(global_block)
    global_slot = global_block * global_capacity + global_rank
    own_entry = global_block == device
    owned = jnp.logical_and(
        own_entry[:, None], global_rank[:, None] == jnp.arange(global_capacity, dtype=jnp.int32)
    )
    entry_doc = jnp.arange(global_entries, dtype=jnp.int32) // GLOB
    global_send_doc = jnp.sum(jnp.where(owned, entry_doc[:, None], 0), axis=0)
    global_send_live = jnp.any(owned, axis=0)
    own_flag = jnp.any(own_entry.reshape(docs_dev, GLOB), axis=1)
    own_slot = jnp.sum(jnp.where(own_entry, global_rank, 0).reshape(docs_dev, GLOB), axis=1)
    neighbours = jnp.stack([(device - 1) % nseq, device, (device + 1) % nseq])
    key_blocks = jnp.concatenate(
        [
            jnp.broadcast_to(neighbours[None, :], (docs_dev, 3)),
            listed_here.reshape(docs_dev, RAND),
            global_ids,
        ],
        axis=1,
    )
    span = key_blocks.shape[1] * block
    key_inside = (key_blocks[:, :, None] * block + offsets < doc_lengths[:, None, None]).reshape(
        docs_dev, span
    )
    keep_local = inside[:, None, None, None, :]
    hidden = tokens.reshape(count, width).astype(jnp.float32)
    held = []
    for layer in range(LAYERS):
        weights = (
            lax.all_gather(qkv_weight[layer], ("docs", "seq"), axis=0, tiled=True),
            lax.all_gather(out_weight[layer], ("docs", "seq"), axis=0, tiled=True),
            lax.all_gather(up_weight[layer], ("docs", "seq"), axis=0, tiled=True),
            lax.all_gather(down_weight[layer], ("docs", "seq"), axis=0, tiled=True),
            lax.all_gather(norm_gains[layer], ("docs", "seq"), axis=1, tiled=True),
        )
        weight_qkv, weight_out, weight_up, weight_down, gain_pair = weights
        gain_pair = gain_pair.astype(jnp.float32)
        lowered = hidden.astype(jnp.bfloat16)
        projected = (
            jnp.dot(lowered, weight_qkv, preferred_element_type=jnp.float32)
            .astype(jnp.bfloat16)
            .reshape(docs_dev, block, 3 * width)
        )
        pairs = projected[:, :, width:]
        window = with_halo(pairs, (("seq", 1),), block)
        outgoing = jnp.where(
            send_live[:, :, None, None],
            jnp.take(pairs, send_doc, axis=0),
            jnp.zeros((), jnp.bfloat16),
        )
        incoming = lax.all_to_all(outgoing, "seq", split_axis=0, concat_axis=0, tiled=True)
        fetched = jnp.take(
            incoming.reshape(nseq * capacity, block, 2 * width), fetch_slot, axis=0
        ).reshape(docs_dev, RAND * block, 2 * width)
        global_send = jnp.where(
            global_send_live[:, None, None],
            jnp.take(projected, global_send_doc, axis=0),
            jnp.zeros((), jnp.bfloat16),
        )
        gathered = lax.all_gather(global_send, "seq", axis=0, tiled=True)
        global_picked = jnp.take(gathered, global_slot, axis=0).reshape(
            docs_dev, GLOB, block, 3 * width
        )
        global_query = global_picked[..., :width].reshape(docs_dev, GLOB, block, heads, HEAD)
        listed_pairs = jnp.concatenate(
            [
                window,
                fetched,
                global_picked[..., width:].reshape(docs_dev, GLOB * block, 2 * width),
            ],
            axis=1,
        )
        query = projected[:, :, :width].reshape(docs_dev, block, heads, HEAD)
        key_part = listed_pairs[:, :, :width].reshape(docs_dev, span, heads, HEAD)
        value_part = listed_pairs[:, :, width:].reshape(docs_dev, span, heads, HEAD)
        probs = sparse_probs(query, key_part, key_inside, scale)
        mixed = jnp.einsum(
            "khbj,kjhd->kbhd",
            probs.astype(jnp.bfloat16),
            value_part,
            preferred_element_type=jnp.float32,
        )
        local_keys = projected[:, :, width : 2 * width].reshape(docs_dev, block, heads, HEAD)
        local_values = projected[:, :, 2 * width :].reshape(docs_dev, block, heads, HEAD)
        wide_scores = global_scores(global_query, local_keys, inside, scale)
        global_top = jnp.max(wide_scores, axis=-1)
        global_total = jnp.sum(
            jnp.where(keep_local, jnp.exp(wide_scores - global_top[..., None]), 0.0), axis=-1
        )
        global_top, global_total = combined_all((global_top, global_total), "seq", merge_stats)
        wide_probs = (
            jnp.where(keep_local, jnp.exp(wide_scores - global_top[..., None]), 0.0)
            / global_total[..., None]
        )
        wide_part = jnp.einsum(
            "kshbj,kjhd->ksbhd",
            wide_probs.astype(jnp.bfloat16),
            local_values,
            preferred_element_type=jnp.float32,
        )
        wide_buffer = (
            jnp.zeros((nseq * global_capacity, block, width), jnp.float32)
            .at[global_slot]
            .set(wide_part.reshape(global_entries, block, width))
        )
        wide_sum = lax.psum_scatter(wide_buffer, "seq", scatter_dimension=0, tiled=True)
        attended = jnp.where(
            own_flag[:, None, None],
            jnp.take(wide_sum, own_slot, axis=0),
            mixed.reshape(docs_dev, block, width),
        )
        attended = attended.reshape(count, width).astype(jnp.bfloat16)
        after_attn = hidden + jnp.dot(attended, weight_out, preferred_element_type=jnp.float32)
        normed = norm_rows(after_attn, gain_pair[0])
        normed_low = normed.astype(jnp.bfloat16)
        up_values = jnp.dot(normed_low, weight_up, preferred_element_type=jnp.float32)
        activated = gelu_tanh(up_values).astype(jnp.bfloat16)
        after_ffn = normed + jnp.dot(activated, weight_down, preferred_element_type=jnp.float32)
        held.append(
            (
                weights,
                lowered,
                projected,
                listed_pairs,
                global_query,
                global_top,
                global_total,
                attended,
                after_attn,
                normed_low,
                up_values,
                activated,
                after_ffn,
            )
        )
        hidden = jnp.where(live_rows, norm_rows(after_ffn, gain_pair[1]), 0.0)
    gradient = cotangent.reshape(count, width).astype(jnp.float32)
    layer_grads = []
    for layer in reversed(range(LAYERS)):
        (
            weights,
            lowered,
            projected,
            listed_pairs,
            global_query,
            global_top,
            global_total,
            attended,
            after_attn,
            normed_low,
            up_values,
            activated,
            after_ffn,
        ) = held[layer]
        weights = (
            lax.all_gather(qkv_weight[layer], ("docs", "seq"), axis=0, tiled=True),
            lax.all_gather(out_weight[layer], ("docs", "seq"), axis=0, tiled=True),
            lax.all_gather(up_weight[layer], ("docs", "seq"), axis=0, tiled=True),
            lax.all_gather(down_weight[layer], ("docs", "seq"), axis=0, tiled=True),
            lax.all_gather(norm_gains[layer], ("docs", "seq"), axis=1, tiled=True),
        )
        weight_qkv, weight_out, weight_up, weight_down, gain_pair = weights
        gain_pair = gain_pair.astype(jnp.float32)
        gradient = jnp.where(live_rows, gradient, 0.0)
        grad_ffn, grad_gain_out = jax.vjp(norm_rows, after_ffn, gain_pair[1])[1](gradient)
        grad_down_low = grad_ffn.astype(jnp.bfloat16)
        grad_down_layer = jnp.einsum(
            "rf,rd->fd", activated, grad_down_low, preferred_element_type=jnp.float32
        )
        grad_activated = jnp.einsum(
            "rd,fd->rf", grad_down_low, weight_down, preferred_element_type=jnp.float32
        )
        grad_up_low = jax.vjp(gelu_tanh, up_values)[1](grad_activated)[0].astype(jnp.bfloat16)
        grad_up_layer = jnp.einsum(
            "rd,rf->df", normed_low, grad_up_low, preferred_element_type=jnp.float32
        )
        grad_normed = grad_ffn + jnp.einsum(
            "rf,df->rd", grad_up_low, weight_up, preferred_element_type=jnp.float32
        )
        grad_attn, grad_gain_mid = jax.vjp(norm_rows, after_attn, gain_pair[0])[1](grad_normed)
        grad_attn_low = grad_attn.astype(jnp.bfloat16)
        grad_out_layer = jnp.einsum(
            "rd,re->de", attended, grad_attn_low, preferred_element_type=jnp.float32
        )
        grad_mixed = (
            jnp.einsum("re,de->rd", grad_attn_low, weight_out, preferred_element_type=jnp.float32)
            .astype(jnp.bfloat16)
            .reshape(docs_dev, block, width)
        )
        query = projected[:, :, :width].reshape(docs_dev, block, heads, HEAD)
        key_part = listed_pairs[:, :, :width].reshape(docs_dev, span, heads, HEAD)
        value_part = listed_pairs[:, :, width:].reshape(docs_dev, span, heads, HEAD)
        probs = sparse_probs(query, key_part, key_inside, scale)
        grad_sparse = jnp.where(
            own_flag[:, None, None], jnp.zeros((), jnp.bfloat16), grad_mixed
        ).reshape(docs_dev, block, heads, HEAD)
        grad_probs = jnp.einsum(
            "kbhd,kjhd->khbj", grad_sparse, value_part, preferred_element_type=jnp.float32
        )
        delta = jnp.sum(probs * grad_probs, axis=-1, keepdims=True)
        grad_scores = (probs * (grad_probs - delta)).astype(jnp.bfloat16)
        grad_query = (
            jnp.einsum("khbj,kjhd->kbhd", grad_scores, key_part, preferred_element_type=jnp.float32)
            * scale
        )
        grad_key_part = (
            jnp.einsum("khbj,kbhd->kjhd", grad_scores, query, preferred_element_type=jnp.float32)
            * scale
        )
        grad_value_part = jnp.einsum(
            "khbj,kbhd->kjhd",
            probs.astype(jnp.bfloat16),
            grad_sparse,
            preferred_element_type=jnp.float32,
        )
        grad_listed = jnp.concatenate(
            [
                grad_key_part.reshape(docs_dev, span, width),
                grad_value_part.reshape(docs_dev, span, width),
            ],
            axis=2,
        )
        wide_out = jnp.where(
            global_send_live[:, None, None],
            jnp.take(grad_mixed, global_send_doc, axis=0),
            jnp.zeros((), jnp.bfloat16),
        )
        wide_all = lax.all_gather(wide_out, "seq", axis=0, tiled=True)
        wide_grad = jnp.take(wide_all, global_slot, axis=0).reshape(
            docs_dev, GLOB, block, heads, HEAD
        )
        local_keys = projected[:, :, width : 2 * width].reshape(docs_dev, block, heads, HEAD)
        local_values = projected[:, :, 2 * width :].reshape(docs_dev, block, heads, HEAD)
        wide_scores = global_scores(global_query, local_keys, inside, scale)
        wide_probs = (
            jnp.where(keep_local, jnp.exp(wide_scores - global_top[..., None]), 0.0)
            / global_total[..., None]
        )
        wide_grad_probs = jnp.einsum(
            "ksbhd,kjhd->kshbj", wide_grad, local_values, preferred_element_type=jnp.float32
        )
        wide_delta = lax.psum(jnp.sum(wide_probs * wide_grad_probs, axis=-1), "seq")
        wide_grad_scores = (wide_probs * (wide_grad_probs - wide_delta[..., None])).astype(
            jnp.bfloat16
        )
        wide_grad_query = (
            jnp.einsum(
                "kshbj,kjhd->ksbhd",
                wide_grad_scores,
                local_keys,
                preferred_element_type=jnp.float32,
            )
            * scale
        )
        wide_grad_keys = (
            jnp.einsum(
                "kshbj,ksbhd->kjhd",
                wide_grad_scores,
                global_query,
                preferred_element_type=jnp.float32,
            )
            * scale
        )
        wide_grad_values = jnp.einsum(
            "kshbj,ksbhd->kjhd",
            wide_probs.astype(jnp.bfloat16),
            wide_grad,
            preferred_element_type=jnp.float32,
        )
        global_grads = jnp.concatenate(
            [
                wide_grad_query.reshape(global_entries, block, width),
                grad_listed[:, (3 + RAND) * block :, :].reshape(global_entries, block, 2 * width),
            ],
            axis=2,
        )
        global_buffer = (
            jnp.zeros((nseq * global_capacity, block, 3 * width), jnp.float32)
            .at[global_slot]
            .set(global_grads)
        )
        global_share = lax.psum_scatter(global_buffer, "seq", scatter_dimension=0, tiled=True)
        global_mine = jnp.where(
            own_flag[:, None, None], jnp.take(global_share, own_slot, axis=0), 0.0
        )
        grad_fetched = grad_listed[:, 3 * block : (3 + RAND) * block, :].reshape(
            entries, block, 2 * width
        )
        back_out = (
            jnp.zeros((nseq * capacity, block, 2 * width), jnp.float32)
            .at[fetch_slot]
            .set(grad_fetched)
            .reshape(nseq, capacity, block, 2 * width)
        )
        back_in = lax.all_to_all(back_out, "seq", split_axis=0, concat_axis=0, tiled=True)
        grad_random = jnp.einsum(
            "dck,dcbf->kbf", owner_pick, back_in, precision=lax.Precision.HIGHEST
        )
        grad_window = grad_listed[:, : 3 * block, :]
        edges = jnp.concatenate([grad_window[:, :block], grad_window[:, 2 * block :]], axis=1)
        beside_all = with_halo(edges, (("seq", 1),), block)
        grad_pairs = (
            grad_window[:, block : 2 * block]
            + beside_all[:, :block]
            + beside_all[:, 3 * block :]
            + grad_random
            + global_mine[:, :, width:]
        )
        grad_pairs = grad_pairs + jnp.concatenate(
            [
                wide_grad_keys.reshape(docs_dev, block, width),
                wide_grad_values.reshape(docs_dev, block, width),
            ],
            axis=2,
        )
        grad_queries = grad_query.reshape(docs_dev, block, width) + global_mine[:, :, :width]
        grad_projected = (
            jnp.concatenate([grad_queries, grad_pairs], axis=2)
            .reshape(count, 3 * width)
            .astype(jnp.bfloat16)
        )
        grad_qkv_layer = jnp.einsum(
            "rd,re->de", lowered, grad_projected, preferred_element_type=jnp.float32
        )
        gradient = grad_attn + jnp.einsum(
            "re,de->rd", grad_projected, weight_qkv, preferred_element_type=jnp.float32
        )
        group_shares = (
            lax.psum_scatter(grad_qkv_layer, "docs", scatter_dimension=0, tiled=True),
            lax.psum_scatter(grad_out_layer, "docs", scatter_dimension=0, tiled=True),
            lax.psum_scatter(grad_up_layer, "docs", scatter_dimension=0, tiled=True),
            lax.psum_scatter(grad_down_layer, "docs", scatter_dimension=0, tiled=True),
            lax.psum_scatter(
                jnp.stack([grad_gain_mid, grad_gain_out]), "docs", scatter_dimension=1, tiled=True
            ),
        )
        shares = (
            lax.psum_scatter(group_shares[0], "seq", scatter_dimension=1, tiled=True),
            lax.psum_scatter(group_shares[1], "seq", scatter_dimension=1, tiled=True),
            lax.psum_scatter(group_shares[2], "seq", scatter_dimension=1, tiled=True),
            lax.psum_scatter(group_shares[3], "seq", scatter_dimension=1, tiled=True),
            lax.psum_scatter(group_shares[4], "seq", scatter_dimension=1, tiled=True),
        )
        layer_grads.insert(0, shares)
    stacked = [
        jnp.stack([layer_grads[number][member] for number in range(LAYERS)]) for member in range(5)
    ]
    return (
        hidden.astype(jnp.bfloat16).reshape(docs_dev, block, width),
        gradient.reshape(docs_dev, block, width),
        stacked[0],
        stacked[1],
        stacked[2],
        stacked[3],
        stacked[4],
    )


PLANES = 4
GROUPS = 4
CHIPS = 16
GROUP_HEADS = 3
CUT = 240
MESH = pl.DeviceIdType.MESH
F32 = jnp.float32
BF16 = jnp.bfloat16


def fits(mesh, docs_dev, heads):
    return (
        mesh.shape["docs"] == 2
        and mesh.shape["seq"] == 16
        and docs_dev == PLANES
        and heads == GROUPS * GROUP_HEADS
    )


def swap(value, bits):
    return lax.ppermute(value, "seq", [(i, i ^ bits) for i in range(16)])


def swap_docs(value):
    return lax.ppermute(value, "docs", [(0, 1), (1, 0)])


def dot(left, right):
    return lax.dot_general(left, right, (((1,), (0,)), ((), ())), preferred_element_type=F32)


def dot_nt(left, right):
    return lax.dot_general(left, right, (((1,), (1,)), ((), ())), preferred_element_type=F32)


def dot_tn(left, right):
    return lax.dot_general(left, right, (((0,), (0,)), ((), ())), preferred_element_type=F32)


def vmem():
    return pl.BlockSpec(memory_space=pltpu.VMEM)


def smem():
    return pl.BlockSpec(memory_space=pltpu.SMEM)


def hbm():
    return pl.BlockSpec(memory_space=pltpu.HBM)


def params():
    return pltpu.CompilerParams(vmem_limit_bytes=56 * 2**20)


QUERIES = 512
BACK_QUERIES = 512


def key_features(info, random_ref, feature_ref):
    lane = lax.broadcasted_iota(jnp.int32, (16, 64), 1)
    block = lax.broadcasted_iota(jnp.int32, (16, 64), 0)
    query = lane % 16
    globals_here = [info[6 + n] for n in range(GLOB)]
    count = jnp.zeros((16, 64), F32)
    for ids in [(query + 15) % 16, query, (query + 1) % 16] + [
        random_ref[n : n + 1, :] for n in range(RAND)
    ]:
        count += jnp.where(block == ids, 1.0, 0.0)
    for number in globals_here:
        count += jnp.where(block == number, 1.0, 0.0)
    for number in globals_here:
        count = jnp.where(query == number, 1.0, count)
    extra = jnp.where(count > 0, jnp.log(jnp.maximum(count, 1.0)), NEGATIVE)
    row = lax.broadcasted_iota(jnp.int32, (64, 64), 0)
    lane = lax.broadcasted_iota(jnp.int32, (64, 64), 1)
    for n in range(16):
        own = jnp.where(64 * n + row < info[2], extra[n : n + 1, :], NEGATIVE)
        high = own.astype(BF16).astype(F32)
        low = jnp.where(own > 0, own - high, 0.0)
        value = jnp.where(lane < 16, high, jnp.where(lane < 32, low, 0.0))
        feature_ref[64 * n : 64 * n + 64, :] = value.astype(BF16)


def halves_beside(rows):
    return jnp.concatenate([rows[:32], rows[32:]], axis=1)


def halves_below(rows):
    return jnp.concatenate([rows[:, :192], rows[:, 192:]], axis=0)


def spread_heads(qkv, feature_ref, key_scr, query_scr):
    row = lax.broadcasted_iota(jnp.int32, (1024, 64), 0) // 64
    lane = lax.broadcasted_iota(jnp.int32, (1024, 64), 1)
    place = jnp.where(jnp.logical_and(lane < 32, lane % 16 == row), 1.0, 0.0).astype(BF16)
    for h in range(GROUP_HEADS):
        key_scr[h] = jnp.concatenate([qkv[:, 128 * h : 128 * h + 64], feature_ref[...]], axis=1)
        query = qkv[:, 384 + 64 * h : 448 + 64 * h] * jnp.asarray(HEAD**-0.5, BF16)
        query_scr[h] = jnp.concatenate([query, place], axis=1)


def expo_columns(scores):
    expo = jnp.exp(scores - jnp.max(scores, axis=0, keepdims=True))
    return expo, 1.0 / jnp.sum(expo, axis=0, keepdims=True)


def load_up(up_ref, wu, wo, sems):
    pltpu.make_async_copy(up_ref.at[:, :, :, pl.ds(1536, 384)], wo, sems.at[0]).start()
    pltpu.make_async_copy(up_ref.at[:, :, :, pl.ds(0, 1536)], wu, sems.at[1]).start()


def load_down(down_ref, wd, sems):
    for plane in range(2):
        for part in range(2):
            source = down_ref.at[plane, :, :, pl.ds(768 * part, 768)]
            pltpu.make_async_copy(source, wd.at[:, plane, part], sems.at[2]).start()


def wait_weight(scr, sem):
    pltpu.make_async_copy(scr, scr, sem).wait()


def inside_rows(info):
    row = lax.broadcasted_iota(jnp.int32, (256, 1), 0)
    length = jnp.zeros_like(row)
    for k in range(PLANES):
        length = jnp.where(row // 64 == k, info[8 + k], length)
    return info[0] * 64 + row % 64 < length


def norm_parts(values):
    centre = values - jnp.mean(values, axis=-1, keepdims=True)
    spread = jnp.mean(centre * centre, axis=-1, keepdims=True)
    rate = lax.rsqrt(spread + EPSILON)
    return centre * rate, rate


def norm_back(unit, rate, gain, grad):
    scaled = grad * gain
    inner = jnp.mean(scaled * unit, axis=-1, keepdims=True)
    outer = jnp.mean(scaled, axis=-1, keepdims=True)
    return rate * (scaled - outer - unit * inner), jnp.sum(grad * unit, axis=0, keepdims=True)


CURVE = 0.7978845608028654


def gelu_parts(values):
    square = values * values
    bend = jnp.tanh(CURVE * (values + 0.044715 * (square * values)))
    return 0.5 * values * (1.0 + bend), bend, square


def gelu_slope(values, bend, square):
    return 0.5 * (1.0 + bend) + 0.5 * values * (1.0 - bend * bend) * (
        CURVE * (1.0 + 3 * 0.044715 * square)
    )


WEIGHT_SCRATCH = [
    pltpu.VMEM((2, 16, 48, 1536), BF16),
    pltpu.VMEM((16, 2, 2, 48, 768), BF16),
    pltpu.VMEM((2, 16, 48, 384), BF16),
]


def feed_back_kernel(
    pieces,
    layer,
    info,
    base_ref,
    extra_ref,
    gain_ref,
    gain_sum_ref,
    mixed_ref,
    h1_ref,
    up_ref,
    h2_ref,
    *refs,
):
    w_refs, refs = refs[:pieces], refs[pieces:]
    dh1_ref, do_ref, dgain_ref, *sum_refs, wu, wd, wo, gu, gd, go, got, sems, pair_sems, out_sems = refs
    load_down(w_refs[1], wd, sems)
    load_up(w_refs[0], wu, wo, sems)
    docs, me = lax.axis_index("docs"), lax.axis_index("seq")
    mate = (docs, flip(me, 1))
    greet([mate])
    units = [(ry, place) for ry in range(2) for place in range(8)]

    def other_docs(ry):
        return docs if ry == 0 else 1 - docs

    def owner(place, rc):
        return flip(me, (place % 2) * 8 + (place // 2 % 2) * 4 + (place // 4) * 2 + rc)

    def to_mate(source, ry, place, first, count, n):
        pltpu.make_async_remote_copy(
            source,
            got.at[ry, place, pl.ds(first, count)],
            pair_sems.at[0, n],
            pair_sems.at[1, n],
            device_id=mate,
            device_id_type=MESH,
        ).start()

    def up_to_mate(part):
        x, z = (me // 2) % 2, me // 4
        across = x if part % 2 == 0 else 1 - x
        low = z % 2 if part // 2 % 2 == 0 else 1 - z % 2
        high = z // 2 if part // 4 == 0 else 1 - z // 2
        for half in range(2):
            source = gu.at[half, 2 * part + 1 - me % 2]
            to_mate(source, other_docs(half), 4 * across + 2 * low + high, 0, 192, 0)

    if layer == 0:
        parts = [
            base_ref[64 * k : 64 * k + 64, :] + extra_ref[k].astype(F32)
            for k in range(PLANES)
        ]
        grad = jnp.concatenate(parts, axis=0)
    else:
        grad = base_ref[...].reshape(256, 768).astype(F32)
    grad = jnp.where(inside_rows(info), grad, 0.0)
    unit2, rate2 = norm_parts(h2_ref[...])
    dh2, dgain1 = norm_back(unit2, rate2, gain_ref[2 * layer + 1 : 2 * layer + 2, :], grad)
    dgain_ref[...] = gain_sum_ref[...] if layer == 0 else jnp.zeros_like(dgain_ref)
    dgain_ref[2 * layer + 1 : 2 * layer + 2, :] = dgain1
    df = dh2.astype(BF16)
    df_turned = df.T
    unit1, rate1 = norm_parts(h1_ref[...])
    x1_low = (unit1 * gain_ref[2 * layer : 2 * layer + 1, :]).astype(BF16)
    wait_weight(wd, sems.at[2])
    wait_weight(wu, sems.at[1])
    dx1 = dh2
    for part in range(8):
        at = 384 * part
        d_act = dot_nt(df, wd[2 * part : 2 * part + 2].reshape(384, 768))
        up = up_ref[:, at : at + 384]
        act, bend, square = gelu_parts(up)
        act = act.astype(BF16)
        dup = (gelu_slope(up, bend, square) * d_act).astype(BF16)
        side, start = part // 4, 384 * (part % 4)
        dx1 += dot_nt(dup, wu[side, :, :, start : start + 384].reshape(768, 384))
        gt_up = dot_tn(dup, x1_low).astype(BF16)
        for n in range(2):
            for half in range(2):
                gu[half, 2 * part + n] = gt_up[
                    192 * n : 192 * n + 192, 384 * half : 384 * half + 384
                ]
        gt_down = dot(df_turned, act).astype(BF16)
        row = 48 * (part % 4)
        for s in range(16):
            gd[part // 4, s, row : row + 48, :] = gt_down[48 * s : 48 * s + 48]
        up_to_mate(part)
        if part % 4 == 3:
            for place in range(8):
                source = gd.at[part // 4, owner(place, 1)]
                to_mate(source, other_docs(part // 4), place, 240, 192, 1)
    dh1, dgain0 = norm_back(unit1, rate1, gain_ref[2 * layer : 2 * layer + 1, :], dx1)
    dgain_ref[2 * layer : 2 * layer + 1, :] = dgain0
    dh1_ref[...] = dh1
    da = dh1.astype(BF16)
    gt_out = dot_tn(da, mixed_ref[...]).astype(BF16)
    for s in range(16):
        for half in range(2):
            go[half, s] = gt_out[48 * s : 48 * s + 48, 384 * half : 384 * half + 384]
    for ry, place in units:
        to_mate(go.at[other_docs(ry), owner(place, 1)], ry, place, 192, 48, 2)
    wait_weight(wo, sems.at[0])
    do = dot_nt(da[:, 0:384], wo[0].reshape(768, 384))
    do += dot_nt(da[:, 384:768], wo[1].reshape(768, 384))
    do = do.astype(BF16)
    for k in range(PLANES):
        for g in range(GROUPS):
            do_ref[4 * k + g] = halves_beside(do[64 * k : 64 * k + 64, 192 * g : 192 * g + 192])
    copies = []
    for n, (scr, first, count) in enumerate(((gu, 0, 192), (gd, 240, 192), (go, 192, 48))):
        part = got.at[:, :, pl.ds(first, count)]
        pltpu.make_async_copy(part, part, pair_sems.at[1, n]).wait()
        for ry, place in units:
            span = slice(first, first + count)
            own = scr[other_docs(ry), owner(place, 0)].astype(F32)
            got[ry, place, span] = (own + got[ry, place, span].astype(F32)).astype(BF16)
            if n == 1:
                source, ref = got.at[ry, place, pl.ds(CUT, 432 - CUT)], sum_refs[2 + place // 4]
                target = ref.at[ry, place % 4]
            elif n == 2:
                source, target = got.at[ry, place, pl.ds(0, CUT)], sum_refs[ry].at[place]
            if n > 0:
                copies.append(pltpu.make_async_copy(source, target, out_sems.at[len(copies)]))
                copies[-1].start()
    for n, scr in enumerate((gu, gd, go)):
        half = scr.at[:, pl.ds(0, 8)]
        pltpu.make_async_copy(half, half, pair_sems.at[0, n]).wait()
    for copy in copies:
        copy.wait()


def feed_back(layer, info, base, extra, gains, gain_sum, saved, weights, number):
    mixed, h1, up, h2 = saved
    return pl.pallas_call(
        functools.partial(feed_back_kernel, len(weights), layer),
        out_shape=(
            jax.ShapeDtypeStruct((256, 768), F32),
            jax.ShapeDtypeStruct((16, 32, 384), BF16),
            jax.ShapeDtypeStruct((8, 768), F32),
            jax.ShapeDtypeStruct((8, CUT, 384), BF16),
            jax.ShapeDtypeStruct((8, CUT, 384), BF16),
            jax.ShapeDtypeStruct((2, 4, 432 - CUT, 384), BF16),
            jax.ShapeDtypeStruct((2, 4, 432 - CUT, 384), BF16),
        ),
        in_specs=[smem()] + [vmem()] * 8 + [hbm() for _ in weights],
        out_specs=(vmem(), vmem(), vmem(), hbm(), hbm(), hbm(), hbm()),
        scratch_shapes=WEIGHT_SCRATCH
        + [
            pltpu.VMEM((2, 16, 192, 384), BF16),
            pltpu.VMEM((2, 16, 192, 384), BF16),
            pltpu.VMEM((2, 16, 48, 384), BF16),
            pltpu.VMEM((2, 8, 432, 384), BF16),
            pltpu.SemaphoreType.DMA((3,)),
            pltpu.SemaphoreType.DMA((2, 3)),
            pltpu.SemaphoreType.DMA((32,)),
        ],
        compiler_params=pltpu.CompilerParams(
            collective_id=number, has_side_effects=True, vmem_limit_bytes=56 * 2**20
        ),
        cost_estimate=pl.CostEstimate(
            flops=6 * 10**9, bytes_accessed=40 * 10**6, transcendentals=10**6
        ),
        name="feed_back",
    )(info, base, extra, gains, gain_sum, mixed, h1, up, h2, *weights)


def flip(index, bits):
    for bit in (1, 2, 4, 8):
        if bits & bit:
            index = index + bit - 2 * bit * ((index // bit) % 2)
    return index


def greet(peers):
    barrier = pltpu.get_barrier_semaphore()
    for peer in peers:
        pl.semaphore_signal(barrier, inc=1, device_id=peer, device_id_type=MESH)
    pl.semaphore_wait(barrier, len(peers))


def remote(source, target, sems, n, peer):
    return pltpu.make_async_remote_copy(
        source, target, sems.at[0, n], sems.at[1, n], device_id=peer, device_id_type=MESH
    )


def comm_params(number):
    return pltpu.CompilerParams(
        collective_id=number, has_side_effects=True, vmem_limit_bytes=16 * 2**20
    )


class Spread:
    def __init__(self, low_ref, x_ref, sems, own_sem):
        self.low_ref, self.x_ref, self.sems = low_ref, x_ref, sems
        self.docs, self.me = lax.axis_index("docs"), lax.axis_index("seq")
        self.own = pltpu.make_async_copy(low_ref.at[self.me // 4], x_ref.at[self.me], own_sem)
        self.hops, self.across, self.mates = [], [], []

    def send(self, source, slot, n, bits):
        peer = (self.docs, flip(self.me, bits))
        copy = remote(source, self.x_ref.at[slot], self.sems, n, peer)
        copy.start()
        return copy

    def begin(self):
        for rz in range(1, 4):
            source = self.low_ref.at[flip(self.me, 4 * rz) // 4]
            self.hops.append(self.send(source, self.me, rz, 4 * rz))
        self.own.start()
        source = self.low_ref.at[self.me // 4]
        self.across.append(self.send(source, self.me, 4, 2))
        self.mates.append(self.send(source, self.me, 8, 1))

    def forward(self, rz):
        self.hops[rz - 1].wait_recv()
        slot = flip(self.me, 4 * rz)
        self.across.append(self.send(self.x_ref.at[slot], slot, 4 + rz, 2))
        self.mates.append(self.send(self.x_ref.at[slot], slot, 8 + rz, 1))

    def from_beside(self):
        for rz in range(4):
            self.across[rz].wait_recv()
            slot = flip(flip(self.me, 4 * rz), 2)
            self.mates.append(self.send(self.x_ref.at[slot], slot, 12 + rz, 1))

    def arrived(self):
        for copy in self.mates:
            copy.wait_recv()
        self.own.wait()

    def finish(self):
        for copy in self.hops + self.across + self.mates:
            copy.wait_send()


class Slabs:
    def __init__(self, source, w_ref, sems, own_sem, docs_first=False):
        self.source, self.w_ref, self.sems = source, w_ref, sems
        self.docs, self.me = lax.axis_index("docs"), lax.axis_index("seq")
        self.plane, self.x, self.core = self.me // 4, (self.me // 2) % 2, self.me % 2
        beside, over = (self.docs, flip(self.me, 2)), (1 - self.docs, self.me)
        self.peers = (over, beside) if docs_first else (beside, over)
        if docs_first:
            self.near = ((self.docs, self.x), (1 - self.docs, self.x))
            self.far = ((self.docs, 1 - self.x), (1 - self.docs, 1 - self.x))
        else:
            self.near = ((self.docs, self.x), (self.docs, 1 - self.x))
            self.far = ((1 - self.docs, self.x), (1 - self.docs, 1 - self.x))
        self.mate = (self.docs, flip(self.me, 1))
        self.own = pltpu.make_async_copy(source, self.slot(self.near[0], self.plane), own_sem)

    def slot(self, at, z):
        return self.w_ref.at[self.core, 8 * at[0] + 2 * z + at[1]]

    def copy(self, at, z, own, send, recv, peer):
        slot = self.slot(at, z)
        return pltpu.make_async_remote_copy(
            self.source if own else slot,
            slot,
            self.sems.at[0, send],
            self.sems.at[1, recv],
            device_id=peer,
            device_id_type=MESH,
        )

    def line(self, z, own, step):
        peer = (self.docs, self.me + 4 * step)
        return self.copy(self.near[0], z, own, z + (0 if step > 0 else 4), z, peer)

    def first(self, z, own=False):
        return self.copy(self.near[0], z, own, 8 + z, 8 + z, self.peers[0])

    def second(self, z, n, own=False):
        return self.copy(self.near[n], z, own, 12 + 4 * n + z, 12 + 4 * n + z, self.peers[1])

    def core_copy(self, at, n, z, own=False):
        return self.copy(at, z, own, 20 + 4 * n + z, 20 + 4 * n + z, self.mate)

    def begin(self):
        self.own.start()
        for step in (1, -1):
            pl.when(self.has(self.plane + step))(self.line(self.plane, True, step).start)
        self.first(self.plane, True).start()
        self.core_copy(self.near[0], 0, self.plane, True).start()

    def has(self, z):
        return jnp.logical_and(z >= 0, z < PLANES)

    def each(self, distance, act):
        if distance == 0:
            act(self.plane, 0)
            return
        for step in (1, -1):
            z = self.plane - step * distance
            pl.when(self.has(z))(functools.partial(act, z, step))

    def from_line(self, distance):
        def act(z, step):
            self.line(z, False, step).wait_recv()
            pl.when(self.has(self.plane + step))(self.line(z, False, step).start)
            self.first(z).start()
            self.core_copy(self.near[0], 0, z).start()

        self.each(distance, act)

    def from_first(self, distance):
        def act(z, step):
            self.first(z).wait_recv()
            self.second(z, 0, distance == 0).start()
            self.second(z, 1).start()
            self.core_copy(self.near[1], 1, z).start()

        self.each(distance, act)

    def from_second(self, distance):
        def act(z, step):
            for n in range(2):
                self.second(z, n).wait_recv()
                self.core_copy(self.far[n], 2 + n, z).start()

        self.each(distance, act)

    def arrived(self):
        for z in range(PLANES):
            for n, at in enumerate(self.near + self.far):
                self.core_copy(at, n, z).wait_recv()
        self.own.wait()

    def finish(self):
        for z in range(PLANES):
            for step in (1, -1):
                sent = jnp.logical_and(
                    (self.plane - z) * step >= 0, self.has(self.plane + step)
                )
                pl.when(sent)(self.line(z, False, step).wait_send)
            self.first(z).wait_send()
            for n, at in enumerate(self.near + self.far):
                if n < 2:
                    self.second(z, n).wait_send()
                self.core_copy(at, n, z).wait_send()


class Rows:
    def __init__(self, source, w_ref, sems, own_sem):
        self.source, self.w_ref, self.sems = source, w_ref, sems
        self.docs, self.me = lax.axis_index("docs"), lax.axis_index("seq")
        self.over = (1 - self.docs, self.me)
        self.own = pltpu.make_async_copy(source, self.slot(self.me // 4), own_sem)
        self.hops, self.moved = [], []

    def slot(self, z):
        return self.w_ref.at[pl.ds(8 * self.docs + 2 * z, 2)]

    def begin(self):
        target = self.slot(self.me // 4)
        for rz in range(1, 4):
            peer = (self.docs, flip(self.me, 4 * rz))
            self.hops.append(remote(self.source, target, self.sems, rz, peer))
            self.hops[-1].start()
        self.own.start()
        self.moved.append(remote(self.source, target, self.sems, 4, self.over))
        self.moved[0].start()

    def forward(self, rz):
        self.hops[rz - 1].wait_recv()
        slot = self.slot(flip(self.me, 4 * rz) // 4)
        self.moved.append(remote(slot, slot, self.sems, 4 + rz, self.over))
        self.moved[-1].start()

    def arrived(self):
        for copy in self.moved:
            copy.wait_recv()
        self.own.wait()

    def finish(self):
        for copy in self.hops + self.moved:
            copy.wait_send()


class Collect:
    def __init__(self, keep_ref, send_ref, land, got_core, got_x, sum_x, near, sums, sems):
        self.keep_ref, self.send_ref, self.land, self.got_core = keep_ref, send_ref, land, got_core
        self.got_x, self.sum_x, self.near, self.sums, self.sems = got_x, sum_x, near, sums, sems
        self.docs, self.me = lax.axis_index("docs"), lax.axis_index("seq")
        self.order = (3, 2, 1, 0)
        self.first, self.across, self.hops = {}, {}, []

    def begin(self):
        mate = (self.docs, flip(self.me, 1))
        for rz in self.order:
            for n in (2 * rz + 1, 2 * rz):
                self.first[n] = remote(
                    self.send_ref.at[n], self.got_core.at[n], self.sems, n, mate
                )
                self.first[n].start()

    def along_x(self):
        beside = (self.docs, flip(self.me, 2))
        for rz in self.order:
            n = 2 * rz + 1
            self.first[n].wait_recv()
            self.sum_x[rz] = add_low(self.keep_ref[n], self.got_core[n])
            self.across[rz] = remote(
                self.sum_x.at[rz], self.got_x.at[rz], self.sems, 8 + rz, beside
            )
            self.across[rz].start()
            n = 2 * rz
            self.first[n].wait_recv()
            self.near[rz] = add_full(self.keep_ref[n], self.got_core[n])

    def along_z(self):
        plane = self.me // 4
        for rz in self.order:
            self.across[rz].wait_recv()
            total = add_low(self.near[rz], self.got_x[rz])
            if rz == 0:
                self.land[plane] = total
            else:
                self.sums[rz] = total
                peer = (self.docs, flip(self.me, 4 * rz))
                copy = remote(self.sums.at[rz], self.land.at[plane], self.sems, 12 + rz, peer)
                copy.start()
                self.hops.append(copy)

    def finish(self):
        for copy in self.hops:
            copy.wait_recv()
        for copy in list(self.first.values()) + list(self.across.values()) + self.hops:
            copy.wait_send()


class Exchange:
    def __init__(self, source, land, sems, own_sem):
        docs, me = lax.axis_index("docs"), lax.axis_index("seq")
        self.copies = []
        for bits in range(15, 0, -1):
            peer = flip(me, bits)
            self.copies.append(remote(source.at[peer], land.at[me], sems, bits, (docs, peer)))
        self.own = pltpu.make_async_copy(source.at[me], land.at[me], own_sem)

    def begin(self):
        for copy in self.copies:
            copy.start()
        self.own.start()

    def arrived(self):
        for copy in self.copies:
            copy.wait_recv()
        self.own.wait()

    def finish(self):
        for copy in self.copies:
            copy.wait_send()


class Line:
    PLACE = (0, 2, 1, 3)

    def __init__(self, own, from_left, from_right, sems):
        self.own, self.landing, self.sems = own, (from_left, from_right), sems
        self.docs, self.me = lax.axis_index("docs"), lax.axis_index("seq")
        self.plane = self.me // 4

    def copy(self, place, target, step):
        side = 0 if step > 0 else 1
        return pltpu.make_async_remote_copy(
            self.own.at[place],
            self.landing[side].at[target],
            self.sems.at[0, side, target],
            self.sems.at[1, side, target],
            device_id=(self.docs, self.me + 4 * step),
            device_id_type=MESH,
        )

    def at(self, plane, act):
        pl.when(self.plane == plane)(act)

    def begin(self, rz):
        for plane, step in ((0, 1), (3, -1)):
            self.at(plane, self.copy(self.PLACE[rz], plane ^ rz, step).start)

    def hop(self, number):
        for plane, target, step in (
            ((1, 3, 1), (2, 0, -1)),
            ((1, 0, -1), (2, 3, 1)),
            ((1, 2, 1), (2, 1, -1)),
        )[number]:
            place, side = self.PLACE[plane ^ target], 0 if step > 0 else 1

            def act(place=place, side=side, target=target, step=step):
                copy = self.copy(place, target, step)
                copy.wait_recv()
                self.own[place] = add_low(self.own[place], self.landing[side][target])
                copy.start()

            self.at(plane, act)

    def total(self, out_ref, rows):
        for plane in range(PLANES):

            def act(plane=plane):
                total = self.own[0, rows].astype(F32)
                for side, step in ((0, 1), (1, -1)):
                    if 0 <= plane - step < PLANES:
                        total = total + self.landing[side][plane, rows].astype(F32)
                out_ref[...] = total

            self.at(plane, act)

    def arrived(self):
        for plane in range(PLANES):

            def act(plane=plane):
                for step in (1, -1):
                    if 0 <= plane - step < PLANES:
                        self.copy(0, plane, step).wait_recv()

            self.at(plane, act)

    def finish(self):
        for plane in range(PLANES):

            def act(plane=plane):
                for target in range(PLANES):
                    step = 1 if target > plane else -1
                    if target != plane:
                        self.copy(self.PLACE[plane ^ target], target, step).wait_send()

            self.at(plane, act)


class Everywhere:
    def __init__(self, total, got, sems):
        self.total, self.got, self.sems = total, got, sems
        docs, me = lax.axis_index("docs"), lax.axis_index("seq")
        self.peers = [(docs, flip(me, bits)) for bits in (1, 2, 4, 8)] + [(1 - docs, me)]
        self.copies = []

    def step(self):
        n = len(self.copies)
        if n > 0:
            self.copies[-1].wait_recv()
            self.total[n] = self.total[n - 1] + self.got[n - 1]
        if n < len(self.peers):
            copy = remote(self.total.at[n], self.got.at[n], self.sems, n, self.peers[n])
            copy.start()
            self.copies.append(copy)

    def finish(self):
        for copy in self.copies:
            copy.wait_send()


class Rest:
    ORDER = (3, 1, 2, 0)

    def __init__(self, a_keep, a_send, b_keep, b_send, scr):
        self.a_keep, self.a_send, self.b_keep, self.b_send = a_keep, a_send, b_keep, b_send
        self.scr = scr
        docs, me = lax.axis_index("docs"), lax.axis_index("seq")
        self.beside, self.over = (docs, flip(me, 2)), (1 - docs, me)
        self.line = Line(scr.own, scr.left, scr.right, scr.line_sems)
        self.sent = []

    def copy(self, n, place):
        scr = self.scr
        source, target, peer = (
            (self.a_send.at[4 + place], scr.a_got.at[4 + place], self.over),
            (self.b_send.at[1, place], scr.b_got.at[1, place], self.beside),
            (self.a_send.at[place], scr.a_got.at[place], self.over),
            (self.b_send.at[0, place], scr.b_got.at[0, place], self.beside),
            (scr.a_far.at[place], scr.a_far_got.at[place], self.beside),
            (scr.b_far.at[place], scr.b_far_got.at[place], self.over),
        )[n]
        return remote(source, target, scr.rest_sems, 4 * n + place, peer)

    def start(self, n, place):
        self.sent.append(self.copy(n, place))
        self.sent[-1].start()

    def first(self, place):
        for n in range(4):
            self.start(n, place)

    def second(self, place):
        scr = self.scr
        self.copy(0, place).wait_recv()
        scr.a_far[place] = add_low(self.a_keep[4 + place], scr.a_got[4 + place])
        self.start(4, place)
        self.copy(1, place).wait_recv()
        scr.b_far[place] = add_low(self.b_keep[1, place], scr.b_got[1, place])
        self.start(5, place)

    def third(self, place):
        scr = self.scr
        self.copy(2, place).wait_recv()
        self.copy(4, place).wait_recv()
        near = add_full(self.a_keep[place], scr.a_got[place]) + scr.a_far_got[place].astype(F32)
        scr.own[place, :CUT] = near.astype(BF16)
        self.copy(3, place).wait_recv()
        self.copy(5, place).wait_recv()
        near = add_full(self.b_keep[0, place], scr.b_got[0, place])
        near = near + scr.b_far_got[place].astype(F32)
        scr.own[place, CUT:] = near.astype(BF16)
        if place > 0:
            self.line.begin(Line.PLACE[place])

    def finish(self):
        for copy in self.sent:
            copy.wait_send()
        self.line.finish()


class Route:
    def __init__(self, source, out_ref, sems):
        self.source, self.out_ref, self.sems = source, out_ref, sems
        self.docs, self.me = lax.axis_index("docs"), lax.axis_index("seq")

    def each(self, act_here, act_there):
        for t in range(3):
            local = 3 * (self.me // 4) + t
            number = 16 * (local // 4) + 4 * (self.me % 4) + local % 4
            owner, slot = number // 3, number % 3
            target = self.out_ref.at[slot]
            here = pltpu.make_async_copy(self.source.at[t], target, self.sems.at[2, slot])
            there = pltpu.make_async_remote_copy(
                self.source.at[t],
                target,
                self.sems.at[0, t],
                self.sems.at[1, slot],
                device_id=(self.docs, owner),
                device_id_type=MESH,
            )
            pl.when(owner == self.me)(functools.partial(act_here, here))
            pl.when(owner != self.me)(functools.partial(act_there, there))

    def begin(self):
        self.each(lambda copy: copy.start(), lambda copy: copy.start())

    def finish(self):
        self.each(lambda copy: copy.wait(), lambda copy: copy.wait_send())
        for slot in range(3):
            number = 3 * self.me + slot
            local = 4 * (number // 16) + number % 4
            source = 4 * (local // 3) + (number % 16) // 4
            target = self.out_ref.at[slot]
            wait = pltpu.make_async_copy(target, target, self.sems.at[1, slot]).wait
            pl.when(source != self.me)(wait)


def back_scratch(width):
    low = 432 - CUT
    sems = pltpu.SemaphoreType.DMA

    def vm(*shape, dtype=BF16):
        return pltpu.VMEM(shape, dtype)

    return dict(
        qkv=vm(1024, 576),
        weight=vm(CHIPS, 48, 640),
        x=vm(16, 64, width),
        a_keep=vm(8, CUT, 384),
        b_keep=vm(2, 4, low, 384),
        load_sems=sems((5,)),
        do=vm(16, 32, 384),
        do_sems=sems((2, 16)),
        do_own=sems,
        key=vm(3, 1024, 128),
        query=vm(3, 1024, 128),
        value=vm(3, 1024, 64),
        turned=vm(3, 64, 1024),
        side=vm(2, 3, 1024, 128),
        dkv=vm(3, 1024, 128, dtype=F32),
        dq=vm(1024 // BACK_QUERIES, 192, BACK_QUERIES, dtype=F32),
        dqkv=vm(1024, 576),
        rows=vm(2, 8, 64, width),
        land=vm(4, 64, width),
        got_core=vm(8, 64, width),
        got_x=vm(4, 64, width),
        sum_x=vm(4, 64, width),
        near=vm(4, 64, width, dtype=F32),
        sums=vm(4, 64, width),
        row_sems=sems((2, 16)),
        a_got=vm(8, CUT, 384),
        b_got=vm(2, 4, low, 384),
        a_far=vm(4, CUT, 384),
        a_far_got=vm(4, CUT, 384),
        b_far=vm(4, low, 384),
        b_far_got=vm(4, low, 384),
        rest_sems=sems((2, 24)),
        own=vm(4, 432, 384),
        left=vm(4, 432, 384),
        right=vm(4, 432, 384),
        line_sems=sems((2, 2, 4)),
        q_grad=vm(2, 4, 144, 384),
        q_got=vm(4, 144, 384),
        q_own=vm(4, 144, 384),
        q_land=vm(4, 144, 384),
        q_sems=sems((2, 4)),
        q_sum=vm(3, 48, 384, dtype=F32),
        route_sems=sems((3, 3)),
        gain_sum=vm(6, 8, width, dtype=F32),
        gain_got=vm(5, 8, width, dtype=F32),
        gain_sems=sems((2, 5)),
    )


def attend_back_kernel(names, last, *refs):
    feature_ref, qkv_ref, do_ref, x_ref, w_ref, a_keep, a_send, b_keep, b_send = refs[:9]
    gain_ref, rows_ref, rest_ref, out_ref, gain_out_ref = refs[9:14]
    scr = types.SimpleNamespace(**dict(zip(names, refs[14:])))
    docs, me = lax.axis_index("docs"), lax.axis_index("seq")
    plane = me // 4
    over = (1 - docs, me)
    loads = {}
    for n, (name, ref) in enumerate(
        dict(qkv=qkv_ref, weight=w_ref, a_keep=a_keep, b_keep=b_keep, x=x_ref).items()
    ):
        loads[name] = pltpu.make_async_copy(ref, getattr(scr, name), scr.load_sems.at[n])
        loads[name].start()
    greet([(docs, flip(me, bits)) for bits in range(15, 0, -1)] + [over])
    exchange = Exchange(do_ref, scr.do, scr.do_sems, scr.do_own)
    exchange.begin()
    rest = Rest(scr.a_keep, a_send, scr.b_keep, b_send, scr)
    rest.first(3)
    rest.first(1)
    gains = Everywhere(scr.gain_sum, scr.gain_got, scr.gain_sems)
    if last:
        scr.gain_sum[0] = gain_ref[...]
        gains.step()

    loads["qkv"].wait()
    qkv = scr.qkv[...]
    spread_heads(qkv, feature_ref, scr.key, scr.query)
    zero = jnp.zeros((1024, 64), BF16)
    for h in range(GROUP_HEADS):
        scr.value[h] = qkv[:, 128 * h + 64 : 128 * h + 128]
        scr.turned[h] = qkv[:, 128 * h : 128 * h + 64].T
        scr.side[0, h] = jnp.concatenate([scr.query[h, :, :64], zero], axis=1)
    loads["a_keep"].wait()
    loads["b_keep"].wait()
    exchange.arrived()
    grad_o = jnp.concatenate([halves_below(scr.do[n]) for n in range(16)], axis=0)
    for h in range(GROUP_HEADS):
        scr.side[1, h] = jnp.concatenate([zero, grad_o[:, 64 * h : 64 * h + 64]], axis=1)

    def part(n, h):
        at = slice(BACK_QUERIES * n, BACK_QUERIES * n + BACK_QUERIES)
        expo, rate = expo_columns(dot_nt(scr.key[h], scr.query[h, at, :]))
        probs = expo * rate
        grad_probs = dot_nt(scr.value[h], scr.side[1, h, at, :][:, 64:])
        delta = jnp.sum(probs * grad_probs, axis=0, keepdims=True)
        grad_scores = (probs * (grad_probs - delta)).astype(BF16)
        scr.dq[n, 64 * h : 64 * h + 64, :] = dot(scr.turned[h], grad_scores) * (HEAD**-0.5)
        dkv = dot(grad_scores, scr.side[0, h, at, :])
        dkv += dot(probs.astype(BF16), scr.side[1, h, at, :])
        if n == 0:
            scr.dkv[h] = dkv
        else:
            scr.dqkv[:, 128 * h : 128 * h + 128] = (scr.dkv[h] + dkv).astype(BF16)

    part(0, 0)
    rest.second(3)
    rest.first(2)
    part(0, 1)
    if last:
        gains.step()
    part(0, 2)
    rest.second(1)
    scr.dqkv[0:512, 384:576] = scr.dq[0].T.astype(BF16)
    part(1, 0)
    rest.third(3)
    part(1, 1)
    rest.second(2)
    part(1, 2)
    rest.third(1)
    rest.line.hop(0)
    if last:
        gains.step()
    scr.dqkv[512:1024, 384:576] = scr.dq[1].T.astype(BF16)
    loads["x"].wait()
    grad = dot_tn(scr.dqkv[...], scr.x[...].reshape(1024, scr.x.shape[-1]))
    order = [6, 7, 8, 0, 2, 4, 1, 3, 5]
    grad = jnp.concatenate([grad[64 * n : 64 * n + 64] for n in order], axis=0).astype(BF16)
    for quarter in range(PLANES):
        apart = flip(plane, quarter)
        place = (apart % 2) * 2 + apart // 2
        for side in range(2):
            at = docs if side == 0 else 1 - docs
            scr.q_grad[at, place] = grad[
                144 * quarter : 144 * quarter + 144, 384 * side : 384 * side + 384
            ]
    crossed = remote(scr.q_grad.at[1], scr.q_got, scr.q_sems, 0, over)
    crossed.start()
    rest.first(0)
    loads["weight"].wait()
    rows = Collect(
        scr.rows.at[0],
        scr.rows.at[1],
        scr.land,
        scr.got_core,
        scr.got_x,
        scr.sum_x,
        scr.near,
        scr.sums,
        scr.row_sems,
    )
    for half in (1, 0):
        part_rows = []
        for n in range(8):
            block = flip(me, (n // 2) * 4 + (n % 2) * 2 + half)
            part_rows.append(scr.dqkv[pl.ds(pl.multiple_of(block * 64, 64), 64), :])
        product = dot_nt(jnp.concatenate(part_rows, axis=0), scr.weight[:, :, :576].reshape(-1, 576))
        scr.rows[half] = product.astype(BF16).reshape(scr.rows.shape[1:])
        if half == 1:
            rows.begin()
    rest.third(2)
    rest.line.hop(1)
    rows.along_x()
    if last:
        gains.step()
    crossed.wait_recv()
    turned = []
    for place in Rest.ORDER:
        rz = Line.PLACE[place]
        scr.q_own[place] = add_low(scr.q_grad[0, place], scr.q_got[place])
        if rz > 0:
            peer = (docs, flip(me, 4 * rz))
            turned.append(
                remote(scr.q_own.at[place], scr.q_land.at[place], scr.q_sems, place, peer)
            )
            turned[-1].start()
    rest.line.hop(2)
    rest.second(0)
    rows.along_z()
    if last:
        gains.step()
    for copy in turned:
        copy.wait_recv()
    total = scr.q_own[0].astype(F32)
    for place in range(1, PLANES):
        total = total + scr.q_land[place].astype(F32)
    scr.q_sum[...] = total.reshape(scr.q_sum.shape)
    route = Route(scr.q_sum, out_ref, scr.route_sems)
    route.begin()
    rest.third(0)
    if last:
        gains.step()
        gain_out_ref[...] = scr.gain_sum[5]
        gains.finish()
    else:
        gain_out_ref[...] = gain_ref[...]
    rest.line.arrived()
    rest.line.total(rest_ref, slice(0, 432))
    rows.finish()
    rows_ref[...] = scr.land[...]
    for piece in (exchange, rest, route):
        piece.finish()
    for copy in turned + [crossed]:
        copy.wait_send()


def attend_back(features, qkv, grad_o, x, weight, sums, gain_grads, last, number):
    width = x.shape[-1]
    scratch = back_scratch(width)
    return pl.pallas_call(
        functools.partial(attend_back_kernel, tuple(scratch), last),
        out_shape=(
            jax.ShapeDtypeStruct((PLANES, 64, width), BF16),
            jax.ShapeDtypeStruct((432, 384), F32),
            jax.ShapeDtypeStruct((3, 48, 384), F32),
            jax.ShapeDtypeStruct((8, width), F32),
        ),
        in_specs=[vmem()] + [hbm()] * 8 + [vmem()],
        out_specs=(vmem(), vmem(), hbm(), vmem()),
        scratch_shapes=list(scratch.values()),
        compiler_params=pltpu.CompilerParams(
            collective_id=number, has_side_effects=True, vmem_limit_bytes=56 * 2**20
        ),
        cost_estimate=pl.CostEstimate(
            flops=8 * 10**9, bytes_accessed=10 * 10**6, transcendentals=3 * 10**6
        ),
        name="attend_back",
    )(features, qkv, grad_o, x, weight, *sums, gain_grads)


def forward_scratch(width):
    sems = pltpu.SemaphoreType.DMA

    def vm(*shape, dtype=BF16):
        return pltpu.VMEM(shape, dtype)

    scratch = dict(
        x=vm(16, 64, width),
        weight=vm(CHIPS, 48, 640),
        qkv=vm(1024, 576),
        key=vm(3, 1024, 128),
        query=vm(3, 1024, 128),
        value=vm(3, 64, 1024),
        turned=vm(192, 1024, dtype=F32),
        o=vm(LAYERS, 16, 32, 384),
        o_got=vm(LAYERS, 16, 32, 384),
        mixed=vm(256, width),
        h1=vm(256, width, dtype=F32),
        up=vm(256, 4 * width, dtype=F32),
        h2=vm(256, width, dtype=F32),
        hidden=vm(256, width, dtype=F32),
        low=vm(4, 64, width),
        act=vm(256, 4 * width),
        wu=WEIGHT_SCRATCH[0],
        wd=WEIGHT_SCRATCH[1],
        wo=WEIGHT_SCRATCH[2],
        weight_sems=sems((3,)),
        load_sems=sems((3,)),
        own_sems=sems((2, 5)),
        save_sems=sems((2, 5)),
    )
    for layer in range(LAYERS):
        scratch[f"row_sems_{layer}"] = sems((2, 16))
        scratch[f"qkv_sems_{layer}"] = sems((2, 8))
        scratch[f"o_sems_{layer}"] = sems((2, 16))
        scratch[f"up_sems_{layer}"] = sems((2, 36))
        scratch[f"down_sems_{layer}"] = sems((2, 36))
    return scratch


def forward_kernel(names, *refs):
    info, random_ref, tokens_ref = refs[:3]
    wq_refs, up_refs, down_refs = (
        [ref.at[layer] for layer in range(LAYERS)] for ref in refs[3:6]
    )
    saved_refs = (refs[6:12], refs[12:18])
    w_refs, wu_refs, wd_refs, gains_ref, result_ref = refs[18:20], refs[20:22], refs[22:24], refs[24], refs[25]
    feature_ref = refs[26]
    scr = types.SimpleNamespace(**dict(zip(names, refs[27:])))
    docs, me = lax.axis_index("docs"), lax.axis_index("seq")
    pltpu.make_async_copy(tokens_ref, scr.low, scr.load_sems.at[2]).start()
    greet([(docs, flip(me, bits)) for bits in range(15, 0, -1)] + [(1 - docs, me)])

    def sems(name, layer):
        return getattr(scr, f"{name}_sems_{layer}")

    qkvs, slabs = [], []
    for layer in range(LAYERS):
        own = scr.own_sems.at[layer]
        qkvs.append(Rows(wq_refs[layer], w_refs[layer], sems("qkv", layer), own.at[0]))
        slabs.append(
            [
                Slabs(up_refs[layer], wu_refs[layer], sems("up", layer), own.at[1]),
                Slabs(down_refs[layer], wd_refs[layer], sems("down", layer), own.at[2], True),
            ]
        )

    def spread(layer, source):
        x_ref = saved_refs[layer][0]
        return Spread(source, x_ref, sems("row", layer), scr.own_sems.at[layer, 3])

    def every(parts, step, *arguments):
        for part in parts:
            getattr(part, step)(*arguments)

    def move(layer, *steps):
        for step in steps:
            name = {"l": "from_line", "f": "from_first", "s": "from_second"}[step[0]]
            every(slabs[layer], name, int(step[1]))

    def save(layer, n, source):
        copy = pltpu.make_async_copy(source, saved_refs[layer][n + 1], scr.save_sems.at[layer, n])
        copy.start()
        return copy

    saves = []

    def attend(layer, rows, ticks):
        qkvs[layer].arrived()
        rows.arrived()
        load_x = pltpu.make_async_copy(saved_refs[layer][0], scr.x, scr.load_sems.at[0])
        load_w = pltpu.make_async_copy(
            w_refs[layer], scr.weight, scr.load_sems.at[1]
        )
        load_x.start()
        load_w.start()
        while saves:
            saves.pop().wait()
        load_x.wait()
        load_w.wait()
        scr.qkv[...] = dot(
            scr.x[...].reshape(1024, scr.x.shape[-1]), scr.weight[:, :, :576].reshape(-1, 576)
        ).astype(BF16)
        if layer == 0:
            share = scr.x.shape[-1] // 32
            shares = [
                scr.weight[chip, 24 * core : 24 * core + 4, 576 : 576 + share]
                for chip in range(CHIPS)
                for core in range(2)
            ]
            gains_ref[0:4] = jnp.concatenate(shares, axis=1).astype(F32)
        saves.append(save(layer, 0, scr.qkv))
        qkv = scr.qkv[...]
        spread_heads(qkv, feature_ref, scr.key, scr.query)
        for h in range(GROUP_HEADS):
            scr.value[h] = qkv[:, 128 * h + 64 : 128 * h + 128].T
        exchange = Exchange(
            scr.o.at[layer], scr.o_got.at[layer], sems("o", layer), scr.own_sems.at[layer, 4]
        )
        for n in range(1024 // QUERIES):
            at = slice(QUERIES * n, QUERIES * n + QUERIES)
            for h in range(GROUP_HEADS):
                expo, rate = expo_columns(dot_nt(scr.key[h], scr.query[h, at, :]))
                scr.turned[64 * h : 64 * h + 64, at] = dot(
                    scr.value[h], (expo * rate).astype(BF16)
                )
                ticks.pop(0)()
            rows_o = scr.turned[:, at].T.astype(BF16)
            for m in range(QUERIES // 64):
                scr.o[layer, n * (QUERIES // 64) + m] = halves_beside(rows_o[64 * m : 64 * m + 64])
        exchange.begin()
        return exchange

    def feed(layer, exchange, ticks):
        exchange.arrived()
        slabs[layer][0].arrived()
        load_up(wu_refs[layer], scr.wu, scr.wo, scr.weight_sems)
        for k in range(PLANES):
            scr.mixed[64 * k : 64 * k + 64, :] = jnp.concatenate(
                [halves_below(scr.o_got[layer, 4 * k + g]) for g in range(GROUPS)], axis=1
            )
        saves.append(save(layer, 1, scr.mixed))
        mixed = scr.mixed[...]
        gain = gains_ref[2 * layer : 2 * layer + 2]
        ticks.pop(0)()
        wait_weight(scr.wo, scr.weight_sems.at[0])
        attended = jnp.concatenate(
            [dot(mixed, scr.wo[side].reshape(768, 384)) for side in range(2)], axis=1
        )
        before = scr.low[...].reshape(256, -1).astype(F32) if layer == 0 else scr.hidden[...]
        h1 = before + attended
        scr.h1[...] = h1
        saves.append(save(layer, 2, scr.h1))
        x1 = norm_parts(h1)[0] * gain[0:1, :]
        x1_low = x1.astype(BF16)
        wait_weight(scr.wu, scr.weight_sems.at[1])
        for side in range(2):
            for part in range(3):
                at = 1536 * side + 512 * part
                up = dot(x1_low, scr.wu[side, :, :, 512 * part : 512 * part + 512].reshape(768, 512))
                scr.up[:, at : at + 512] = up
                scr.act[:, at : at + 512] = gelu_parts(up)[0].astype(BF16)
            ticks.pop(0)()
        saves.append(save(layer, 3, scr.up))
        slabs[layer][1].arrived()
        load_down(wd_refs[layer], scr.wd, scr.weight_sems)
        wait_weight(scr.wd, scr.weight_sems.at[2])
        h2 = x1 + dot(scr.act[...], scr.wd[...].reshape(3072, 768))
        scr.h2[...] = h2
        saves.append(save(layer, 4, scr.h2))
        out = jnp.where(inside_rows(info), norm_parts(h2)[0] * gain[1:2, :], 0.0)
        low = out.astype(BF16)
        if layer == 0:
            scr.hidden[...] = out
            scr.low[...] = low.reshape(scr.low.shape)
        else:
            result_ref[...] = low.reshape(result_ref.shape)

    def nothing():
        pass

    def step(layer, *steps):
        return lambda: move(layer, *steps)

    rows_0 = spread(0, tokens_ref)
    rows_0.begin()
    qkvs[0].begin()
    every(slabs[0], "begin")
    key_features(info, random_ref, feature_ref)
    for rz in range(1, 4):
        rows_0.forward(rz)
        qkvs[0].forward(rz)
        if rz == 1:
            move(0, "f0")
    rows_0.from_beside()
    pltpu.make_async_copy(tokens_ref, scr.low, scr.load_sems.at[2]).wait()
    exchange_0 = attend(
        0,
        rows_0,
        [
            step(0, "l1"),
            nothing,
            step(0, "f1"),
            step(0, "l2"),
            lambda: every(slabs[1], "begin"),
            step(0, "s0"),
        ],
    )
    move(0, "l3", "f2", "s1", "f3")
    move(1, "l1")
    move(0, "s2")
    move(1, "l2")
    qkvs[1].begin()
    move(0, "s3")
    feed(0, exchange_0, [step(1, "l3"), step(1, "f0"), nothing])
    rows_1 = spread(1, scr.low)
    rows_1.begin()
    for rz in range(1, 4):
        rows_1.forward(rz)
    for rz in range(1, 4):
        qkvs[1].forward(rz)
    rows_1.from_beside()
    move(1, "f1", "f2")
    exchange_1 = attend(
        1,
        rows_1,
        [nothing, step(1, "f3"), nothing, step(1, "s0"), nothing, step(1, "s1")],
    )
    move(1, "s2", "s3")
    feed(1, exchange_1, [nothing] * 3)
    for copy in saves:
        copy.wait()
    every([rows_0, rows_1, exchange_0, exchange_1] + qkvs + slabs[0] + slabs[1], "finish")


def forward(info, random_lists, tokens, wq, up, down, number):
    width = tokens.shape[-1]
    scratch = forward_scratch(width)

    def out(*shape, dtype=BF16):
        return jax.ShapeDtypeStruct(shape, dtype)

    saved = [
        out(16, 64, width),
        out(1024, 576),
        out(256, width),
        out(256, width, dtype=F32),
        out(256, 4 * width, dtype=F32),
        out(256, width, dtype=F32),
    ]
    shapes = saved + saved + [out(CHIPS, 48, 640)] * 2
    shapes += [out(2, CHIPS, 48, 1920)] * 2 + [out(2, CHIPS, 48, 1536)] * 2
    shapes += [out(4, width, dtype=F32), out(PLANES, 64, width), out(1024, 64)]
    return pl.pallas_call(
        functools.partial(forward_kernel, tuple(scratch)),
        out_shape=tuple(shapes),
        in_specs=[smem(), vmem()] + [hbm()] * 4,
        out_specs=tuple([hbm()] * (len(shapes) - 3) + [vmem()] * 3),
        scratch_shapes=list(scratch.values()),
        compiler_params=pltpu.CompilerParams(
            collective_id=number, has_side_effects=True, vmem_limit_bytes=58 * 2**20
        ),
        name="forward",
    )(info, random_lists, tokens, wq, up, down)


def pick(stack, index):
    return lax.dynamic_index_in_dim(stack, index, 0, keepdims=False)


def pack_qkv(shards, gains, me, core):
    rows = shards.shape[1]
    parts = shards.reshape(LAYERS, rows, 3, GROUPS, GROUP_HEADS, HEAD)
    pairs = jnp.transpose(parts[:, :, 1:], (3, 0, 1, 4, 2, 5)).reshape(GROUPS, LAYERS, rows, 384)
    query = jnp.transpose(parts[:, :, 0], (2, 0, 1, 3, 4)).reshape(GROUPS, LAYERS, rows, 192)
    share = gains.shape[-1]
    beside = jnp.pad(gains.reshape(2 * LAYERS, share), ((0, rows - 2 * LAYERS), (0, 64 - share)))
    beside = jnp.broadcast_to(beside, (GROUPS, LAYERS, rows, 64))
    packed = jnp.concatenate([pairs, query, beside], axis=3)
    group = me & 3
    got = [pick(packed, group)] + [swap(pick(packed, group ^ r), r) for r in range(1, 4)]

    def in_order(own, other):
        return jnp.where(
            core == 0,
            jnp.concatenate([own, other], axis=1),
            jnp.concatenate([other, own], axis=1),
        )

    here, there = in_order(got[0], got[1]), in_order(got[2], got[3])
    both = jnp.where(
        (me >> 1) & 1 == 0,
        jnp.stack([here, there], axis=1),
        jnp.stack([there, here], axis=1),
    )
    return both


def pack_rest(out_weight, up_weight, down_weight, core):
    def mine(shard, side):
        half = shard.shape[2] // 2
        return lax.dynamic_slice_in_dim(shard, side * half, half, axis=2)

    def both(side):
        return jnp.concatenate([mine(up_weight, side), mine(out_weight, side)], axis=2)

    own, got = both(core), swap(both(1 - core), 1)
    rows = jnp.where(
        core == 0,
        jnp.concatenate([own, got], axis=1),
        jnp.concatenate([got, own], axis=1),
    )
    return rows, jnp.concatenate([down_weight[:, :48], down_weight[:, 48:]], axis=2)


def add_low(first, second):
    return (first.astype(F32) + second.astype(F32)).astype(BF16)


def add_full(first, second):
    return first.astype(F32) + second.astype(F32)


def split_rest(total):
    down = total[240:].reshape(4, 48, 384)
    return (
        total[192:240].T,
        total[:192].T,
        jnp.transpose(down, (0, 2, 1)).reshape(1536, 48),
    )


def local_two_by_sixteen(
    tokens,
    qkv_weight,
    out_weight,
    up_weight,
    down_weight,
    norm_gains,
    doc_lengths,
    global_ids,
    random_ids,
    cotangent,
):
    docs_dev, block, width = tokens.shape
    me = lax.axis_index("seq").astype(jnp.int32)
    docs = lax.axis_index("docs").astype(jnp.int32)
    plane, core = me >> 2, me & 1
    chip = docs * 8 + (me >> 1)
    info = jnp.concatenate(
        [
            jnp.stack([me, chip, pick(doc_lengths, plane), plane, docs, core]),
            pick(global_ids, plane),
            doc_lengths,
        ]
    )
    own_random = lax.dynamic_index_in_dim(random_ids, plane, 1, keepdims=False)
    random_lists = jnp.pad(jnp.tile(own_random.T, (1, 4)), ((0, 8 - RAND), (0, 0)))

    wq = pack_qkv(qkv_weight, norm_gains, me, core)
    up, down = pack_rest(out_weight, up_weight, down_weight, core)
    share = width // 32
    made = forward(info, random_lists, tokens, wq, up, down, 0)
    features = made[20]
    held, weights = (made[:6], made[6:12]), made[12:14]
    rest = list(zip(made[14:16], made[16:18]))
    gain = made[18]
    base, grad_o, gain_grads, *sums = feed_back(
        1, info, cotangent, gain, gain, gain, held[1][2:], rest[1], 1
    )
    extra, rest_grads_1, qkv_1, gain_grads = attend_back(
        features, held[1][1], grad_o, held[1][0], weights[1], sums, gain_grads, False, 2
    )
    base, grad_o, gain_grads, *sums = feed_back(
        0, info, base, extra, gain, gain_grads, held[0][2:], rest[0], 3
    )
    extra, rest_grads, qkv_0, gain_grads = attend_back(
        features, held[0][1], grad_o, held[0][0], weights[0], sums, gain_grads, True, 4
    )
    grad_tokens = base.reshape(docs_dev, block, width) + extra.astype(F32)
    gain_grads = lax.dynamic_slice_in_dim(gain_grads, (docs * 16 + me) * share, share, axis=1)
    rest = [split_rest(part) for part in (rest_grads, rest_grads_1)]
    qkv_grads = jnp.stack([qkv_0, qkv_1])
    return (
        made[19],
        grad_tokens,
        jnp.transpose(qkv_grads, (0, 3, 1, 2)).reshape(LAYERS, 384, 144),
        *(jnp.stack(pair) for pair in zip(*rest)),
        gain_grads[:4].reshape(LAYERS, 2, share),
    )


def solution(mesh):
    def local(*args):
        docs_dev, _, width = args[0].shape
        if fits(mesh, docs_dev, width // HEAD):
            return local_two_by_sixteen(*args)
        return local_any_mesh(*args)

    return jax.shard_map(
        local,
        mesh=mesh,
        in_specs=(
            P("docs", "seq", None),
            P(None, ("docs", "seq"), None),
            P(None, ("docs", "seq"), None),
            P(None, ("docs", "seq"), None),
            P(None, ("docs", "seq"), None),
            P(None, None, ("docs", "seq")),
            P("docs"),
            P("docs", None),
            P(None, "docs", None),
            P("docs", "seq", None),
        ),
        out_specs=(
            P("docs", "seq", None),
            P("docs", "seq", None),
            P(None, "docs", "seq"),
            P(None, "docs", "seq"),
            P(None, "docs", "seq"),
            P(None, "docs", "seq"),
            P(None, None, ("docs", "seq")),
        ),
        check_vma=False,
    )
```

```python
import functools
import types

import jax
import jax.numpy as jnp
from jax import lax
from jax.experimental import pallas as pl
from jax.experimental.pallas import tpu as pltpu
from jax.sharding import PartitionSpec as P

HEAD = 64
RAND = 3
GLOB = 2
LAYERS = 2


NEGATIVE = -1e30
EPSILON = 1e-05


def with_halo(cells, sides, width):
    for axis, dim in sides:
        count = lax.axis_size(axis)
        head = lax.slice_in_dim(cells, 0, width, axis=dim)
        tail = lax.slice_in_dim(cells, cells.shape[dim] - width, cells.shape[dim], axis=dim)
        cells = jnp.concatenate(
            [
                lax.ppermute(tail, axis, [(i, (i + 1) % count) for i in range(count)]),
                cells,
                lax.ppermute(head, axis, [((i + 1) % count, i) for i in range(count)]),
            ],
            axis=dim,
        )
    return cells


def combined_all(value, axis, join):
    pieces = jax.tree.map(lambda part: lax.all_gather(part, axis), value)
    head = jax.tree.map(lambda part: part[0], pieces)
    tail = jax.tree.map(lambda part: part[1:], pieces)
    so_far, _ = lax.scan(lambda so_far, piece: (join(so_far, piece), None), head, tail)
    return so_far


def norm_rows(values, gain):
    centre = values - jnp.mean(values, axis=-1, keepdims=True)
    spread = jnp.mean(centre * centre, axis=-1, keepdims=True)
    return centre * lax.rsqrt(spread + EPSILON) * gain


def gelu_tanh(values):
    return jax.nn.gelu(values, approximate=True)


def earlier_equal(values):
    length = values.shape[-1]
    order = jnp.arange(length, dtype=jnp.int32)
    before = order[None, :] < order[:, None]
    same = values[..., :, None] == values[..., None, :]
    return jnp.sum(jnp.logical_and(same, before), axis=-1)


def merge_stats(first, second):
    highest = jnp.maximum(first[0], second[0])
    return (
        highest,
        first[1] * jnp.exp(first[0] - highest) + second[1] * jnp.exp(second[0] - highest),
    )


def sparse_probs(query, key_part, key_inside, scale):
    scores = (
        jnp.einsum("kbhd,kjhd->khbj", query, key_part, preferred_element_type=jnp.float32) * scale
    )
    scores = jnp.where(key_inside[:, None, None, :], scores, NEGATIVE)
    expo = jnp.exp(scores - jnp.max(scores, axis=-1, keepdims=True))
    return expo / jnp.sum(expo, axis=-1, keepdims=True)


def global_scores(global_query, local_keys, inside, scale):
    scores = (
        jnp.einsum(
            "ksbhd,kjhd->kshbj", global_query, local_keys, preferred_element_type=jnp.float32
        )
        * scale
    )
    return jnp.where(inside[:, None, None, None, :], scores, NEGATIVE)


def local_any_mesh(
    tokens,
    qkv_weight,
    out_weight,
    up_weight,
    down_weight,
    norm_gains,
    doc_lengths,
    global_ids,
    random_ids,
    cotangent,
):
    nseq = lax.axis_size("seq")
    device = lax.axis_index("seq")
    docs_dev, block, width = tokens.shape
    count = docs_dev * block
    heads = width // HEAD
    scale = HEAD ** (-0.5)
    capacity = max(2, (docs_dev * RAND + nseq - 1) // nseq)
    global_capacity = (docs_dev * GLOB + nseq - 1) // nseq
    entries = docs_dev * RAND
    global_entries = docs_dev * GLOB
    offsets = jnp.arange(block, dtype=jnp.int32)
    inside = (device * block + offsets)[None, :] < doc_lengths[:, None]
    live_rows = inside.reshape(count, 1)
    wanted = random_ids.reshape(nseq, entries)
    wanted_rank = earlier_equal(wanted)
    slot_ids = jnp.arange(capacity, dtype=jnp.int32)
    hits = jnp.logical_and((wanted == device)[:, :, None], wanted_rank[:, :, None] == slot_ids)
    hits = jnp.any(hits.reshape(nseq, docs_dev, RAND, capacity), axis=2)
    hits = jnp.transpose(hits, (0, 2, 1))
    doc_ids = jnp.arange(docs_dev, dtype=jnp.int32)
    send_doc = jnp.sum(jnp.where(hits, doc_ids, 0), axis=2)
    send_live = jnp.any(hits, axis=2)
    owner_pick = hits.astype(jnp.float32)
    listed_here = lax.dynamic_index_in_dim(wanted, device, 0, keepdims=False)
    listed_rank = lax.dynamic_index_in_dim(wanted_rank, device, 0, keepdims=False)
    fetch_slot = listed_here * capacity + listed_rank
    global_block = global_ids.reshape(global_entries)
    global_rank = earlier_equal(global_block)
    global_slot = global_block * global_capacity + global_rank
    own_entry = global_block == device
    owned = jnp.logical_and(
        own_entry[:, None], global_rank[:, None] == jnp.arange(global_capacity, dtype=jnp.int32)
    )
    entry_doc = jnp.arange(global_entries, dtype=jnp.int32) // GLOB
    global_send_doc = jnp.sum(jnp.where(owned, entry_doc[:, None], 0), axis=0)
    global_send_live = jnp.any(owned, axis=0)
    own_flag = jnp.any(own_entry.reshape(docs_dev, GLOB), axis=1)
    own_slot = jnp.sum(jnp.where(own_entry, global_rank, 0).reshape(docs_dev, GLOB), axis=1)
    neighbours = jnp.stack([(device - 1) % nseq, device, (device + 1) % nseq])
    key_blocks = jnp.concatenate(
        [
            jnp.broadcast_to(neighbours[None, :], (docs_dev, 3)),
            listed_here.reshape(docs_dev, RAND),
            global_ids,
        ],
        axis=1,
    )
    span = key_blocks.shape[1] * block
    key_inside = (key_blocks[:, :, None] * block + offsets < doc_lengths[:, None, None]).reshape(
        docs_dev, span
    )
    keep_local = inside[:, None, None, None, :]
    hidden = tokens.reshape(count, width).astype(jnp.float32)
    held = []
    for layer in range(LAYERS):
        weights = (
            lax.all_gather(qkv_weight[layer], ("docs", "seq"), axis=0, tiled=True),
            lax.all_gather(out_weight[layer], ("docs", "seq"), axis=0, tiled=True),
            lax.all_gather(up_weight[layer], ("docs", "seq"), axis=0, tiled=True),
            lax.all_gather(down_weight[layer], ("docs", "seq"), axis=0, tiled=True),
            lax.all_gather(norm_gains[layer], ("docs", "seq"), axis=1, tiled=True),
        )
        weight_qkv, weight_out, weight_up, weight_down, gain_pair = weights
        gain_pair = gain_pair.astype(jnp.float32)
        lowered = hidden.astype(jnp.bfloat16)
        projected = (
            jnp.dot(lowered, weight_qkv, preferred_element_type=jnp.float32)
            .astype(jnp.bfloat16)
            .reshape(docs_dev, block, 3 * width)
        )
        pairs = projected[:, :, width:]
        window = with_halo(pairs, (("seq", 1),), block)
        outgoing = jnp.where(
            send_live[:, :, None, None],
            jnp.take(pairs, send_doc, axis=0),
            jnp.zeros((), jnp.bfloat16),
        )
        incoming = lax.all_to_all(outgoing, "seq", split_axis=0, concat_axis=0, tiled=True)
        fetched = jnp.take(
            incoming.reshape(nseq * capacity, block, 2 * width), fetch_slot, axis=0
        ).reshape(docs_dev, RAND * block, 2 * width)
        global_send = jnp.where(
            global_send_live[:, None, None],
            jnp.take(projected, global_send_doc, axis=0),
            jnp.zeros((), jnp.bfloat16),
        )
        gathered = lax.all_gather(global_send, "seq", axis=0, tiled=True)
        global_picked = jnp.take(gathered, global_slot, axis=0).reshape(
            docs_dev, GLOB, block, 3 * width
        )
        global_query = global_picked[..., :width].reshape(docs_dev, GLOB, block, heads, HEAD)
        listed_pairs = jnp.concatenate(
            [
                window,
                fetched,
                global_picked[..., width:].reshape(docs_dev, GLOB * block, 2 * width),
            ],
            axis=1,
        )
        query = projected[:, :, :width].reshape(docs_dev, block, heads, HEAD)
        key_part = listed_pairs[:, :, :width].reshape(docs_dev, span, heads, HEAD)
        value_part = listed_pairs[:, :, width:].reshape(docs_dev, span, heads, HEAD)
        probs = sparse_probs(query, key_part, key_inside, scale)
        mixed = jnp.einsum(
            "khbj,kjhd->kbhd",
            probs.astype(jnp.bfloat16),
            value_part,
            preferred_element_type=jnp.float32,
        )
        local_keys = projected[:, :, width : 2 * width].reshape(docs_dev, block, heads, HEAD)
        local_values = projected[:, :, 2 * width :].reshape(docs_dev, block, heads, HEAD)
        wide_scores = global_scores(global_query, local_keys, inside, scale)
        global_top = jnp.max(wide_scores, axis=-1)
        global_total = jnp.sum(
            jnp.where(keep_local, jnp.exp(wide_scores - global_top[..., None]), 0.0), axis=-1
        )
        global_top, global_total = combined_all((global_top, global_total), "seq", merge_stats)
        wide_probs = (
            jnp.where(keep_local, jnp.exp(wide_scores - global_top[..., None]), 0.0)
            / global_total[..., None]
        )
        wide_part = jnp.einsum(
            "kshbj,kjhd->ksbhd",
            wide_probs.astype(jnp.bfloat16),
            local_values,
            preferred_element_type=jnp.float32,
        )
        wide_buffer = (
            jnp.zeros((nseq * global_capacity, block, width), jnp.float32)
            .at[global_slot]
            .set(wide_part.reshape(global_entries, block, width))
        )
        wide_sum = lax.psum_scatter(wide_buffer, "seq", scatter_dimension=0, tiled=True)
        attended = jnp.where(
            own_flag[:, None, None],
            jnp.take(wide_sum, own_slot, axis=0),
            mixed.reshape(docs_dev, block, width),
        )
        attended = attended.reshape(count, width).astype(jnp.bfloat16)
        after_attn = hidden + jnp.dot(attended, weight_out, preferred_element_type=jnp.float32)
        normed = norm_rows(after_attn, gain_pair[0])
        normed_low = normed.astype(jnp.bfloat16)
        up_values = jnp.dot(normed_low, weight_up, preferred_element_type=jnp.float32)
        activated = gelu_tanh(up_values).astype(jnp.bfloat16)
        after_ffn = normed + jnp.dot(activated, weight_down, preferred_element_type=jnp.float32)
        held.append(
            (
                weights,
                lowered,
                projected,
                listed_pairs,
                global_query,
                global_top,
                global_total,
                attended,
                after_attn,
                normed_low,
                up_values,
                activated,
                after_ffn,
            )
        )
        hidden = jnp.where(live_rows, norm_rows(after_ffn, gain_pair[1]), 0.0)
    gradient = cotangent.reshape(count, width).astype(jnp.float32)
    layer_grads = []
    for layer in reversed(range(LAYERS)):
        (
            weights,
            lowered,
            projected,
            listed_pairs,
            global_query,
            global_top,
            global_total,
            attended,
            after_attn,
            normed_low,
            up_values,
            activated,
            after_ffn,
        ) = held[layer]
        weights = (
            lax.all_gather(qkv_weight[layer], ("docs", "seq"), axis=0, tiled=True),
            lax.all_gather(out_weight[layer], ("docs", "seq"), axis=0, tiled=True),
            lax.all_gather(up_weight[layer], ("docs", "seq"), axis=0, tiled=True),
            lax.all_gather(down_weight[layer], ("docs", "seq"), axis=0, tiled=True),
            lax.all_gather(norm_gains[layer], ("docs", "seq"), axis=1, tiled=True),
        )
        weight_qkv, weight_out, weight_up, weight_down, gain_pair = weights
        gain_pair = gain_pair.astype(jnp.float32)
        gradient = jnp.where(live_rows, gradient, 0.0)
        grad_ffn, grad_gain_out = jax.vjp(norm_rows, after_ffn, gain_pair[1])[1](gradient)
        grad_down_low = grad_ffn.astype(jnp.bfloat16)
        grad_down_layer = jnp.einsum(
            "rf,rd->fd", activated, grad_down_low, preferred_element_type=jnp.float32
        )
        grad_activated = jnp.einsum(
            "rd,fd->rf", grad_down_low, weight_down, preferred_element_type=jnp.float32
        )
        grad_up_low = jax.vjp(gelu_tanh, up_values)[1](grad_activated)[0].astype(jnp.bfloat16)
        grad_up_layer = jnp.einsum(
            "rd,rf->df", normed_low, grad_up_low, preferred_element_type=jnp.float32
        )
        grad_normed = grad_ffn + jnp.einsum(
            "rf,df->rd", grad_up_low, weight_up, preferred_element_type=jnp.float32
        )
        grad_attn, grad_gain_mid = jax.vjp(norm_rows, after_attn, gain_pair[0])[1](grad_normed)
        grad_attn_low = grad_attn.astype(jnp.bfloat16)
        grad_out_layer = jnp.einsum(
            "rd,re->de", attended, grad_attn_low, preferred_element_type=jnp.float32
        )
        grad_mixed = (
            jnp.einsum("re,de->rd", grad_attn_low, weight_out, preferred_element_type=jnp.float32)
            .astype(jnp.bfloat16)
            .reshape(docs_dev, block, width)
        )
        query = projected[:, :, :width].reshape(docs_dev, block, heads, HEAD)
        key_part = listed_pairs[:, :, :width].reshape(docs_dev, span, heads, HEAD)
        value_part = listed_pairs[:, :, width:].reshape(docs_dev, span, heads, HEAD)
        probs = sparse_probs(query, key_part, key_inside, scale)
        grad_sparse = jnp.where(
            own_flag[:, None, None], jnp.zeros((), jnp.bfloat16), grad_mixed
        ).reshape(docs_dev, block, heads, HEAD)
        grad_probs = jnp.einsum(
            "kbhd,kjhd->khbj", grad_sparse, value_part, preferred_element_type=jnp.float32
        )
        delta = jnp.sum(probs * grad_probs, axis=-1, keepdims=True)
        grad_scores = (probs * (grad_probs - delta)).astype(jnp.bfloat16)
        grad_query = (
            jnp.einsum("khbj,kjhd->kbhd", grad_scores, key_part, preferred_element_type=jnp.float32)
            * scale
        )
        grad_key_part = (
            jnp.einsum("khbj,kbhd->kjhd", grad_scores, query, preferred_element_type=jnp.float32)
            * scale
        )
        grad_value_part = jnp.einsum(
            "khbj,kbhd->kjhd",
            probs.astype(jnp.bfloat16),
            grad_sparse,
            preferred_element_type=jnp.float32,
        )
        grad_listed = jnp.concatenate(
            [
                grad_key_part.reshape(docs_dev, span, width),
                grad_value_part.reshape(docs_dev, span, width),
            ],
            axis=2,
        )
        wide_out = jnp.where(
            global_send_live[:, None, None],
            jnp.take(grad_mixed, global_send_doc, axis=0),
            jnp.zeros((), jnp.bfloat16),
        )
        wide_all = lax.all_gather(wide_out, "seq", axis=0, tiled=True)
        wide_grad = jnp.take(wide_all, global_slot, axis=0).reshape(
            docs_dev, GLOB, block, heads, HEAD
        )
        local_keys = projected[:, :, width : 2 * width].reshape(docs_dev, block, heads, HEAD)
        local_values = projected[:, :, 2 * width :].reshape(docs_dev, block, heads, HEAD)
        wide_scores = global_scores(global_query, local_keys, inside, scale)
        wide_probs = (
            jnp.where(keep_local, jnp.exp(wide_scores - global_top[..., None]), 0.0)
            / global_total[..., None]
        )
        wide_grad_probs = jnp.einsum(
            "ksbhd,kjhd->kshbj", wide_grad, local_values, preferred_element_type=jnp.float32
        )
        wide_delta = lax.psum(jnp.sum(wide_probs * wide_grad_probs, axis=-1), "seq")
        wide_grad_scores = (wide_probs * (wide_grad_probs - wide_delta[..., None])).astype(
            jnp.bfloat16
        )
        wide_grad_query = (
            jnp.einsum(
                "kshbj,kjhd->ksbhd",
                wide_grad_scores,
                local_keys,
                preferred_element_type=jnp.float32,
            )
            * scale
        )
        wide_grad_keys = (
            jnp.einsum(
                "kshbj,ksbhd->kjhd",
                wide_grad_scores,
                global_query,
                preferred_element_type=jnp.float32,
            )
            * scale
        )
        wide_grad_values = jnp.einsum(
            "kshbj,ksbhd->kjhd",
            wide_probs.astype(jnp.bfloat16),
            wide_grad,
            preferred_element_type=jnp.float32,
        )
        global_grads = jnp.concatenate(
            [
                wide_grad_query.reshape(global_entries, block, width),
                grad_listed[:, (3 + RAND) * block :, :].reshape(global_entries, block, 2 * width),
            ],
            axis=2,
        )
        global_buffer = (
            jnp.zeros((nseq * global_capacity, block, 3 * width), jnp.float32)
            .at[global_slot]
            .set(global_grads)
        )
        global_share = lax.psum_scatter(global_buffer, "seq", scatter_dimension=0, tiled=True)
        global_mine = jnp.where(
            own_flag[:, None, None], jnp.take(global_share, own_slot, axis=0), 0.0
        )
        grad_fetched = grad_listed[:, 3 * block : (3 + RAND) * block, :].reshape(
            entries, block, 2 * width
        )
        back_out = (
            jnp.zeros((nseq * capacity, block, 2 * width), jnp.float32)
            .at[fetch_slot]
            .set(grad_fetched)
            .reshape(nseq, capacity, block, 2 * width)
        )
        back_in = lax.all_to_all(back_out, "seq", split_axis=0, concat_axis=0, tiled=True)
        grad_random = jnp.einsum(
            "dck,dcbf->kbf", owner_pick, back_in, precision=lax.Precision.HIGHEST
        )
        grad_window = grad_listed[:, : 3 * block, :]
        edges = jnp.concatenate([grad_window[:, :block], grad_window[:, 2 * block :]], axis=1)
        beside_all = with_halo(edges, (("seq", 1),), block)
        grad_pairs = (
            grad_window[:, block : 2 * block]
            + beside_all[:, :block]
            + beside_all[:, 3 * block :]
            + grad_random
            + global_mine[:, :, width:]
        )
        grad_pairs = grad_pairs + jnp.concatenate(
            [
                wide_grad_keys.reshape(docs_dev, block, width),
                wide_grad_values.reshape(docs_dev, block, width),
            ],
            axis=2,
        )
        grad_queries = grad_query.reshape(docs_dev, block, width) + global_mine[:, :, :width]
        grad_projected = (
            jnp.concatenate([grad_queries, grad_pairs], axis=2)
            .reshape(count, 3 * width)
            .astype(jnp.bfloat16)
        )
        grad_qkv_layer = jnp.einsum(
            "rd,re->de", lowered, grad_projected, preferred_element_type=jnp.float32
        )
        gradient = grad_attn + jnp.einsum(
            "re,de->rd", grad_projected, weight_qkv, preferred_element_type=jnp.float32
        )
        group_shares = (
            lax.psum_scatter(grad_qkv_layer, "docs", scatter_dimension=0, tiled=True),
            lax.psum_scatter(grad_out_layer, "docs", scatter_dimension=0, tiled=True),
            lax.psum_scatter(grad_up_layer, "docs", scatter_dimension=0, tiled=True),
            lax.psum_scatter(grad_down_layer, "docs", scatter_dimension=0, tiled=True),
            lax.psum_scatter(
                jnp.stack([grad_gain_mid, grad_gain_out]), "docs", scatter_dimension=1, tiled=True
            ),
        )
        shares = (
            lax.psum_scatter(group_shares[0], "seq", scatter_dimension=1, tiled=True),
            lax.psum_scatter(group_shares[1], "seq", scatter_dimension=1, tiled=True),
            lax.psum_scatter(group_shares[2], "seq", scatter_dimension=1, tiled=True),
            lax.psum_scatter(group_shares[3], "seq", scatter_dimension=1, tiled=True),
            lax.psum_scatter(group_shares[4], "seq", scatter_dimension=1, tiled=True),
        )
        layer_grads.insert(0, shares)
    stacked = [
        jnp.stack([layer_grads[number][member] for number in range(LAYERS)]) for member in range(5)
    ]
    return (
        hidden.astype(jnp.bfloat16).reshape(docs_dev, block, width),
        gradient.reshape(docs_dev, block, width),
        stacked[0],
        stacked[1],
        stacked[2],
        stacked[3],
        stacked[4],
    )


PLANES = 4
GROUPS = 4
CHIPS = 16
GROUP_HEADS = 3
CUT = 240
MESH = pl.DeviceIdType.MESH
F32 = jnp.float32
BF16 = jnp.bfloat16


def fits(mesh, docs_dev, heads):
    return (
        mesh.shape["docs"] == 2
        and mesh.shape["seq"] == 16
        and docs_dev == PLANES
        and heads == GROUPS * GROUP_HEADS
    )


def swap(value, bits):
    return lax.ppermute(value, "seq", [(i, i ^ bits) for i in range(16)])


def swap_docs(value):
    return lax.ppermute(value, "docs", [(0, 1), (1, 0)])


def dot(left, right):
    return lax.dot_general(left, right, (((1,), (0,)), ((), ())), preferred_element_type=F32)


def dot_nt(left, right):
    return lax.dot_general(left, right, (((1,), (1,)), ((), ())), preferred_element_type=F32)


def dot_tn(left, right):
    return lax.dot_general(left, right, (((0,), (0,)), ((), ())), preferred_element_type=F32)


def vmem():
    return pl.BlockSpec(memory_space=pltpu.VMEM)


def smem():
    return pl.BlockSpec(memory_space=pltpu.SMEM)


def hbm():
    return pl.BlockSpec(memory_space=pltpu.HBM)


def params():
    return pltpu.CompilerParams(vmem_limit_bytes=56 * 2**20)


QUERIES = 512
BACK_QUERIES = 512


def key_features(lengths, globals_ref, random_ref, feature_ref):
    plane = lax.axis_index("seq") // 4
    lane = lax.broadcasted_iota(jnp.int32, (16, 64), 1)
    block = lax.broadcasted_iota(jnp.int32, (16, 64), 0)
    query = lane % 16
    globals_here = [globals_ref[plane, n] for n in range(GLOB)]
    count = jnp.zeros((16, 64), F32)
    for ids in [(query + 15) % 16, query, (query + 1) % 16]:
        count += jnp.where(block == ids, 1.0, 0.0)
    for n in range(RAND):
        ids = jnp.zeros((16, 64), jnp.int32)
        for i in range(16):
            ids = jnp.where(query == i, random_ref[i, plane, n], ids)
        count += jnp.where(block == ids, 1.0, 0.0)
    for number in globals_here:
        count += jnp.where(block == number, 1.0, 0.0)
    for number in globals_here:
        count = jnp.where(query == number, 1.0, count)
    extra = jnp.where(count > 0, jnp.log(jnp.maximum(count, 1.0)), NEGATIVE)
    row = lax.broadcasted_iota(jnp.int32, (64, 64), 0)
    lane = lax.broadcasted_iota(jnp.int32, (64, 64), 1)
    for n in range(16):
        own = jnp.where(64 * n + row < lengths[plane], extra[n : n + 1, :], NEGATIVE)
        high = own.astype(BF16).astype(F32)
        low = jnp.where(own > 0, own - high, 0.0)
        value = jnp.where(lane < 16, high, jnp.where(lane < 32, low, 0.0))
        feature_ref[64 * n : 64 * n + 64, :] = value.astype(BF16)


def halves_beside(rows):
    return jnp.concatenate([rows[:32], rows[32:]], axis=1)


def halves_below(rows):
    return jnp.concatenate([rows[:, :192], rows[:, 192:]], axis=0)


def spread_heads(qkv, feature_ref, key_scr, query_scr):
    row = lax.broadcasted_iota(jnp.int32, (1024, 64), 0) // 64
    lane = lax.broadcasted_iota(jnp.int32, (1024, 64), 1)
    place = jnp.where(jnp.logical_and(lane < 32, lane % 16 == row), 1.0, 0.0).astype(BF16)
    for h in range(GROUP_HEADS):
        key_scr[h] = jnp.concatenate([qkv[:, 128 * h : 128 * h + 64], feature_ref[...]], axis=1)
        query = qkv[:, 384 + 64 * h : 448 + 64 * h] * jnp.asarray(HEAD**-0.5, BF16)
        query_scr[h] = jnp.concatenate([query, place], axis=1)


def expo_columns(scores):
    expo = jnp.exp(scores - jnp.max(scores, axis=0, keepdims=True))
    return expo, 1.0 / jnp.sum(expo, axis=0, keepdims=True)


def load_up(up_ref, wu, wo, sems):
    pltpu.make_async_copy(up_ref.at[:, :, :, pl.ds(1536, 384)], wo, sems.at[0]).start()
    pltpu.make_async_copy(up_ref.at[:, :, :, pl.ds(0, 1536)], wu, sems.at[1]).start()


def load_down(down_ref, wd, sems):
    for plane in range(2):
        for part in range(2):
            source = down_ref.at[plane, :, :, pl.ds(768 * part, 768)]
            pltpu.make_async_copy(source, wd.at[:, plane, part], sems.at[2]).start()


def wait_weight(scr, sem):
    pltpu.make_async_copy(scr, scr, sem).wait()


def inside_rows(lengths):
    row = lax.broadcasted_iota(jnp.int32, (256, 1), 0)
    length = jnp.zeros_like(row)
    for k in range(PLANES):
        length = jnp.where(row // 64 == k, lengths[k], length)
    return lax.axis_index("seq") * 64 + row % 64 < length


def norm_parts(values):
    centre = values - jnp.mean(values, axis=-1, keepdims=True)
    spread = jnp.mean(centre * centre, axis=-1, keepdims=True)
    rate = lax.rsqrt(spread + EPSILON)
    return centre * rate, rate


def norm_back(unit, rate, gain, grad):
    scaled = grad * gain
    inner = jnp.mean(scaled * unit, axis=-1, keepdims=True)
    outer = jnp.mean(scaled, axis=-1, keepdims=True)
    return rate * (scaled - outer - unit * inner), jnp.sum(grad * unit, axis=0, keepdims=True)


CURVE = 0.7978845608028654


def gelu_parts(values):
    square = values * values
    bend = jnp.tanh(CURVE * (values + 0.044715 * (square * values)))
    return 0.5 * values * (1.0 + bend), bend, square


def gelu_slope(values, bend, square):
    return 0.5 * (1.0 + bend) + 0.5 * values * (1.0 - bend * bend) * (
        CURVE * (1.0 + 3 * 0.044715 * square)
    )


WEIGHT_SCRATCH = [
    pltpu.VMEM((2, 16, 48, 1536), BF16),
    pltpu.VMEM((16, 2, 2, 48, 768), BF16),
    pltpu.VMEM((2, 16, 48, 384), BF16),
]


def feed_back_kernel(
    pieces,
    layer,
    lengths,
    base_ref,
    extra_ref,
    gain_ref,
    gain_sum_ref,
    mixed_ref,
    h1_ref,
    up_ref,
    h2_ref,
    *refs,
):
    w_refs, refs = refs[:pieces], refs[pieces:]
    dh1_ref, do_ref, dgain_ref, *sum_refs, wu, wd, wo, gu, gd, go, got, sems, pair_sems, out_sems = refs
    load_down(w_refs[1], wd, sems)
    load_up(w_refs[0], wu, wo, sems)
    docs, me = lax.axis_index("docs"), lax.axis_index("seq")
    mate = (docs, flip(me, 1))
    greet([mate])
    units = [(ry, place) for ry in range(2) for place in range(8)]

    def other_docs(ry):
        return docs if ry == 0 else 1 - docs

    def owner(place, rc):
        return flip(me, (place % 2) * 8 + (place // 2 % 2) * 4 + (place // 4) * 2 + rc)

    def to_mate(source, ry, place, first, count, n):
        pltpu.make_async_remote_copy(
            source,
            got.at[ry, place, pl.ds(first, count)],
            pair_sems.at[0, n],
            pair_sems.at[1, n],
            device_id=mate,
            device_id_type=MESH,
        ).start()

    def up_to_mate(part):
        x, z = (me // 2) % 2, me // 4
        across = x if part % 2 == 0 else 1 - x
        low = z % 2 if part // 2 % 2 == 0 else 1 - z % 2
        high = z // 2 if part // 4 == 0 else 1 - z // 2
        for half in range(2):
            source = gu.at[half, 2 * part + 1 - me % 2]
            to_mate(source, other_docs(half), 4 * across + 2 * low + high, 0, 192, 0)

    if layer == 0:
        parts = [
            base_ref[64 * k : 64 * k + 64, :] + extra_ref[k].astype(F32)
            for k in range(PLANES)
        ]
        grad = jnp.concatenate(parts, axis=0)
    else:
        grad = base_ref[...].reshape(256, 768).astype(F32)
    grad = jnp.where(inside_rows(lengths), grad, 0.0)
    unit2, rate2 = norm_parts(h2_ref[...])
    dh2, dgain1 = norm_back(unit2, rate2, gain_ref[2 * layer + 1 : 2 * layer + 2, :], grad)
    dgain_ref[...] = gain_sum_ref[...] if layer == 0 else jnp.zeros_like(dgain_ref)
    dgain_ref[2 * layer + 1 : 2 * layer + 2, :] = dgain1
    df = dh2.astype(BF16)
    df_turned = df.T
    unit1, rate1 = norm_parts(h1_ref[...])
    x1_low = (unit1 * gain_ref[2 * layer : 2 * layer + 1, :]).astype(BF16)
    wait_weight(wd, sems.at[2])
    wait_weight(wu, sems.at[1])
    dx1 = dh2
    for part in range(8):
        at = 384 * part
        d_act = dot_nt(df, wd[2 * part : 2 * part + 2].reshape(384, 768))
        up = up_ref[:, at : at + 384]
        act, bend, square = gelu_parts(up)
        act = act.astype(BF16)
        dup = (gelu_slope(up, bend, square) * d_act).astype(BF16)
        side, start = part // 4, 384 * (part % 4)
        dx1 += dot_nt(dup, wu[side, :, :, start : start + 384].reshape(768, 384))
        gt_up = dot_tn(dup, x1_low).astype(BF16)
        for n in range(2):
            for half in range(2):
                gu[half, 2 * part + n] = gt_up[
                    192 * n : 192 * n + 192, 384 * half : 384 * half + 384
                ]
        gt_down = dot(df_turned, act).astype(BF16)
        row = 48 * (part % 4)
        for s in range(16):
            gd[part // 4, s, row : row + 48, :] = gt_down[48 * s : 48 * s + 48]
        up_to_mate(part)
        if part % 4 == 3:
            for place in range(8):
                source = gd.at[part // 4, owner(place, 1)]
                to_mate(source, other_docs(part // 4), place, 240, 192, 1)
    dh1, dgain0 = norm_back(unit1, rate1, gain_ref[2 * layer : 2 * layer + 1, :], dx1)
    dgain_ref[2 * layer : 2 * layer + 1, :] = dgain0
    dh1_ref[...] = dh1
    da = dh1.astype(BF16)
    gt_out = dot_tn(da, mixed_ref[...]).astype(BF16)
    for s in range(16):
        for half in range(2):
            go[half, s] = gt_out[48 * s : 48 * s + 48, 384 * half : 384 * half + 384]
    for ry, place in units:
        to_mate(go.at[other_docs(ry), owner(place, 1)], ry, place, 192, 48, 2)
    wait_weight(wo, sems.at[0])
    do = dot_nt(da[:, 0:384], wo[0].reshape(768, 384))
    do += dot_nt(da[:, 384:768], wo[1].reshape(768, 384))
    do = do.astype(BF16)
    for k in range(PLANES):
        for g in range(GROUPS):
            do_ref[4 * k + g] = halves_beside(do[64 * k : 64 * k + 64, 192 * g : 192 * g + 192])
    copies = []
    for n, (scr, first, count) in enumerate(((gu, 0, 192), (gd, 240, 192), (go, 192, 48))):
        part = got.at[:, :, pl.ds(first, count)]
        pltpu.make_async_copy(part, part, pair_sems.at[1, n]).wait()
        for ry, place in units:
            span = slice(first, first + count)
            own = scr[other_docs(ry), owner(place, 0)].astype(F32)
            got[ry, place, span] = (own + got[ry, place, span].astype(F32)).astype(BF16)
            if n == 1:
                source, ref = got.at[ry, place, pl.ds(CUT, 432 - CUT)], sum_refs[2 + place // 4]
                target = ref.at[ry, place % 4]
            elif n == 2:
                source, target = got.at[ry, place, pl.ds(0, CUT)], sum_refs[ry].at[place]
            if n > 0:
                copies.append(pltpu.make_async_copy(source, target, out_sems.at[len(copies)]))
                copies[-1].start()
    for n, scr in enumerate((gu, gd, go)):
        half = scr.at[:, pl.ds(0, 8)]
        pltpu.make_async_copy(half, half, pair_sems.at[0, n]).wait()
    for copy in copies:
        copy.wait()


def feed_back(layer, lengths, base, extra, gains, gain_sum, saved, weights, number):
    mixed, h1, up, h2 = saved
    return pl.pallas_call(
        functools.partial(feed_back_kernel, len(weights), layer),
        out_shape=(
            jax.ShapeDtypeStruct((256, 768), F32),
            jax.ShapeDtypeStruct((16, 32, 384), BF16),
            jax.ShapeDtypeStruct((8, 768), F32),
            jax.ShapeDtypeStruct((8, CUT, 384), BF16),
            jax.ShapeDtypeStruct((8, CUT, 384), BF16),
            jax.ShapeDtypeStruct((2, 4, 432 - CUT, 384), BF16),
            jax.ShapeDtypeStruct((2, 4, 432 - CUT, 384), BF16),
        ),
        in_specs=[smem()] + [vmem()] * 8 + [hbm() for _ in weights],
        out_specs=(vmem(), vmem(), vmem(), hbm(), hbm(), hbm(), hbm()),
        scratch_shapes=WEIGHT_SCRATCH
        + [
            pltpu.VMEM((2, 16, 192, 384), BF16),
            pltpu.VMEM((2, 16, 192, 384), BF16),
            pltpu.VMEM((2, 16, 48, 384), BF16),
            pltpu.VMEM((2, 8, 432, 384), BF16),
            pltpu.SemaphoreType.DMA((3,)),
            pltpu.SemaphoreType.DMA((2, 3)),
            pltpu.SemaphoreType.DMA((32,)),
        ],
        compiler_params=pltpu.CompilerParams(
            collective_id=number, has_side_effects=True, vmem_limit_bytes=56 * 2**20
        ),
        cost_estimate=pl.CostEstimate(
            flops=6 * 10**9, bytes_accessed=40 * 10**6, transcendentals=10**6
        ),
        name="feed_back",
    )(lengths, base, extra, gains, gain_sum, mixed, h1, up, h2, *weights)


def flip(index, bits):
    for bit in (1, 2, 4, 8):
        if bits & bit:
            index = index + bit - 2 * bit * ((index // bit) % 2)
    return index


def greet(peers):
    barrier = pltpu.get_barrier_semaphore()
    for peer in peers:
        pl.semaphore_signal(barrier, inc=1, device_id=peer, device_id_type=MESH)
    pl.semaphore_wait(barrier, len(peers))


def remote(source, target, sems, n, peer):
    return pltpu.make_async_remote_copy(
        source, target, sems.at[0, n], sems.at[1, n], device_id=peer, device_id_type=MESH
    )


def comm_params(number):
    return pltpu.CompilerParams(
        collective_id=number, has_side_effects=True, vmem_limit_bytes=16 * 2**20
    )


class Spread:
    def __init__(self, low_ref, x_ref, sems, own_sem):
        self.low_ref, self.x_ref, self.sems = low_ref, x_ref, sems
        self.docs, self.me = lax.axis_index("docs"), lax.axis_index("seq")
        self.own = pltpu.make_async_copy(low_ref.at[self.me // 4], x_ref.at[self.me], own_sem)
        self.hops, self.across, self.mates = [], [], []

    def send(self, source, slot, n, bits):
        peer = (self.docs, flip(self.me, bits))
        copy = remote(source, self.x_ref.at[slot], self.sems, n, peer)
        copy.start()
        return copy

    def begin(self):
        for rz in range(1, 4):
            source = self.low_ref.at[flip(self.me, 4 * rz) // 4]
            self.hops.append(self.send(source, self.me, rz, 4 * rz))
        self.own.start()
        source = self.low_ref.at[self.me // 4]
        self.across.append(self.send(source, self.me, 4, 2))
        self.mates.append(self.send(source, self.me, 8, 1))

    def forward(self, rz):
        self.hops[rz - 1].wait_recv()
        slot = flip(self.me, 4 * rz)
        self.across.append(self.send(self.x_ref.at[slot], slot, 4 + rz, 2))
        self.mates.append(self.send(self.x_ref.at[slot], slot, 8 + rz, 1))

    def from_beside(self):
        for rz in range(4):
            self.across[rz].wait_recv()
            slot = flip(flip(self.me, 4 * rz), 2)
            self.mates.append(self.send(self.x_ref.at[slot], slot, 12 + rz, 1))

    def arrived(self):
        for copy in self.mates:
            copy.wait_recv()
        self.own.wait()

    def finish(self):
        for copy in self.hops + self.across + self.mates:
            copy.wait_send()


class Slabs:
    def __init__(self, source, w_ref, sems, own_sem, docs_first=False):
        self.source, self.w_ref, self.sems = source, w_ref, sems
        self.docs, self.me = lax.axis_index("docs"), lax.axis_index("seq")
        self.plane, self.x, self.core = self.me // 4, (self.me // 2) % 2, self.me % 2
        beside, over = (self.docs, flip(self.me, 2)), (1 - self.docs, self.me)
        self.peers = (over, beside) if docs_first else (beside, over)
        if docs_first:
            self.near = ((self.docs, self.x), (1 - self.docs, self.x))
            self.far = ((self.docs, 1 - self.x), (1 - self.docs, 1 - self.x))
        else:
            self.near = ((self.docs, self.x), (self.docs, 1 - self.x))
            self.far = ((1 - self.docs, self.x), (1 - self.docs, 1 - self.x))
        self.mate = (self.docs, flip(self.me, 1))
        self.own = pltpu.make_async_copy(source, self.slot(self.near[0], self.plane), own_sem)

    def slot(self, at, z):
        return self.w_ref.at[self.core, 8 * at[0] + 2 * z + at[1]]

    def copy(self, at, z, own, send, recv, peer):
        slot = self.slot(at, z)
        return pltpu.make_async_remote_copy(
            self.source if own else slot,
            slot,
            self.sems.at[0, send],
            self.sems.at[1, recv],
            device_id=peer,
            device_id_type=MESH,
        )

    def line(self, z, own, step):
        peer = (self.docs, self.me + 4 * step)
        return self.copy(self.near[0], z, own, z + (0 if step > 0 else 4), z, peer)

    def first(self, z, own=False):
        return self.copy(self.near[0], z, own, 8 + z, 8 + z, self.peers[0])

    def second(self, z, n, own=False):
        return self.copy(self.near[n], z, own, 12 + 4 * n + z, 12 + 4 * n + z, self.peers[1])

    def core_copy(self, at, n, z, own=False):
        return self.copy(at, z, own, 20 + 4 * n + z, 20 + 4 * n + z, self.mate)

    def begin(self):
        self.own.start()
        for step in (1, -1):
            pl.when(self.has(self.plane + step))(self.line(self.plane, True, step).start)
        self.first(self.plane, True).start()
        self.core_copy(self.near[0], 0, self.plane, True).start()

    def has(self, z):
        return jnp.logical_and(z >= 0, z < PLANES)

    def each(self, distance, act):
        if distance == 0:
            act(self.plane, 0)
            return
        for step in (1, -1):
            z = self.plane - step * distance
            pl.when(self.has(z))(functools.partial(act, z, step))

    def from_line(self, distance):
        def act(z, step):
            self.line(z, False, step).wait_recv()
            pl.when(self.has(self.plane + step))(self.line(z, False, step).start)
            self.first(z).start()
            self.core_copy(self.near[0], 0, z).start()

        self.each(distance, act)

    def from_first(self, distance):
        def act(z, step):
            self.first(z).wait_recv()
            self.second(z, 0, distance == 0).start()
            self.second(z, 1).start()
            self.core_copy(self.near[1], 1, z).start()

        self.each(distance, act)

    def from_second(self, distance):
        def act(z, step):
            for n in range(2):
                self.second(z, n).wait_recv()
                self.core_copy(self.far[n], 2 + n, z).start()

        self.each(distance, act)

    def arrived(self):
        for z in range(PLANES):
            for n, at in enumerate(self.near + self.far):
                self.core_copy(at, n, z).wait_recv()
        self.own.wait()

    def finish(self):
        for z in range(PLANES):
            for step in (1, -1):
                sent = jnp.logical_and(
                    (self.plane - z) * step >= 0, self.has(self.plane + step)
                )
                pl.when(sent)(self.line(z, False, step).wait_send)
            self.first(z).wait_send()
            for n, at in enumerate(self.near + self.far):
                if n < 2:
                    self.second(z, n).wait_send()
                self.core_copy(at, n, z).wait_send()


class Rows:
    def __init__(self, source, w_ref, sems, own_sem):
        self.source, self.w_ref, self.sems = source, w_ref, sems
        self.docs, self.me = lax.axis_index("docs"), lax.axis_index("seq")
        self.over = (1 - self.docs, self.me)
        self.own = pltpu.make_async_copy(source, self.slot(self.me // 4), own_sem)
        self.hops, self.moved = [], []

    def slot(self, z):
        return self.w_ref.at[pl.ds(8 * self.docs + 2 * z, 2)]

    def begin(self):
        target = self.slot(self.me // 4)
        for rz in range(1, 4):
            peer = (self.docs, flip(self.me, 4 * rz))
            self.hops.append(remote(self.source, target, self.sems, rz, peer))
            self.hops[-1].start()
        self.own.start()
        self.moved.append(remote(self.source, target, self.sems, 4, self.over))
        self.moved[0].start()

    def forward(self, rz):
        self.hops[rz - 1].wait_recv()
        slot = self.slot(flip(self.me, 4 * rz) // 4)
        self.moved.append(remote(slot, slot, self.sems, 4 + rz, self.over))
        self.moved[-1].start()

    def arrived(self):
        for copy in self.moved:
            copy.wait_recv()
        self.own.wait()

    def finish(self):
        for copy in self.hops + self.moved:
            copy.wait_send()


class Collect:
    def __init__(self, keep_ref, send_ref, land, got_core, got_x, sum_x, near, sums, sems):
        self.keep_ref, self.send_ref, self.land, self.got_core = keep_ref, send_ref, land, got_core
        self.got_x, self.sum_x, self.near, self.sums, self.sems = got_x, sum_x, near, sums, sems
        self.docs, self.me = lax.axis_index("docs"), lax.axis_index("seq")
        self.order = (3, 2, 1, 0)
        self.first, self.across, self.hops = {}, {}, []

    def begin(self):
        mate = (self.docs, flip(self.me, 1))
        for rz in self.order:
            for n in (2 * rz + 1, 2 * rz):
                self.first[n] = remote(
                    self.send_ref.at[n], self.got_core.at[n], self.sems, n, mate
                )
                self.first[n].start()

    def along_x(self):
        beside = (self.docs, flip(self.me, 2))
        for rz in self.order:
            n = 2 * rz + 1
            self.first[n].wait_recv()
            self.sum_x[rz] = add_low(self.keep_ref[n], self.got_core[n])
            self.across[rz] = remote(
                self.sum_x.at[rz], self.got_x.at[rz], self.sems, 8 + rz, beside
            )
            self.across[rz].start()
            n = 2 * rz
            self.first[n].wait_recv()
            self.near[rz] = add_full(self.keep_ref[n], self.got_core[n])

    def along_z(self):
        plane = self.me // 4
        for rz in self.order:
            self.across[rz].wait_recv()
            total = add_low(self.near[rz], self.got_x[rz])
            if rz == 0:
                self.land[plane] = total
            else:
                self.sums[rz] = total
                peer = (self.docs, flip(self.me, 4 * rz))
                copy = remote(self.sums.at[rz], self.land.at[plane], self.sems, 12 + rz, peer)
                copy.start()
                self.hops.append(copy)

    def finish(self):
        for copy in self.hops:
            copy.wait_recv()
        for copy in list(self.first.values()) + list(self.across.values()) + self.hops:
            copy.wait_send()


class Exchange:
    def __init__(self, source, land, sems, own_sem):
        docs, me = lax.axis_index("docs"), lax.axis_index("seq")
        self.copies = []
        for bits in range(15, 0, -1):
            peer = flip(me, bits)
            self.copies.append(remote(source.at[peer], land.at[me], sems, bits, (docs, peer)))
        self.own = pltpu.make_async_copy(source.at[me], land.at[me], own_sem)

    def begin(self):
        for copy in self.copies:
            copy.start()
        self.own.start()

    def arrived(self):
        for copy in self.copies:
            copy.wait_recv()
        self.own.wait()

    def finish(self):
        for copy in self.copies:
            copy.wait_send()


class Line:
    PLACE = (0, 2, 1, 3)

    def __init__(self, own, from_left, from_right, sems):
        self.own, self.landing, self.sems = own, (from_left, from_right), sems
        self.docs, self.me = lax.axis_index("docs"), lax.axis_index("seq")
        self.plane = self.me // 4

    def copy(self, place, target, step):
        side = 0 if step > 0 else 1
        return pltpu.make_async_remote_copy(
            self.own.at[place],
            self.landing[side].at[target],
            self.sems.at[0, side, target],
            self.sems.at[1, side, target],
            device_id=(self.docs, self.me + 4 * step),
            device_id_type=MESH,
        )

    def at(self, plane, act):
        pl.when(self.plane == plane)(act)

    def begin(self, rz):
        for plane, step in ((0, 1), (3, -1)):
            self.at(plane, self.copy(self.PLACE[rz], plane ^ rz, step).start)

    def hop(self, number):
        for plane, target, step in (
            ((1, 3, 1), (2, 0, -1)),
            ((1, 0, -1), (2, 3, 1)),
            ((1, 2, 1), (2, 1, -1)),
        )[number]:
            place, side = self.PLACE[plane ^ target], 0 if step > 0 else 1

            def act(place=place, side=side, target=target, step=step):
                copy = self.copy(place, target, step)
                copy.wait_recv()
                self.own[place] = add_low(self.own[place], self.landing[side][target])
                copy.start()

            self.at(plane, act)

    def total(self, out_ref, rows):
        for plane in range(PLANES):

            def act(plane=plane):
                total = self.own[0, rows].astype(F32)
                for side, step in ((0, 1), (1, -1)):
                    if 0 <= plane - step < PLANES:
                        total = total + self.landing[side][plane, rows].astype(F32)
                out_ref[...] = total

            self.at(plane, act)

    def arrived(self):
        for plane in range(PLANES):

            def act(plane=plane):
                for step in (1, -1):
                    if 0 <= plane - step < PLANES:
                        self.copy(0, plane, step).wait_recv()

            self.at(plane, act)

    def finish(self):
        for plane in range(PLANES):

            def act(plane=plane):
                for target in range(PLANES):
                    step = 1 if target > plane else -1
                    if target != plane:
                        self.copy(self.PLACE[plane ^ target], target, step).wait_send()

            self.at(plane, act)


class Everywhere:
    def __init__(self, total, got, sems):
        self.total, self.got, self.sems = total, got, sems
        docs, me = lax.axis_index("docs"), lax.axis_index("seq")
        self.peers = [(docs, flip(me, bits)) for bits in (1, 2, 4, 8)] + [(1 - docs, me)]
        self.copies = []

    def step(self):
        n = len(self.copies)
        if n > 0:
            self.copies[-1].wait_recv()
            self.total[n] = self.total[n - 1] + self.got[n - 1]
        if n < len(self.peers):
            copy = remote(self.total.at[n], self.got.at[n], self.sems, n, self.peers[n])
            copy.start()
            self.copies.append(copy)

    def finish(self):
        for copy in self.copies:
            copy.wait_send()


class Rest:
    ORDER = (3, 1, 2, 0)

    def __init__(self, a_keep, a_send, b_keep, b_send, scr):
        self.a_keep, self.a_send, self.b_keep, self.b_send = a_keep, a_send, b_keep, b_send
        self.scr = scr
        docs, me = lax.axis_index("docs"), lax.axis_index("seq")
        self.beside, self.over = (docs, flip(me, 2)), (1 - docs, me)
        self.line = Line(scr.own, scr.left, scr.right, scr.line_sems)
        self.sent = []

    def copy(self, n, place):
        scr = self.scr
        source, target, peer = (
            (self.a_send.at[4 + place], scr.a_got.at[4 + place], self.over),
            (self.b_send.at[1, place], scr.b_got.at[1, place], self.beside),
            (self.a_send.at[place], scr.a_got.at[place], self.over),
            (self.b_send.at[0, place], scr.b_got.at[0, place], self.beside),
            (scr.a_far.at[place], scr.a_far_got.at[place], self.beside),
            (scr.b_far.at[place], scr.b_far_got.at[place], self.over),
        )[n]
        return remote(source, target, scr.rest_sems, 4 * n + place, peer)

    def start(self, n, place):
        self.sent.append(self.copy(n, place))
        self.sent[-1].start()

    def first(self, place):
        for n in range(4):
            self.start(n, place)

    def second(self, place):
        scr = self.scr
        self.copy(0, place).wait_recv()
        scr.a_far[place] = add_low(self.a_keep[4 + place], scr.a_got[4 + place])
        self.start(4, place)
        self.copy(1, place).wait_recv()
        scr.b_far[place] = add_low(self.b_keep[1, place], scr.b_got[1, place])
        self.start(5, place)

    def third(self, place):
        scr = self.scr
        self.copy(2, place).wait_recv()
        self.copy(4, place).wait_recv()
        near = add_full(self.a_keep[place], scr.a_got[place]) + scr.a_far_got[place].astype(F32)
        scr.own[place, :CUT] = near.astype(BF16)
        self.copy(3, place).wait_recv()
        self.copy(5, place).wait_recv()
        near = add_full(self.b_keep[0, place], scr.b_got[0, place])
        near = near + scr.b_far_got[place].astype(F32)
        scr.own[place, CUT:] = near.astype(BF16)
        if place > 0:
            self.line.begin(Line.PLACE[place])

    def finish(self):
        for copy in self.sent:
            copy.wait_send()
        self.line.finish()


class Route:
    def __init__(self, source, out_ref, sems):
        self.source, self.out_ref, self.sems = source, out_ref, sems
        self.docs, self.me = lax.axis_index("docs"), lax.axis_index("seq")

    def each(self, act_here, act_there):
        for t in range(3):
            local = 3 * (self.me // 4) + t
            number = 16 * (local // 4) + 4 * (self.me % 4) + local % 4
            owner, slot = number // 3, number % 3
            target = self.out_ref.at[slot]
            here = pltpu.make_async_copy(self.source.at[t], target, self.sems.at[2, slot])
            there = pltpu.make_async_remote_copy(
                self.source.at[t],
                target,
                self.sems.at[0, t],
                self.sems.at[1, slot],
                device_id=(self.docs, owner),
                device_id_type=MESH,
            )
            pl.when(owner == self.me)(functools.partial(act_here, here))
            pl.when(owner != self.me)(functools.partial(act_there, there))

    def begin(self):
        self.each(lambda copy: copy.start(), lambda copy: copy.start())

    def finish(self):
        self.each(lambda copy: copy.wait(), lambda copy: copy.wait_send())
        for slot in range(3):
            number = 3 * self.me + slot
            local = 4 * (number // 16) + number % 4
            source = 4 * (local // 3) + (number % 16) // 4
            target = self.out_ref.at[slot]
            wait = pltpu.make_async_copy(target, target, self.sems.at[1, slot]).wait
            pl.when(source != self.me)(wait)


def back_scratch(width):
    low = 432 - CUT
    sems = pltpu.SemaphoreType.DMA

    def vm(*shape, dtype=BF16):
        return pltpu.VMEM(shape, dtype)

    return dict(
        qkv=vm(1024, 576),
        weight=vm(CHIPS, 48, 640),
        x=vm(16, 64, width),
        a_keep=vm(8, CUT, 384),
        b_keep=vm(2, 4, low, 384),
        load_sems=sems((5,)),
        do=vm(16, 32, 384),
        do_sems=sems((2, 16)),
        do_own=sems,
        key=vm(3, 1024, 128),
        query=vm(3, 1024, 128),
        value=vm(3, 1024, 64),
        turned=vm(3, 64, 1024),
        side=vm(2, 3, 1024, 128),
        dkv=vm(3, 1024, 128, dtype=F32),
        dq=vm(1024 // BACK_QUERIES, 192, BACK_QUERIES, dtype=F32),
        dqkv=vm(1024, 576),
        rows=vm(2, 8, 64, width),
        land=vm(4, 64, width),
        got_core=vm(8, 64, width),
        got_x=vm(4, 64, width),
        sum_x=vm(4, 64, width),
        near=vm(4, 64, width, dtype=F32),
        sums=vm(4, 64, width),
        row_sems=sems((2, 16)),
        a_got=vm(8, CUT, 384),
        b_got=vm(2, 4, low, 384),
        a_far=vm(4, CUT, 384),
        a_far_got=vm(4, CUT, 384),
        b_far=vm(4, low, 384),
        b_far_got=vm(4, low, 384),
        rest_sems=sems((2, 24)),
        own=vm(4, 432, 384),
        left=vm(4, 432, 384),
        right=vm(4, 432, 384),
        line_sems=sems((2, 2, 4)),
        q_grad=vm(2, 4, 144, 384),
        q_got=vm(4, 144, 384),
        q_own=vm(4, 144, 384),
        q_land=vm(4, 144, 384),
        q_sems=sems((2, 4)),
        q_sum=vm(3, 48, 384, dtype=F32),
        route_sems=sems((3, 3)),
        gain_sum=vm(6, 8, width, dtype=F32),
        gain_got=vm(5, 8, width, dtype=F32),
        gain_sems=sems((2, 5)),
    )


def attend_back_kernel(names, last, *refs):
    feature_ref, qkv_ref, do_ref, x_ref, w_ref, a_keep, a_send, b_keep, b_send = refs[:9]
    gain_ref, rows_ref, rest_ref, out_ref, gain_out_ref = refs[9:14]
    scr = types.SimpleNamespace(**dict(zip(names, refs[14:])))
    docs, me = lax.axis_index("docs"), lax.axis_index("seq")
    plane = me // 4
    over = (1 - docs, me)
    loads = {}
    for n, (name, ref) in enumerate(
        dict(qkv=qkv_ref, weight=w_ref, a_keep=a_keep, b_keep=b_keep, x=x_ref).items()
    ):
        loads[name] = pltpu.make_async_copy(ref, getattr(scr, name), scr.load_sems.at[n])
        loads[name].start()
    greet([(docs, flip(me, bits)) for bits in range(15, 0, -1)] + [over])
    exchange = Exchange(do_ref, scr.do, scr.do_sems, scr.do_own)
    exchange.begin()
    rest = Rest(scr.a_keep, a_send, scr.b_keep, b_send, scr)
    rest.first(3)
    rest.first(1)
    gains = Everywhere(scr.gain_sum, scr.gain_got, scr.gain_sems)
    if last:
        scr.gain_sum[0] = gain_ref[...]
        gains.step()

    loads["qkv"].wait()
    qkv = scr.qkv[...]
    spread_heads(qkv, feature_ref, scr.key, scr.query)
    zero = jnp.zeros((1024, 64), BF16)
    for h in range(GROUP_HEADS):
        scr.value[h] = qkv[:, 128 * h + 64 : 128 * h + 128]
        scr.turned[h] = qkv[:, 128 * h : 128 * h + 64].T
        scr.side[0, h] = jnp.concatenate([scr.query[h, :, :64], zero], axis=1)
    loads["a_keep"].wait()
    loads["b_keep"].wait()
    exchange.arrived()
    grad_o = jnp.concatenate([halves_below(scr.do[n]) for n in range(16)], axis=0)
    for h in range(GROUP_HEADS):
        scr.side[1, h] = jnp.concatenate([zero, grad_o[:, 64 * h : 64 * h + 64]], axis=1)

    def part(n, h):
        at = slice(BACK_QUERIES * n, BACK_QUERIES * n + BACK_QUERIES)
        expo, rate = expo_columns(dot_nt(scr.key[h], scr.query[h, at, :]))
        probs = expo * rate
        grad_probs = dot_nt(scr.value[h], scr.side[1, h, at, :][:, 64:])
        delta = jnp.sum(probs * grad_probs, axis=0, keepdims=True)
        grad_scores = (probs * (grad_probs - delta)).astype(BF16)
        scr.dq[n, 64 * h : 64 * h + 64, :] = dot(scr.turned[h], grad_scores) * (HEAD**-0.5)
        dkv = dot(grad_scores, scr.side[0, h, at, :])
        dkv += dot(probs.astype(BF16), scr.side[1, h, at, :])
        if n == 0:
            scr.dkv[h] = dkv
        else:
            scr.dqkv[:, 128 * h : 128 * h + 128] = (scr.dkv[h] + dkv).astype(BF16)

    part(0, 0)
    rest.second(3)
    rest.first(2)
    part(0, 1)
    if last:
        gains.step()
    part(0, 2)
    rest.second(1)
    scr.dqkv[0:512, 384:576] = scr.dq[0].T.astype(BF16)
    part(1, 0)
    rest.third(3)
    part(1, 1)
    rest.second(2)
    part(1, 2)
    rest.third(1)
    rest.line.hop(0)
    if last:
        gains.step()
    scr.dqkv[512:1024, 384:576] = scr.dq[1].T.astype(BF16)
    loads["x"].wait()
    grad = dot_tn(scr.dqkv[...], scr.x[...].reshape(1024, scr.x.shape[-1]))
    order = [6, 7, 8, 0, 2, 4, 1, 3, 5]
    grad = jnp.concatenate([grad[64 * n : 64 * n + 64] for n in order], axis=0).astype(BF16)
    for quarter in range(PLANES):
        apart = flip(plane, quarter)
        place = (apart % 2) * 2 + apart // 2
        for side in range(2):
            at = docs if side == 0 else 1 - docs
            scr.q_grad[at, place] = grad[
                144 * quarter : 144 * quarter + 144, 384 * side : 384 * side + 384
            ]
    crossed = remote(scr.q_grad.at[1], scr.q_got, scr.q_sems, 0, over)
    crossed.start()
    rest.first(0)
    loads["weight"].wait()
    rows = Collect(
        scr.rows.at[0],
        scr.rows.at[1],
        scr.land,
        scr.got_core,
        scr.got_x,
        scr.sum_x,
        scr.near,
        scr.sums,
        scr.row_sems,
    )
    for half in (1, 0):
        part_rows = []
        for n in range(8):
            block = flip(me, (n // 2) * 4 + (n % 2) * 2 + half)
            part_rows.append(scr.dqkv[pl.ds(pl.multiple_of(block * 64, 64), 64), :])
        product = dot_nt(jnp.concatenate(part_rows, axis=0), scr.weight[:, :, :576].reshape(-1, 576))
        scr.rows[half] = product.astype(BF16).reshape(scr.rows.shape[1:])
        if half == 1:
            rows.begin()
    rest.third(2)
    rest.line.hop(1)
    rows.along_x()
    if last:
        gains.step()
    crossed.wait_recv()
    turned = []
    for place in Rest.ORDER:
        rz = Line.PLACE[place]
        scr.q_own[place] = add_low(scr.q_grad[0, place], scr.q_got[place])
        if rz > 0:
            peer = (docs, flip(me, 4 * rz))
            turned.append(
                remote(scr.q_own.at[place], scr.q_land.at[place], scr.q_sems, place, peer)
            )
            turned[-1].start()
    rest.line.hop(2)
    rest.second(0)
    rows.along_z()
    if last:
        gains.step()
    for copy in turned:
        copy.wait_recv()
    total = scr.q_own[0].astype(F32)
    for place in range(1, PLANES):
        total = total + scr.q_land[place].astype(F32)
    scr.q_sum[...] = total.reshape(scr.q_sum.shape)
    route = Route(scr.q_sum, out_ref, scr.route_sems)
    route.begin()
    rest.third(0)
    if last:
        gains.step()
        gain_out_ref[...] = scr.gain_sum[5]
        gains.finish()
    else:
        gain_out_ref[...] = gain_ref[...]
    rest.line.arrived()
    rest.line.total(rest_ref, slice(0, 432))
    rows.finish()
    rows_ref[...] = scr.land[...]
    for piece in (exchange, rest, route):
        piece.finish()
    for copy in turned + [crossed]:
        copy.wait_send()


def attend_back(features, qkv, grad_o, x, weight, sums, gain_grads, last, number):
    width = x.shape[-1]
    scratch = back_scratch(width)
    return pl.pallas_call(
        functools.partial(attend_back_kernel, tuple(scratch), last),
        out_shape=(
            jax.ShapeDtypeStruct((PLANES, 64, width), BF16),
            jax.ShapeDtypeStruct((432, 384), F32),
            jax.ShapeDtypeStruct((3, 48, 384), F32),
            jax.ShapeDtypeStruct((8, width), F32),
        ),
        in_specs=[vmem()] + [hbm()] * 8 + [vmem()],
        out_specs=(vmem(), vmem(), hbm(), vmem()),
        scratch_shapes=list(scratch.values()),
        compiler_params=pltpu.CompilerParams(
            collective_id=number, has_side_effects=True, vmem_limit_bytes=56 * 2**20
        ),
        cost_estimate=pl.CostEstimate(
            flops=8 * 10**9, bytes_accessed=10 * 10**6, transcendentals=3 * 10**6
        ),
        name="attend_back",
    )(features, qkv, grad_o, x, weight, *sums, gain_grads)


def forward_scratch(width):
    sems = pltpu.SemaphoreType.DMA

    def vm(*shape, dtype=BF16):
        return pltpu.VMEM(shape, dtype)

    scratch = dict(
        x=vm(16, 64, width),
        weight=vm(CHIPS, 48, 640),
        qkv=vm(1024, 576),
        key=vm(3, 1024, 128),
        query=vm(3, 1024, 128),
        value=vm(3, 64, 1024),
        turned=vm(192, 1024, dtype=F32),
        o=vm(LAYERS, 16, 32, 384),
        o_got=vm(LAYERS, 16, 32, 384),
        mixed=vm(256, width),
        h1=vm(256, width, dtype=F32),
        up=vm(256, 4 * width, dtype=F32),
        h2=vm(256, width, dtype=F32),
        hidden=vm(256, width, dtype=F32),
        low=vm(4, 64, width),
        act=vm(256, 4 * width),
        wu=WEIGHT_SCRATCH[0],
        wd=WEIGHT_SCRATCH[1],
        wo=WEIGHT_SCRATCH[2],
        weight_sems=sems((3,)),
        load_sems=sems((3,)),
        own_sems=sems((2, 5)),
        save_sems=sems((2, 5)),
    )
    for layer in range(LAYERS):
        scratch[f"row_sems_{layer}"] = sems((2, 16))
        scratch[f"qkv_sems_{layer}"] = sems((2, 8))
        scratch[f"o_sems_{layer}"] = sems((2, 16))
        scratch[f"up_sems_{layer}"] = sems((2, 36))
        scratch[f"down_sems_{layer}"] = sems((2, 36))
    return scratch


def forward_kernel(names, *refs):
    lengths, globals_ref, random_ref, tokens_ref = refs[:4]
    wq_refs, up_refs, down_refs = (
        [ref.at[layer] for layer in range(LAYERS)] for ref in refs[4:7]
    )
    saved_refs = (refs[7:13], refs[13:19])
    w_refs, wu_refs, wd_refs, gains_ref, result_ref = refs[19:21], refs[21:23], refs[23:25], refs[25], refs[26]
    feature_ref = refs[27]
    scr = types.SimpleNamespace(**dict(zip(names, refs[28:])))
    docs, me = lax.axis_index("docs"), lax.axis_index("seq")
    pltpu.make_async_copy(tokens_ref, scr.low, scr.load_sems.at[2]).start()
    greet([(docs, flip(me, bits)) for bits in range(15, 0, -1)] + [(1 - docs, me)])

    def sems(name, layer):
        return getattr(scr, f"{name}_sems_{layer}")

    qkvs, slabs = [], []
    for layer in range(LAYERS):
        own = scr.own_sems.at[layer]
        qkvs.append(Rows(wq_refs[layer], w_refs[layer], sems("qkv", layer), own.at[0]))
        slabs.append(
            [
                Slabs(up_refs[layer], wu_refs[layer], sems("up", layer), own.at[1]),
                Slabs(down_refs[layer], wd_refs[layer], sems("down", layer), own.at[2], True),
            ]
        )

    def spread(layer, source):
        x_ref = saved_refs[layer][0]
        return Spread(source, x_ref, sems("row", layer), scr.own_sems.at[layer, 3])

    def every(parts, step, *arguments):
        for part in parts:
            getattr(part, step)(*arguments)

    def move(layer, *steps):
        for step in steps:
            name = {"l": "from_line", "f": "from_first", "s": "from_second"}[step[0]]
            every(slabs[layer], name, int(step[1]))

    def save(layer, n, source):
        copy = pltpu.make_async_copy(source, saved_refs[layer][n + 1], scr.save_sems.at[layer, n])
        copy.start()
        return copy

    saves = []

    def attend(layer, rows, ticks):
        qkvs[layer].arrived()
        rows.arrived()
        load_x = pltpu.make_async_copy(saved_refs[layer][0], scr.x, scr.load_sems.at[0])
        load_w = pltpu.make_async_copy(
            w_refs[layer], scr.weight, scr.load_sems.at[1]
        )
        load_x.start()
        load_w.start()
        while saves:
            saves.pop().wait()
        load_x.wait()
        load_w.wait()
        scr.qkv[...] = dot(
            scr.x[...].reshape(1024, scr.x.shape[-1]), scr.weight[:, :, :576].reshape(-1, 576)
        ).astype(BF16)
        if layer == 0:
            share = scr.x.shape[-1] // 32
            shares = [
                scr.weight[chip, 24 * core : 24 * core + 4, 576 : 576 + share]
                for chip in range(CHIPS)
                for core in range(2)
            ]
            gains_ref[0:4] = jnp.concatenate(shares, axis=1).astype(F32)
        saves.append(save(layer, 0, scr.qkv))
        qkv = scr.qkv[...]
        spread_heads(qkv, feature_ref, scr.key, scr.query)
        for h in range(GROUP_HEADS):
            scr.value[h] = qkv[:, 128 * h + 64 : 128 * h + 128].T
        exchange = Exchange(
            scr.o.at[layer], scr.o_got.at[layer], sems("o", layer), scr.own_sems.at[layer, 4]
        )
        for n in range(1024 // QUERIES):
            at = slice(QUERIES * n, QUERIES * n + QUERIES)
            for h in range(GROUP_HEADS):
                expo, rate = expo_columns(dot_nt(scr.key[h], scr.query[h, at, :]))
                scr.turned[64 * h : 64 * h + 64, at] = dot(
                    scr.value[h], (expo * rate).astype(BF16)
                )
                ticks.pop(0)()
            rows_o = scr.turned[:, at].T.astype(BF16)
            for m in range(QUERIES // 64):
                scr.o[layer, n * (QUERIES // 64) + m] = halves_beside(rows_o[64 * m : 64 * m + 64])
        exchange.begin()
        return exchange

    def feed(layer, exchange, ticks):
        exchange.arrived()
        slabs[layer][0].arrived()
        load_up(wu_refs[layer], scr.wu, scr.wo, scr.weight_sems)
        for k in range(PLANES):
            scr.mixed[64 * k : 64 * k + 64, :] = jnp.concatenate(
                [halves_below(scr.o_got[layer, 4 * k + g]) for g in range(GROUPS)], axis=1
            )
        saves.append(save(layer, 1, scr.mixed))
        mixed = scr.mixed[...]
        gain = gains_ref[2 * layer : 2 * layer + 2]
        ticks.pop(0)()
        wait_weight(scr.wo, scr.weight_sems.at[0])
        attended = jnp.concatenate(
            [dot(mixed, scr.wo[side].reshape(768, 384)) for side in range(2)], axis=1
        )
        before = scr.low[...].reshape(256, -1).astype(F32) if layer == 0 else scr.hidden[...]
        h1 = before + attended
        scr.h1[...] = h1
        saves.append(save(layer, 2, scr.h1))
        x1 = norm_parts(h1)[0] * gain[0:1, :]
        x1_low = x1.astype(BF16)
        wait_weight(scr.wu, scr.weight_sems.at[1])
        for side in range(2):
            for part in range(3):
                at = 1536 * side + 512 * part
                up = dot(x1_low, scr.wu[side, :, :, 512 * part : 512 * part + 512].reshape(768, 512))
                scr.up[:, at : at + 512] = up
                scr.act[:, at : at + 512] = gelu_parts(up)[0].astype(BF16)
            ticks.pop(0)()
        saves.append(save(layer, 3, scr.up))
        slabs[layer][1].arrived()
        load_down(wd_refs[layer], scr.wd, scr.weight_sems)
        wait_weight(scr.wd, scr.weight_sems.at[2])
        h2 = x1 + dot(scr.act[...], scr.wd[...].reshape(3072, 768))
        scr.h2[...] = h2
        saves.append(save(layer, 4, scr.h2))
        out = jnp.where(inside_rows(lengths), norm_parts(h2)[0] * gain[1:2, :], 0.0)
        low = out.astype(BF16)
        if layer == 0:
            scr.hidden[...] = out
            scr.low[...] = low.reshape(scr.low.shape)
        else:
            result_ref[...] = low.reshape(result_ref.shape)

    def nothing():
        pass

    def step(layer, *steps):
        return lambda: move(layer, *steps)

    rows_0 = spread(0, tokens_ref)
    rows_0.begin()
    qkvs[0].begin()
    every(slabs[0], "begin")
    key_features(lengths, globals_ref, random_ref, feature_ref)
    for rz in range(1, 4):
        rows_0.forward(rz)
        qkvs[0].forward(rz)
        if rz == 1:
            move(0, "f0")
    rows_0.from_beside()
    pltpu.make_async_copy(tokens_ref, scr.low, scr.load_sems.at[2]).wait()
    exchange_0 = attend(
        0,
        rows_0,
        [
            step(0, "l1"),
            nothing,
            step(0, "f1"),
            step(0, "l2"),
            lambda: every(slabs[1], "begin"),
            step(0, "s0"),
        ],
    )
    move(0, "l3", "f2", "s1", "f3")
    move(1, "l1")
    move(0, "s2")
    move(1, "l2")
    qkvs[1].begin()
    move(0, "s3")
    feed(0, exchange_0, [step(1, "l3"), step(1, "f0"), nothing])
    rows_1 = spread(1, scr.low)
    rows_1.begin()
    for rz in range(1, 4):
        rows_1.forward(rz)
    for rz in range(1, 4):
        qkvs[1].forward(rz)
    rows_1.from_beside()
    move(1, "f1", "f2")
    exchange_1 = attend(
        1,
        rows_1,
        [nothing, step(1, "f3"), nothing, step(1, "s0"), nothing, step(1, "s1")],
    )
    move(1, "s2", "s3")
    feed(1, exchange_1, [nothing] * 3)
    for copy in saves:
        copy.wait()
    every([rows_0, rows_1, exchange_0, exchange_1] + qkvs + slabs[0] + slabs[1], "finish")


def forward(lengths, global_ids, random_ids, tokens, wq, up, down, number):
    width = tokens.shape[-1]
    scratch = forward_scratch(width)

    def out(*shape, dtype=BF16):
        return jax.ShapeDtypeStruct(shape, dtype)

    saved = [
        out(16, 64, width),
        out(1024, 576),
        out(256, width),
        out(256, width, dtype=F32),
        out(256, 4 * width, dtype=F32),
        out(256, width, dtype=F32),
    ]
    shapes = saved + saved + [out(CHIPS, 48, 640)] * 2
    shapes += [out(2, CHIPS, 48, 1920)] * 2 + [out(2, CHIPS, 48, 1536)] * 2
    shapes += [out(4, width, dtype=F32), out(PLANES, 64, width), out(1024, 64)]
    return pl.pallas_call(
        functools.partial(forward_kernel, tuple(scratch)),
        out_shape=tuple(shapes),
        in_specs=[smem()] * 3 + [hbm()] * 4,
        out_specs=tuple([hbm()] * (len(shapes) - 3) + [vmem()] * 3),
        scratch_shapes=list(scratch.values()),
        compiler_params=pltpu.CompilerParams(
            collective_id=number, has_side_effects=True, vmem_limit_bytes=58 * 2**20
        ),
        name="forward",
    )(lengths, global_ids, random_ids, tokens, wq, up, down)


def pick(stack, index):
    return lax.dynamic_index_in_dim(stack, index, 0, keepdims=False)


def pack_qkv(shards, gains, rest, me, core):
    rows = shards.shape[1]
    parts = shards.reshape(LAYERS, rows, 3, GROUPS, GROUP_HEADS, HEAD)
    pairs = jnp.transpose(parts[:, :, 1:], (3, 0, 1, 4, 2, 5)).reshape(GROUPS, LAYERS, rows, 384)
    query = jnp.transpose(parts[:, :, 0], (2, 0, 1, 3, 4)).reshape(GROUPS, LAYERS, rows, 192)
    share = gains.shape[-1]
    beside = jnp.pad(gains.reshape(2 * LAYERS, share), ((0, rows - 2 * LAYERS), (0, 64 - share)))
    beside = jnp.broadcast_to(beside, (GROUPS, LAYERS, rows, 64))
    packed = jnp.concatenate([pairs, query, beside], axis=3)
    packed, rest = lax.optimization_barrier((packed, rest))
    group = me & 3
    got = [pick(packed, group)] + [swap(pick(packed, group ^ r), r) for r in range(1, 4)]

    def in_order(own, other):
        return jnp.where(
            core == 0,
            jnp.concatenate([own, other], axis=1),
            jnp.concatenate([other, own], axis=1),
        )

    here, there = in_order(got[0], got[1]), in_order(got[2], got[3])
    both = jnp.where(
        (me >> 1) & 1 == 0,
        jnp.stack([here, there], axis=1),
        jnp.stack([there, here], axis=1),
    )
    return both, rest


def pack_rest(out_weight, up_weight, down_weight, core):
    def mine(shard, side):
        half = shard.shape[2] // 2
        return jnp.where(side == 0, shard[:, :, :half], shard[:, :, half:])

    def both(side):
        return jnp.concatenate([mine(up_weight, side), mine(out_weight, side)], axis=2)

    own, got = both(core), swap(both(1 - core), 1)
    rows = jnp.where(
        core == 0,
        jnp.concatenate([own, got], axis=1),
        jnp.concatenate([got, own], axis=1),
    )
    return rows, jnp.concatenate([down_weight[:, :48], down_weight[:, 48:]], axis=2)


def add_low(first, second):
    return (first.astype(F32) + second.astype(F32)).astype(BF16)


def add_full(first, second):
    return first.astype(F32) + second.astype(F32)


def split_rest(total):
    down = total[240:].reshape(4, 48, 384)
    return (
        total[192:240].T,
        total[:192].T,
        jnp.transpose(down, (0, 2, 1)).reshape(1536, 48),
    )


def local_two_by_sixteen(
    tokens,
    qkv_weight,
    out_weight,
    up_weight,
    down_weight,
    norm_gains,
    doc_lengths,
    global_ids,
    random_ids,
    cotangent,
):
    docs_dev, block, width = tokens.shape
    me = lax.axis_index("seq").astype(jnp.int32)
    docs = lax.axis_index("docs").astype(jnp.int32)
    plane, core = me >> 2, me & 1
    chip = docs * 8 + (me >> 1)
    wq, rest = pack_qkv(qkv_weight, norm_gains, (out_weight, up_weight, down_weight), me, core)
    up, down = pack_rest(*rest, core)
    share = width // 32
    made = forward(doc_lengths, global_ids, random_ids, tokens, wq, up, down, 0)
    features = made[20]
    held, weights = (made[:6], made[6:12]), made[12:14]
    rest = list(zip(made[14:16], made[16:18]))
    gain = made[18]
    base, grad_o, gain_grads, *sums = feed_back(
        1, doc_lengths, cotangent, gain, gain, gain, held[1][2:], rest[1], 1
    )
    extra, rest_grads_1, qkv_1, gain_grads = attend_back(
        features, held[1][1], grad_o, held[1][0], weights[1], sums, gain_grads, False, 2
    )
    base, grad_o, gain_grads, *sums = feed_back(
        0, doc_lengths, base, extra, gain, gain_grads, held[0][2:], rest[0], 3
    )
    extra, rest_grads, qkv_0, gain_grads = attend_back(
        features, held[0][1], grad_o, held[0][0], weights[0], sums, gain_grads, True, 4
    )
    grad_tokens = base.reshape(docs_dev, block, width) + extra.astype(F32)
    gain_grads = lax.dynamic_slice_in_dim(gain_grads, (docs * 16 + me) * share, share, axis=1)
    rest = [split_rest(part) for part in (rest_grads, rest_grads_1)]
    qkv_grads = jnp.stack([qkv_0, qkv_1])
    return (
        made[19],
        grad_tokens,
        jnp.transpose(qkv_grads, (0, 3, 1, 2)).reshape(LAYERS, 384, 144),
        *(jnp.stack(pair) for pair in zip(*rest)),
        gain_grads[:4].reshape(LAYERS, 2, share),
    )


def solution(mesh):
    def local(*args):
        docs_dev, _, width = args[0].shape
        if fits(mesh, docs_dev, width // HEAD):
            return local_two_by_sixteen(*args)
        return local_any_mesh(*args)

    return jax.shard_map(
        local,
        mesh=mesh,
        in_specs=(
            P("docs", "seq", None),
            P(None, ("docs", "seq"), None),
            P(None, ("docs", "seq"), None),
            P(None, ("docs", "seq"), None),
            P(None, ("docs", "seq"), None),
            P(None, None, ("docs", "seq")),
            P("docs"),
            P("docs", None),
            P(None, "docs", None),
            P("docs", "seq", None),
        ),
        out_specs=(
            P("docs", "seq", None),
            P("docs", "seq", None),
            P(None, "docs", "seq"),
            P(None, "docs", "seq"),
            P(None, "docs", "seq"),
            P(None, "docs", "seq"),
            P(None, None, ("docs", "seq")),
        ),
        check_vma=False,
    )
```
